32 devices in a mesh: section: 2 (over core), dp: 4 (over z), tensor: 4 (over y, x).
Axes of the slice: x: 2, y: 2, z: 4, core: 2. Of those that a mesh axis runs over, the one named last changes fastest.
Arguments:
- tokens: bfloat16 [4, 1, 1024, 768], P(None, None, ('dp', 'tensor')), may hold values from -6 to 6
- cotangent: bfloat16 [4, 1, 1024, 768], P(None, None, ('dp', 'tensor')), may hold values from -6 to 6
- lengths: int32 [4, 1], replicated, may hold values from 256 to 1024, as said below
- random_blocks: int32 [2, 12, 16, 3], P('section', 'tensor'), may hold values from 2 to 15, as said below
- projections: bfloat16 [2, 3, 768, 768], P('section', None, 'dp', 'tensor'), may hold values from -0.21875 to 0.21875
- query_value_bias: bfloat16 [2, 2, 12, 64], P('section', None, 'tensor', 'dp'), may hold values from -3 to 3
- output_weight: bfloat16 [2, 768, 768], P('section', 'tensor', 'dp'), may hold values from -0.4375 to 0.4375
- expand_weight: bfloat16 [2, 768, 3072], P('section', 'dp', 'tensor'), may hold values from -0.21875 to 0.21875
- expand_bias: bfloat16 [2, 48, 64], P('section', 'tensor', 'dp'), may hold values from -3 to 3
- contract_weight: bfloat16 [2, 3072, 768], P('section', 'tensor', 'dp'), may hold values from -0.109375 to 0.109375
- norm_gains: bfloat16 [2, 2, 768], P('section', None, 'dp'), may hold values from 0.5 to 1.5
- row_biases: bfloat16 [2, 4, 768], P('section', None, 'dp'), may hold values from -2 to 2
Outputs:
- activations: bfloat16 [2, 4, 1, 1024, 768], P('section', None, None, ('dp', 'tensor'))
- input_grads: float32 [2, 4, 1, 1024, 768], P('section', None, None, ('dp', 'tensor'))
- projections_grad: float32 [2, 3, 768, 768], P('section', None, 'dp', 'tensor')
- query_value_bias_grad: float32 [2, 2, 12, 64], P('section', None, 'tensor', 'dp')
- output_weight_grad: float32 [2, 768, 768], P('section', 'tensor', 'dp')
- expand_weight_grad: float32 [2, 768, 3072], P('section', 'dp', 'tensor')
- expand_bias_grad: float32 [2, 48, 64], P('section', 'tensor', 'dp')
- contract_weight_grad: float32 [2, 3072, 768], P('section', 'tensor', 'dp')
- norm_gains_grad: float32 [2, 2, 768], P('section', None, 'dp')
- row_biases_grad: float32 [2, 4, 768], P('section', None, 'dp')
The draws below stay inside these ranges and needn't reach their ends.
Inputs may be any that keep to these rules, and one draw needn't show every extreme that they name: `lengths`: every length is at least 256; at least one slot of the whole batch has length 1024. `random_blocks`: for each layer, head and query block i the 3 numbers are distinct and none of them is below 2 or equal to i - 1, i or i + 1.
All inputs are finite; a program needn't handle non-finite values.
Results may differ from the reference program's by a relative error of at most 0.02.
Values may be sent and summed in bfloat16 or wider, within the bound.
No kernel may reach another device: no remote copies, remote signals or barrier semaphores. Data moves between devices by JAX's collectives and lax.ppermute only.
A program may use at most 192 MiB of HBM per device.

```python
from functools import partial
import jax
import jax.numpy as jnp
from jax import lax

HEADS = 12
HD = 64
D = 768
FF = 3072
BLOCK = 64
GLOBAL = 2
RAND = 3
KEYB = 8
MB = 4
SLOTS = 1
SLOT = 1024
NB = 16


def draw_lengths(key, part):
    key = jax.random.fold_in(key, 11)
    first_key, second_key = jax.random.split(key)
    drawn = jax.random.randint(first_key, (MB * SLOTS,), SLOT // 4, SLOT + 1)
    longest = jax.random.randint(second_key, (), 0, MB * SLOTS)
    drawn = jnp.where(jnp.arange(MB * SLOTS) == longest, SLOT, drawn)
    return drawn.reshape(MB, SLOTS).astype(jnp.int32)


def draw_random_blocks(key, part):
    key = jax.random.fold_in(key, 23)
    ranking = jax.random.randint(key, (2, HEADS, NB, NB), 0, 1 << 20)
    columns = jnp.arange(NB, dtype=jnp.int32)[None, None, None, :]
    own_rows = jnp.arange(NB, dtype=jnp.int32)[None, None, :, None]
    banned = (columns < GLOBAL) | (jnp.abs(columns - own_rows) <= 1)
    ranking = jnp.where(banned, -1, ranking * NB + columns)
    selected_entries = lax.top_k(ranking, RAND)[1]
    return selected_entries.astype(jnp.int32)


def levels(key, shape, cuts, smallest, largest):
    def one(dim, parts):
        heights = jax.random.uniform(jax.random.fold_in(jax.random.fold_in(key, 6), dim), (parts,), jnp.float32, smallest / len(cuts), largest / len(cuts))
        return jnp.repeat(jnp.exp(heights), shape[dim] // parts).reshape((-1,) + (1,) * (len(shape) - dim - 1))

    factor_of = one(*cuts[0])
    for cut in cuts[1:]:
        factor_of = factor_of * one(*cut)
    return factor_of


def gaussian(stream_key, dims, deviation, bound, cuts=(), kind=jnp.bfloat16):
    array = jax.random.normal(stream_key, dims, jnp.float32) * deviation
    if len(cuts) > 0:
        array = levels(stream_key, dims, cuts, -0.22, 0.18) * array
    return jnp.clip(array, min=-bound, max=bound).astype(kind)


def setup_inputs(seed: int = 0) -> dict:
    arg_keys = jax.random.split(jax.random.key(seed), 13)
    tokens = gaussian(arg_keys[0], (MB, SLOTS, SLOT, D), 1.0, 6.0, ((2, 16),))
    cotangent = gaussian(arg_keys[1], (MB, SLOTS, SLOT, D), 1.0, 6.0, ((2, 16),))
    lengths = draw_lengths(jax.random.fold_in(arg_keys[12], 71), 0)
    random_blocks = draw_random_blocks(jax.random.fold_in(arg_keys[12], 71), 0)
    projections = gaussian(arg_keys[4], (2, 3, D, D), D ** -0.5, 0.21875, ((0, 2), (2, 4), (3, 4)))
    query_value_bias = gaussian(arg_keys[5], (2, 2, HEADS, HD), 0.5, 3.0, ((0, 2), (2, 4), (3, 4)))
    output_weight = gaussian(arg_keys[6], (2, D, D), (D // 4) ** -0.5, 0.4375, ((0, 2), (1, 4), (2, 4)))
    expand_weight = gaussian(arg_keys[7], (2, D, FF), D ** -0.5, 0.21875, ((0, 2), (1, 4), (2, 4)))
    expand_bias = gaussian(arg_keys[8], (2, FF // HD, HD), 0.5, 3.0, ((0, 2), (1, 4), (2, 4)))
    contract_weight = gaussian(arg_keys[9], (2, FF, D), FF ** -0.5, 0.109375, ((0, 2), (1, 4), (2, 4)))
    norm_gains = jnp.clip(1.0 + 0.1 * jax.random.normal(arg_keys[10], (2, 2, D), jnp.float32), 0.5, 1.5).astype(jnp.bfloat16)
    row_biases = gaussian(arg_keys[11], (2, 4, D), 0.3, 2.0, ((0, 2), (2, 4)))
    return {"tokens": tokens, "cotangent": cotangent, "lengths": lengths, "random_blocks": random_blocks, "projections": projections, "query_value_bias": query_value_bias, "output_weight": output_weight, "expand_weight": expand_weight, "expand_bias": expand_bias, "contract_weight": contract_weight, "norm_gains": norm_gains, "row_biases": row_biases}


@jax.custom_vjp
def low(v):
    return lax.optimization_barrier(v.astype(jnp.bfloat16)).astype(jnp.float32)

@jax.custom_vjp
def low_back(v):
    return v

def low_keep(v):
    return (low(v), None)

def low_pass(kept, grad):
    return (grad,)

def back_keep(v):
    return (v, None)

def back_low(kept, grad):
    return (low(grad),)
low.defvjp(low_keep, low_pass)
low_back.defvjp(back_keep, back_low)
HIGHEST = lax.Precision.HIGHEST
EPSILON = 1e-12
MASKED = -1e+30

def normalize(values, gain_row, bias_row):
    average = lax.optimization_barrier(jnp.mean(values, axis=-1, keepdims=True))
    centered = values - average
    spread = lax.optimization_barrier(jnp.mean(centered * centered, axis=-1, keepdims=True))
    return centered * lax.rsqrt(spread + EPSILON) * gain_row + bias_row

def block_lists(random_ids):
    blocks = jnp.arange(NB, dtype=jnp.int32)
    leading = jnp.broadcast_to(jnp.arange(GLOBAL, dtype=jnp.int32), (NB, GLOBAL))
    window = jnp.stack([blocks - 1, blocks, blocks + 1], axis=1)
    fixed_ids = jnp.concatenate([leading, window], axis=1)
    fixed_ok = jnp.concatenate([jnp.ones((NB, GLOBAL), jnp.bool_), (blocks - 1 >= GLOBAL)[:, None], jnp.ones((NB, 1), jnp.bool_), (blocks + 1 < NB)[:, None]], axis=1)
    count_of_heads = random_ids.shape[0]
    key_ids = jnp.concatenate([jnp.broadcast_to(fixed_ids, (count_of_heads, NB, GLOBAL + 3)), random_ids.astype(jnp.int32)], axis=2)
    key_ok = jnp.concatenate([jnp.broadcast_to(fixed_ok, (count_of_heads, NB, GLOBAL + 3)), jnp.ones((count_of_heads, NB, RAND), jnp.bool_)], axis=2)
    return (jnp.clip(key_ids, 0, NB - 1), key_ok)

def attend_slot(packed, random_ids):
    query_rows, key_rows, value_rows, length = packed
    score_scale = HD ** (-0.5)

    def heads_first(source):
        return source.reshape(NB, BLOCK, HEADS, HD).transpose(2, 0, 1, 3)
    query_heads = heads_first(query_rows)
    key_heads = heads_first(key_rows)
    value_heads = heads_first(value_rows)
    key_ids, key_ok = block_lists(random_ids)
    picked_keys = jax.vmap(lambda source, selected_entries: source[selected_entries])(key_heads, key_ids)
    picked_values = jax.vmap(lambda source, selected_entries: source[selected_entries])(value_heads, key_ids)
    positions = key_ids[..., None] * BLOCK + jnp.arange(BLOCK, dtype=jnp.int32)
    allowed = (key_ok[..., None] & (positions < length)).reshape(HEADS, NB, 1, KEYB * BLOCK)
    scores = jnp.einsum('hiqd,himkd->hiqmk', query_heads, picked_keys, precision=HIGHEST) * score_scale
    scores = low_back(scores.reshape(HEADS, NB, BLOCK, KEYB * BLOCK))
    scores = jnp.where(allowed, scores, MASKED)
    log_total = jax.nn.logsumexp(scores, axis=-1, keepdims=True)
    weights = low(jnp.exp(scores - log_total))
    sparse_out = jnp.einsum('hiqn,hind->hiqd', weights, picked_values.reshape(HEADS, NB, KEYB * BLOCK, HD), precision=HIGHEST)
    leading_query = query_heads[:, :GLOBAL].reshape(HEADS, GLOBAL * BLOCK, HD)
    all_keys = key_heads.reshape(HEADS, SLOT, HD)
    all_values = value_heads.reshape(HEADS, SLOT, HD)
    dense_scores = low_back(jnp.einsum('hqd,hkd->hqk', leading_query, all_keys, precision=HIGHEST) * score_scale)
    dense_scores = jnp.where(jnp.arange(SLOT, dtype=jnp.int32) < length, dense_scores, MASKED)
    dense_total = jax.nn.logsumexp(dense_scores, axis=-1, keepdims=True)
    dense_weights = low(jnp.exp(dense_scores - dense_total))
    dense_out = jnp.einsum('hqk,hkd->hqd', dense_weights, all_values, precision=HIGHEST).reshape(HEADS, GLOBAL, BLOCK, HD)
    merged = jnp.concatenate([dense_out, sparse_out[:, GLOBAL:]], axis=1)
    return merged.transpose(1, 2, 0, 3).reshape(SLOT, HEADS * HD)

def layer(inputs, params, slot_lengths, random_ids):
    projections, query_value_bias, output_weight, expand_weight, expand_bias, contract_weight, norm_gains, row_biases = params
    projected = jnp.einsum('std,cde->cste', inputs, projections, precision=HIGHEST)
    queries = low_back(low(projected[0] + query_value_bias[0].reshape(D)))
    key_rows = low_back(low(projected[1]))
    value_rows = low_back(low(projected[2] + query_value_bias[1].reshape(D)))
    attend = jax.checkpoint(lambda packed: attend_slot(packed, random_ids))
    mixed_heads = low_back(low(lax.map(attend, (queries, key_rows, value_rows, slot_lengths))))
    attended = low_back(jnp.einsum('ste,ed->std', mixed_heads, output_weight, precision=HIGHEST)) + row_biases[0]
    middle = normalize(inputs + attended, norm_gains[0], row_biases[2])
    hidden = low_back(jnp.einsum('std,df->stf', low(middle), expand_weight, precision=HIGHEST) + expand_bias.reshape(FF))
    activated = low(jax.nn.gelu(hidden, approximate=True))
    feed_out = low_back(jnp.einsum('stf,fd->std', activated, contract_weight, precision=HIGHEST)) + row_biases[1]
    valid_rows = (jnp.arange(SLOT, dtype=jnp.int32)[None, :] < slot_lengths[:, None]).astype(jnp.float32)
    return normalize(middle + feed_out, norm_gains[1], row_biases[3]) * valid_rows[..., None]

def reference(tokens, cotangent, lengths, random_blocks, projections, query_value_bias, output_weight, expand_weight, expand_bias, contract_weight, norm_gains, row_biases):
    all_weights = (projections, query_value_bias, output_weight, expand_weight, expand_bias, contract_weight, norm_gains, row_biases)
    params = [tuple((weight[section_index].astype(jnp.float32) for weight in all_weights)) for section_index in range(2)]
    totals = [jax.tree.map(jnp.zeros_like, params[section_index]) for section_index in range(2)]
    first_outs, second_outs, first_grads, second_grads = ([], [], [], [])
    for micro_index in range(MB):
        inputs = tokens[micro_index].astype(jnp.float32)
        first_output, first_back = jax.vjp(partial(layer, slot_lengths=lengths[micro_index], random_ids=random_blocks[0]), inputs, params[0])
        second_output, second_back = jax.vjp(partial(layer, slot_lengths=lengths[micro_index], random_ids=random_blocks[1]), low(first_output), params[1])
        passed_grad, second_params = second_back(cotangent[micro_index].astype(jnp.float32))
        passed_grad = low(passed_grad)
        input_grad, first_params = first_back(passed_grad)
        totals[0] = jax.tree.map(jnp.add, totals[0], first_params)
        totals[1] = jax.tree.map(jnp.add, totals[1], second_params)
        first_outs.append(first_output.astype(jnp.bfloat16))
        second_outs.append(second_output.astype(jnp.bfloat16))
        first_grads.append(input_grad)
        second_grads.append(passed_grad)
    activations = jnp.stack([jnp.stack(first_outs), jnp.stack(second_outs)])
    input_grads = jnp.stack([jnp.stack(first_grads), jnp.stack(second_grads)])
    stacked = [jnp.stack([totals[0][position], totals[1][position]]) for position in range(8)]
    return (activations, input_grads, stacked[0], stacked[1], stacked[2], stacked[3], stacked[4], stacked[5], stacked[6], stacked[7])
```

```python
from functools import partial

import jax
import jax.numpy as jnp
from jax import lax
from jax.experimental import pallas as pl
from jax.experimental.pallas import tpu as pltpu
from jax.sharding import PartitionSpec as P

HD = 64
BLOCK = 64
GLOBAL = 2
EPSILON = 1e-12
MASKED = -1e30
GELU_A = 0.7978845608028654
GELU_B = 0.044715
F32 = jnp.float32
BF16 = jnp.bfloat16
MIB = 1 << 20


def nt(a, b):
    return lax.dot_general(a, b, (((1,), (1,)), ((), ())), preferred_element_type=F32)


def nn(a, b):
    return jnp.dot(a, b, preferred_element_type=F32)


def call(kernel, outs, *args, flops=0, limit=24):
    spec = pl.BlockSpec(memory_space=pltpu.VMEM)
    size = sum(a.size * a.dtype.itemsize for a in args)
    size += sum(o.size * o.dtype.itemsize for o in outs)
    return pl.pallas_call(
        kernel,
        out_shape=tuple(outs),
        in_specs=[spec] * len(args),
        out_specs=tuple(spec for _ in outs),
        compiler_params=pltpu.CompilerParams(vmem_limit_bytes=limit * MIB),
        cost_estimate=pl.CostEstimate(flops=flops, bytes_accessed=size, transcendentals=0),
    )(*args)


def sds(shape, dtype):
    return jax.ShapeDtypeStruct(shape, dtype)


def qkv_kernel(x_ref, w_ref, bias_ref, tail_ref, q_ref, kv_ref):
    kw = q_ref.shape[1]
    x = x_ref[...]
    q = (nn(x, w_ref[0]) + bias_ref[0:1]).astype(BF16)
    q_ref[...] = (q.astype(F32) * HD ** (-0.5)).astype(BF16)
    k = nn(x, w_ref[1]).astype(BF16)
    kv_ref[:, :kw] = (k.astype(F32) + tail_ref[...]).astype(BF16)
    kv_ref[:, kw:] = (nn(x, w_ref[2]) + bias_ref[1:2]).astype(BF16)


def head_mask(h, kw):
    lane = lax.broadcasted_iota(jnp.int32, (1, kw), 1)
    return ((lane >= h * HD) & (lane < (h + 1) * HD)).astype(F32)


def spread(allow_ref, h, rows, group):
    parts = [
        jnp.broadcast_to(allow_ref[h, g : g + 1, :], (group, allow_ref.shape[2]))
        for g in range(rows // group)
    ]
    return jnp.concatenate(parts, axis=0)


def attention_kernel(heads, chunk, q_ref, allow_ref, w_ref, *refs):
    parts, (out_ref, o_ref, total_ref) = (refs[:-3], refs[-3:])
    rows, kw = q_ref.shape
    group = rows // allow_ref.shape[1]
    k = jnp.concatenate([part[:, :kw] for part in parts], axis=0)
    vt = jnp.concatenate([part[:, kw:] for part in parts], axis=0).T
    q = q_ref[...].astype(F32)
    lines = []
    for h in range(heads):
        qa = (q * head_mask(h, kw) + spread(allow_ref, h, rows, group)).astype(BF16)
        vh = vt[h * HD : (h + 1) * HD]
        cells = []
        for c in range(0, rows, chunk):
            scores = nt(k, qa[c : c + chunk])
            top = jnp.max(scores, axis=0, keepdims=True)
            p = jnp.exp(scores - top)
            total = jnp.sum(p, axis=0, keepdims=True)
            cells.append(nn(vh, p.astype(BF16)) / total)
            total_ref[h : h + 1, c : c + chunk] = top + jnp.log(total)
        lines.append(jnp.concatenate(cells, axis=1))
    lines.append(jnp.zeros((kw - heads * HD, rows), F32))
    mixed = jnp.concatenate(lines, axis=0).T.astype(BF16)
    o_ref[...] = mixed
    out_ref[...] = nt(mixed, w_ref[3]).astype(BF16)


def attention_back_kernel(heads, chunk, grad_ref, w_ref, q_ref, allow_ref, o_ref, total_ref, *refs):
    count = (len(refs) - 1) // 2
    parts, dq_ref, outs = (refs[:count], refs[count], refs[count + 1 :])
    rows, kw = q_ref.shape
    group = rows // allow_ref.shape[1]
    k = jnp.concatenate([part[:, :kw] for part in parts], axis=0)
    v = jnp.concatenate([part[:, kw:] for part in parts], axis=0)
    kt = k.T
    q = q_ref[...].astype(F32)
    mixed_grad = nn(grad_ref[...], w_ref[3]).astype(BF16).astype(F32)
    product = mixed_grad * o_ref[...].astype(F32)
    masks = jnp.concatenate([head_mask(h, kw) for h in range(8)], axis=0)
    inner = lax.dot_general(
        masks,
        product,
        (((1,), (1,)), ((), ())),
        preferred_element_type=F32,
        precision=lax.Precision.HIGHEST,
    )
    dk = None
    dv = None
    lines = []
    for h in range(heads):
        qm = q * head_mask(h, kw)
        qa = (qm + spread(allow_ref, h, rows, group)).astype(BF16)
        qm = qm.astype(BF16)
        gm = (mixed_grad * head_mask(h, kw)).astype(BF16)
        kh = kt[h * HD : (h + 1) * HD]
        cells = []
        for c in range(0, rows, chunk):
            scores = nt(k, qa[c : c + chunk])
            p = jnp.exp(scores - total_ref[h : h + 1, c : c + chunk])
            dp = nt(v, gm[c : c + chunk])
            ds = (p * (dp - inner[h : h + 1, c : c + chunk])).astype(BF16)
            dv_term = nn(p.astype(BF16), gm[c : c + chunk])
            dk_term = nn(ds, qm[c : c + chunk])
            dv = dv_term if dv is None else dv + dv_term
            dk = dk_term if dk is None else dk + dk_term
            cells.append(nn(kh, ds))
        lines.append(jnp.concatenate(cells, axis=1))
    dq = jnp.concatenate(lines, axis=0).T * HD ** (-0.5)
    dq_ref[...] = dq.astype(BF16)
    start = 0
    for out in outs:
        size = out.shape[0]
        out[:, :kw] = dk[start : start + size].astype(BF16)
        out[:, kw:] = dv[start : start + size].astype(BF16)
        start += size


def projection_back_kernel(dq_ref, own_ref, other_ref, w_ref, triple_ref, out_ref, sums_ref):
    e = dq_ref.shape[1]
    kw = own_ref.shape[1] // 2
    dq = dq_ref[...]
    dkv = own_ref[...].astype(F32) + other_ref[...].astype(F32)
    dk = dkv[:, :e].astype(BF16)
    dv = dkv[:, kw : kw + e].astype(BF16)
    triple_ref[0] = dq
    triple_ref[1] = dk
    triple_ref[2] = dv
    total = nt(dq, w_ref[0, :, :e]) + nt(dk, w_ref[1, :, :e]) + nt(dv, w_ref[2, :, :e])
    out_ref[...] = total.astype(BF16)
    sums_ref[...] = jnp.zeros_like(sums_ref)
    sums_ref[0:1] = jnp.sum(dq.astype(F32), axis=0, keepdims=True)
    sums_ref[1:2] = jnp.sum(dv.astype(F32), axis=0, keepdims=True)


def norm(values):
    average = jnp.mean(values, axis=-1, keepdims=True)
    centered = values - average
    spread_now = jnp.mean(centered * centered, axis=-1, keepdims=True)
    inverse = lax.rsqrt(spread_now + EPSILON)
    return (centered * inverse, inverse)


def total_of(terms_ref):
    total = terms_ref[0].astype(F32)
    for i in range(1, terms_ref.shape[0]):
        total = total + terms_ref[i].astype(F32)
    return total


def first_norm_kernel(x_ref, terms_ref, vec_ref, middle_ref, low_ref, unit_ref, inverse_ref):
    values = x_ref[...].astype(F32) + total_of(terms_ref) + vec_ref[2:3]
    unit, inverse = norm(values)
    middle = unit * vec_ref[0:1] + vec_ref[4:5]
    middle_ref[...] = middle
    low_ref[...] = middle.astype(BF16)
    unit_ref[...] = unit
    inverse_ref[...] = inverse


def second_norm_kernel(middle_ref, terms_ref, vec_ref, valid_ref, low_ref, unit_ref, inverse_ref):
    unit, inverse = norm(middle_ref[...] + total_of(terms_ref) + vec_ref[3:4])
    result = (unit * vec_ref[1:2] + vec_ref[5:6]) * valid_ref[...]
    low_ref[...] = result.astype(BF16)
    unit_ref[...] = unit
    inverse_ref[...] = inverse


def norm_back(grad, unit, inverse, gain):
    scaled = grad * gain
    return inverse * (
        scaled
        - jnp.mean(scaled, axis=-1, keepdims=True)
        - unit * jnp.mean(scaled * unit, axis=-1, keepdims=True)
    )


def norm_sums(sums_ref, grad, unit, result):
    sums_ref[...] = jnp.zeros_like(sums_ref)
    sums_ref[0:1] = jnp.sum(grad * unit, axis=0, keepdims=True)
    sums_ref[1:2] = jnp.sum(grad, axis=0, keepdims=True)
    sums_ref[2:3] = jnp.sum(result, axis=0, keepdims=True)


def second_back_kernel(
    up_ref, valid_ref, unit_ref, inverse_ref, vec_ref, second_ref, low_ref, sums_ref
):
    grad = up_ref[...].astype(F32) * valid_ref[...]
    unit = unit_ref[...]
    second = norm_back(grad, unit, inverse_ref[...], vec_ref[1:2])
    second_ref[...] = second
    low_ref[...] = second.astype(BF16)
    norm_sums(sums_ref, grad, unit, second)


def first_back_kernel(
    second_ref, terms_ref, unit_ref, inverse_ref, vec_ref, first_ref, low_ref, sums_ref
):
    grad = second_ref[...] + total_of(terms_ref)
    unit = unit_ref[...]
    first = norm_back(grad, unit, inverse_ref[...], vec_ref[0:1])
    first_ref[...] = first
    low_ref[...] = first.astype(BF16)
    norm_sums(sums_ref, grad, unit, first)


def input_kernel(first_ref, terms_ref, out_ref):
    out_ref[...] = (first_ref[...] + total_of(terms_ref)).astype(BF16)


def feed_kernel(x_ref, w_ref, vec_ref, active_ref, slope_ref, out_ref):
    v = nn(x_ref[...], w_ref[0]) + vec_ref[6:7]
    th = jnp.tanh(GELU_A * (v + GELU_B * v * v * v))
    half = 0.5 * (1.0 + th)
    slope = half + 0.5 * v * (1.0 - th * th) * GELU_A * (1.0 + 3.0 * GELU_B * v * v)
    active = (v * half).astype(BF16)
    active_ref[...] = active
    slope_ref[...] = slope.astype(BF16)
    out_ref[...] = nt(active, w_ref[1]).astype(BF16)


def feed_back_kernel(grad_ref, w_ref, slope_ref, hidden_ref, out_ref, sums_ref):
    active_grad = nn(grad_ref[...], w_ref[1])
    hidden = (active_grad * slope_ref[...].astype(F32)).astype(BF16)
    hidden_ref[...] = hidden
    sums_ref[...] = jnp.zeros_like(sums_ref)
    sums_ref[0:1] = jnp.sum(hidden.astype(F32), axis=0, keepdims=True)
    out_ref[...] = nt(hidden, w_ref[0]).astype(BF16)


def swap(x):
    return lax.ppermute(x, "section", [(0, 1), (1, 0)])


def gather_rows(x):
    return lax.all_gather(x, "tensor", axis=0, tiled=True)


def scatter_rows(x):
    size = lax.axis_size("tensor")
    parts = x.reshape(size, x.shape[0] // size, x.shape[1])
    return lax.all_to_all(parts, "tensor", 0, 0)


def deal(x, micro, plane, sub):
    section = lax.axis_index("section")
    place = lax.axis_index("dp")
    across = lax.axis_size("dp")
    odd = place % 2
    got = []
    for p in range(2):
        route = []
        for c in range(2):
            for d in range(across):
                r, dd = (d // micro, d % micro)
                m = 2 * c + (p ^ (dd & 1))
                route.append((c * across + d, (dd >> 1) * across + m * sub + r))
        chosen = 2 * section + (p ^ odd)
        payload = lax.dynamic_index_in_dim(x, chosen, 0, keepdims=False)
        got.append(lax.ppermute(payload, ("section", "dp"), route))
    flip = plane % 2 == 1
    return jnp.concatenate(
        [jnp.where(flip, got[1], got[0]), jnp.where(flip, got[0], got[1])], axis=0
    )


def undeal(pair, micro, plane, sub):
    section = lax.axis_index("section")
    across = lax.axis_size("dp")
    place = lax.axis_index("dp")
    rows = pair[0].shape[0] // 2
    stacked = jnp.concatenate(pair, axis=0).reshape(4, rows, pair[0].shape[1])
    got = [[None, None], [None, None]]
    for p in range(2):
        for u in range(2):
            route = []
            for s in range(2):
                for source in range(across):
                    m, r = (source // sub, source % sub)
                    j = p ^ (m & 1)
                    layer = u ^ (m >> 1)
                    route.append(
                        (s * across + source, layer * across + r * micro + 2 * s + j)
                    )
            j = p ^ (plane % 2)
            layer = u ^ (plane // 2)
            payload = lax.dynamic_index_in_dim(stacked, layer * 2 + j, 0, keepdims=False)
            got[p][u] = lax.ppermute(payload, ("section", "dp"), route)
    odd = place % 2 == 1
    late = section == 1
    result = []
    for m in range(micro):
        a, b = (m & 1, m >> 1)
        result.append(
            jnp.where(
                odd,
                jnp.where(late, got[1 - a][1 - b], got[1 - a][b]),
                jnp.where(late, got[a][1 - b], got[a][b]),
            )
        )
    return jnp.stack(result)


def body(
    tokens,
    cotangent,
    lengths,
    random_blocks,
    projections,
    query_value_bias,
    output_weight,
    expand_weight,
    expand_bias,
    contract_weight,
    norm_gains,
    row_biases,
):
    section = lax.axis_index("section")
    place = lax.axis_index("dp")
    seat = lax.axis_index("tensor")
    across = lax.axis_size("dp")
    ways = lax.axis_size("tensor")
    micro = tokens.shape[0]
    sub = across // micro
    plane = place // sub
    share = place % sub
    local = tokens.shape[2]
    width = tokens.shape[3]
    e = projections.shape[3]
    heads = e // HD
    units = expand_weight.shape[2]
    slice_width = projections.shape[2]
    bias_width = query_value_bias.shape[3]
    rows = 2 * local * ways
    keys = rows * 2 * sub
    blocks = keys // BLOCK
    kw = -(-(e + blocks + 1) // 128) * 128
    first = section == 0

    x0 = deal(tokens[:, 0], micro, plane, sub)
    upstream = deal(cotangent[:, 0], micro, plane, sub)

    attn_shard = jnp.concatenate([projections[0], output_weight[0].T[None]], axis=0)
    feed_shard = jnp.stack([expand_weight[0], contract_weight[0].T])
    small = jnp.concatenate(
        [query_value_bias.reshape(1, -1), expand_bias.reshape(1, -1),
         norm_gains.reshape(1, -1), row_biases.reshape(1, -1)], axis=1
    )
    small_all = lax.all_gather(small, ("section", "dp"), axis=0, tiled=True).astype(F32)
    random_all = lax.all_gather(random_blocks, "section", axis=0, tiled=True)
    attn_own = lax.all_gather(attn_shard, "dp", axis=0)
    feed_own = lax.all_gather(feed_shard, "dp", axis=0)
    attn_other = swap(attn_own)
    feed_other = swap(feed_own)

    def arranged(own, other, pad):
        natural = jnp.where(first, own, other).transpose(1, 0, 2, 3)
        natural = natural.reshape(natural.shape[0], width, natural.shape[3])
        return jnp.pad(natural, ((0, 0), (0, 0), (0, pad)))

    attn_weights = [
        arranged(attn_own, attn_other, kw - e),
        arranged(attn_other, attn_own, kw - e),
    ]
    feed_weights = [arranged(feed_own, feed_other, 0), arranged(feed_other, feed_own, 0)]

    small_all = small_all.reshape(2, across, -1)
    cuts = (2 * heads * bias_width, units // HD * bias_width, 2 * slice_width, 4 * slice_width)
    pieces = []
    begin = 0
    for cut in cuts:
        pieces.append(small_all[:, :, begin : begin + cut])
        begin += cut
    pair_bias = pieces[0].reshape(2, across, 2, heads, bias_width).transpose(0, 2, 3, 1, 4)
    pair_bias = jnp.pad(pair_bias.reshape(2, 2, e), ((0, 0), (0, 0), (0, kw - e)))
    unit_bias = pieces[1].reshape(2, across, units // HD, bias_width).transpose(0, 2, 1, 3)
    unit_bias = unit_bias.reshape(2, 1, units)
    gains = pieces[2].reshape(2, across, 2, slice_width).transpose(0, 2, 1, 3).reshape(2, 2, width)
    biases = pieces[3].reshape(2, across, 4, slice_width).transpose(0, 2, 1, 3).reshape(2, 4, width)
    vectors = jnp.concatenate([gains, biases, unit_bias, jnp.zeros((2, 1, width), F32)], axis=1)

    length = lax.dynamic_index_in_dim(lengths[:, 0], plane, 0, keepdims=False)
    group_start = (share * micro + 2 * section) * ways * local
    gathered = (
        group_start
        + jnp.arange(ways, dtype=jnp.int32)[:, None, None] * local
        + jnp.arange(2, dtype=jnp.int32)[None, :, None] * ways * local
        + jnp.arange(local, dtype=jnp.int32)[None, None, :]
    )
    mine = lax.dynamic_index_in_dim(gathered, seat, 0, keepdims=False).reshape(2 * local, 1)
    valid = (mine < length).astype(F32)
    gathered = gathered.reshape(rows, 1)
    lane = jnp.arange(kw, dtype=jnp.int32)[None, :]
    key_tail = jnp.where(
        lane == e + gathered // BLOCK,
        1.0,
        jnp.where((lane == e + blocks) & (gathered >= length), MASKED, 0.0),
    ).astype(F32)
    query_block = gathered[::local, 0] // BLOCK
    block_now = query_block[None, :, None]
    picked = jnp.take(random_all, query_block, axis=2)
    key_block = (lane - e)[0][None, None, :]
    seen = (
        (block_now < GLOBAL)
        | (key_block < GLOBAL)
        | (jnp.abs(key_block - block_now) <= 1)
        | jnp.any(picked[..., None] == key_block[None, :, :, None, :], axis=3)
    )
    inside = (key_block >= 0) & (key_block < blocks)
    allow = jnp.where(inside & ~seen, MASKED, 0.0)
    allow = jnp.where(key_block == blocks, 1.0, allow).astype(F32)

    def all_parts(own):
        pair = [own, swap(own)]
        if sub == 1:
            return pair
        groups = [[m * sub + r for r in range(sub)] for m in range(micro)]
        return [
            lax.all_gather(
                jnp.concatenate(pair, axis=0), "dp", axis=0, tiled=True, axis_index_groups=groups
            )
        ]

    def own_parts(parts):
        if sub == 1:
            return parts
        groups = [[m * sub + r for r in range(sub)] for m in range(micro)]
        total = lax.psum_scatter(
            parts[0], "dp", scatter_dimension=0, tiled=True, axis_index_groups=groups
        )
        return [total[:rows], total[rows:]]

    chunk = min(rows, 256)
    mine_rows = 2 * local
    row_norm = [
        sds((mine_rows, width), BF16),
        sds((mine_rows, width), F32),
        sds((mine_rows, 1), F32),
    ]

    saved = []
    x = x0
    for l in range(2):
        wa, wf, vec = (attn_weights[l], feed_weights[l], vectors[l])
        x_all = gather_rows(x)
        q, kv = call(
            qkv_kernel,
            [sds((rows, kw), BF16), sds((rows, 2 * kw), BF16)],
            x_all, wa, pair_bias[l], key_tail,
            flops=6 * rows * width * kw,
        )
        parts = all_parts(kv)
        attended, mixed, totals = call(
            partial(attention_kernel, heads, chunk),
            [sds((rows, width), BF16), sds((rows, kw), BF16), sds((8, rows), F32)],
            q, allow[l], wa, *parts,
            flops=4 * rows * keys * kw, limit=40,
        )
        middle, middle_low, unit1, inverse1 = call(
            first_norm_kernel,
            [sds((mine_rows, width), F32)] + row_norm,
            x, scatter_rows(attended), vec,
        )
        middle_all = gather_rows(middle_low)
        active, slope, fed = call(
            feed_kernel,
            [sds((rows, units), BF16), sds((rows, units), BF16), sds((rows, width), BF16)],
            middle_all, wf, vec,
            flops=4 * rows * width * units, limit=32,
        )
        low, unit2, inverse2 = call(
            second_norm_kernel, row_norm, middle, scatter_rows(fed), vec, valid
        )
        saved.append(
            (x_all, q, parts, mixed, totals, unit1, inverse1, middle_all, active, slope,
             unit2, inverse2, low)
        )
        x = low

    grads = [None, None]
    inputs_low = [None, None]
    for l in (1, 0):
        wa, wf, vec = (attn_weights[l], feed_weights[l], vectors[l])
        (x_all, q, parts, mixed, totals, unit1, inverse1, middle_all, active, slope,
         unit2, inverse2, low) = saved[l]
        norm_outs = [
            sds((mine_rows, width), F32), sds((mine_rows, width), BF16), sds((8, width), F32)
        ]
        second, feed_low, second_sums = call(
            second_back_kernel, norm_outs, upstream, valid, unit2, inverse2, vec
        )
        feed_grad = gather_rows(feed_low)
        hidden, fed_back, unit_sums = call(
            feed_back_kernel,
            [sds((rows, units), BF16), sds((rows, width), BF16), sds((8, units), F32)],
            feed_grad, wf, slope,
            flops=4 * rows * width * units, limit=32,
        )
        expand_grad = jnp.einsum("nd,nf->df", middle_all, hidden, preferred_element_type=F32)
        contract_grad = jnp.einsum("nd,nf->df", feed_grad, active, preferred_element_type=F32)
        feed_pack = jnp.stack([expand_grad.astype(BF16), contract_grad.astype(BF16)])
        first_grad, first_low, first_sums = call(
            first_back_kernel, norm_outs, second, scatter_rows(fed_back), unit1, inverse1, vec
        )
        attended_grad = gather_rows(first_low)
        back = call(
            partial(attention_back_kernel, heads, chunk),
            [sds((rows, e), BF16)] + [sds(part.shape, BF16) for part in parts],
            attended_grad, wa, q, allow[l], mixed, totals, *parts,
            flops=10 * rows * keys * kw, limit=48,
        )
        dkv_own, dkv_other = own_parts(list(back[1:]))
        triple, projected, pair_sums = call(
            projection_back_kernel,
            [sds((3, rows, e), BF16), sds((rows, width), BF16), sds((8, e), F32)],
            back[0], dkv_own, swap(dkv_other), wa,
            flops=6 * rows * width * kw,
        )
        output_grad = jnp.einsum(
            "nd,ne->de", attended_grad, mixed[:, :e], preferred_element_type=F32
        )
        projections_grad = jnp.einsum("nd,cne->cde", x_all, triple, preferred_element_type=F32)
        attn_pack = jnp.concatenate(
            [projections_grad.astype(BF16), output_grad.astype(BF16)[None]], axis=0
        )
        (input_low,) = call(
            input_kernel, [sds((mine_rows, width), BF16)], first_grad, scatter_rows(projected)
        )
        inputs_low[l] = input_low
        upstream = input_low
        pair_row = jnp.pad(
            pair_sums[:2].reshape(1, 2 * e), ((0, 0), (0, width - 2 * e))
        )
        small_grad = jnp.concatenate(
            [first_sums[0:1], second_sums[0:1], first_sums[2:3], second_sums[2:3],
             first_sums[1:2], second_sums[1:2], unit_sums[0:1], pair_row], axis=0
        )
        grads[l] = (
            lax.psum_scatter(attn_pack, "dp", scatter_dimension=1, tiled=True),
            lax.psum_scatter(feed_pack, "dp", scatter_dimension=1, tiled=True),
            small_grad,
        )

    def settled(index):
        sent = jnp.where(first, grads[1][index], grads[0][index])
        kept = jnp.where(first, grads[0][index], grads[1][index])
        return kept.astype(F32) + swap(sent).astype(F32)

    attn_grad = settled(0)
    feed_grads = settled(1)
    small_pair = jnp.stack([grads[0][2], grads[1][2]])
    small_pair = lax.psum(small_pair, ("section", "dp"))
    small_own = lax.dynamic_index_in_dim(small_pair, section, 0, keepdims=False)
    norm_rows = lax.psum(small_own[:6], "tensor")
    norm_rows = norm_rows.reshape(6, across, slice_width)
    norm_rows = lax.dynamic_index_in_dim(norm_rows, place, 1, keepdims=False)
    unit_row = lax.dynamic_index_in_dim(
        small_own[6].reshape(units // HD, across, bias_width), place, 1, keepdims=False
    )
    pair_rows = lax.dynamic_index_in_dim(
        small_own[7, : 2 * e].reshape(2, heads, across, bias_width), place, 2, keepdims=False
    )
    activations = undeal([saved[0][-1], saved[1][-1]], micro, plane, sub)
    input_grads = undeal(inputs_low, micro, plane, sub).astype(F32)
    return (
        activations[None, :, None],
        input_grads[None, :, None],
        attn_grad[None, :3],
        pair_rows[None],
        attn_grad[3].T[None],
        feed_grads[0][None],
        unit_row[None],
        feed_grads[1].T[None],
        norm_rows[None, :2],
        norm_rows[None, 2:],
    )


def solution(mesh):
    in_specs = (
        P(None, None, ("dp", "tensor"), None),
        P(None, None, ("dp", "tensor"), None),
        P(),
        P("section", "tensor", None, None),
        P("section", None, "dp", "tensor"),
        P("section", None, "tensor", "dp"),
        P("section", "tensor", "dp"),
        P("section", "dp", "tensor"),
        P("section", "tensor", "dp"),
        P("section", "tensor", "dp"),
        P("section", None, "dp"),
        P("section", None, "dp"),
    )
    out_specs = (
        P("section", None, None, ("dp", "tensor"), None),
        P("section", None, None, ("dp", "tensor"), None),
        P("section", None, "dp", "tensor"),
        P("section", None, "tensor", "dp"),
        P("section", "tensor", "dp"),
        P("section", "dp", "tensor"),
        P("section", "tensor", "dp"),
        P("section", "tensor", "dp"),
        P("section", None, "dp"),
        P("section", None, "dp"),
    )
    return jax.shard_map(body, mesh=mesh, in_specs=in_specs, out_specs=out_specs, check_vma=False)
```

```python
import math
from functools import partial

import jax
import jax.numpy as jnp
from jax import lax
from jax.experimental import pallas as pl
from jax.experimental.pallas import tpu as pltpu
from jax.sharding import PartitionSpec as P

HD = 64
BLOCK = 64
GLOBAL = 2
EPSILON = 1e-12
MASKED = -1e30
GELU_A = 0.7978845608028654
GELU_B = 0.044715
F32 = jnp.float32
BF16 = jnp.bfloat16
MIB = 1 << 20
PLACES = ("section", "dp")


def nt(a, b):
    return lax.dot_general(a, b, (((1,), (1,)), ((), ())), preferred_element_type=F32)


def tn(a, b):
    return lax.dot_general(a, b, (((0,), (0,)), ((), ())), preferred_element_type=F32)


def nn(a, b):
    return jnp.dot(a, b, preferred_element_type=F32)


def sds(shape, dtype):
    return jax.ShapeDtypeStruct(shape, dtype)


class Far:
    def __init__(self, array, shape=None, cuts=None, plain=False):
        self.array = array
        self.shape = array.shape if shape is None else shape
        self.cuts = [((), ())] if cuts is None else cuts
        self.plain = plain


def at(ref, index):
    return ref.at[index] if index else ref


class Arriving:
    def __init__(self, source, buffer, sems, first, cuts):
        self.buffer = buffer
        self.shape = buffer.shape
        self.copies = [
            pltpu.make_async_copy(at(source, a), at(buffer, b), sems.at[first + i])
            for i, (a, b) in enumerate(cuts)
        ]
        for copy in self.copies:
            copy.start()
        self.there = False

    def settle(self):
        if not self.there:
            for copy in self.copies:
                copy.wait()
            self.there = True

    def __getitem__(self, index):
        self.settle()
        return self.buffer[index]


class Leaving:
    def __init__(self, target, buffer, sem):
        self.target = target
        self.buffer = buffer
        self.shape = target.shape
        self.sem = sem
        self.copy = None

    def __setitem__(self, index, value):
        self.buffer[index] = value

    def send(self, source=None):
        self.copy = pltpu.make_async_copy(
            self.buffer if source is None else source, self.target, self.sem
        )
        self.copy.start()

    def finish(self):
        if self.copy is None:
            self.send()
        self.copy.wait()


def call(kernel, outs, *args, flops=0, limit=16, scratch=()):
    arrays = []
    in_specs = []
    out_specs = []
    out_shapes = []
    buffers = []
    size = 0
    semaphores = 0
    for arg in args:
        if isinstance(arg, Far):
            arrays.append(pltpu.with_memory_space_constraint(arg.array, pltpu.HBM))
            in_specs.append(pl.BlockSpec(memory_space=pltpu.HBM))
            buffers.append(pltpu.VMEM(arg.shape, arg.array.dtype))
            semaphores += len(arg.cuts)
            size += math.prod(arg.shape) * arg.array.dtype.itemsize
        else:
            arrays.append(arg)
            scalar = arg.dtype == jnp.int32
            in_specs.append(pl.BlockSpec(memory_space=pltpu.SMEM if scalar else pltpu.VMEM))
            size += arg.size * arg.dtype.itemsize
    for out in outs:
        if isinstance(out, Far):
            out_shapes.append(pltpu.HBM(out.shape, out.array.dtype))
            out_specs.append(pl.BlockSpec(memory_space=pltpu.HBM))
            if not out.plain:
                buffers.append(pltpu.VMEM(out.shape, out.array.dtype))
            semaphores += 1
            size += math.prod(out.shape) * out.array.dtype.itemsize
        else:
            out_shapes.append(out)
            out_specs.append(pl.BlockSpec(memory_space=pltpu.VMEM))
            size += out.size * out.dtype.itemsize

    def whole(*refs):
        refs = list(refs)
        ins = refs[: len(args)]
        results = refs[len(args) : len(args) + len(outs)]
        rest = refs[len(args) + len(outs) :]
        sems = rest.pop() if semaphores else None
        given = []
        used = 0
        for arg, ref in zip(args, ins):
            if isinstance(arg, Far):
                given.append(Arriving(ref, rest.pop(0), sems, used, arg.cuts))
                used += len(arg.cuts)
            else:
                given.append(ref)
        leaving = []
        for out, ref in zip(outs, results):
            if isinstance(out, Far):
                buffer = None if out.plain else rest.pop(0)
                leaving.append(Leaving(ref, buffer, sems.at[used]))
                given.append(leaving[-1])
                used += 1
            else:
                given.append(ref)
        kernel(*given, *rest)
        for item in given:
            if isinstance(item, Arriving):
                item.settle()
        for item in leaving:
            item.finish()

    scratch_shapes = buffers + list(scratch)
    if semaphores:
        scratch_shapes = scratch_shapes + [pltpu.SemaphoreType.DMA((semaphores,))]
    return pl.pallas_call(
        whole,
        out_shape=tuple(out_shapes),
        in_specs=in_specs,
        out_specs=tuple(out_specs),
        scratch_shapes=scratch_shapes,
        compiler_params=pltpu.CompilerParams(vmem_limit_bytes=limit * MIB),
        cost_estimate=pl.CostEstimate(flops=flops, bytes_accessed=size, transcendentals=0),
    )(*arrays)


SECTION, PLACE, PLANE, SEAT, START, LENGTH, FLIP = range(7)


def positions(where_ref, count, ways, local, first):
    row = lax.broadcasted_iota(jnp.int32, (count, 1), 0) + first
    group = jnp.bitwise_xor(row // local % 2, where_ref[FLIP])
    return (
        where_ref[START] + group * (ways * local) + row // (2 * local) * local + row % local
    )


def core_is(where_ref, core):
    return pl.when(where_ref[SECTION] == core)


def prepare_kernel(
    where_ref, projections_ref, output_ref, expand_ref, contract_ref, pair_ref, unit_ref,
    gain_ref, bias_ref, attn_out, keep_out, send_out, small
):
    step, e = projections_ref.shape[2:]
    heads, _, c = pair_ref.shape[1:]
    attn_out[:step, :e] = projections_ref[0, 0]
    attn_out[:step, e : 2 * e] = projections_ref[0, 2]
    attn_out[:step, 2 * e : 3 * e] = projections_ref[0, 1]
    attn_out[:step, 3 * e :] = output_ref[0].T
    small[...] = jnp.zeros_like(small)
    small[0:2, :step] = gain_ref[0].astype(F32)
    small[2:6, :step] = bias_ref[0].astype(F32)
    small[: unit_ref.shape[1], 256 : 256 + c] = unit_ref[0].astype(F32)
    for i in range(heads):
        small[i : i + 1, 384 : 384 + c] = pair_ref[0, i, 0:1].astype(F32)
        small[i : i + 1, 512 : 512 + c] = pair_ref[0, i, 1:2].astype(F32)
    attn_out[step:] = small[...].astype(BF16)
    attn_out.send()
    expand = expand_ref[0]
    contract = contract_ref[0]

    @core_is(where_ref, 0)
    def _():
        keep_out[...] = expand
        send_out[...] = contract

    @core_is(where_ref, 1)
    def _():
        keep_out[...] = contract
        send_out[...] = expand


def unpack_kernel(c, e, raw_ref, vec_ref, pair_ref):
    places = raw_ref.shape[0]
    width = vec_ref.shape[1]
    w = width // places

    def of_heads(rows, lanes, z):
        source = lax.broadcasted_iota(jnp.int32, (128, lanes), 0)
        target = lax.broadcasted_iota(jnp.int32, (128, lanes), 1)
        repeat = ((target % c == source) & (source < c)).astype(F32).astype(BF16)
        spread_rows = nn(rows, repeat)
        head = lax.broadcasted_iota(jnp.int32, spread_rows.shape, 0)
        lane = lax.broadcasted_iota(jnp.int32, spread_rows.shape, 1)
        keep = (lane // HD == head) & (lane % HD // c == z)
        return jnp.sum(jnp.where(keep, spread_rows, 0.0), axis=0, keepdims=True)

    norms = jnp.zeros((16, width), F32)
    units = jnp.zeros((1, width), F32)
    queries = jnp.zeros((1, 256), F32)
    values = jnp.zeros((1, 256), F32)
    for z in range(places):
        rows = raw_ref[z]
        source = lax.broadcasted_iota(jnp.int32, (256, width), 0)
        target = lax.broadcasted_iota(jnp.int32, (256, width), 1)
        move = ((target == source + z * w) & (source < w)).astype(F32).astype(BF16)
        norms = norms + nn(rows[:, :256], move)
        units = units + of_heads(rows[:, 256:384], width, z)
        queries = queries + of_heads(rows[:, 384:512], 256, z)
        values = values + of_heads(rows[:, 512:640], 256, z)
    vec_ref[...] = norms[:8]
    vec_ref[6:7] = units
    pair_ref[...] = jnp.zeros_like(pair_ref)
    pair_ref[0:1] = jnp.where(lax.broadcasted_iota(jnp.int32, (1, 256), 1) < e, queries, 0.0)
    values = jnp.where(lax.broadcasted_iota(jnp.int32, (1, 256), 1) < e, values, 0.0)
    pair_ref[1:2] = pltpu.roll(values, 256 - e, 1)


def qkv_kernel(ways, local, blocks, e, where_ref, x_ref, w_ref, bias_ref, q_ref, kv_ref, *kept):
    kw = q_ref.shape[1]
    vw = kv_ref.shape[1] - kw
    x = x_ref[...]
    kept[0].send(x_ref)
    lead = 2 * e // 128 * 128
    q = (nn(x, w_ref[:, :256]) + bias_ref[0:1]).astype(BF16).astype(F32) * HD ** (-0.5)
    lane = lax.broadcasted_iota(jnp.int32, (1, 256), 1)
    q = jnp.where(lane < e, q, 0.0).astype(BF16)
    q_ref[:, :256] = q
    if kw > 256:
        q_ref[:, 256:] = jnp.zeros((q.shape[0], kw - 256), BF16)
    kept[1].send(q_ref)
    position = positions(where_ref, x.shape[0], ways, local, 0)
    block = position // BLOCK
    lane = lax.broadcasted_iota(jnp.int32, (1, kw), 1)
    hidden = (position >= where_ref[LENGTH]) & (lane == e + blocks)
    tail = jnp.where(lane == e + block, 1.0, jnp.where(hidden, MASKED, 0.0))
    k = nn(x, w_ref[:, lead : lead + 256])
    if kw > 256:
        k = jnp.concatenate([k, jnp.zeros((k.shape[0], kw - 256), F32)], axis=1)
    kv_ref[:, :kw] = jnp.where(lane < e, k, tail).astype(BF16)
    kv_ref[:, kw:] = (nn(x, w_ref[:, 128 : 128 + vw]) + bias_ref[1:2]).astype(BF16)
    kept[2].send(kv_ref)


def head_mask(first, lanes):
    lane = lax.broadcasted_iota(jnp.int32, (1, lanes), 1)
    return ((lane >= first) & (lane < first + HD)).astype(F32)


def seen_rows(where_ref, random_ref, layer, h, rows, ways, local, kw, e, blocks):
    lane = lax.broadcasted_iota(jnp.int32, (1, kw), 1)
    key = lane - e
    parts = []
    for g in range(rows // local):
        group = jnp.bitwise_xor(g % 2, where_ref[FLIP])
        position = where_ref[START] + group * (ways * local) + g // 2 * local
        block = position // BLOCK
        seen = (key < GLOBAL) | (jnp.abs(key - block) <= 1) | (block < GLOBAL)
        for i in range(random_ref.shape[3]):
            seen = seen | (key == random_ref[layer, h, block, i])
        hidden = (key >= 0) & (key < blocks) & jnp.logical_not(seen)
        line = jnp.where(key == blocks, 1.0, jnp.where(hidden, MASKED, 0.0))
        parts.append(jnp.broadcast_to(line, (local, kw)))
    return jnp.concatenate(parts, axis=0)


def attention_kernel(
    heads, layer, ways, local, blocks, chunk, count, where_ref, random_ref, q_ref, w_ref, *refs
):
    parts, (out_ref, mixed_out, total_out), kept = (
        refs[:count], refs[count : count + 3], refs[count + 3 :]
    )
    rows, kw = q_ref.shape
    e = heads * HD
    vw = parts[0].shape[1] - kw
    shift = vw - e
    for out, part in zip(kept, parts[1:]):
        out.send(part)
    k = jnp.concatenate([part[:, :kw] for part in parts], axis=0)
    vt = jnp.concatenate([part[:, kw:] for part in parts], axis=0).T
    q = q_ref[...].astype(F32)
    lines = [jnp.zeros((shift, rows), F32)]
    totals = []
    for h in range(heads):
        seen = seen_rows(where_ref, random_ref, layer, h, rows, ways, local, kw, e, blocks)
        qa = (q * head_mask(h * HD, kw) + seen).astype(BF16)
        vh = vt[shift + h * HD : shift + (h + 1) * HD]
        cells = []
        sums = []
        for c in range(0, rows, chunk):
            scores = nt(k, qa[c : c + chunk])
            top = jnp.max(scores, axis=0, keepdims=True)
            p = jnp.exp(scores - top)
            total = jnp.sum(p, axis=0, keepdims=True)
            cells.append(nn(vh, p.astype(BF16)) / total)
            sums.append(top + jnp.log(total))
        lines.append(jnp.concatenate(cells, axis=1))
        totals.append(jnp.concatenate(sums, axis=1))
    total_out[...] = jnp.concatenate(totals + [jnp.zeros((8 - heads, rows), F32)], axis=0)
    total_out.send()
    mixed = jnp.concatenate(lines, axis=0).T.astype(BF16)
    mixed_out[...] = mixed
    mixed_out.send()
    out_ref[...] = nt(mixed, w_ref[...]).astype(BF16)


def attention_back_kernel(
    heads, layer, ways, local, blocks, chunk, where_ref, random_ref, grad_ref, w_ref, mixed_ref,
    q_ref, total_ref, *refs
):
    count = (len(refs) - 2) // 2
    parts, dq_ref, small_ref, outs = (
        refs[:count], refs[count], refs[count + 1], refs[count + 2 :]
    )
    rows, kw = q_ref.shape
    e = heads * HD
    vw = mixed_ref.shape[1]
    shift = vw - e
    width = grad_ref.shape[2]
    grad = grad_ref[:, : 2 * local].reshape(rows, width)
    small = grad_ref[0, 2 * local :].astype(F32)
    for i in range(1, ways):
        small = small + grad_ref[i, 2 * local :].astype(F32)
    small_ref[...] = small
    mixed_grad = nn(grad, w_ref[...]).astype(BF16).astype(F32)
    product = mixed_grad * mixed_ref[...].astype(F32)
    masks = jnp.concatenate([head_mask(shift + h * HD, vw) for h in range(8)], axis=0)
    inner = lax.dot_general(
        masks, product, (((1,), (1,)), ((), ())),
        preferred_element_type=F32, precision=lax.Precision.HIGHEST,
    )
    q = q_ref[...].astype(F32)
    k = jnp.concatenate([part[:, :kw] for part in parts], axis=0)
    v = jnp.concatenate([part[:, kw:] for part in parts], axis=0)
    kt = k[:, :256].T
    totals = total_ref[...]
    dk = None
    dv = None
    lines = []
    for h in range(heads):
        seen = seen_rows(where_ref, random_ref, layer, h, rows, ways, local, kw, e, blocks)
        qm = q * head_mask(h * HD, kw)
        qa = (qm + seen).astype(BF16)
        qm = qm[:, :256].astype(BF16)
        gm = (mixed_grad * head_mask(shift + h * HD, vw)).astype(BF16)
        kh = kt[h * HD : (h + 1) * HD]
        cells = []
        for c in range(0, rows, chunk):
            scores = nt(k, qa[c : c + chunk])
            p = jnp.exp(scores - totals[h : h + 1, c : c + chunk])
            dp = nt(v, gm[c : c + chunk])
            ds = (p * (dp - inner[h : h + 1, c : c + chunk])).astype(BF16)
            dv_term = nn(p.astype(BF16), gm[c : c + chunk])
            dk_term = nn(ds, qm[c : c + chunk])
            dv = dv_term if dv is None else dv + dv_term
            dk = dk_term if dk is None else dk + dk_term
            cells.append(nn(kh, ds))
        lines.append(jnp.concatenate(cells, axis=1))
    lines.append(jnp.zeros((256 - e, rows), F32))
    dq = jnp.concatenate(lines, axis=0).T * HD ** (-0.5)
    dq_ref[...] = dq.astype(BF16)
    start = 0
    for out in outs:
        size = out.shape[0]
        out[:, :256] = dk[start : start + size].astype(BF16)
        out[:, 256:] = dv[start : start + size].astype(BF16)
        start += size


def projection_back_kernel(e, dq_ref, own_ref, other_ref, w_ref, triple_ref, out_ref, sums_ref):
    vw = own_ref.shape[1] - 256
    width = w_ref.shape[1]
    lead = 2 * e // 128 * 128
    rows = dq_ref.shape[0]
    dq = dq_ref[...]
    dkv = (own_ref[...].astype(F32) + other_ref[...].astype(F32)).astype(BF16).astype(F32)
    dv = dkv[:, 256:]
    head = dq.astype(F32)
    nothing = jnp.zeros((rows, 128), F32)
    triple = jnp.concatenate(
        [head[:, :128], head[:, 128:] + dv[:, :128], dv[:, 128:], dkv[:, :256], nothing], axis=1
    ).astype(BF16)
    triple_ref[...] = triple
    sums_ref[...] = jnp.zeros_like(sums_ref)
    sums_ref[0:1] = jnp.sum(triple.astype(F32), axis=0, keepdims=True)
    out_ref[...] = nt(triple, w_ref[...]).astype(BF16)


def norm(values):
    average = jnp.mean(values, axis=-1, keepdims=True)
    centered = values - average
    spread_now = jnp.mean(centered * centered, axis=-1, keepdims=True)
    inverse = lax.rsqrt(spread_now + EPSILON)
    return (centered * inverse, inverse)


def total_of(terms_ref):
    total = terms_ref[0].astype(F32)
    for i in range(1, terms_ref.shape[0]):
        total = total + terms_ref[i].astype(F32)
    return total


def first_norm_kernel(x_ref, terms_ref, vec_ref, middle_ref, low_ref, unit_out, inverse_out):
    values = x_ref[...].astype(F32) + total_of(terms_ref) + vec_ref[2:3]
    unit, inverse = norm(values)
    unit_out[...] = unit
    unit_out.send()
    inverse_out[...] = jnp.broadcast_to(inverse, inverse_out.shape)
    inverse_out.send()
    middle = unit * vec_ref[0:1] + vec_ref[4:5]
    middle_ref[...] = middle
    low_ref[...] = middle.astype(BF16)


def valid_rows(where_ref, ways, local):
    position = positions(where_ref, 2 * local, ways, local, where_ref[SEAT] * 2 * local)
    return (position < where_ref[LENGTH]).astype(F32)


def place_parts(where_ref, early, later, outs):
    half = early.shape[0] // 2
    late_plane = where_ref[PLANE] // 2
    for u in range(2):
        for p in range(2):
            @pl.when(late_plane == u)
            def _(u=u, p=p):
                outs[2 * p + u][...] = early[p * half : (p + 1) * half]

            @pl.when(late_plane != u)
            def _(u=u, p=p):
                outs[2 * p + u][...] = later[p * half : (p + 1) * half]


def second_norm_kernel(ways, where_ref, middle_ref, terms_ref, vec_ref, *refs):
    if len(refs) == 4:
        low_ref, kept, unit_out, inverse_out = refs
    else:
        early_ref, unit_out, inverse_out = (refs[0], refs[-2], refs[-1])
    unit, inverse = norm(middle_ref[...] + total_of(terms_ref) + vec_ref[3:4])
    unit_out[...] = unit
    unit_out.send()
    inverse_out[...] = jnp.broadcast_to(inverse, inverse_out.shape)
    inverse_out.send()
    result = unit * vec_ref[1:2] + vec_ref[5:6]
    low = (result * valid_rows(where_ref, ways, unit.shape[0] // 2)).astype(BF16)
    if len(refs) == 4:
        low_ref[...] = low
        kept.send(low_ref)
    else:
        place_parts(where_ref, early_ref[...], low, refs[1:5])


def norm_back(grad, unit, inverse, gain):
    scaled = grad * gain
    return inverse * (
        scaled
        - jnp.mean(scaled, axis=-1, keepdims=True)
        - unit * jnp.mean(scaled * unit, axis=-1, keepdims=True)
    )


def second_back_kernel(
    ways, where_ref, up_ref, vec_ref, unit_ref, inverse_ref, second_ref, low_ref, sums_ref
):
    grad = up_ref[...].astype(F32) * valid_rows(where_ref, ways, up_ref.shape[0] // 2)
    unit = unit_ref[...]
    second = norm_back(grad, unit, inverse_ref[:, 0:1], vec_ref[1:2])
    second_ref[...] = second
    low_ref[...] = second.astype(BF16)
    sums_ref[...] = jnp.zeros_like(sums_ref)
    sums_ref[0:1] = jnp.sum(grad * unit, axis=0, keepdims=True)
    sums_ref[1:2] = jnp.sum(grad, axis=0, keepdims=True)
    sums_ref[2:3] = jnp.sum(second, axis=0, keepdims=True)


def first_back_kernel(
    second_ref, terms_ref, vec_ref, before_ref, unit_ref, inverse_ref, first_ref, low_ref
):
    grad = second_ref[...] + total_of(terms_ref)
    unit = unit_ref[...]
    first = norm_back(grad, unit, inverse_ref[:, 0:1], vec_ref[0:1])
    first_ref[...] = first
    rows = first.shape[0]
    low_ref[:rows] = first.astype(BF16)
    before = before_ref[...]
    low_ref[rows:] = jnp.concatenate(
        [jnp.sum(grad * unit, axis=0, keepdims=True), before[0:1],
         jnp.sum(first, axis=0, keepdims=True), before[2:3],
         jnp.sum(grad, axis=0, keepdims=True), before[1:2],
         jnp.zeros((10, first.shape[1]), F32)], axis=0
    ).astype(BF16)


def input_kernel(first_ref, terms_ref, out_ref, kept):
    out_ref[...] = (first_ref[...] + total_of(terms_ref)).astype(BF16)
    kept.send(out_ref)


def last_input_kernel(where_ref, first_ref, terms_ref, later_ref, *outs):
    low = (first_ref[...] + total_of(terms_ref)).astype(BF16)
    place_parts(where_ref, low, later_ref[...], outs)


def place_out_kernel(where_ref, *refs):
    out_ref = refs[-1]
    odd = where_ref[PLACE] % 2
    for p in range(2):
        for u in range(2):
            m = 2 * jnp.bitwise_xor(where_ref[SECTION], u) + jnp.bitwise_xor(odd, p)
            out_ref[0, m, 0] = refs[2 * p + u][...].astype(out_ref.dtype)


def feed_kernel(x_ref, vec_ref, expand_ref, contract_ref, out_ref, active_out, slope_out, kept):
    kept.send(x_ref)
    v = nn(x_ref[...], expand_ref[...]) + vec_ref[6:7]
    th = jnp.tanh(GELU_A * (v + GELU_B * v * v * v))
    half = 0.5 * (1.0 + th)
    active = (v * half).astype(BF16)
    active_out[...] = active
    active_out.send()
    slope = half + 0.5 * v * (1.0 - th * th) * GELU_A * (1.0 + 3.0 * GELU_B * v * v)
    slope_out[...] = slope.astype(BF16)
    slope_out.send()
    out_ref[...] = nt(active, contract_ref[...]).astype(BF16)


def feed_back_kernel(
    grad_ref, contract_ref, slope_ref, expand_ref, hidden_ref, out_ref, sums_ref
):
    active_grad = nn(grad_ref[...], contract_ref[...])
    hidden = (active_grad * slope_ref[...].astype(F32)).astype(BF16)
    hidden_ref[...] = hidden
    sums_ref[...] = jnp.zeros_like(sums_ref)
    sums_ref[0:1] = jnp.sum(hidden.astype(F32), axis=0, keepdims=True)
    out_ref[...] = nt(hidden, expand_ref[...]).astype(BF16)


def feed_pack_kernel(where_ref, hidden_ref, grad_ref, middle_ref, active_ref, keep_ref, send_ref):
    def put(value, core):
        @core_is(where_ref, core)
        def _():
            keep_ref[...] = value

        @core_is(where_ref, 1 - core)
        def _():
            send_ref[...] = value

    put(tn(middle_ref[...], hidden_ref[...]).astype(BF16), 0)
    put(tn(grad_ref[...], active_ref[...]).astype(BF16), 1)


def attn_pack_kernel(
    relative, step, e, where_ref, triple_ref, grad_ref, norm_ref, unit_ref, pair_ref, x_ref,
    mixed_ref, out_ref, whole
):
    x = x_ref[...]
    width = x.shape[1]
    vw = mixed_ref.shape[1]
    places = width // step
    local = grad_ref.shape[1] - 16
    grad = grad_ref[:, :local].reshape(x.shape)
    total = tn(x, triple_ref[...])
    last = total[:, width - vw :] + tn(grad, mixed_ref[...])
    whole[:, : width - vw] = total[:, : width - vw].astype(BF16)
    whole[:, width - vw :] = last.astype(BF16)
    small = jnp.concatenate(
        [norm_ref[:6], unit_ref[0:1], pair_ref[0:1], jnp.zeros((8, width), F32)], axis=0
    ).astype(BF16)
    if relative:
        for k in range(places):
            begin = jnp.bitwise_xor(where_ref[PLACE], k) * step if places > 1 else 0
            out_ref[k, :step] = whole[pl.ds(pl.multiple_of(begin, step), step)]
            out_ref[k, step:] = small
    else:
        half = step // 2
        for i in range(2):
            for k in range(places):
                begin = k * step + i * half
                out_ref[i, k, :half] = whole[begin : begin + half]
                out_ref[i, k, half:] = small


def pair_sum_kernel(mine_ref, other_ref, own_ref, *sent_refs):
    own_ref[...] = mine_ref[0].astype(F32) + other_ref[0].astype(F32)
    for k, sent in enumerate(sent_refs):
        sent[...] = (
            mine_ref[k + 1].astype(F32) + other_ref[k + 1].astype(F32)
        ).astype(BF16)


def attn_out_kernel(
    step, e, c, where_ref, *refs
):
    early, (mine_ref, other_ref), outs = (refs[:-8], refs[-8:-6], refs[-6:])
    projections_ref, output_ref, gain_ref, bias_ref, unit_ref, pair_ref = outs
    width = mine_ref.shape[1]

    def fill(total):
        weights = total[:step]
        small = total[step : step + 8]
        projections_ref[0, 0] = weights[:, :e]
        projections_ref[0, 1] = weights[:, 2 * e : 3 * e]
        projections_ref[0, 2] = pltpu.roll(weights, width - e, 1)[:, :e]
        output_ref[0] = pltpu.roll(weights, e, 1)[:, :e].T
        mine = pltpu.roll(small, lax.rem(width - where_ref[PLACE] * step, width), 1)
        gain_ref[0] = mine[0:2, :step]
        bias_ref[0] = mine[2:6, :step]

        def column(row, head):
            shift = lax.rem(2 * width - head * HD - where_ref[PLACE] * c, width)
            return pltpu.roll(small, shift, 1)[row : row + 1, :c]

        for head in range(unit_ref.shape[1]):
            unit_ref[0, head : head + 1] = column(6, head)
        for head in range(pair_ref.shape[2]):
            pair_ref[0, 0, head : head + 1] = column(7, head)
            pair_ref[0, 1, head : head + 1] = column(7, head + e // HD)

    @core_is(where_ref, 0)
    def _():
        total = early[0][...]
        for term in early[1:]:
            total = total + term[...].astype(F32)
        fill(total)

    @core_is(where_ref, 1)
    def _():
        mine = mine_ref[...].astype(F32)
        other = other_ref[...].astype(F32)
        fill(jnp.concatenate([other[: step // 2], mine], axis=0))


def feed_out_kernel(where_ref, first_ref, second_ref, other_ref, expand_ref, contract_ref):
    @core_is(where_ref, 0)
    def _():
        expand_ref[0] = first_ref[...].astype(F32)
        contract_ref[0] = other_ref[...].astype(F32)

    @core_is(where_ref, 1)
    def _():
        expand_ref[0] = other_ref[...].astype(F32)
        contract_ref[0] = second_ref[...].astype(F32)


def swap(x):
    return lax.ppermute(x, "section", [(0, 1), (1, 0)])


def gather_rows(x):
    return lax.all_gather(x, "tensor", axis=0, tiled=True)


def scatter_rows(x):
    size = lax.axis_size("tensor")
    parts = x.reshape(size, x.shape[0] // size, x.shape[1])
    return lax.all_to_all(parts, "tensor", 0, 0)


def deal(x, micro, sub):
    section = lax.axis_index("section")
    across = lax.axis_size("dp")
    odd = lax.axis_index("dp") % 2
    got = []
    for p in range(2):
        route = []
        for c in range(2):
            for d in range(across):
                r, dd = (d // micro, d % micro)
                m = 2 * c + (p ^ (dd & 1))
                route.append((c * across + d, (dd >> 1) * across + m * sub + r))
        chosen = 2 * section + (p ^ odd)
        payload = lax.dynamic_index_in_dim(x, chosen, 0, keepdims=False)
        got.append(lax.ppermute(payload, PLACES, route))
    return jnp.concatenate(got, axis=0)


def undeal(parts, micro, sub):
    across = lax.axis_size("dp")
    got = []
    for p in range(2):
        for u in range(2):
            route = []
            for s in range(2):
                for source in range(across):
                    m, r = (source // sub, source % sub)
                    j = p ^ (m & 1)
                    layer = u ^ (m >> 1)
                    route.append((s * across + source, layer * across + r * micro + 2 * s + j))
            got.append(lax.ppermute(parts[2 * p + u], PLACES, route))
    return got


def across_layer(x, layer, k):
    across = lax.axis_size("dp")
    route = [(layer * across + d, layer * across + (d ^ k)) for d in range(across)]
    return lax.ppermute(x, PLACES, route)


def together(*values):
    return lax.optimization_barrier(values)


def body(
    tokens,
    cotangent,
    lengths,
    random_blocks,
    projections,
    query_value_bias,
    output_weight,
    expand_weight,
    expand_bias,
    contract_weight,
    norm_gains,
    row_biases,
):
    section = lax.axis_index("section")
    place = lax.axis_index("dp")
    seat = lax.axis_index("tensor")
    across = lax.axis_size("dp")
    ways = lax.axis_size("tensor")
    micro = tokens.shape[0]
    sub = across // micro
    plane = place // sub
    share = place % sub
    local = tokens.shape[2]
    width = tokens.shape[3]
    e = projections.shape[3]
    heads = e // HD
    units = expand_weight.shape[2]
    step = projections.shape[2]
    c = query_value_bias.shape[3]
    mine = 2 * local
    rows = mine * ways
    keys = rows * 2 * sub
    blocks = keys // BLOCK
    kw = -(-(e + blocks + 1) // 128) * 128
    vw = 256
    whole_tiles = step % 32 == 0
    start = (share * micro + 2 * section) * ways * local
    length = lax.dynamic_index_in_dim(lengths[:, 0], plane, 0, keepdims=False)
    where = jnp.stack([section, place, plane, seat, start, length, plane % 2, 0]).astype(jnp.int32)
    random_all = lax.all_gather(random_blocks, "section", axis=0, tiled=True)

    x = deal(tokens[:, 0], micro, sub)

    attn_shard, feed_keep, feed_send = call(
        prepare_kernel,
        [Far(sds((step + 16, 4 * e), BF16))] + [sds((step, units), BF16)] * 2,
        where, Far(projections), Far(output_weight), Far(expand_weight),
        Far(contract_weight.transpose(0, 2, 1)), Far(query_value_bias.transpose(0, 2, 1, 3)),
        Far(expand_bias), Far(norm_gains), Far(row_biases),
        scratch=[pltpu.VMEM((16, 4 * e), F32)],
    )
    feed_traded = swap(feed_send)
    attn_all = lax.all_gather(attn_shard, PLACES, axis=0, tiled=True)
    attn_all = attn_all.reshape(2, across, step + 16, 4 * e)
    feed_all = []
    for l in range(2):
        half = jnp.where(section == l, feed_keep, feed_traded)
        feed_all.append(
            lax.all_gather(half, PLACES, axis=0, tiled=True).reshape(2, width, units)
        )
    upstream = deal(cotangent[:, 0], micro, sub)
    if not whole_tiles:
        attn_flat = attn_all[:, :, :step].reshape(2, width, 4 * e)
    vectors = []
    pair_bias = []
    for l in range(2):
        small = [((l, z, pl.ds(step, 16)), (z,)) for z in range(across)]
        if whole_tiles:
            small = Far(attn_all, (across, 16, 4 * e), small)
        else:
            small = attn_all[l, :, step:]
        vec, pair = call(
            partial(unpack_kernel, c, e), [sds((8, width), F32), sds((8, 256), F32)], small
        )
        vectors.append(vec)
        pair_bias.append(pair)

    def attn_weight(l, first, size):
        lanes = pl.ds(first, size)
        if not whole_tiles:
            return Far(attn_flat, (width, size), [((l, slice(None), lanes), ())])
        cuts = [
            ((l, z, pl.ds(0, step), lanes), (pl.ds(z * step, step),)) for z in range(across)
        ]
        return Far(attn_all, (width, size), cuts)

    def feed_weight(l, i):
        return Far(feed_all[l], (width, units), [((i,), ())])

    def all_parts(own):
        pair = [own, swap(own)]
        if sub == 1:
            return pair
        groups = [[m * sub + r for r in range(sub)] for m in range(micro)]
        return [
            lax.all_gather(
                jnp.concatenate(pair, axis=0), "dp", axis=0, tiled=True, axis_index_groups=groups
            )
        ]

    def own_parts(parts):
        if sub == 1:
            return parts
        groups = [[m * sub + r for r in range(sub)] for m in range(micro)]
        total = lax.psum_scatter(
            parts[0], "dp", scatter_dimension=0, tiled=True, axis_index_groups=groups
        )
        return [total[:rows], total[rows:]]

    chunk = min(rows, 256)
    near_rows = sds((mine, width), BF16)
    far_unit = [Far(sds((mine, width), F32)), Far(sds((mine, 128), F32))]

    saved = []
    for l in range(2):
        vec = vectors[l]
        x_all = gather_rows(x)
        q, kv, x_kept, q_kept, kv_kept = call(
            partial(qkv_kernel, ways, local, blocks, e),
            [sds((rows, kw), BF16), sds((rows, kw + vw), BF16),
             Far(sds((rows, width), BF16), plain=True), Far(sds((rows, kw), BF16), plain=True),
             Far(sds((rows, kw + vw), BF16), plain=True)],
            where, x_all, attn_weight(l, 0, 4 * e), pair_bias[l],
            flops=6 * rows * width * 256,
        )
        parts = all_parts(kv)
        attended, mixed, totals, *others = call(
            partial(attention_kernel, heads, l, ways, local, blocks, chunk, len(parts)),
            [sds((rows, width), BF16), Far(sds((rows, vw), BF16)), Far(sds((8, rows), F32))]
            + [Far(sds(part.shape, BF16), plain=True) for part in parts[1:]],
            where, random_all, q, attn_weight(l, 4 * e - vw, vw), *parts,
            flops=4 * rows * keys * kw, limit=24,
        )
        parts_kept = [kv_kept, others[0]] if sub == 1 else parts
        terms = scatter_rows(attended)
        terms, feed_all[l] = together(terms, feed_all[l])
        middle, middle_low, unit1, inverse1 = call(
            first_norm_kernel, [sds((mine, width), F32), near_rows] + far_unit, x, terms, vec
        )
        middle_all = gather_rows(middle_low)
        fed, active, slope, middle_kept = call(
            feed_kernel,
            [sds((rows, width), BF16), Far(sds((rows, units), BF16)),
             Far(sds((rows, units), BF16)), Far(sds((rows, width), BF16), plain=True)],
            middle_all, vec, feed_weight(l, 0), feed_weight(l, 1),
            flops=4 * rows * width * units,
        )
        terms = scatter_rows(fed)
        if l == 0:
            x, low_kept, unit2, inverse2 = call(
                partial(second_norm_kernel, ways),
                [near_rows, Far(near_rows, plain=True)] + far_unit,
                where, middle, terms, vec,
            )
        else:
            *places, unit2, inverse2 = call(
                partial(second_norm_kernel, ways),
                [sds((local, width), BF16)] * 4 + far_unit,
                where, middle, terms, vec, Far(low_kept),
            )
        saved.append(
            (x_kept, q_kept, parts_kept, mixed, totals, unit1, inverse1, middle_kept, active,
             slope, unit2, inverse2)
        )
    activation_rows = undeal(places, micro, sub)

    feed_parts = [None, None]
    for l in (1, 0):
        vec = vectors[l]
        (x_kept, q_kept, parts_kept, mixed, totals, unit1, inverse1, middle_kept, active,
         slope, unit2, inverse2) = saved[l]
        near_f32 = sds((mine, width), F32)
        second, feed_low, second_sums = call(
            partial(second_back_kernel, ways),
            [near_f32, near_rows, sds((8, width), F32)],
            where, upstream, vec, Far(unit2), Far(inverse2),
        )
        feed_grad = gather_rows(feed_low)
        hidden, fed_back, unit_sums = call(
            feed_back_kernel,
            [sds((rows, units), BF16), sds((rows, width), BF16), sds((8, units), F32)],
            feed_grad, feed_weight(l, 1), Far(slope), feed_weight(l, 0),
            flops=4 * rows * width * units,
        )
        terms = scatter_rows(fed_back)
        feed_kept, feed_sent = call(
            feed_pack_kernel,
            [sds((width, units), BF16)] * 2,
            where, hidden, feed_grad, Far(middle_kept), Far(active),
            flops=4 * rows * width * units,
        )
        terms, feed_kept, feed_sent = together(terms, feed_kept, feed_sent)
        feed_half = (feed_kept.astype(F32) + swap(feed_sent).astype(F32)).astype(BF16)
        first_grad, first_low = call(
            first_back_kernel,
            [near_f32, sds((mine + 16, width), BF16)],
            second, terms, vec, second_sums, Far(unit1), Far(inverse1),
        )
        attended_grad = gather_rows(first_low).reshape(ways, mine + 16, width)
        attended_grad, feed_half = together(attended_grad, feed_half)
        feed_parts[l] = lax.psum_scatter(feed_half, "dp", scatter_dimension=0, tiled=True)
        dq, norm_sums, *dkv = call(
            partial(attention_back_kernel, heads, l, ways, local, blocks, chunk),
            [sds((rows, 256), BF16), sds((16, width), F32)]
            + [sds((part.shape[0], 256 + vw), BF16) for part in parts_kept],
            where, random_all, attended_grad, attn_weight(l, 4 * e - vw, vw), Far(mixed),
            Far(q_kept), Far(totals), *[Far(part) for part in parts_kept],
            flops=10 * rows * keys * kw, limit=32,
        )
        dkv_own, dkv_other = own_parts(dkv)
        triple, projected, pair_sums = call(
            partial(projection_back_kernel, e),
            [sds((rows, 4 * e), BF16), sds((rows, width), BF16), sds((8, 4 * e), F32)],
            dq, dkv_own, swap(dkv_other), attn_weight(l, 0, 4 * e),
            flops=6 * rows * width * 256,
        )
        terms = scatter_rows(projected)
        cut = step if whole_tiles else width
        pieces = width // cut
        pack_shape = (pieces, cut + 16, 4 * e) if l == 0 else (2, pieces, cut // 2 + 16, 4 * e)
        (pack,) = call(
            partial(attn_pack_kernel, l == 0, cut, e),
            [sds(pack_shape, BF16)],
            where, triple, attended_grad, norm_sums, unit_sums, pair_sums, Far(x_kept),
            Far(mixed),
            flops=8 * rows * width * 256,
            scratch=[pltpu.VMEM((width, 4 * e), BF16)],
        )
        if not whole_tiles:
            pack = split_pack(pack, l == 0, across)
        if l == 1:
            terms, pack = together(terms, pack)
            attn_part = lax.psum_scatter(
                pack.reshape((-1,) + pack.shape[2:]), PLACES, scatter_dimension=0
            )
            upstream, later = call(
                input_kernel, [near_rows, Far(near_rows, plain=True)], first_grad, terms
            )
        else:
            traded = lax.ppermute(pack, "section", [(1, 0)])
            if whole_tiles:
                sums = call(
                    pair_sum_kernel,
                    [sds(pack.shape[1:], F32)] + [sds(pack.shape[1:], BF16)] * (across - 1),
                    pack, traded,
                )
                early = [sums[0]] + [across_layer(sums[k], 0, k) for k in range(1, across)]
            else:
                total = (pack.astype(F32) + traded.astype(F32)).astype(BF16)
                early = [
                    lax.psum_scatter(total, "dp", scatter_dimension=0).astype(F32)
                ]
            places = call(
                last_input_kernel, [sds((local, width), BF16)] * 4,
                where, first_grad, terms, Far(later),
            )
            input_rows = undeal(places, micro, sub)

    feed_other = swap(jnp.where(section == 0, feed_parts[1], feed_parts[0]))
    expand_out, contract_out = call(
        feed_out_kernel, [sds((1, step, units), F32)] * 2,
        where, feed_parts[0], feed_parts[1], feed_other,
    )
    attn_other = lax.ppermute(attn_part, "section", [(0, 1)])
    projections_out, output_out, gains_out, biases_out, units_out, pairs_out = call(
        partial(attn_out_kernel, step, e, c),
        [sds((1, 3, step, e), F32), sds((1, e, step), F32), sds((1, 2, step), F32),
         sds((1, 4, step), F32), sds((1, units // HD, c), F32), sds((1, 2, heads, c), F32)],
        where, *early, attn_part, attn_other,
    )
    (activations,) = call(
        place_out_kernel, [sds((1, micro, 1, local, width), BF16)], where, *activation_rows
    )
    (input_grads,) = call(
        place_out_kernel, [sds((1, micro, 1, local, width), F32)], where, *input_rows
    )
    return (
        activations,
        input_grads,
        projections_out,
        pairs_out,
        output_out,
        expand_out,
        units_out,
        contract_out.transpose(0, 2, 1),
        gains_out,
        biases_out,
    )


def split_pack(pack, relative, across):
    if relative:
        weights, small = (pack[0, :-16], pack[0, -16:])
        weights = weights.reshape(across, -1, weights.shape[1])
        small = jnp.broadcast_to(small, (across,) + small.shape)
        return jnp.concatenate([weights, small], axis=1)
    weights = pack[:, 0, :-16].reshape(-1, pack.shape[3])
    weights = weights.reshape(across, 2, -1, pack.shape[3]).transpose(1, 0, 2, 3)
    small = jnp.broadcast_to(pack[0, 0, -16:], (2, across, 16, pack.shape[3]))
    return jnp.concatenate([weights, small], axis=2)


def solution(mesh):
    in_specs = (
        P(None, None, ("dp", "tensor"), None),
        P(None, None, ("dp", "tensor"), None),
        P(),
        P("section", "tensor", None, None),
        P("section", None, "dp", "tensor"),
        P("section", None, "tensor", "dp"),
        P("section", "tensor", "dp"),
        P("section", "dp", "tensor"),
        P("section", "tensor", "dp"),
        P("section", "tensor", "dp"),
        P("section", None, "dp"),
        P("section", None, "dp"),
    )
    out_specs = (
        P("section", None, None, ("dp", "tensor"), None),
        P("section", None, None, ("dp", "tensor"), None),
        P("section", None, "dp", "tensor"),
        P("section", None, "tensor", "dp"),
        P("section", "tensor", "dp"),
        P("section", "dp", "tensor"),
        P("section", "tensor", "dp"),
        P("section", "tensor", "dp"),
        P("section", None, "dp"),
        P("section", None, "dp"),
    )
    return jax.shard_map(body, mesh=mesh, in_specs=in_specs, out_specs=out_specs, check_vma=False)
```

```python
import math
from functools import partial

import jax
import jax.numpy as jnp
from jax import lax
from jax.experimental import pallas as pl
from jax.experimental.pallas import tpu as pltpu
from jax.sharding import PartitionSpec as P

HD = 64
BLOCK = 64
GLOBAL = 2
EPSILON = 1e-12
MASKED = -1e30
GELU_A = 0.7978845608028654
GELU_B = 0.044715
F32 = jnp.float32
BF16 = jnp.bfloat16
MIB = 1 << 20
PLACES = ("section", "dp")


def nt(a, b):
    return lax.dot_general(a, b, (((1,), (1,)), ((), ())), preferred_element_type=F32)


def tn(a, b):
    return lax.dot_general(a, b, (((0,), (0,)), ((), ())), preferred_element_type=F32)


def nn(a, b):
    return jnp.dot(a, b, preferred_element_type=F32)


def sds(shape, dtype):
    return jax.ShapeDtypeStruct(shape, dtype)


class Far:
    def __init__(self, array, shape=None, cuts=None, plain=False):
        self.array = array
        self.shape = array.shape if shape is None else shape
        self.cuts = [((), ())] if cuts is None else cuts
        self.plain = plain


def at(ref, index):
    return ref.at[index] if index else ref


class Arriving:
    def __init__(self, source, buffer, sems, first, cuts):
        self.buffer = buffer
        self.shape = buffer.shape
        self.copies = [
            pltpu.make_async_copy(at(source, a), at(buffer, b), sems.at[first + i])
            for i, (a, b) in enumerate(cuts)
        ]
        for copy in self.copies:
            copy.start()
        self.there = False

    def settle(self):
        if not self.there:
            for copy in self.copies:
                copy.wait()
            self.there = True

    def __getitem__(self, index):
        self.settle()
        return self.buffer[index]


class Leaving:
    def __init__(self, target, buffer, sem):
        self.target = target
        self.buffer = buffer
        self.shape = target.shape
        self.sem = sem
        self.copy = None

    def __setitem__(self, index, value):
        self.buffer[index] = value

    def send(self, source=None):
        self.copy = pltpu.make_async_copy(
            self.buffer if source is None else source, self.target, self.sem
        )
        self.copy.start()

    def finish(self):
        if self.copy is None:
            self.send()
        self.copy.wait()


def call(kernel, outs, *args, flops=0, limit=16, scratch=()):
    arrays = []
    in_specs = []
    out_specs = []
    out_shapes = []
    buffers = []
    size = 0
    semaphores = 0
    for arg in args:
        if isinstance(arg, Far):
            arrays.append(pltpu.with_memory_space_constraint(arg.array, pltpu.HBM))
            in_specs.append(pl.BlockSpec(memory_space=pltpu.HBM))
            buffers.append(pltpu.VMEM(arg.shape, arg.array.dtype))
            semaphores += len(arg.cuts)
            size += math.prod(arg.shape) * arg.array.dtype.itemsize
        else:
            arrays.append(arg)
            scalar = arg.dtype == jnp.int32
            in_specs.append(pl.BlockSpec(memory_space=pltpu.SMEM if scalar else pltpu.VMEM))
            size += arg.size * arg.dtype.itemsize
    for out in outs:
        if isinstance(out, Far):
            out_shapes.append(pltpu.HBM(out.shape, out.array.dtype))
            out_specs.append(pl.BlockSpec(memory_space=pltpu.HBM))
            if not out.plain:
                buffers.append(pltpu.VMEM(out.shape, out.array.dtype))
            semaphores += 1
            size += math.prod(out.shape) * out.array.dtype.itemsize
        else:
            out_shapes.append(out)
            out_specs.append(pl.BlockSpec(memory_space=pltpu.VMEM))
            size += out.size * out.dtype.itemsize

    def whole(*refs):
        refs = list(refs)
        ins = refs[: len(args)]
        results = refs[len(args) : len(args) + len(outs)]
        rest = refs[len(args) + len(outs) :]
        sems = rest.pop() if semaphores else None
        given = []
        used = 0
        for arg, ref in zip(args, ins):
            if isinstance(arg, Far):
                given.append(Arriving(ref, rest.pop(0), sems, used, arg.cuts))
                used += len(arg.cuts)
            else:
                given.append(ref)
        leaving = []
        for out, ref in zip(outs, results):
            if isinstance(out, Far):
                buffer = None if out.plain else rest.pop(0)
                leaving.append(Leaving(ref, buffer, sems.at[used]))
                given.append(leaving[-1])
                used += 1
            else:
                given.append(ref)
        kernel(*given, *rest)
        for item in given:
            if isinstance(item, Arriving):
                item.settle()
        for item in leaving:
            item.finish()

    scratch_shapes = buffers + list(scratch)
    if semaphores:
        scratch_shapes = scratch_shapes + [pltpu.SemaphoreType.DMA((semaphores,))]
    return pl.pallas_call(
        whole,
        out_shape=tuple(out_shapes),
        in_specs=in_specs,
        out_specs=tuple(out_specs),
        scratch_shapes=scratch_shapes,
        compiler_params=pltpu.CompilerParams(vmem_limit_bytes=limit * MIB),
        cost_estimate=pl.CostEstimate(flops=flops, bytes_accessed=size, transcendentals=0),
    )(*arrays)


SECTION, PLACE, PLANE, SEAT, START, LENGTH, FLIP = range(7)


def positions(where_ref, count, ways, local, first):
    row = lax.broadcasted_iota(jnp.int32, (count, 1), 0) + first
    group = jnp.bitwise_xor(row // local % 2, where_ref[FLIP])
    return (
        where_ref[START] + group * (ways * local) + row // (2 * local) * local + row % local
    )


def core_is(where_ref, core):
    return pl.when(where_ref[SECTION] == core)


def prepare_kernel(
    where_ref, projections_ref, output_ref, expand_ref, contract_ref, pair_ref, unit_ref,
    gain_ref, bias_ref, attn_keep, attn_send, keep_out, send_out, whole, small
):
    step, e = projections_ref.shape[2:]
    heads, _, c = pair_ref.shape[1:]
    half = step // 2
    whole[:, :e] = projections_ref[0, 0]
    whole[:, e : 2 * e] = projections_ref[0, 2]
    whole[:, 2 * e : 3 * e] = projections_ref[0, 1]
    whole[:, 3 * e :] = output_ref[0].T
    small[...] = jnp.zeros_like(small)
    small[0:2, :step] = gain_ref[0].astype(F32)
    small[2:6, :step] = bias_ref[0].astype(F32)
    small[: unit_ref.shape[1], 256 : 256 + c] = unit_ref[0].astype(F32)
    for i in range(heads):
        small[i : i + 1, 384 : 384 + c] = pair_ref[0, i, 0:1].astype(F32)
        small[i : i + 1, 512 : 512 + c] = pair_ref[0, i, 1:2].astype(F32)
    attn_keep[half:] = small[...].astype(BF16)
    attn_send[half:] = small[...].astype(BF16)
    expand = expand_ref[0]
    contract = contract_ref[0]

    @core_is(where_ref, 0)
    def _():
        attn_keep[:half] = whole[:half]
        attn_send[:half] = whole[half:]
        keep_out[...] = expand
        send_out[...] = contract

    @core_is(where_ref, 1)
    def _():
        attn_keep[:half] = whole[half:]
        attn_send[:half] = whole[:half]
        keep_out[...] = contract
        send_out[...] = expand


def unpack_kernel(c, e, raw_ref, vec_ref, pair_ref):
    places = raw_ref.shape[0]
    width = vec_ref.shape[1]
    w = width // places

    def of_heads(rows, lanes, z):
        source = lax.broadcasted_iota(jnp.int32, (128, lanes), 0)
        target = lax.broadcasted_iota(jnp.int32, (128, lanes), 1)
        repeat = ((target % c == source) & (source < c)).astype(F32).astype(BF16)
        spread_rows = nn(rows, repeat)
        head = lax.broadcasted_iota(jnp.int32, spread_rows.shape, 0)
        lane = lax.broadcasted_iota(jnp.int32, spread_rows.shape, 1)
        keep = (lane // HD == head) & (lane % HD // c == z)
        return jnp.sum(jnp.where(keep, spread_rows, 0.0), axis=0, keepdims=True)

    norms = jnp.zeros((16, width), F32)
    units = jnp.zeros((1, width), F32)
    queries = jnp.zeros((1, 256), F32)
    values = jnp.zeros((1, 256), F32)
    for z in range(places):
        rows = raw_ref[z]
        source = lax.broadcasted_iota(jnp.int32, (256, width), 0)
        target = lax.broadcasted_iota(jnp.int32, (256, width), 1)
        move = ((target == source + z * w) & (source < w)).astype(F32).astype(BF16)
        norms = norms + nn(rows[:, :256], move)
        units = units + of_heads(rows[:, 256:384], width, z)
        queries = queries + of_heads(rows[:, 384:512], 256, z)
        values = values + of_heads(rows[:, 512:640], 256, z)
    vec_ref[...] = norms[:8]
    vec_ref[6:7] = units
    pair_ref[...] = jnp.zeros_like(pair_ref)
    pair_ref[0:1] = jnp.where(lax.broadcasted_iota(jnp.int32, (1, 256), 1) < e, queries, 0.0)
    values = jnp.where(lax.broadcasted_iota(jnp.int32, (1, 256), 1) < e, values, 0.0)
    pair_ref[1:2] = pltpu.roll(values, 256 - e, 1)


def qkv_kernel(ways, local, blocks, e, where_ref, x_ref, w_ref, bias_ref, q_ref, kv_ref, *kept):
    kw = q_ref.shape[1]
    vw = kv_ref.shape[1] - kw
    x = x_ref[...]
    kept[0].send(x_ref)
    lead = 2 * e // 128 * 128
    q = (nn(x, w_ref[:, :256]) + bias_ref[0:1]).astype(BF16).astype(F32) * HD ** (-0.5)
    lane = lax.broadcasted_iota(jnp.int32, (1, 256), 1)
    q = jnp.where(lane < e, q, 0.0).astype(BF16)
    q_ref[:, :256] = q
    if kw > 256:
        q_ref[:, 256:] = jnp.zeros((q.shape[0], kw - 256), BF16)
    kept[1].send(q_ref)
    position = positions(where_ref, x.shape[0], ways, local, 0)
    block = position // BLOCK
    lane = lax.broadcasted_iota(jnp.int32, (1, kw), 1)
    hidden = (position >= where_ref[LENGTH]) & (lane == e + blocks)
    tail = jnp.where(lane == e + block, 1.0, jnp.where(hidden, MASKED, 0.0))
    k = nn(x, w_ref[:, lead : lead + 256])
    if kw > 256:
        k = jnp.concatenate([k, jnp.zeros((k.shape[0], kw - 256), F32)], axis=1)
    kv_ref[:, :kw] = jnp.where(lane < e, k, tail).astype(BF16)
    kv_ref[:, kw:] = (nn(x, w_ref[:, 128 : 128 + vw]) + bias_ref[1:2]).astype(BF16)
    kept[2].send(kv_ref)


def head_mask(first, lanes):
    lane = lax.broadcasted_iota(jnp.int32, (1, lanes), 1)
    return ((lane >= first) & (lane < first + HD)).astype(F32)


def seen_rows(where_ref, random_ref, layer, h, rows, ways, local, kw, e, blocks):
    lane = lax.broadcasted_iota(jnp.int32, (1, kw), 1)
    key = lane - e
    parts = []
    for g in range(rows // local):
        group = jnp.bitwise_xor(g % 2, where_ref[FLIP])
        position = where_ref[START] + group * (ways * local) + g // 2 * local
        block = position // BLOCK
        seen = (key < GLOBAL) | (jnp.abs(key - block) <= 1) | (block < GLOBAL)
        for i in range(random_ref.shape[3]):
            seen = seen | (key == random_ref[layer, h, block, i])
        hidden = (key >= 0) & (key < blocks) & jnp.logical_not(seen)
        line = jnp.where(key == blocks, 1.0, jnp.where(hidden, MASKED, 0.0))
        parts.append(jnp.broadcast_to(line, (local, kw)))
    return jnp.concatenate(parts, axis=0)


def attention_kernel(
    heads, layer, ways, local, blocks, chunk, count, where_ref, random_ref, q_ref, w_ref, *refs
):
    parts, (out_ref, mixed_out, total_out), kept = (
        refs[:count], refs[count : count + 3], refs[count + 3 :]
    )
    rows, kw = q_ref.shape
    e = heads * HD
    vw = parts[0].shape[1] - kw
    shift = vw - e
    for out, part in zip(kept, parts[1:]):
        out.send(part)
    k = jnp.concatenate([part[:, :kw] for part in parts], axis=0)
    vt = jnp.concatenate([part[:, kw:] for part in parts], axis=0).T
    q = q_ref[...].astype(F32)
    lines = [jnp.zeros((shift, rows), F32)]
    totals = []
    for h in range(heads):
        seen = seen_rows(where_ref, random_ref, layer, h, rows, ways, local, kw, e, blocks)
        qa = (q * head_mask(h * HD, kw) + seen).astype(BF16)
        vh = vt[shift + h * HD : shift + (h + 1) * HD]
        cells = []
        sums = []
        for c in range(0, rows, chunk):
            scores = nt(k, qa[c : c + chunk])
            top = jnp.max(scores, axis=0, keepdims=True)
            p = jnp.exp(scores - top)
            total = jnp.sum(p, axis=0, keepdims=True)
            cells.append(nn(vh, p.astype(BF16)) / total)
            sums.append(top + jnp.log(total))
        lines.append(jnp.concatenate(cells, axis=1))
        totals.append(jnp.concatenate(sums, axis=1))
    total_out[...] = jnp.concatenate(totals + [jnp.zeros((8 - heads, rows), F32)], axis=0)
    total_out.send()
    mixed = jnp.concatenate(lines, axis=0).T.astype(BF16)
    mixed_out[...] = mixed
    mixed_out.send()
    out_ref[...] = nt(mixed, w_ref[...]).astype(BF16)


def attention_back_kernel(
    heads, layer, ways, local, blocks, chunk, where_ref, random_ref, grad_ref, w_ref, mixed_ref,
    q_ref, total_ref, *refs
):
    count = (len(refs) - 2) // 2
    parts, dq_ref, small_ref, outs = (
        refs[:count], refs[count], refs[count + 1], refs[count + 2 :]
    )
    rows, kw = q_ref.shape
    e = heads * HD
    vw = mixed_ref.shape[1]
    shift = vw - e
    width = grad_ref.shape[2]
    grad = grad_ref[:, : 2 * local].reshape(rows, width)
    small = grad_ref[0, 2 * local :].astype(F32)
    for i in range(1, ways):
        small = small + grad_ref[i, 2 * local :].astype(F32)
    small_ref[...] = small
    mixed_grad = nn(grad, w_ref[...]).astype(BF16).astype(F32)
    product = mixed_grad * mixed_ref[...].astype(F32)
    masks = jnp.concatenate([head_mask(shift + h * HD, vw) for h in range(8)], axis=0)
    inner = lax.dot_general(
        masks, product, (((1,), (1,)), ((), ())),
        preferred_element_type=F32, precision=lax.Precision.HIGHEST,
    )
    q = q_ref[...].astype(F32)
    k = jnp.concatenate([part[:, :kw] for part in parts], axis=0)
    v = jnp.concatenate([part[:, kw:] for part in parts], axis=0)
    kt = k[:, :256].T
    totals = total_ref[...]
    dk = None
    dv = None
    lines = []
    for h in range(heads):
        seen = seen_rows(where_ref, random_ref, layer, h, rows, ways, local, kw, e, blocks)
        qm = q * head_mask(h * HD, kw)
        qa = (qm + seen).astype(BF16)
        qm = qm[:, :256].astype(BF16)
        gm = (mixed_grad * head_mask(shift + h * HD, vw)).astype(BF16)
        kh = kt[h * HD : (h + 1) * HD]
        cells = []
        for c in range(0, rows, chunk):
            scores = nt(k, qa[c : c + chunk])
            p = jnp.exp(scores - totals[h : h + 1, c : c + chunk])
            dp = nt(v, gm[c : c + chunk])
            ds = (p * (dp - inner[h : h + 1, c : c + chunk])).astype(BF16)
            dv_term = nn(p.astype(BF16), gm[c : c + chunk])
            dk_term = nn(ds, qm[c : c + chunk])
            dv = dv_term if dv is None else dv + dv_term
            dk = dk_term if dk is None else dk + dk_term
            cells.append(nn(kh, ds))
        lines.append(jnp.concatenate(cells, axis=1))
    lines.append(jnp.zeros((256 - e, rows), F32))
    dq = jnp.concatenate(lines, axis=0).T * HD ** (-0.5)
    dq_ref[...] = dq.astype(BF16)
    start = 0
    for out in outs:
        size = out.shape[0]
        out[:, :256] = dk[start : start + size].astype(BF16)
        out[:, 256:] = dv[start : start + size].astype(BF16)
        start += size


def projection_back_kernel(e, dq_ref, own_ref, other_ref, w_ref, triple_ref, out_ref, sums_ref):
    vw = own_ref.shape[1] - 256
    width = w_ref.shape[1]
    lead = 2 * e // 128 * 128
    rows = dq_ref.shape[0]
    dq = dq_ref[...]
    dkv = (own_ref[...].astype(F32) + other_ref[...].astype(F32)).astype(BF16).astype(F32)
    dv = dkv[:, 256:]
    head = dq.astype(F32)
    nothing = jnp.zeros((rows, 128), F32)
    triple = jnp.concatenate(
        [head[:, :128], head[:, 128:] + dv[:, :128], dv[:, 128:], dkv[:, :256], nothing], axis=1
    ).astype(BF16)
    triple_ref[...] = triple
    sums_ref[...] = jnp.zeros_like(sums_ref)
    sums_ref[0:1] = jnp.sum(triple.astype(F32), axis=0, keepdims=True)
    out_ref[...] = nt(triple, w_ref[...]).astype(BF16)


def norm(values):
    average = jnp.mean(values, axis=-1, keepdims=True)
    centered = values - average
    spread_now = jnp.mean(centered * centered, axis=-1, keepdims=True)
    inverse = lax.rsqrt(spread_now + EPSILON)
    return (centered * inverse, inverse)


def total_of(terms_ref):
    total = terms_ref[0].astype(F32)
    for i in range(1, terms_ref.shape[0]):
        total = total + terms_ref[i].astype(F32)
    return total


def first_norm_kernel(x_ref, terms_ref, vec_ref, middle_ref, low_ref, unit_out, inverse_out):
    values = x_ref[...].astype(F32) + total_of(terms_ref) + vec_ref[2:3]
    unit, inverse = norm(values)
    unit_out[...] = unit
    unit_out.send()
    inverse_out[...] = jnp.broadcast_to(inverse, inverse_out.shape)
    inverse_out.send()
    middle = unit * vec_ref[0:1] + vec_ref[4:5]
    middle_ref[...] = middle
    low_ref[...] = middle.astype(BF16)


def valid_rows(where_ref, ways, local):
    position = positions(where_ref, 2 * local, ways, local, where_ref[SEAT] * 2 * local)
    return (position < where_ref[LENGTH]).astype(F32)


def place_parts(where_ref, early, later, outs):
    half = early.shape[0] // 2
    late_plane = where_ref[PLANE] // 2
    for u in range(2):
        for p in range(2):
            @pl.when(late_plane == u)
            def _(u=u, p=p):
                outs[2 * p + u][...] = early[p * half : (p + 1) * half]

            @pl.when(late_plane != u)
            def _(u=u, p=p):
                outs[2 * p + u][...] = later[p * half : (p + 1) * half]


def second_norm_kernel(ways, where_ref, middle_ref, terms_ref, vec_ref, *refs):
    if len(refs) == 4:
        low_ref, kept, unit_out, inverse_out = refs
    else:
        early_ref, unit_out, inverse_out = (refs[0], refs[-2], refs[-1])
    unit, inverse = norm(middle_ref[...] + total_of(terms_ref) + vec_ref[3:4])
    unit_out[...] = unit
    unit_out.send()
    inverse_out[...] = jnp.broadcast_to(inverse, inverse_out.shape)
    inverse_out.send()
    result = unit * vec_ref[1:2] + vec_ref[5:6]
    low = (result * valid_rows(where_ref, ways, unit.shape[0] // 2)).astype(BF16)
    if len(refs) == 4:
        low_ref[...] = low
        kept.send(low_ref)
    else:
        place_parts(where_ref, early_ref[...], low, refs[1:5])


def norm_back(grad, unit, inverse, gain):
    scaled = grad * gain
    return inverse * (
        scaled
        - jnp.mean(scaled, axis=-1, keepdims=True)
        - unit * jnp.mean(scaled * unit, axis=-1, keepdims=True)
    )


def second_back_kernel(
    ways, where_ref, up_ref, vec_ref, unit_ref, inverse_ref, second_ref, low_ref, sums_ref
):
    grad = up_ref[...].astype(F32) * valid_rows(where_ref, ways, up_ref.shape[0] // 2)
    unit = unit_ref[...]
    second = norm_back(grad, unit, inverse_ref[:, 0:1], vec_ref[1:2])
    second_ref[...] = second
    low_ref[...] = second.astype(BF16)
    sums_ref[...] = jnp.zeros_like(sums_ref)
    sums_ref[0:1] = jnp.sum(grad * unit, axis=0, keepdims=True)
    sums_ref[1:2] = jnp.sum(grad, axis=0, keepdims=True)
    sums_ref[2:3] = jnp.sum(second, axis=0, keepdims=True)


def first_back_kernel(
    second_ref, terms_ref, vec_ref, before_ref, unit_ref, inverse_ref, first_ref, low_ref
):
    grad = second_ref[...] + total_of(terms_ref)
    unit = unit_ref[...]
    first = norm_back(grad, unit, inverse_ref[:, 0:1], vec_ref[0:1])
    first_ref[...] = first
    rows = first.shape[0]
    low_ref[:rows] = first.astype(BF16)
    before = before_ref[...]
    low_ref[rows:] = jnp.concatenate(
        [jnp.sum(grad * unit, axis=0, keepdims=True), before[0:1],
         jnp.sum(first, axis=0, keepdims=True), before[2:3],
         jnp.sum(grad, axis=0, keepdims=True), before[1:2],
         jnp.zeros((10, first.shape[1]), F32)], axis=0
    ).astype(BF16)


def input_kernel(first_ref, terms_ref, out_ref, kept):
    out_ref[...] = (first_ref[...] + total_of(terms_ref)).astype(BF16)
    kept.send(out_ref)


def last_input_kernel(where_ref, first_ref, terms_ref, later_ref, *outs):
    low = (first_ref[...] + total_of(terms_ref)).astype(BF16)
    place_parts(where_ref, low, later_ref[...], outs)


def place_out_kernel(where_ref, *refs):
    out_ref = refs[-1]
    odd = where_ref[PLACE] % 2
    for p in range(2):
        for u in range(2):
            m = 2 * jnp.bitwise_xor(where_ref[SECTION], u) + jnp.bitwise_xor(odd, p)
            out_ref[0, m, 0] = refs[2 * p + u][...].astype(out_ref.dtype)


def feed_kernel(x_ref, vec_ref, expand_ref, contract_ref, out_ref, active_out, slope_out, kept):
    kept.send(x_ref)
    v = nn(x_ref[...], expand_ref[...]) + vec_ref[6:7]
    th = jnp.tanh(GELU_A * (v + GELU_B * v * v * v))
    half = 0.5 * (1.0 + th)
    active = (v * half).astype(BF16)
    active_out[...] = active
    active_out.send()
    slope = half + 0.5 * v * (1.0 - th * th) * GELU_A * (1.0 + 3.0 * GELU_B * v * v)
    slope_out[...] = slope.astype(BF16)
    slope_out.send()
    out_ref[...] = nt(active, contract_ref[...]).astype(BF16)


def feed_back_kernel(
    grad_ref, contract_ref, slope_ref, expand_ref, hidden_ref, out_ref, sums_ref
):
    active_grad = nn(grad_ref[...], contract_ref[...])
    hidden = (active_grad * slope_ref[...].astype(F32)).astype(BF16)
    hidden_ref[...] = hidden
    hidden_ref.send()
    sums_ref[...] = jnp.zeros_like(sums_ref)
    sums_ref[0:1] = jnp.sum(hidden.astype(F32), axis=0, keepdims=True)
    out_ref[...] = nt(hidden, expand_ref[...]).astype(BF16)


def feed_pack_kernel(where_ref, hidden_ref, grad_ref, middle_ref, active_ref, keep_ref, send_ref):
    def put(value, core):
        @core_is(where_ref, core)
        def _():
            keep_ref[...] = value

        @core_is(where_ref, 1 - core)
        def _():
            send_ref[...] = value

    put(tn(middle_ref[...], hidden_ref[...]).astype(BF16), 0)
    put(tn(grad_ref[...], active_ref[...]).astype(BF16), 1)


def attn_pack_kernel(
    relative, step, e, where_ref, triple_ref, grad_ref, norm_ref, unit_ref, pair_ref, x_ref,
    mixed_ref, out_ref, whole
):
    x = x_ref[...]
    width = x.shape[1]
    vw = mixed_ref.shape[1]
    places = width // step
    local = grad_ref.shape[1] - 16
    grad = grad_ref[:, :local].reshape(x.shape)
    total = tn(x, triple_ref[...])
    last = total[:, width - vw :] + tn(grad, mixed_ref[...])
    whole[:, : width - vw] = total[:, : width - vw].astype(BF16)
    whole[:, width - vw :] = last.astype(BF16)
    small = jnp.concatenate(
        [norm_ref[:6], unit_ref[0:1], pair_ref[0:1], jnp.zeros((8, width), F32)], axis=0
    ).astype(BF16)
    if relative:
        for k in range(places):
            begin = jnp.bitwise_xor(where_ref[PLACE], k) * step if places > 1 else 0
            out_ref[k, :step] = whole[pl.ds(pl.multiple_of(begin, step), step)]
            out_ref[k, step:] = small
    else:
        half = step // 2
        for i in range(2):
            for k in range(places):
                begin = k * step + i * half
                out_ref[i, k, :half] = whole[begin : begin + half]
                out_ref[i, k, half:] = small


def pair_sum_kernel(mine_ref, other_ref, own_ref, *sent_refs):
    own_ref[...] = mine_ref[0].astype(F32) + other_ref[0].astype(F32)
    for k, sent in enumerate(sent_refs):
        sent[...] = (
            mine_ref[k + 1].astype(F32) + other_ref[k + 1].astype(F32)
        ).astype(BF16)


def attn_out_kernel(
    step, e, c, where_ref, *refs
):
    early, (mine_ref, other_ref), outs = (refs[:-8], refs[-8:-6], refs[-6:])
    projections_ref, output_ref, gain_ref, bias_ref, unit_ref, pair_ref = outs
    width = mine_ref.shape[1]

    def fill(total):
        weights = total[:step]
        small = total[step : step + 8]
        projections_ref[0, 0] = weights[:, :e]
        projections_ref[0, 1] = weights[:, 2 * e : 3 * e]
        projections_ref[0, 2] = pltpu.roll(weights, width - e, 1)[:, :e]
        output_ref[0] = pltpu.roll(weights, e, 1)[:, :e].T
        mine = pltpu.roll(small, lax.rem(width - where_ref[PLACE] * step, width), 1)
        gain_ref[0] = mine[0:2, :step]
        bias_ref[0] = mine[2:6, :step]

        def column(row, head):
            shift = lax.rem(2 * width - head * HD - where_ref[PLACE] * c, width)
            return pltpu.roll(small, shift, 1)[row : row + 1, :c]

        for head in range(unit_ref.shape[0]):
            unit_ref[head] = column(6, head)
        for head in range(pair_ref.shape[1]):
            pair_ref[0, head, 0:1] = column(7, head)
            pair_ref[0, head, 1:2] = column(7, head + e // HD)

    @core_is(where_ref, 0)
    def _():
        total = early[0][...]
        for term in early[1:]:
            total = total + term[...].astype(F32)
        fill(total)

    @core_is(where_ref, 1)
    def _():
        mine = mine_ref[...].astype(F32)
        other = other_ref[...].astype(F32)
        fill(jnp.concatenate([other[: step // 2], mine], axis=0))


def feed_out_kernel(where_ref, first_ref, second_ref, other_ref, expand_ref, contract_ref):
    @core_is(where_ref, 0)
    def _():
        expand_ref[0] = first_ref[...].astype(F32)
        contract_ref[0] = other_ref[...].astype(F32)

    @core_is(where_ref, 1)
    def _():
        expand_ref[0] = other_ref[...].astype(F32)
        contract_ref[0] = second_ref[...].astype(F32)


def swap(x):
    return lax.ppermute(x, "section", [(0, 1), (1, 0)])


def gather_rows(x):
    return lax.all_gather(x, "tensor", axis=0, tiled=True)


def scatter_rows(x):
    size = lax.axis_size("tensor")
    parts = x.reshape(size, x.shape[0] // size, x.shape[1])
    return lax.all_to_all(parts, "tensor", 0, 0)


def deal(x, micro, sub):
    section = lax.axis_index("section")
    across = lax.axis_size("dp")
    odd = lax.axis_index("dp") % 2
    got = []
    for p in range(2):
        route = []
        for c in range(2):
            for d in range(across):
                r, dd = (d // micro, d % micro)
                m = 2 * c + (p ^ (dd & 1))
                route.append((c * across + d, (dd >> 1) * across + m * sub + r))
        chosen = 2 * section + (p ^ odd)
        payload = lax.dynamic_index_in_dim(x, chosen, 0, keepdims=False)
        got.append(lax.ppermute(payload, PLACES, route))
    return jnp.concatenate(got, axis=0)


def undeal(parts, micro, sub):
    across = lax.axis_size("dp")
    got = []
    for p in range(2):
        for u in range(2):
            route = []
            for s in range(2):
                for source in range(across):
                    m, r = (source // sub, source % sub)
                    j = p ^ (m & 1)
                    layer = u ^ (m >> 1)
                    route.append((s * across + source, layer * across + r * micro + 2 * s + j))
            got.append(lax.ppermute(parts[2 * p + u], PLACES, route))
    return got


def across_layer(x, layer, k):
    across = lax.axis_size("dp")
    route = [(layer * across + d, layer * across + (d ^ k)) for d in range(across)]
    return lax.ppermute(x, PLACES, route)


def together(*values):
    return lax.optimization_barrier(values)


def body(
    tokens,
    cotangent,
    lengths,
    random_blocks,
    projections,
    query_value_bias,
    output_weight,
    expand_weight,
    expand_bias,
    contract_weight,
    norm_gains,
    row_biases,
):
    section = lax.axis_index("section")
    place = lax.axis_index("dp")
    seat = lax.axis_index("tensor")
    across = lax.axis_size("dp")
    ways = lax.axis_size("tensor")
    micro = tokens.shape[0]
    sub = across // micro
    plane = place // sub
    share = place % sub
    local = tokens.shape[2]
    width = tokens.shape[3]
    e = projections.shape[3]
    heads = e // HD
    units = expand_weight.shape[2]
    step = projections.shape[2]
    c = query_value_bias.shape[3]
    mine = 2 * local
    rows = mine * ways
    keys = rows * 2 * sub
    blocks = keys // BLOCK
    kw = -(-(e + blocks + 1) // 128) * 128
    vw = 256
    whole_tiles = step % 32 == 0
    start = (share * micro + 2 * section) * ways * local
    length = lax.dynamic_index_in_dim(lengths[:, 0], plane, 0, keepdims=False)
    where = jnp.stack([section, place, plane, seat, start, length, plane % 2, 0]).astype(jnp.int32)
    random_all = lax.all_gather(random_blocks, "section", axis=0, tiled=True)

    attn_keep, attn_send, feed_keep, feed_send = call(
        prepare_kernel,
        [sds((step // 2 + 16, 4 * e), BF16)] * 2 + [sds((step, units), BF16)] * 2,
        where, Far(projections), Far(output_weight), Far(expand_weight),
        Far(contract_weight.transpose(0, 2, 1)), Far(query_value_bias.transpose(0, 2, 1, 3)),
        Far(expand_bias), Far(norm_gains), Far(row_biases),
        scratch=[pltpu.VMEM((step, 4 * e), BF16), pltpu.VMEM((16, 4 * e), F32)],
    )
    attn_traded = swap(attn_send)
    feed_traded = swap(feed_send)
    attn_all = []
    feed_all = []
    for l in range(2):
        own = section == l
        whole = lax.all_gather(jnp.where(own, attn_keep, attn_traded), PLACES, axis=0, tiled=True)
        attn_all.append(whole.reshape(2, across, step // 2 + 16, 4 * e))
        whole = lax.all_gather(jnp.where(own, feed_keep, feed_traded), PLACES, axis=0, tiled=True)
        feed_all.append(whole.reshape(2, width, units))

    x = deal(tokens[:, 0], micro, sub)
    upstream = deal(cotangent[:, 0], micro, sub)
    x, random_all = together(x, random_all)
    if not whole_tiles:
        attn_flat = [
            whole[:, :, : step // 2].transpose(1, 0, 2, 3).reshape(width, 4 * e)
            for whole in attn_all
        ]
    vectors = []
    pair_bias = []
    for l in range(2):
        small = [((0, z, pl.ds(step // 2, 16)), (z,)) for z in range(across)]
        if whole_tiles:
            small = Far(attn_all[l], (across, 16, 4 * e), small)
        else:
            small = attn_all[l][0, :, step // 2 :]
        vec, pair = call(
            partial(unpack_kernel, c, e), [sds((8, width), F32), sds((8, 256), F32)], small
        )
        vectors.append(vec)
        pair_bias.append(pair)

    def attn_weight(l, first, size):
        lanes = pl.ds(first, size)
        if not whole_tiles:
            return Far(attn_flat[l], (width, size), [((slice(None), lanes), ())])
        half = step // 2
        cuts = [
            ((i, z, pl.ds(0, half), lanes), (pl.ds(z * step + i * half, half),))
            for z in range(across)
            for i in range(2)
        ]
        return Far(attn_all[l], (width, size), cuts)

    def feed_weight(l, i):
        return Far(feed_all[l], (width, units), [((i,), ())])

    def all_parts(own):
        pair = [own, swap(own)]
        if sub == 1:
            return pair
        groups = [[m * sub + r for r in range(sub)] for m in range(micro)]
        return [
            lax.all_gather(
                jnp.concatenate(pair, axis=0), "dp", axis=0, tiled=True, axis_index_groups=groups
            )
        ]

    def own_parts(parts):
        if sub == 1:
            return parts
        groups = [[m * sub + r for r in range(sub)] for m in range(micro)]
        total = lax.psum_scatter(
            parts[0], "dp", scatter_dimension=0, tiled=True, axis_index_groups=groups
        )
        return [total[:rows], total[rows:]]

    chunk = min(rows, 256)
    near_rows = sds((mine, width), BF16)
    far_unit = [Far(sds((mine, width), F32)), Far(sds((mine, 128), F32))]

    saved = []
    for l in range(2):
        vec = vectors[l]
        x_all = gather_rows(x)
        q, kv, x_kept, q_kept, kv_kept = call(
            partial(qkv_kernel, ways, local, blocks, e),
            [sds((rows, kw), BF16), sds((rows, kw + vw), BF16),
             Far(sds((rows, width), BF16), plain=True), Far(sds((rows, kw), BF16), plain=True),
             Far(sds((rows, kw + vw), BF16), plain=True)],
            where, x_all, attn_weight(l, 0, 4 * e), pair_bias[l],
            flops=6 * rows * width * 256,
        )
        parts = all_parts(kv)
        attended, mixed, totals, *others = call(
            partial(attention_kernel, heads, l, ways, local, blocks, chunk, len(parts)),
            [Far(sds((rows, width), BF16)), Far(sds((rows, vw), BF16)), Far(sds((8, rows), F32))]
            + [Far(sds(part.shape, BF16), plain=True) for part in parts[1:]],
            where, random_all, q, attn_weight(l, 4 * e - vw, vw), *parts,
            flops=4 * rows * keys * kw, limit=24,
        )
        parts_kept = [kv_kept, others[0]] if sub == 1 else parts
        terms = scatter_rows(attended)
        terms, feed_all[l] = together(terms, feed_all[l])
        if l == 0:
            terms, upstream = together(terms, upstream)
        middle, middle_low, unit1, inverse1 = call(
            first_norm_kernel, [sds((mine, width), F32), near_rows] + far_unit, x, terms, vec
        )
        middle_all = gather_rows(middle_low)
        fed, active, slope, middle_kept = call(
            feed_kernel,
            [Far(sds((rows, width), BF16)), Far(sds((rows, units), BF16)),
             Far(sds((rows, units), BF16)), Far(sds((rows, width), BF16), plain=True)],
            middle_all, vec, feed_weight(l, 0), feed_weight(l, 1),
            flops=4 * rows * width * units,
        )
        terms = scatter_rows(fed)
        if l == 0:
            x, low_kept, unit2, inverse2 = call(
                partial(second_norm_kernel, ways),
                [near_rows, Far(near_rows, plain=True)] + far_unit,
                where, middle, terms, vec,
            )
        else:
            *places, unit2, inverse2 = call(
                partial(second_norm_kernel, ways),
                [sds((local, width), BF16)] * 4 + far_unit,
                where, middle, terms, vec, Far(low_kept),
            )
        saved.append(
            (x_kept, q_kept, parts_kept, mixed, totals, unit1, inverse1, middle_kept, active,
             slope, unit2, inverse2)
        )
    activation_rows = undeal(places, micro, sub)

    feed_parts = [None, None]
    for l in (1, 0):
        vec = vectors[l]
        (x_kept, q_kept, parts_kept, mixed, totals, unit1, inverse1, middle_kept, active,
         slope, unit2, inverse2) = saved[l]
        near_f32 = sds((mine, width), F32)
        second, feed_low, second_sums = call(
            partial(second_back_kernel, ways),
            [near_f32, near_rows, sds((8, width), F32)],
            where, upstream, vec, Far(unit2), Far(inverse2),
        )
        feed_grad = gather_rows(feed_low)
        hidden, fed_back, unit_sums = call(
            feed_back_kernel,
            [Far(sds((rows, units), BF16)), Far(sds((rows, width), BF16)), sds((8, units), F32)],
            feed_grad, feed_weight(l, 1), Far(slope), feed_weight(l, 0),
            flops=4 * rows * width * units,
        )
        terms = scatter_rows(fed_back)
        feed_kept, feed_sent = call(
            feed_pack_kernel,
            [sds((width, units), BF16)] * 2,
            where, Far(hidden), feed_grad, Far(middle_kept), Far(active),
            flops=4 * rows * width * units,
        )
        terms, feed_kept, feed_sent = together(terms, feed_kept, feed_sent)
        if l == 0:
            terms, feed_parts[1] = together(terms, feed_parts[1])
        feed_half = (feed_kept.astype(F32) + swap(feed_sent).astype(F32)).astype(BF16)
        first_grad, first_low = call(
            first_back_kernel,
            [Far(near_f32), sds((mine + 16, width), BF16)],
            second, terms, vec, second_sums, Far(unit1), Far(inverse1),
        )
        attended_grad = gather_rows(first_low).reshape(ways, mine + 16, width)
        attended_grad, feed_half = together(attended_grad, feed_half)
        if l == 0:
            attended_grad, attn_part = together(attended_grad, attn_part)
        feed_parts[l] = lax.psum_scatter(feed_half, "dp", scatter_dimension=0, tiled=True)
        dq, norm_sums, *dkv = call(
            partial(attention_back_kernel, heads, l, ways, local, blocks, chunk),
            [sds((rows, 256), BF16), sds((16, width), F32)]
            + [sds((part.shape[0], 256 + vw), BF16) for part in parts_kept],
            where, random_all, attended_grad, attn_weight(l, 4 * e - vw, vw), Far(mixed),
            Far(q_kept), Far(totals), *[Far(part) for part in parts_kept],
            flops=10 * rows * keys * kw, limit=32,
        )
        dkv_own, dkv_other = own_parts(dkv)
        triple, projected, pair_sums = call(
            partial(projection_back_kernel, e),
            [sds((rows, 4 * e), BF16), Far(sds((rows, width), BF16)), sds((8, 4 * e), F32)],
            dq, dkv_own, swap(dkv_other), attn_weight(l, 0, 4 * e),
            flops=6 * rows * width * 256,
        )
        terms = scatter_rows(projected)
        cut = step if whole_tiles else width
        pieces = width // cut
        pack_shape = (pieces, cut + 16, 4 * e) if l == 0 else (2, pieces, cut // 2 + 16, 4 * e)
        (pack,) = call(
            partial(attn_pack_kernel, l == 0, cut, e),
            [sds(pack_shape, BF16)],
            where, triple, attended_grad, norm_sums, unit_sums, pair_sums, Far(x_kept),
            Far(mixed),
            flops=8 * rows * width * 256,
            scratch=[pltpu.VMEM((width, 4 * e), BF16)],
        )
        if not whole_tiles:
            pack = split_pack(pack, l == 0, across)
        if l == 1:
            terms, pack = together(terms, pack)
            attn_part = lax.psum_scatter(
                pack.reshape((-1,) + pack.shape[2:]), PLACES, scatter_dimension=0
            )
            upstream, later = call(
                input_kernel, [near_rows, Far(near_rows, plain=True)], Far(first_grad), terms
            )
        else:
            traded = lax.ppermute(pack, "section", [(1, 0)])
            if whole_tiles:
                sums = call(
                    pair_sum_kernel,
                    [sds(pack.shape[1:], F32)] + [sds(pack.shape[1:], BF16)] * (across - 1),
                    pack, traded,
                )
                early = [sums[0]] + [across_layer(sums[k], 0, k) for k in range(1, across)]
            else:
                total = (pack.astype(F32) + traded.astype(F32)).astype(BF16)
                early = [
                    lax.psum_scatter(total, "dp", scatter_dimension=0).astype(F32)
                ]
            places = call(
                last_input_kernel, [sds((local, width), BF16)] * 4,
                where, Far(first_grad), terms, Far(later),
            )
            input_rows = undeal(places, micro, sub)

    feed_other = swap(jnp.where(section == 0, feed_parts[1], feed_parts[0]))
    expand_out, contract_out = call(
        feed_out_kernel, [sds((1, step, units), F32)] * 2,
        where, feed_parts[0], feed_parts[1], feed_other,
    )
    attn_other = lax.ppermute(attn_part, "section", [(0, 1)])
    projections_out, output_out, gains_out, biases_out, units_out, pairs_out = call(
        partial(attn_out_kernel, step, e, c),
        [sds((1, 3, step, e), F32), sds((1, e, step), F32), sds((1, 2, step), F32),
         sds((1, 4, step), F32), sds((units // HD, 1, c), F32), sds((1, heads, 2, c), F32)],
        where, *early, attn_part, attn_other,
    )
    (activations,) = call(
        place_out_kernel, [sds((1, micro, 1, local, width), BF16)], where, *activation_rows
    )
    (input_grads,) = call(
        place_out_kernel, [sds((1, micro, 1, local, width), F32)], where, *input_rows
    )
    return (
        activations,
        input_grads,
        projections_out,
        pairs_out.transpose(0, 2, 1, 3),
        output_out,
        expand_out,
        units_out.transpose(1, 0, 2),
        contract_out.transpose(0, 2, 1),
        gains_out,
        biases_out,
    )


def split_pack(pack, relative, across):
    if relative:
        weights, small = (pack[0, :-16], pack[0, -16:])
        weights = weights.reshape(across, -1, weights.shape[1])
        small = jnp.broadcast_to(small, (across,) + small.shape)
        return jnp.concatenate([weights, small], axis=1)
    weights = pack[:, 0, :-16].reshape(-1, pack.shape[3])
    weights = weights.reshape(across, 2, -1, pack.shape[3]).transpose(1, 0, 2, 3)
    small = jnp.broadcast_to(pack[0, 0, -16:], (2, across, 16, pack.shape[3]))
    return jnp.concatenate([weights, small], axis=2)


def solution(mesh):
    in_specs = (
        P(None, None, ("dp", "tensor"), None),
        P(None, None, ("dp", "tensor"), None),
        P(),
        P("section", "tensor", None, None),
        P("section", None, "dp", "tensor"),
        P("section", None, "tensor", "dp"),
        P("section", "tensor", "dp"),
        P("section", "dp", "tensor"),
        P("section", "tensor", "dp"),
        P("section", "tensor", "dp"),
        P("section", None, "dp"),
        P("section", None, "dp"),
    )
    out_specs = (
        P("section", None, None, ("dp", "tensor"), None),
        P("section", None, None, ("dp", "tensor"), None),
        P("section", None, "dp", "tensor"),
        P("section", None, "tensor", "dp"),
        P("section", "tensor", "dp"),
        P("section", "dp", "tensor"),
        P("section", "tensor", "dp"),
        P("section", "tensor", "dp"),
        P("section", None, "dp"),
        P("section", None, "dp"),
    )
    return jax.shard_map(body, mesh=mesh, in_specs=in_specs, out_specs=out_specs, check_vma=False)
```

```python
import math
from functools import partial

import jax
import jax.numpy as jnp
from jax import lax
from jax.experimental import pallas as pl
from jax.experimental.pallas import tpu as pltpu
from jax.sharding import PartitionSpec as P

HD = 64
BLOCK = 64
GLOBAL = 2
EPSILON = 1e-12
MASKED = -1e30
GELU_A = 0.7978845608028654
GELU_B = 0.044715
F32 = jnp.float32
BF16 = jnp.bfloat16
MIB = 1 << 20
PLACES = ("section", "dp")


def nt(a, b):
    return lax.dot_general(a, b, (((1,), (1,)), ((), ())), preferred_element_type=F32)


def tn(a, b):
    return lax.dot_general(a, b, (((0,), (0,)), ((), ())), preferred_element_type=F32)


def nn(a, b):
    return jnp.dot(a, b, preferred_element_type=F32)


def sds(shape, dtype):
    return jax.ShapeDtypeStruct(shape, dtype)


class Far:
    def __init__(self, array, shape=None, cuts=None, plain=False, into=None):
        self.array = array
        self.shape = array.shape if shape is None else shape
        self.cuts = [((), ())] if cuts is None else cuts
        self.plain = plain
        self.into = into


class Raw:
    def __init__(self, array):
        self.array = array


def at(ref, index):
    return ref.at[index] if index else ref


class Arriving:
    def __init__(self, source, buffer, sems, first, cuts):
        self.buffer = buffer
        self.shape = buffer.shape
        self.copies = [
            pltpu.make_async_copy(at(source, a), at(buffer, b), sems.at[first + i])
            for i, (a, b) in enumerate(cuts)
        ]
        for copy in self.copies:
            copy.start()
        self.there = False

    def settle(self):
        if not self.there:
            for copy in self.copies:
                copy.wait()
            self.there = True

    def __getitem__(self, index):
        self.settle()
        return self.buffer[index]


class Leaving:
    def __init__(self, target, buffer, sem):
        self.target = target
        self.buffer = buffer
        self.shape = target.shape
        self.sem = sem
        self.copy = None

    def __setitem__(self, index, value):
        self.buffer[index] = value

    def send(self, source=None):
        self.copy = pltpu.make_async_copy(
            self.buffer if source is None else source, self.target, self.sem
        )
        self.copy.start()

    def finish(self):
        if self.copy is None:
            self.send()
        self.copy.wait()


def call(kernel, outs, *args, flops=0, limit=16, scratch=()):
    arrays = []
    in_specs = []
    out_specs = []
    out_shapes = []
    buffers = []
    size = 0
    semaphores = 0
    for arg in args:
        if isinstance(arg, Raw):
            arrays.append(pltpu.with_memory_space_constraint(arg.array, pltpu.HBM))
            in_specs.append(pl.BlockSpec(memory_space=pltpu.HBM))
        elif isinstance(arg, Far):
            arrays.append(pltpu.with_memory_space_constraint(arg.array, pltpu.HBM))
            in_specs.append(pl.BlockSpec(memory_space=pltpu.HBM))
            if arg.into is None:
                buffers.append(pltpu.VMEM(arg.shape, arg.array.dtype))
            semaphores += len(arg.cuts)
            size += math.prod(arg.shape) * arg.array.dtype.itemsize
        else:
            arrays.append(arg)
            scalar = arg.dtype == jnp.int32
            in_specs.append(pl.BlockSpec(memory_space=pltpu.SMEM if scalar else pltpu.VMEM))
            size += arg.size * arg.dtype.itemsize
    for out in outs:
        if isinstance(out, Raw):
            out_shapes.append(pltpu.HBM(out.array.shape, out.array.dtype))
            out_specs.append(pl.BlockSpec(memory_space=pltpu.HBM))
        elif isinstance(out, Far):
            out_shapes.append(pltpu.HBM(out.shape, out.array.dtype))
            out_specs.append(pl.BlockSpec(memory_space=pltpu.HBM))
            if not out.plain:
                buffers.append(pltpu.VMEM(out.shape, out.array.dtype))
            semaphores += 1
            size += math.prod(out.shape) * out.array.dtype.itemsize
        else:
            out_shapes.append(out)
            out_specs.append(pl.BlockSpec(memory_space=pltpu.VMEM))
            size += out.size * out.dtype.itemsize

    def whole(*refs):
        refs = list(refs)
        ins = refs[: len(args)]
        results = refs[len(args) : len(args) + len(outs)]
        rest = refs[len(args) + len(outs) :]
        sems = rest.pop() if semaphores else None
        given = []
        used = 0
        for arg, ref in zip(args, ins):
            if isinstance(arg, Far):
                buffer = rest.pop(0) if arg.into is None else results[arg.into]
                given.append(Arriving(ref, buffer, sems, used, arg.cuts))
                used += len(arg.cuts)
            else:
                given.append(ref)
        leaving = []
        for out, ref in zip(outs, results):
            if isinstance(out, Far):
                buffer = None if out.plain else rest.pop(0)
                leaving.append(Leaving(ref, buffer, sems.at[used]))
                given.append(leaving[-1])
                used += 1
            else:
                given.append(ref)
        kernel(*given, *rest)
        for item in given:
            if isinstance(item, Arriving):
                item.settle()
        for item in leaving:
            item.finish()

    scratch_shapes = buffers + list(scratch)
    if semaphores:
        scratch_shapes = scratch_shapes + [pltpu.SemaphoreType.DMA((semaphores,))]
    return pl.pallas_call(
        whole,
        out_shape=tuple(out_shapes),
        in_specs=in_specs,
        out_specs=tuple(out_specs),
        scratch_shapes=scratch_shapes,
        compiler_params=pltpu.CompilerParams(vmem_limit_bytes=limit * MIB),
        cost_estimate=pl.CostEstimate(flops=flops, bytes_accessed=size, transcendentals=0),
    )(*arrays)


SECTION, PLACE, PLANE, SEAT, START, LENGTH, FLIP = range(7)


def positions(where_ref, count, ways, local, first):
    row = lax.broadcasted_iota(jnp.int32, (count, 1), 0) + first
    group = jnp.bitwise_xor(row // local % 2, where_ref[FLIP])
    return (
        where_ref[START] + group * (ways * local) + row // (2 * local) * local + row % local
    )


def core_is(where_ref, core):
    return pl.when(where_ref[SECTION] == core)


def prepare_kernel(
    where_ref, projections_ref, output_ref, expand_ref, contract_ref, pair_ref, unit_ref,
    gain_ref, bias_ref, attn_keep, attn_send, keep_out, send_out, whole, small
):
    step, e = projections_ref.shape[2:]
    heads, _, c = pair_ref.shape[1:]
    half = step // 2
    whole[:, :e] = projections_ref[0, 0]
    whole[:, e : 2 * e] = projections_ref[0, 2]
    whole[:, 2 * e : 3 * e] = projections_ref[0, 1]
    whole[:, 3 * e :] = output_ref[0].T
    small[...] = jnp.zeros_like(small)
    small[0:2, :step] = gain_ref[0].astype(F32)
    small[2:6, :step] = bias_ref[0].astype(F32)
    small[: unit_ref.shape[1], 256 : 256 + c] = unit_ref[0].astype(F32)
    for i in range(heads):
        small[i : i + 1, 384 : 384 + c] = pair_ref[0, i, 0:1].astype(F32)
        small[i : i + 1, 512 : 512 + c] = pair_ref[0, i, 1:2].astype(F32)
    attn_keep[half:] = small[...].astype(BF16)
    attn_send[half:] = small[...].astype(BF16)
    expand = expand_ref[0]
    contract = contract_ref[0]

    @core_is(where_ref, 0)
    def _():
        attn_keep[:half] = whole[:half]
        attn_send[:half] = whole[half:]
        keep_out[...] = expand
        send_out[...] = contract

    @core_is(where_ref, 1)
    def _():
        attn_keep[:half] = whole[half:]
        attn_send[:half] = whole[:half]
        keep_out[...] = contract
        send_out[...] = expand


def unpack(c, e, raw_ref, vec_ref):
    places = raw_ref.shape[0]
    width = vec_ref.shape[1]
    w = width // places

    def of_heads(rows, lanes, z):
        source = lax.broadcasted_iota(jnp.int32, (128, lanes), 0)
        target = lax.broadcasted_iota(jnp.int32, (128, lanes), 1)
        repeat = ((target % c == source) & (source < c)).astype(F32).astype(BF16)
        spread_rows = nn(rows, repeat)
        head = lax.broadcasted_iota(jnp.int32, spread_rows.shape, 0)
        lane = lax.broadcasted_iota(jnp.int32, spread_rows.shape, 1)
        keep = (lane // HD == head) & (lane % HD // c == z)
        return jnp.sum(jnp.where(keep, spread_rows, 0.0), axis=0, keepdims=True)

    norms = jnp.zeros((16, width), F32)
    units = jnp.zeros((1, width), F32)
    queries = jnp.zeros((1, 256), F32)
    values = jnp.zeros((1, 256), F32)
    for z in range(places):
        rows = raw_ref[z]
        source = lax.broadcasted_iota(jnp.int32, (256, width), 0)
        target = lax.broadcasted_iota(jnp.int32, (256, width), 1)
        move = ((target == source + z * w) & (source < w)).astype(F32).astype(BF16)
        norms = norms + nn(rows[:, :256], move)
        units = units + of_heads(rows[:, 256:384], width, z)
        queries = queries + of_heads(rows[:, 384:512], 256, z)
        values = values + of_heads(rows[:, 512:640], 256, z)
    vec_ref[...] = norms[:8]
    vec_ref[6:7] = units
    lane = lax.broadcasted_iota(jnp.int32, (1, 256), 1)
    queries = jnp.where(lane < e, queries, 0.0)
    values = jnp.where(lane < e, values, 0.0)
    return (queries, pltpu.roll(values, 256 - e, 1))


def qkv_kernel(
    ways, local, blocks, c, e, where_ref, x_ref, raw_ref, w_ref, q_ref, kv_ref, vec_ref, *kept
):
    kw = q_ref.shape[1]
    vw = kv_ref.shape[1] - kw
    x = x_ref[...]
    kept[0].send(x_ref)
    query_bias, value_bias = unpack(c, e, raw_ref, vec_ref)
    lead = 2 * e // 128 * 128
    q = (nn(x, w_ref[:, :256]) + query_bias).astype(BF16).astype(F32) * HD ** (-0.5)
    lane = lax.broadcasted_iota(jnp.int32, (1, 256), 1)
    q = jnp.where(lane < e, q, 0.0).astype(BF16)
    q_ref[:, :256] = q
    if kw > 256:
        q_ref[:, 256:] = jnp.zeros((q.shape[0], kw - 256), BF16)
    kept[1].send(q_ref)
    position = positions(where_ref, x.shape[0], ways, local, 0)
    block = position // BLOCK
    lane = lax.broadcasted_iota(jnp.int32, (1, kw), 1)
    hidden = (position >= where_ref[LENGTH]) & (lane == e + blocks)
    tail = jnp.where(lane == e + block, 1.0, jnp.where(hidden, MASKED, 0.0))
    k = nn(x, w_ref[:, lead : lead + 256])
    if kw > 256:
        k = jnp.concatenate([k, jnp.zeros((k.shape[0], kw - 256), F32)], axis=1)
    kv_ref[:, :kw] = jnp.where(lane < e, k, tail).astype(BF16)
    kv_ref[:, kw:] = (nn(x, w_ref[:, 128 : 128 + vw]) + value_bias).astype(BF16)
    kept[2].send(kv_ref)


def head_mask(first, lanes):
    lane = lax.broadcasted_iota(jnp.int32, (1, lanes), 1)
    return ((lane >= first) & (lane < first + HD)).astype(F32)


def seen_rows(where_ref, random_ref, layer, h, rows, ways, local, kw, e, blocks):
    lane = lax.broadcasted_iota(jnp.int32, (1, kw), 1)
    key = lane - e
    parts = []
    for g in range(rows // local):
        group = jnp.bitwise_xor(g % 2, where_ref[FLIP])
        position = where_ref[START] + group * (ways * local) + g // 2 * local
        block = position // BLOCK
        seen = (key < GLOBAL) | (jnp.abs(key - block) <= 1) | (block < GLOBAL)
        for i in range(random_ref.shape[3]):
            seen = seen | (key == random_ref[layer, h, block, i])
        hidden = (key >= 0) & (key < blocks) & jnp.logical_not(seen)
        line = jnp.where(key == blocks, 1.0, jnp.where(hidden, MASKED, 0.0))
        parts.append(jnp.broadcast_to(line, (local, kw)))
    return jnp.concatenate(parts, axis=0)


def attention_kernel(
    heads, layer, ways, local, blocks, chunk, count, where_ref, random_ref, q_ref, w_ref, *refs
):
    parts, (out_ref, mixed_out, total_out), kept = (
        refs[:count], refs[count : count + 3], refs[count + 3 :]
    )
    rows, kw = q_ref.shape
    e = heads * HD
    vw = parts[0].shape[1] - kw
    shift = vw - e
    for out, part in zip(kept, parts[1:]):
        out.send(part)
    k = jnp.concatenate([part[:, :kw] for part in parts], axis=0)
    vt = jnp.concatenate([part[:, kw:] for part in parts], axis=0).T
    q = q_ref[...].astype(F32)
    lines = [jnp.zeros((shift, rows), F32)]
    totals = []
    for h in range(heads):
        seen = seen_rows(where_ref, random_ref, layer, h, rows, ways, local, kw, e, blocks)
        qa = (q * head_mask(h * HD, kw) + seen).astype(BF16)
        vh = vt[shift + h * HD : shift + (h + 1) * HD]
        cells = []
        sums = []
        for c in range(0, rows, chunk):
            scores = nt(k, qa[c : c + chunk])
            top = jnp.max(scores, axis=0, keepdims=True)
            p = jnp.exp(scores - top)
            total = jnp.sum(p, axis=0, keepdims=True)
            cells.append(nn(vh, p.astype(BF16)) / total)
            sums.append(top + jnp.log(total))
        lines.append(jnp.concatenate(cells, axis=1))
        totals.append(jnp.concatenate(sums, axis=1))
    total_out[...] = jnp.concatenate(totals + [jnp.zeros((8 - heads, rows), F32)], axis=0)
    total_out.send()
    mixed = jnp.concatenate(lines, axis=0).T.astype(BF16)
    mixed_out[...] = mixed
    mixed_out.send()
    out_ref[...] = nt(mixed, w_ref[...]).astype(BF16)


def attention_back_kernel(
    heads, layer, ways, local, blocks, chunk, where_ref, random_ref, grad_ref, w_ref, mixed_ref,
    q_ref, total_ref, *refs
):
    count = (len(refs) - 6) // 2
    parts, (kept_ref, traded_ref), (dq_ref, small_ref, _, half_out), outs = (
        refs[:count], refs[count : count + 2], refs[count + 2 : count + 6], refs[count + 6 :]
    )
    rows, kw = q_ref.shape
    e = heads * HD
    vw = mixed_ref.shape[1]
    shift = vw - e
    width = grad_ref.shape[2]
    grad = grad_ref[:, : 2 * local].reshape(rows, width)
    small = grad_ref[0, 2 * local :].astype(F32)
    for i in range(1, ways):
        small = small + grad_ref[i, 2 * local :].astype(F32)
    small_ref[...] = small
    mixed_grad = nn(grad, w_ref[:, w_ref.shape[1] - vw :]).astype(BF16).astype(F32)
    product = mixed_grad * mixed_ref[...].astype(F32)
    masks = jnp.concatenate([head_mask(shift + h * HD, vw) for h in range(8)], axis=0)
    inner = lax.dot_general(
        masks, product, (((1,), (1,)), ((), ())),
        preferred_element_type=F32, precision=lax.Precision.HIGHEST,
    )
    q = q_ref[...].astype(F32)
    k = jnp.concatenate([part[:, :kw] for part in parts], axis=0)
    v = jnp.concatenate([part[:, kw:] for part in parts], axis=0)
    kt = k[:, :256].T
    totals = total_ref[...]
    half_out[...] = (kept_ref[...].astype(F32) + traded_ref[...].astype(F32)).astype(BF16)
    half_out.send()
    dk = None
    dv = None
    lines = []
    for h in range(heads):
        seen = seen_rows(where_ref, random_ref, layer, h, rows, ways, local, kw, e, blocks)
        qm = q * head_mask(h * HD, kw)
        qa = (qm + seen).astype(BF16)
        qm = qm[:, :256].astype(BF16)
        gm = (mixed_grad * head_mask(shift + h * HD, vw)).astype(BF16)
        kh = kt[h * HD : (h + 1) * HD]
        cells = []
        for c in range(0, rows, chunk):
            scores = nt(k, qa[c : c + chunk])
            p = jnp.exp(scores - totals[h : h + 1, c : c + chunk])
            dp = nt(v, gm[c : c + chunk])
            ds = (p * (dp - inner[h : h + 1, c : c + chunk])).astype(BF16)
            dv_term = nn(p.astype(BF16), gm[c : c + chunk])
            dk_term = nn(ds, qm[c : c + chunk])
            dv = dv_term if dv is None else dv + dv_term
            dk = dk_term if dk is None else dk + dk_term
            cells.append(nn(kh, ds))
        lines.append(jnp.concatenate(cells, axis=1))
    lines.append(jnp.zeros((256 - e, rows), F32))
    dq = jnp.concatenate(lines, axis=0).T * HD ** (-0.5)
    dq_ref[...] = dq.astype(BF16)
    start = 0
    for out in outs:
        size = out.shape[0]
        out[:, :256] = dk[start : start + size].astype(BF16)
        out[:, 256:] = dv[start : start + size].astype(BF16)
        start += size


def projection_back_kernel(e, dq_ref, own_ref, other_ref, w_ref, triple_ref, out_ref, sums_ref):
    vw = own_ref.shape[1] - 256
    width = w_ref.shape[1]
    lead = 2 * e // 128 * 128
    rows = dq_ref.shape[0]
    dq = dq_ref[...]
    dkv = (own_ref[...].astype(F32) + other_ref[...].astype(F32)).astype(BF16).astype(F32)
    dv = dkv[:, 256:]
    head = dq.astype(F32)
    nothing = jnp.zeros((rows, 128), F32)
    triple = jnp.concatenate(
        [head[:, :128], head[:, 128:] + dv[:, :128], dv[:, 128:], dkv[:, :256], nothing], axis=1
    ).astype(BF16)
    triple_ref[...] = triple
    sums_ref[...] = jnp.zeros_like(sums_ref)
    sums_ref[0:1] = jnp.sum(triple.astype(F32), axis=0, keepdims=True)
    out_ref[...] = nt(triple, w_ref[...]).astype(BF16)


def norm(values):
    average = jnp.mean(values, axis=-1, keepdims=True)
    centered = values - average
    spread_now = jnp.mean(centered * centered, axis=-1, keepdims=True)
    inverse = lax.rsqrt(spread_now + EPSILON)
    return (centered * inverse, inverse)


def total_of(terms_ref):
    total = terms_ref[0].astype(F32)
    for i in range(1, terms_ref.shape[0]):
        total = total + terms_ref[i].astype(F32)
    return total


def first_norm_kernel(x_ref, terms_ref, vec_ref, middle_ref, low_ref, unit_out, inverse_out):
    values = x_ref[...].astype(F32) + total_of(terms_ref) + vec_ref[2:3]
    unit, inverse = norm(values)
    unit_out[...] = unit
    unit_out.send()
    inverse_out[...] = jnp.broadcast_to(inverse, inverse_out.shape)
    inverse_out.send()
    middle = unit * vec_ref[0:1] + vec_ref[4:5]
    middle_ref[...] = middle
    low_ref[...] = middle.astype(BF16)


def valid_rows(where_ref, ways, local):
    position = positions(where_ref, 2 * local, ways, local, where_ref[SEAT] * 2 * local)
    return (position < where_ref[LENGTH]).astype(F32)


def place_parts(where_ref, early, later, outs):
    half = early.shape[0] // 2
    late_plane = where_ref[PLANE] // 2
    for u in range(2):
        for p in range(2):
            @pl.when(late_plane == u)
            def _(u=u, p=p):
                outs[2 * p + u][...] = early[p * half : (p + 1) * half]

            @pl.when(late_plane != u)
            def _(u=u, p=p):
                outs[2 * p + u][...] = later[p * half : (p + 1) * half]


def norm_back(grad, unit, inverse, gain):
    scaled = grad * gain
    return inverse * (
        scaled
        - jnp.mean(scaled, axis=-1, keepdims=True)
        - unit * jnp.mean(scaled * unit, axis=-1, keepdims=True)
    )


def second_norm(ways, where_ref, middle_ref, terms_ref, vec_ref):
    unit, inverse = norm(middle_ref[...] + total_of(terms_ref) + vec_ref[3:4])
    result = unit * vec_ref[1:2] + vec_ref[5:6]
    valid = valid_rows(where_ref, ways, unit.shape[0] // 2)
    return ((result * valid).astype(BF16), unit, inverse, valid)


def second_back(grad, unit, inverse, vec_ref, second_ref, low_ref, sums_ref):
    second = norm_back(grad, unit, inverse, vec_ref[1:2])
    low_ref[...] = second.astype(BF16)
    second_ref[...] = second
    sums_ref[...] = jnp.zeros_like(sums_ref)
    sums_ref[0:1] = jnp.sum(grad * unit, axis=0, keepdims=True)
    sums_ref[1:2] = jnp.sum(grad, axis=0, keepdims=True)
    sums_ref[2:3] = jnp.sum(second, axis=0, keepdims=True)


def second_norm_kernel(
    ways, where_ref, middle_ref, terms_ref, vec_ref, low_ref, kept, unit_out, inverse_out
):
    low, unit, inverse, _ = second_norm(ways, where_ref, middle_ref, terms_ref, vec_ref)
    low_ref[...] = low
    kept.send(low_ref)
    unit_out[...] = unit
    unit_out.send()
    inverse_out[...] = jnp.broadcast_to(inverse, inverse_out.shape)
    inverse_out.send()


def turn_kernel(
    ways, where_ref, middle_ref, terms_ref, vec_ref, up_ref, second_ref, low_ref, sums_ref, kept
):
    low, unit, inverse, valid = second_norm(ways, where_ref, middle_ref, terms_ref, vec_ref)
    kept[...] = low
    kept.send()
    second_back(
        up_ref[...].astype(F32) * valid, unit, inverse, vec_ref, second_ref, low_ref, sums_ref
    )


def between_kernel(
    ways, where_ref, terms_ref, vec_ref, first_ref, unit_ref, inverse_ref, second_ref, low_ref,
    sums_ref, kept
):
    low = (first_ref[...] + total_of(terms_ref)).astype(BF16)
    kept[...] = low
    kept.send()
    grad = low.astype(F32) * valid_rows(where_ref, ways, low.shape[0] // 2)
    second_back(
        grad, unit_ref[...], inverse_ref[:, 0:1], vec_ref, second_ref, low_ref, sums_ref
    )


def first_back_kernel(
    second_ref, terms_ref, vec_ref, before_ref, unit_ref, inverse_ref, first_ref, low_ref
):
    grad = second_ref[...] + total_of(terms_ref)
    unit = unit_ref[...]
    first = norm_back(grad, unit, inverse_ref[:, 0:1], vec_ref[0:1])
    first_ref[...] = first
    rows = first.shape[0]
    low_ref[:rows] = first.astype(BF16)
    before = before_ref[...]
    low_ref[rows:] = jnp.concatenate(
        [jnp.sum(grad * unit, axis=0, keepdims=True), before[0:1],
         jnp.sum(first, axis=0, keepdims=True), before[2:3],
         jnp.sum(grad, axis=0, keepdims=True), before[1:2],
         jnp.zeros((10, first.shape[1]), F32)], axis=0
    ).astype(BF16)


def last_input_kernel(where_ref, terms_ref, first_ref, later_ref, *outs):
    low = (first_ref[...] + total_of(terms_ref)).astype(BF16)
    place_parts(where_ref, low, later_ref[...], outs)


def place_out_kernel(where_ref, *refs):
    parts, out_ref = (refs[:-1], refs[-1])
    odd = where_ref[PLACE] % 2
    for p in range(2):
        for u in range(2):
            m = 2 * jnp.bitwise_xor(where_ref[SECTION], u) + jnp.bitwise_xor(odd, p)
            out_ref[0, m, 0] = parts[2 * p + u][...].astype(F32)


def activation_out_kernel(micro, sub, where_ref, first_ref, last_ref, out_ref, sems):
    local = out_ref.shape[3]
    place = where_ref[PLACE]
    side = place % micro // 2

    def copies(ref):
        result = []
        for m in range(micro):
            source = side * (micro * sub) + m * sub + place // micro
            row = (2 * source + jnp.bitwise_xor(place % 2, m & 1)) * local
            rows = pl.ds(pl.multiple_of(row, local), local)
            result.append(pltpu.make_async_copy(ref.at[rows], out_ref.at[0, m, 0], sems.at[m]))
        return result

    for core, ref in enumerate((first_ref, last_ref)):
        @core_is(where_ref, core)
        def _(ref=ref):
            for copy in copies(ref):
                copy.start()
            for copy in copies(ref):
                copy.wait()


def feed_kernel(x_ref, vec_ref, expand_ref, contract_ref, out_ref, active_out, slope_out, kept):
    kept.send(x_ref)
    v = nn(x_ref[...], expand_ref[...]) + vec_ref[6:7]
    th = jnp.tanh(GELU_A * (v + GELU_B * v * v * v))
    half = 0.5 * (1.0 + th)
    active = (v * half).astype(BF16)
    active_out[...] = active
    active_out.send()
    slope = half + 0.5 * v * (1.0 - th * th) * GELU_A * (1.0 + 3.0 * GELU_B * v * v)
    slope_out[...] = slope.astype(BF16)
    slope_out.send()
    out_ref[...] = nt(active, contract_ref[...]).astype(BF16)


def feed_back_kernel(
    grad_ref, contract_ref, slope_ref, expand_ref, hidden_ref, out_ref, sums_ref
):
    active_grad = nn(grad_ref[...], contract_ref[...])
    hidden = (active_grad * slope_ref[...].astype(F32)).astype(BF16)
    hidden_ref[...] = hidden
    hidden_ref.send()
    sums_ref[...] = jnp.zeros_like(sums_ref)
    sums_ref[0:1] = jnp.sum(hidden.astype(F32), axis=0, keepdims=True)
    out_ref[...] = nt(hidden, expand_ref[...]).astype(BF16)


def feed_pack_kernel(where_ref, hidden_ref, grad_ref, middle_ref, active_ref, keep_ref, send_ref):
    def put(value, core):
        @core_is(where_ref, core)
        def _():
            keep_ref[...] = value

        @core_is(where_ref, 1 - core)
        def _():
            send_ref[...] = value

    put(tn(middle_ref[...], hidden_ref[...]).astype(BF16), 0)
    put(tn(grad_ref[...], active_ref[...]).astype(BF16), 1)


def attn_pack_kernel(
    relative, step, e, where_ref, triple_ref, grad_ref, norm_ref, unit_ref, pair_ref, x_ref,
    mixed_ref, out_ref
):
    x = x_ref[...]
    width = x.shape[1]
    vw = mixed_ref.shape[1]
    places = width // step
    local = grad_ref.shape[1] - 16
    grad = grad_ref[:, :local].reshape(x.shape)
    total = tn(x, triple_ref[...])
    last = total[:, width - vw :] + tn(grad, mixed_ref[...])
    weights = jnp.concatenate([total[:, : width - vw], last], axis=1).astype(BF16)
    small = jnp.concatenate(
        [norm_ref[:6], unit_ref[0:1], pair_ref[0:1], jnp.zeros((8, width), F32)], axis=0
    ).astype(BF16)
    for z in range(places):
        begin = z * step
        if relative:
            k = jnp.bitwise_xor(where_ref[PLACE], z) if places > 1 else 0
            out_ref[k, :step] = weights[begin : begin + step]
            out_ref[k, step:] = small
        else:
            half = step // 2
            for i in range(2):
                out_ref[i, z, :half] = weights[begin + i * half : begin + (i + 1) * half]
                out_ref[i, z, half:] = small


def pair_sum_kernel(mine_ref, other_ref, own_ref, *sent_refs):
    own_ref[...] = mine_ref[0].astype(F32) + other_ref[0].astype(F32)
    for k, sent in enumerate(sent_refs):
        sent[...] = (
            mine_ref[k + 1].astype(F32) + other_ref[k + 1].astype(F32)
        ).astype(BF16)


def attn_out_kernel(
    step, e, c, where_ref, *refs
):
    early, (mine_ref, other_ref), outs = (refs[:-8], refs[-8:-6], refs[-6:])
    projections_ref, output_ref, gain_ref, bias_ref, unit_ref, pair_ref = outs
    width = mine_ref.shape[1]

    def fill(total):
        weights = total[:step]
        small = total[step : step + 8]
        projections_ref[0, 0] = weights[:, :e]
        projections_ref[0, 1] = weights[:, 2 * e : 3 * e]
        projections_ref[0, 2] = pltpu.roll(weights, width - e, 1)[:, :e]
        output_ref[0] = pltpu.roll(weights, e, 1)[:, :e].T
        mine = pltpu.roll(small, lax.rem(width - where_ref[PLACE] * step, width), 1)
        gain_ref[0] = mine[0:2, :step]
        bias_ref[0] = mine[2:6, :step]

        def column(row, head):
            shift = lax.rem(2 * width - head * HD - where_ref[PLACE] * c, width)
            return pltpu.roll(small, shift, 1)[row : row + 1, :c]

        for head in range(unit_ref.shape[0]):
            unit_ref[head] = column(6, head)
        for head in range(pair_ref.shape[1]):
            pair_ref[0, head, 0:1] = column(7, head)
            pair_ref[0, head, 1:2] = column(7, head + e // HD)

    @core_is(where_ref, 0)
    def _():
        total = early[0][...]
        for term in early[1:]:
            total = total + term[...].astype(F32)
        fill(total)

    @core_is(where_ref, 1)
    def _():
        mine = mine_ref[...].astype(F32)
        other = other_ref[...].astype(F32)
        fill(jnp.concatenate([other[: step // 2], mine], axis=0))


def feed_out_kernel(where_ref, first_ref, second_ref, other_ref, expand_ref, contract_ref):
    @core_is(where_ref, 0)
    def _():
        expand_ref[0] = first_ref[...].astype(F32)
        contract_ref[0] = other_ref[...].astype(F32)

    @core_is(where_ref, 1)
    def _():
        expand_ref[0] = other_ref[...].astype(F32)
        contract_ref[0] = second_ref[...].astype(F32)


def swap(x):
    return lax.ppermute(x, "section", [(0, 1), (1, 0)])


def gather_rows(x):
    return lax.all_gather(x, "tensor", axis=0, tiled=True)


def scatter_rows(x):
    size = lax.axis_size("tensor")
    parts = x.reshape(size, x.shape[0] // size, x.shape[1])
    return lax.all_to_all(parts, "tensor", 0, 0)


def deal(x, micro, sub):
    section = lax.axis_index("section")
    across = lax.axis_size("dp")
    odd = lax.axis_index("dp") % 2
    got = []
    for p in range(2):
        route = []
        for c in range(2):
            for d in range(across):
                r, dd = (d // micro, d % micro)
                m = 2 * c + (p ^ (dd & 1))
                route.append((c * across + d, (dd >> 1) * across + m * sub + r))
        chosen = 2 * section + (p ^ odd)
        payload = lax.dynamic_index_in_dim(x, chosen, 0, keepdims=False)
        got.append(lax.ppermute(payload, PLACES, route))
    return jnp.concatenate(got, axis=0)


def undeal(parts, micro, sub):
    across = lax.axis_size("dp")
    got = []
    for p in range(2):
        for u in range(2):
            route = []
            for s in range(2):
                for source in range(across):
                    m, r = (source // sub, source % sub)
                    j = p ^ (m & 1)
                    layer = u ^ (m >> 1)
                    route.append((s * across + source, layer * across + r * micro + 2 * s + j))
            got.append(lax.ppermute(parts[2 * p + u], PLACES, route))
    return got


def across_layer(x, layer, k):
    across = lax.axis_size("dp")
    route = [(layer * across + d, layer * across + (d ^ k)) for d in range(across)]
    return lax.ppermute(x, PLACES, route)


def together(*values):
    return lax.optimization_barrier(values)


def after(x, token):
    return lax.optimization_barrier((x, token))[0]


def body(
    tokens,
    cotangent,
    lengths,
    random_blocks,
    projections,
    query_value_bias,
    output_weight,
    expand_weight,
    expand_bias,
    contract_weight,
    norm_gains,
    row_biases,
):
    section = lax.axis_index("section")
    place = lax.axis_index("dp")
    seat = lax.axis_index("tensor")
    across = lax.axis_size("dp")
    ways = lax.axis_size("tensor")
    micro = tokens.shape[0]
    sub = across // micro
    plane = place // sub
    share = place % sub
    local = tokens.shape[2]
    width = tokens.shape[3]
    e = projections.shape[3]
    heads = e // HD
    units = expand_weight.shape[2]
    step = projections.shape[2]
    c = query_value_bias.shape[3]
    mine = 2 * local
    rows = mine * ways
    keys = rows * 2 * sub
    blocks = keys // BLOCK
    kw = -(-(e + blocks + 1) // 128) * 128
    vw = 256
    whole_tiles = step % 32 == 0
    start = (share * micro + 2 * section) * ways * local
    length = lax.dynamic_index_in_dim(lengths[:, 0], plane, 0, keepdims=False)
    where = jnp.stack([section, place, plane, seat, start, length, plane % 2, 0]).astype(jnp.int32)
    random_all = lax.all_gather(random_blocks, "section", axis=0, tiled=True)

    attn_keep, attn_send, feed_keep, feed_send = call(
        prepare_kernel,
        [sds((step // 2 + 16, 4 * e), BF16)] * 2 + [sds((step, units), BF16)] * 2,
        where, Far(projections), Far(output_weight), Far(expand_weight),
        Far(contract_weight.transpose(0, 2, 1)), Far(query_value_bias.transpose(0, 2, 1, 3)),
        Far(expand_bias), Far(norm_gains), Far(row_biases),
        scratch=[pltpu.VMEM((step, 4 * e), BF16), pltpu.VMEM((16, 4 * e), F32)],
    )
    x = deal(tokens[:, 0], micro, sub)
    attn_send, feed_send, x = together(attn_send, feed_send, x)
    attn_traded = swap(attn_send)
    feed_traded = swap(feed_send)
    attn_all = []
    feed_all = []
    for l in range(2):
        own = section == l
        whole = lax.all_gather(jnp.where(own, attn_keep, attn_traded), PLACES, axis=0, tiled=True)
        attn_all.append(whole.reshape(2, across, step // 2 + 16, 4 * e))
        whole = lax.all_gather(jnp.where(own, feed_keep, feed_traded), PLACES, axis=0, tiled=True)
        feed_all.append(whole.reshape(2, width, units))

    upstream = deal(cotangent[:, 0], micro, sub)
    x, random_all = together(x, random_all)
    if not whole_tiles:
        attn_flat = [
            whole[:, :, : step // 2].transpose(1, 0, 2, 3).reshape(width, 4 * e)
            for whole in attn_all
        ]
    def small_rows(l):
        if not whole_tiles:
            return attn_all[l][0, :, step // 2 :]
        cuts = [((0, z, pl.ds(step // 2, 16)), (z,)) for z in range(across)]
        return Far(attn_all[l], (across, 16, 4 * e), cuts)

    def attn_weight(l, first, size, into=None):
        lanes = pl.ds(first, size)
        if not whole_tiles:
            return Far(attn_flat[l], (width, size), [((slice(None), lanes), ())], into=into)
        half = step // 2
        cuts = [
            ((i, z, pl.ds(0, half), lanes), (pl.ds(z * step + i * half, half),))
            for z in range(across)
            for i in range(2)
        ]
        return Far(attn_all[l], (width, size), cuts, into=into)

    def feed_weight(l, i):
        return Far(feed_all[l], (width, units), [((i,), ())])

    def all_parts(own):
        pair = [own, swap(own)]
        if sub == 1:
            return pair
        groups = [[m * sub + r for r in range(sub)] for m in range(micro)]
        return [
            lax.all_gather(
                jnp.concatenate(pair, axis=0), "dp", axis=0, tiled=True, axis_index_groups=groups
            )
        ]

    def own_parts(parts):
        if sub == 1:
            return parts
        groups = [[m * sub + r for r in range(sub)] for m in range(micro)]
        total = lax.psum_scatter(
            parts[0], "dp", scatter_dimension=0, tiled=True, axis_index_groups=groups
        )
        return [total[:rows], total[rows:]]

    chunk = min(rows, 256)
    near_rows = sds((mine, width), BF16)
    near_f32 = sds((mine, width), F32)
    turn_outs = [near_f32, near_rows, sds((8, width), F32)]
    far_unit = [Far(sds((mine, width), F32)), Far(sds((mine, 128), F32))]

    saved = []
    vectors = []
    for l in range(2):
        x_all = gather_rows(x)
        q, kv, vec, x_kept, q_kept, kv_kept = call(
            partial(qkv_kernel, ways, local, blocks, c, e),
            [sds((rows, kw), BF16), sds((rows, kw + vw), BF16), sds((8, width), F32),
             Far(sds((rows, width), BF16), plain=True), Far(sds((rows, kw), BF16), plain=True),
             Far(sds((rows, kw + vw), BF16), plain=True)],
            where, x_all, small_rows(l), attn_weight(l, 0, 4 * e),
            flops=6 * rows * width * 256,
        )
        vectors.append(vec)
        parts = all_parts(kv)
        attended, mixed, totals, *others = call(
            partial(attention_kernel, heads, l, ways, local, blocks, chunk, len(parts)),
            [Far(sds((rows, width), BF16)), Far(sds((rows, vw), BF16)), Far(sds((8, rows), F32))]
            + [Far(sds(part.shape, BF16), plain=True) for part in parts[1:]],
            where, random_all, q, attn_weight(l, 4 * e - vw, vw), *parts,
            flops=4 * rows * keys * kw, limit=24,
        )
        parts_kept = [kv_kept, others[0]] if sub == 1 else parts
        terms = scatter_rows(attended)
        if l == 1:
            terms, upstream = together(terms, upstream)
        middle, middle_low, unit1, inverse1 = call(
            first_norm_kernel, [sds((mine, width), F32), near_rows] + far_unit, x, terms, vec
        )
        middle_all = gather_rows(middle_low)
        fed, active, slope, middle_kept = call(
            feed_kernel,
            [Far(sds((rows, width), BF16)), Far(sds((rows, units), BF16)),
             Far(sds((rows, units), BF16)), Far(sds((rows, width), BF16), plain=True)],
            middle_all, vec, feed_weight(l, 0), feed_weight(l, 1),
            flops=4 * rows * width * units,
        )
        terms = scatter_rows(fed)
        if l == 0:
            x, low_kept, unit2, inverse2 = call(
                partial(second_norm_kernel, ways),
                [near_rows, Far(near_rows, plain=True)] + far_unit,
                where, middle, terms, vec,
            )
            first_rows = lax.all_gather(low_kept, PLACES, axis=0, tiled=True)
        else:
            terms, first_rows = together(terms, first_rows)
            second, feed_low, second_sums, last_kept = call(
                partial(turn_kernel, ways), turn_outs + [Far(near_rows)],
                where, middle, terms, vec, upstream,
            )
        saved.append(
            (x_kept, q_kept, parts_kept, mixed, totals, unit1, inverse1, middle_kept, active,
             slope)
        )
        if l == 0:
            norm_kept = (unit2, inverse2)
    last_rows = lax.all_gather(last_kept, PLACES, axis=0, tiled=True)
    feed_parts = [None, None]
    for l in (1, 0):
        vec = vectors[l]
        (x_kept, q_kept, parts_kept, mixed, totals, unit1, inverse1, middle_kept, active,
         slope) = saved[l]
        feed_grad = gather_rows(feed_low)
        hidden, fed_back, unit_sums = call(
            feed_back_kernel,
            [Far(sds((rows, units), BF16)), Far(sds((rows, width), BF16)), sds((8, units), F32)],
            feed_grad, feed_weight(l, 1), Far(slope), feed_weight(l, 0),
            flops=4 * rows * width * units,
        )
        terms = scatter_rows(fed_back)
        feed_kept, feed_sent = call(
            feed_pack_kernel,
            [Far(sds((width, units), BF16))] * 2,
            where, Far(hidden), feed_grad, Far(middle_kept), Far(active),
            flops=4 * rows * width * units,
        )
        terms, feed_sent = together(terms, feed_sent)
        feed_traded = swap(feed_sent)
        if l == 0:
            terms, feed_parts[1] = together(terms, feed_parts[1])
        first_grad, first_low = call(
            first_back_kernel,
            [Far(near_f32), sds((mine + 16, width), BF16)],
            second, terms, vec, second_sums, Far(unit1), Far(inverse1),
        )
        attended_grad = gather_rows(first_low).reshape(ways, mine + 16, width)
        if l == 1:
            attended_grad, last_rows = together(attended_grad, last_rows)
        dq, norm_sums, w_next, feed_half, *dkv = call(
            partial(attention_back_kernel, heads, l, ways, local, blocks, chunk),
            [sds((rows, 256), BF16), sds((16, width), F32), sds((width, 4 * e), BF16),
             Far(sds((width, units), BF16))]
            + [sds((part.shape[0], 256 + vw), BF16) for part in parts_kept],
            where, random_all, attended_grad, attn_weight(l, 0, 4 * e, into=2), Far(mixed),
            Far(q_kept), Far(totals), *[Far(part) for part in parts_kept],
            Far(feed_kept), Far(feed_traded),
            flops=10 * rows * keys * kw, limit=44,
        )
        dkv_own, dkv_other = own_parts(dkv)
        feed_parts[l] = lax.psum_scatter(feed_half, "dp", scatter_dimension=0, tiled=True)
        dkv_traded = swap(dkv_other)
        triple, projected, pair_sums = call(
            partial(projection_back_kernel, e),
            [sds((rows, 4 * e), BF16), Far(sds((rows, width), BF16)), sds((8, 4 * e), F32)],
            dq, dkv_own, dkv_traded, w_next,
            flops=6 * rows * width * 256,
        )
        terms = scatter_rows(projected)
        cut = step if whole_tiles else width
        pieces = width // cut
        pack_shape = (pieces, cut + 16, 4 * e) if l == 0 else (2, pieces, cut // 2 + 16, 4 * e)
        (pack,) = call(
            partial(attn_pack_kernel, l == 0, cut, e),
            [sds(pack_shape, BF16)],
            where, triple, attended_grad, norm_sums, unit_sums, pair_sums, Far(x_kept),
            Far(mixed),
            flops=8 * rows * width * 256,
        )
        if not whole_tiles:
            pack = split_pack(pack, l == 0, across)
        if l == 1:
            terms, pack = together(terms, pack)
            attn_part = lax.psum_scatter(
                pack.reshape((-1,) + pack.shape[2:]), PLACES, scatter_dimension=0
            )
            second, feed_low, second_sums, later = call(
                partial(between_kernel, ways),
                turn_outs + [Far(near_rows)],
                where, terms, vectors[0], Far(first_grad), Far(norm_kept[0]), Far(norm_kept[1]),
            )
        else:
            traded = lax.ppermute(pack, "section", [(1, 0)])
            if whole_tiles:
                sums = call(
                    pair_sum_kernel,
                    [sds(pack.shape[1:], F32)] + [sds(pack.shape[1:], BF16)] * (across - 1),
                    pack, traded,
                )
                terms, attn_part, *sums = together(terms, attn_part, *sums)
                early = [sums[0]] + [across_layer(sums[k], 0, k) for k in range(1, across)]
            else:
                total = (pack.astype(F32) + traded.astype(F32)).astype(BF16)
                early = [
                    lax.psum_scatter(total, "dp", scatter_dimension=0).astype(F32)
                ]
            places = call(
                last_input_kernel, [sds((local, width), BF16)] * 4,
                where, terms, Far(first_grad), Far(later),
            )
            back_rows = undeal(places, micro, sub)
            feed_parts = list(together(*feed_parts, places[0], early[-1])[:2])

    feed_other = swap(jnp.where(section == 0, feed_parts[1], feed_parts[0]))
    expand_out, contract_out = call(
        feed_out_kernel, [sds((1, step, units), F32)] * 2,
        where, feed_parts[0], feed_parts[1], feed_other,
    )
    attn_other = lax.ppermute(attn_part, "section", [(0, 1)])
    projections_out, output_out, gains_out, biases_out, units_out, pairs_out = call(
        partial(attn_out_kernel, step, e, c),
        [sds((1, 3, step, e), F32), sds((1, e, step), F32), sds((1, 2, step), F32),
         sds((1, 4, step), F32), sds((units // HD, 1, c), F32), sds((1, heads, 2, c), F32)],
        where, *early, attn_part, attn_other,
    )
    (activations,) = call(
        partial(activation_out_kernel, micro, sub),
        [sds((1, micro, 1, local, width), BF16)],
        where, Raw(first_rows), Raw(last_rows),
        scratch=[pltpu.SemaphoreType.DMA((micro,))],
    )
    back_rows[0], expand_out, contract_out, projections_out, activations = together(
        back_rows[0], expand_out, contract_out, projections_out, activations
    )
    (input_grads,) = call(
        place_out_kernel, [sds((1, micro, 1, local, width), F32)], where, *back_rows
    )
    return (
        activations,
        input_grads,
        projections_out,
        pairs_out.transpose(0, 2, 1, 3),
        output_out,
        expand_out,
        units_out.transpose(1, 0, 2),
        contract_out.transpose(0, 2, 1),
        gains_out,
        biases_out,
    )


def split_pack(pack, relative, across):
    if relative:
        weights, small = (pack[0, :-16], pack[0, -16:])
        weights = weights.reshape(across, -1, weights.shape[1])
        small = jnp.broadcast_to(small, (across,) + small.shape)
        return jnp.concatenate([weights, small], axis=1)
    weights = pack[:, 0, :-16].reshape(-1, pack.shape[3])
    weights = weights.reshape(across, 2, -1, pack.shape[3]).transpose(1, 0, 2, 3)
    small = jnp.broadcast_to(pack[0, 0, -16:], (2, across, 16, pack.shape[3]))
    return jnp.concatenate([weights, small], axis=2)


def solution(mesh):
    in_specs = (
        P(None, None, ("dp", "tensor"), None),
        P(None, None, ("dp", "tensor"), None),
        P(),
        P("section", "tensor", None, None),
        P("section", None, "dp", "tensor"),
        P("section", None, "tensor", "dp"),
        P("section", "tensor", "dp"),
        P("section", "dp", "tensor"),
        P("section", "tensor", "dp"),
        P("section", "tensor", "dp"),
        P("section", None, "dp"),
        P("section", None, "dp"),
    )
    out_specs = (
        P("section", None, None, ("dp", "tensor"), None),
        P("section", None, None, ("dp", "tensor"), None),
        P("section", None, "dp", "tensor"),
        P("section", None, "tensor", "dp"),
        P("section", "tensor", "dp"),
        P("section", "dp", "tensor"),
        P("section", "tensor", "dp"),
        P("section", "tensor", "dp"),
        P("section", None, "dp"),
        P("section", None, "dp"),
    )
    return jax.shard_map(body, mesh=mesh, in_specs=in_specs, out_specs=out_specs, check_vma=False)
```

```python
import math
from functools import partial

import jax
import jax.numpy as jnp
from jax import lax
from jax.experimental import pallas as pl
from jax.experimental.pallas import tpu as pltpu
from jax.sharding import PartitionSpec as P

HD = 64
BLOCK = 64
GLOBAL = 2
EPSILON = 1e-12
MASKED = -1e30
GELU_A = 0.7978845608028654
GELU_B = 0.044715
F32 = jnp.float32
BF16 = jnp.bfloat16
MIB = 1 << 20
PLACES = ("section", "dp")


def nt(a, b):
    return lax.dot_general(a, b, (((1,), (1,)), ((), ())), preferred_element_type=F32)


def tn(a, b):
    return lax.dot_general(a, b, (((0,), (0,)), ((), ())), preferred_element_type=F32)


def nn(a, b):
    return jnp.dot(a, b, preferred_element_type=F32)


def sds(shape, dtype):
    return jax.ShapeDtypeStruct(shape, dtype)


class Far:
    def __init__(self, array, shape=None, cuts=None, plain=False, into=None, parts=1):
        self.array = array
        self.shape = array.shape if shape is None else shape
        self.cuts = [((), ())] if cuts is None else cuts
        self.plain = plain
        self.into = into
        self.parts = parts


class Raw:
    def __init__(self, array):
        self.array = array


def at(ref, index):
    return ref.at[index] if index else ref


class Arriving:
    def __init__(self, source, buffer, sems, first, cuts):
        self.buffer = buffer
        self.shape = buffer.shape
        self.copies = [
            pltpu.make_async_copy(at(source, a), at(buffer, b), sems.at[first + i])
            for i, (a, b) in enumerate(cuts)
        ]
        for copy in self.copies:
            copy.start()
        self.there = False

    def settle(self):
        if not self.there:
            for copy in self.copies:
                copy.wait()
            self.there = True

    def __getitem__(self, index):
        self.settle()
        return self.buffer[index]


class Leaving:
    def __init__(self, target, buffer, sems, first):
        self.target = target
        self.buffer = buffer
        self.shape = target.shape
        self.sems = sems
        self.first = first
        self.copies = []

    def __setitem__(self, index, value):
        self.buffer[index] = value

    def send(self, source=None, rows=None):
        source = self.buffer if source is None else source
        target = self.target
        if rows is not None:
            source, target = (source.at[rows], target.at[rows])
        copy = pltpu.make_async_copy(source, target, self.sems.at[self.first + len(self.copies)])
        copy.start()
        self.copies.append(copy)

    def finish(self):
        if not self.copies:
            self.send()
        for copy in self.copies:
            copy.wait()


def call(kernel, outs, *args, flops=0, limit=16, scratch=()):
    arrays = []
    in_specs = []
    out_specs = []
    out_shapes = []
    buffers = []
    size = 0
    semaphores = 0
    for arg in args:
        if isinstance(arg, Raw):
            arrays.append(pltpu.with_memory_space_constraint(arg.array, pltpu.HBM))
            in_specs.append(pl.BlockSpec(memory_space=pltpu.HBM))
        elif isinstance(arg, Far):
            arrays.append(pltpu.with_memory_space_constraint(arg.array, pltpu.HBM))
            in_specs.append(pl.BlockSpec(memory_space=pltpu.HBM))
            if arg.into is None:
                buffers.append(pltpu.VMEM(arg.shape, arg.array.dtype))
            semaphores += len(arg.cuts)
            size += math.prod(arg.shape) * arg.array.dtype.itemsize
        else:
            arrays.append(arg)
            scalar = arg.dtype == jnp.int32
            in_specs.append(pl.BlockSpec(memory_space=pltpu.SMEM if scalar else pltpu.VMEM))
            size += arg.size * arg.dtype.itemsize
    for out in outs:
        if isinstance(out, Raw):
            out_shapes.append(pltpu.HBM(out.array.shape, out.array.dtype))
            out_specs.append(pl.BlockSpec(memory_space=pltpu.HBM))
        elif isinstance(out, Far):
            out_shapes.append(pltpu.HBM(out.shape, out.array.dtype))
            out_specs.append(pl.BlockSpec(memory_space=pltpu.HBM))
            if not out.plain:
                buffers.append(pltpu.VMEM(out.shape, out.array.dtype))
            semaphores += out.parts
            size += math.prod(out.shape) * out.array.dtype.itemsize
        else:
            out_shapes.append(out)
            out_specs.append(pl.BlockSpec(memory_space=pltpu.VMEM))
            size += out.size * out.dtype.itemsize

    def whole(*refs):
        refs = list(refs)
        ins = refs[: len(args)]
        results = refs[len(args) : len(args) + len(outs)]
        rest = refs[len(args) + len(outs) :]
        sems = rest.pop() if semaphores else None
        given = []
        used = 0
        for arg, ref in zip(args, ins):
            if isinstance(arg, Far):
                buffer = rest.pop(0) if arg.into is None else results[arg.into]
                given.append(Arriving(ref, buffer, sems, used, arg.cuts))
                used += len(arg.cuts)
            else:
                given.append(ref)
        leaving = []
        for out, ref in zip(outs, results):
            if isinstance(out, Far):
                buffer = None if out.plain else rest.pop(0)
                leaving.append(Leaving(ref, buffer, sems, used))
                given.append(leaving[-1])
                used += out.parts
            else:
                given.append(ref)
        kernel(*given, *rest)
        for item in given:
            if isinstance(item, Arriving):
                item.settle()
        for item in leaving:
            item.finish()

    scratch_shapes = buffers + list(scratch)
    if semaphores:
        scratch_shapes = scratch_shapes + [pltpu.SemaphoreType.DMA((semaphores,))]
    return pl.pallas_call(
        whole,
        out_shape=tuple(out_shapes),
        in_specs=in_specs,
        out_specs=tuple(out_specs),
        scratch_shapes=scratch_shapes,
        compiler_params=pltpu.CompilerParams(vmem_limit_bytes=limit * MIB),
        cost_estimate=pl.CostEstimate(flops=flops, bytes_accessed=size, transcendentals=0),
    )(*arrays)


SECTION, PLACE, PLANE, SEAT, START, LENGTH, FLIP = range(7)


def positions(where_ref, count, ways, local, first):
    row = lax.broadcasted_iota(jnp.int32, (count, 1), 0) + first
    group = jnp.bitwise_xor(row // local % 2, where_ref[FLIP])
    return (
        where_ref[START] + group * (ways * local) + row // (2 * local) * local + row % local
    )


def core_is(where_ref, core):
    return pl.when(where_ref[SECTION] == core)


def prepare_kernel(
    where_ref, projections_ref, output_ref, expand_ref, contract_ref, pair_ref, unit_ref,
    gain_ref, bias_ref, attn_keep, attn_send, keep_out, send_out, whole, small
):
    step, e = projections_ref.shape[2:]
    heads, _, c = pair_ref.shape[1:]
    half = step // 2
    whole[:, :e] = projections_ref[0, 0]
    whole[:, e : 2 * e] = projections_ref[0, 2]
    whole[:, 2 * e : 3 * e] = projections_ref[0, 1]
    whole[:, 3 * e :] = output_ref[0].T
    small[...] = jnp.zeros_like(small)
    small[0:2, :step] = gain_ref[0].astype(F32)
    small[2:6, :step] = bias_ref[0].astype(F32)
    small[: unit_ref.shape[1], 256 : 256 + c] = unit_ref[0].astype(F32)
    for i in range(heads):
        small[i : i + 1, 384 : 384 + c] = pair_ref[0, i, 0:1].astype(F32)
        small[i : i + 1, 512 : 512 + c] = pair_ref[0, i, 1:2].astype(F32)
    attn_keep[half:] = small[...].astype(BF16)
    attn_send[half:] = small[...].astype(BF16)
    expand = expand_ref[0]
    contract = contract_ref[0]

    @core_is(where_ref, 0)
    def _():
        attn_keep[:half] = whole[:half]
        attn_send[:half] = whole[half:]
        keep_out[...] = expand
        send_out[...] = contract

    @core_is(where_ref, 1)
    def _():
        attn_keep[:half] = whole[half:]
        attn_send[:half] = whole[:half]
        keep_out[...] = contract
        send_out[...] = expand


def unpack(c, e, raw_ref, vec_ref):
    places = raw_ref.shape[0]
    width = vec_ref.shape[1]
    w = width // places

    def of_heads(rows, lanes, z):
        source = lax.broadcasted_iota(jnp.int32, (128, lanes), 0)
        target = lax.broadcasted_iota(jnp.int32, (128, lanes), 1)
        repeat = ((target % c == source) & (source < c)).astype(F32).astype(BF16)
        spread_rows = nn(rows, repeat)
        head = lax.broadcasted_iota(jnp.int32, spread_rows.shape, 0)
        lane = lax.broadcasted_iota(jnp.int32, spread_rows.shape, 1)
        keep = (lane // HD == head) & (lane % HD // c == z)
        return jnp.sum(jnp.where(keep, spread_rows, 0.0), axis=0, keepdims=True)

    norms = jnp.zeros((16, width), F32)
    units = jnp.zeros((1, width), F32)
    queries = jnp.zeros((1, 256), F32)
    values = jnp.zeros((1, 256), F32)
    for z in range(places):
        rows = raw_ref[z]
        source = lax.broadcasted_iota(jnp.int32, (256, width), 0)
        target = lax.broadcasted_iota(jnp.int32, (256, width), 1)
        move = ((target == source + z * w) & (source < w)).astype(F32).astype(BF16)
        norms = norms + nn(rows[:, :256], move)
        units = units + of_heads(rows[:, 256:384], width, z)
        queries = queries + of_heads(rows[:, 384:512], 256, z)
        values = values + of_heads(rows[:, 512:640], 256, z)
    vec_ref[...] = norms[:8]
    vec_ref[6:7] = units
    lane = lax.broadcasted_iota(jnp.int32, (1, 256), 1)
    queries = jnp.where(lane < e, queries, 0.0)
    values = jnp.where(lane < e, values, 0.0)
    return (queries, pltpu.roll(values, 256 - e, 1))


def qkv_kernel(
    ways, local, blocks, c, e, where_ref, x_ref, raw_ref, w_ref, q_ref, kv_ref, vec_ref, *kept
):
    kw = q_ref.shape[1]
    vw = kv_ref.shape[1] - kw
    x = x_ref[...]
    kept[0].send(x_ref)
    query_bias, value_bias = unpack(c, e, raw_ref, vec_ref)
    lead = 2 * e // 128 * 128
    q = (nn(x, w_ref[:, :256]) + query_bias).astype(BF16).astype(F32) * HD ** (-0.5)
    lane = lax.broadcasted_iota(jnp.int32, (1, 256), 1)
    q = jnp.where(lane < e, q, 0.0).astype(BF16)
    q_ref[:, :256] = q
    if kw > 256:
        q_ref[:, 256:] = jnp.zeros((q.shape[0], kw - 256), BF16)
    kept[1].send(q_ref)
    position = positions(where_ref, x.shape[0], ways, local, 0)
    block = position // BLOCK
    lane = lax.broadcasted_iota(jnp.int32, (1, kw), 1)
    hidden = (position >= where_ref[LENGTH]) & (lane == e + blocks)
    tail = jnp.where(lane == e + block, 1.0, jnp.where(hidden, MASKED, 0.0))
    k = nn(x, w_ref[:, lead : lead + 256])
    if kw > 256:
        k = jnp.concatenate([k, jnp.zeros((k.shape[0], kw - 256), F32)], axis=1)
    kv_ref[:, :kw] = jnp.where(lane < e, k, tail).astype(BF16)
    kv_ref[:, kw:] = (nn(x, w_ref[:, 128 : 128 + vw]) + value_bias).astype(BF16)
    kept[2].send(kv_ref)


def head_mask(first, lanes):
    lane = lax.broadcasted_iota(jnp.int32, (1, lanes), 1)
    return ((lane >= first) & (lane < first + HD)).astype(F32)


def seen_rows(where_ref, random_refs, layer, h, rows, ways, local, kw, e, blocks):
    lane = lax.broadcasted_iota(jnp.int32, (1, kw), 1)
    key = lane - e
    parts = []
    for g in range(rows // local):
        group = jnp.bitwise_xor(g % 2, where_ref[FLIP])
        position = where_ref[START] + group * (ways * local) + g // 2 * local
        block = position // BLOCK
        seen = (key < GLOBAL) | (jnp.abs(key - block) <= 1) | (block < GLOBAL)
        for i in range(random_refs[0].shape[3]):
            picked = [ref[0, h, block, i] for ref in random_refs]
            seen = seen | (key == jnp.where(where_ref[SECTION] == layer, *picked))
        hidden = (key >= 0) & (key < blocks) & jnp.logical_not(seen)
        line = jnp.where(key == blocks, 1.0, jnp.where(hidden, MASKED, 0.0))
        parts.append(jnp.broadcast_to(line, (local, kw)))
    return jnp.concatenate(parts, axis=0)


def attention_kernel(
    heads, layer, ways, local, blocks, chunk, count, where_ref, own_ref, other_ref, q_ref, w_ref,
    *refs
):
    random_refs = (own_ref, other_ref)
    parts, (out_ref, mixed_out, total_out), kept = (
        refs[:count], refs[count : count + 3], refs[count + 3 :]
    )
    rows, kw = q_ref.shape
    e = heads * HD
    vw = parts[0].shape[1] - kw
    shift = vw - e
    for out, part in zip(kept, parts[1:]):
        out.send(part)
    k = jnp.concatenate([part[:, :kw] for part in parts], axis=0)
    vt = jnp.concatenate([part[:, kw:] for part in parts], axis=0).T
    q = q_ref[...].astype(F32)
    lines = [jnp.zeros((shift, rows), F32)]
    totals = []
    for h in range(heads):
        seen = seen_rows(where_ref, random_refs, layer, h, rows, ways, local, kw, e, blocks)
        qa = (q * head_mask(h * HD, kw) + seen).astype(BF16)
        vh = vt[shift + h * HD : shift + (h + 1) * HD]
        cells = []
        sums = []
        for c in range(0, rows, chunk):
            scores = nt(k, qa[c : c + chunk])
            top = jnp.max(scores, axis=0, keepdims=True)
            p = jnp.exp(scores - top)
            total = jnp.sum(p, axis=0, keepdims=True)
            cells.append(nn(vh, p.astype(BF16)) / total)
            sums.append(top + jnp.log(total))
        lines.append(jnp.concatenate(cells, axis=1))
        totals.append(jnp.concatenate(sums, axis=1))
    total_out[...] = jnp.concatenate(totals + [jnp.zeros((8 - heads, rows), F32)], axis=0)
    total_out.send()
    mixed = jnp.concatenate(lines, axis=0).T.astype(BF16)
    mixed_out[...] = mixed
    mixed_out.send()
    out_ref[...] = nt(mixed, w_ref[...]).astype(BF16)


def attention_back_kernel(
    heads, layer, ways, local, blocks, chunk, count, where_ref, own_ref, other_ref, grad_ref,
    w_ref, mixed_ref, q_ref, total_ref, *refs
):
    random_refs = (own_ref, other_ref)
    parts, refs = (refs[:count], refs[count:])
    if len(refs) == 2 + count:
        dq_ref, small_ref, *outs = refs
        adds = None
    else:
        *adds, dq_ref, small_ref = refs[:4]
        outs = refs[4 : 4 + count]
        half_out = refs[-1]
    rows, kw = q_ref.shape
    e = heads * HD
    vw = mixed_ref.shape[1]
    shift = vw - e
    width = grad_ref.shape[2]
    grad = grad_ref[:, : 2 * local].reshape(rows, width)
    small = grad_ref[0, 2 * local :].astype(F32)
    for i in range(1, ways):
        small = small + grad_ref[i, 2 * local :].astype(F32)
    small_ref[...] = small
    mixed_grad = nn(grad, w_ref[:, w_ref.shape[1] - vw :]).astype(BF16).astype(F32)
    product = mixed_grad * mixed_ref[...].astype(F32)
    masks = jnp.concatenate([head_mask(shift + h * HD, vw) for h in range(8)], axis=0)
    inner = lax.dot_general(
        masks, product, (((1,), (1,)), ((), ())),
        preferred_element_type=F32, precision=lax.Precision.HIGHEST,
    )
    q = q_ref[...].astype(F32)
    k = jnp.concatenate([part[:, :kw] for part in parts], axis=0)
    v = jnp.concatenate([part[:, kw:] for part in parts], axis=0)
    kt = k[:, :256].T
    totals = total_ref[...]
    if adds:
        half_out[...] = (adds[0][...].astype(F32) + adds[1][...].astype(F32)).astype(BF16)
        half_out.send()
    dk = None
    dv = None
    lines = []
    for h in range(heads):
        seen = seen_rows(where_ref, random_refs, layer, h, rows, ways, local, kw, e, blocks)
        qm = q * head_mask(h * HD, kw)
        qa = (qm + seen).astype(BF16)
        qm = qm[:, :256].astype(BF16)
        gm = (mixed_grad * head_mask(shift + h * HD, vw)).astype(BF16)
        kh = kt[h * HD : (h + 1) * HD]
        cells = []
        for c in range(0, rows, chunk):
            scores = nt(k, qa[c : c + chunk])
            p = jnp.exp(scores - totals[h : h + 1, c : c + chunk])
            dp = nt(v, gm[c : c + chunk])
            ds = (p * (dp - inner[h : h + 1, c : c + chunk])).astype(BF16)
            dv_term = nn(p.astype(BF16), gm[c : c + chunk])
            dk_term = nn(ds, qm[c : c + chunk])
            dv = dv_term if dv is None else dv + dv_term
            dk = dk_term if dk is None else dk + dk_term
            cells.append(nn(kh, ds))
        lines.append(jnp.concatenate(cells, axis=1))
    lines.append(jnp.zeros((256 - e, rows), F32))
    dq = jnp.concatenate(lines, axis=0).T * HD ** (-0.5)
    dq_ref[...] = dq.astype(BF16)
    start = 0
    for out in outs:
        size = out.shape[0]
        out[:, :256] = dk[start : start + size].astype(BF16)
        out[:, 256:] = dv[start : start + size].astype(BF16)
        start += size


def projection_back_kernel(e, dq_ref, own_ref, other_ref, w_ref, triple_ref, out_ref, sums_ref):
    vw = own_ref.shape[1] - 256
    width = w_ref.shape[1]
    lead = 2 * e // 128 * 128
    rows = dq_ref.shape[0]
    dq = dq_ref[...]
    dkv = (own_ref[...].astype(F32) + other_ref[...].astype(F32)).astype(BF16).astype(F32)
    dv = dkv[:, 256:]
    head = dq.astype(F32)
    nothing = jnp.zeros((rows, 128), F32)
    triple = jnp.concatenate(
        [head[:, :128], head[:, 128:] + dv[:, :128], dv[:, 128:], dkv[:, :256], nothing], axis=1
    ).astype(BF16)
    triple_ref[...] = triple
    sums_ref[...] = jnp.zeros_like(sums_ref)
    sums_ref[0:1] = jnp.sum(triple.astype(F32), axis=0, keepdims=True)
    out_ref[...] = nt(triple, w_ref[...]).astype(BF16)


def norm(values):
    average = jnp.mean(values, axis=-1, keepdims=True)
    centered = values - average
    spread_now = jnp.mean(centered * centered, axis=-1, keepdims=True)
    inverse = lax.rsqrt(spread_now + EPSILON)
    return (centered * inverse, inverse)


def total_of(terms_ref):
    total = terms_ref[0].astype(F32)
    for i in range(1, terms_ref.shape[0]):
        total = total + terms_ref[i].astype(F32)
    return total


def first_norm_kernel(x_ref, terms_ref, vec_ref, middle_ref, low_ref, unit_out, inverse_out):
    values = x_ref[...].astype(F32) + total_of(terms_ref) + vec_ref[2:3]
    unit, inverse = norm(values)
    unit_out[...] = unit
    unit_out.send()
    inverse_out[...] = jnp.broadcast_to(inverse, inverse_out.shape)
    inverse_out.send()
    middle = unit * vec_ref[0:1] + vec_ref[4:5]
    middle_ref[...] = middle
    low_ref[...] = middle.astype(BF16)


def valid_rows(where_ref, ways, local):
    position = positions(where_ref, 2 * local, ways, local, where_ref[SEAT] * 2 * local)
    return (position < where_ref[LENGTH]).astype(F32)


def place_parts(where_ref, early, later, outs):
    half = early.shape[0] // 2
    late_plane = where_ref[PLANE] // 2
    for u in range(2):
        for p in range(2):
            @pl.when(late_plane == u)
            def _(u=u, p=p):
                outs[2 * p + u][...] = early[p * half : (p + 1) * half]

            @pl.when(late_plane != u)
            def _(u=u, p=p):
                outs[2 * p + u][...] = later[p * half : (p + 1) * half]


def norm_back(grad, unit, inverse, gain):
    scaled = grad * gain
    return inverse * (
        scaled
        - jnp.mean(scaled, axis=-1, keepdims=True)
        - unit * jnp.mean(scaled * unit, axis=-1, keepdims=True)
    )


def second_norm(ways, where_ref, middle_ref, terms_ref, vec_ref):
    unit, inverse = norm(middle_ref[...] + total_of(terms_ref) + vec_ref[3:4])
    result = unit * vec_ref[1:2] + vec_ref[5:6]
    valid = valid_rows(where_ref, ways, unit.shape[0] // 2)
    return ((result * valid).astype(BF16), unit, inverse, valid)


def second_back(grad, unit, inverse, vec_ref, second_ref, low_ref, sums_ref):
    second = norm_back(grad, unit, inverse, vec_ref[1:2])
    low_ref[...] = second.astype(BF16)
    second_ref[...] = second
    sums_ref[...] = jnp.zeros_like(sums_ref)
    sums_ref[0:1] = jnp.sum(grad * unit, axis=0, keepdims=True)
    sums_ref[1:2] = jnp.sum(grad, axis=0, keepdims=True)
    sums_ref[2:3] = jnp.sum(second, axis=0, keepdims=True)


def second_norm_kernel(
    ways, where_ref, middle_ref, terms_ref, vec_ref, low_ref, kept, unit_out, inverse_out
):
    low, unit, inverse, _ = second_norm(ways, where_ref, middle_ref, terms_ref, vec_ref)
    low_ref[...] = low
    kept.send(low_ref)
    unit_out[...] = unit
    unit_out.send()
    inverse_out[...] = jnp.broadcast_to(inverse, inverse_out.shape)
    inverse_out.send()


def turn_kernel(
    ways, where_ref, middle_ref, terms_ref, vec_ref, up_ref, _, second_ref, low_ref, sums_ref,
    ahead, kept
):
    low, unit, inverse, valid = second_norm(ways, where_ref, middle_ref, terms_ref, vec_ref)
    kept[...] = low
    kept.send()
    second_back(
        up_ref[...].astype(F32) * valid, unit, inverse, vec_ref, second_ref, low_ref, sums_ref
    )


def between_kernel(
    ways, where_ref, terms_ref, vec_ref, first_ref, unit_ref, inverse_ref, _, second_ref, low_ref,
    sums_ref, ahead, kept
):
    low = (first_ref[...] + total_of(terms_ref)).astype(BF16)
    kept[...] = low
    kept.send()
    grad = low.astype(F32) * valid_rows(where_ref, ways, low.shape[0] // 2)
    second_back(
        grad, unit_ref[...], inverse_ref[:, 0:1], vec_ref, second_ref, low_ref, sums_ref
    )


def first_back_kernel(
    second_ref, terms_ref, vec_ref, before_ref, unit_ref, inverse_ref, _, first_ref, low_ref, ahead
):
    grad = second_ref[...] + total_of(terms_ref)
    unit = unit_ref[...]
    first = norm_back(grad, unit, inverse_ref[:, 0:1], vec_ref[0:1])
    first_ref[...] = first
    rows = first.shape[0]
    low_ref[:rows] = first.astype(BF16)
    before = before_ref[...]
    low_ref[rows:] = jnp.concatenate(
        [jnp.sum(grad * unit, axis=0, keepdims=True), before[0:1],
         jnp.sum(first, axis=0, keepdims=True), before[2:3],
         jnp.sum(grad, axis=0, keepdims=True), before[1:2],
         jnp.zeros((10, first.shape[1]), F32)], axis=0
    ).astype(BF16)


def last_input_kernel(where_ref, terms_ref, first_ref, later_ref, *outs):
    low = (first_ref[...] + total_of(terms_ref)).astype(BF16)
    place_parts(where_ref, low, later_ref[...], outs)


def place_out_kernel(where_ref, *refs):
    parts, out_ref = (refs[:-1], refs[-1])
    odd = where_ref[PLACE] % 2
    for p in range(2):
        for u in range(2):
            m = 2 * jnp.bitwise_xor(where_ref[SECTION], u) + jnp.bitwise_xor(odd, p)
            out_ref[0, m, 0] = parts[2 * p + u][...].astype(F32)


def activation_out_kernel(micro, sub, where_ref, first_ref, last_ref, out_ref, sems):
    local = out_ref.shape[3]
    place = where_ref[PLACE]
    side = place % micro // 2

    def copies(ref):
        result = []
        for m in range(micro):
            source = side * (micro * sub) + m * sub + place // micro
            row = (2 * source + jnp.bitwise_xor(place % 2, m & 1)) * local
            rows = pl.ds(pl.multiple_of(row, local), local)
            result.append(pltpu.make_async_copy(ref.at[rows], out_ref.at[0, m, 0], sems.at[m]))
        return result

    for core, ref in enumerate((first_ref, last_ref)):
        @core_is(where_ref, core)
        def _(ref=ref):
            for copy in copies(ref):
                copy.start()
            for copy in copies(ref):
                copy.wait()


def halves(rows):
    return [pl.ds(begin, rows // 2) for begin in (0, rows // 2)]


def feed_kernel(x_ref, vec_ref, expand_ref, contract_ref, out_ref, active_out, slope_out, kept):
    kept.send(x_ref)
    parts = halves(x_ref.shape[0])
    values = [nn(x_ref[part], expand_ref[...]) + vec_ref[6:7] for part in parts]
    for part, v in zip(parts, values):
        th = jnp.tanh(v * (GELU_A + GELU_A * GELU_B * (v * v)))
        half = 0.5 + 0.5 * th
        active = (v * half).astype(BF16)
        active_out[part] = active
        active_out.send(rows=part)
        slope = half + v * (1.0 - th * th) * (0.5 * GELU_A + 1.5 * GELU_A * GELU_B * (v * v))
        slope_out[part] = slope.astype(BF16)
        slope_out.send(rows=part)
        out_ref[part] = nt(active, contract_ref[...]).astype(BF16)
        out_ref.send(rows=part)


def feed_back_kernel(
    grad_ref, contract_ref, slope_ref, expand_ref, hidden_ref, out_ref, sums_ref
):
    parts = halves(grad_ref.shape[0])
    values = [nn(grad_ref[part], contract_ref[...]) for part in parts]
    total = jnp.zeros((1, hidden_ref.shape[1]), F32)
    for part, value in zip(parts, values):
        hidden = (value * slope_ref[part].astype(F32)).astype(BF16)
        hidden_ref[part] = hidden
        hidden_ref.send(rows=part)
        total = total + jnp.sum(hidden.astype(F32), axis=0, keepdims=True)
        out_ref[part] = nt(hidden, expand_ref[...]).astype(BF16)
        out_ref.send(rows=part)
    sums_ref[...] = jnp.zeros_like(sums_ref)
    sums_ref[0:1] = total


def feed_pack_kernel(where_ref, hidden_ref, grad_ref, middle_ref, active_ref, *outs):
    width = middle_ref.shape[1]
    expand = tn(middle_ref[...], hidden_ref[...]).astype(BF16)
    contract = tn(grad_ref[...], active_ref[...]).astype(BF16)
    if len(outs) == 1:
        outs[0][:width] = expand
        outs[0][width:] = contract
        return

    @core_is(where_ref, 0)
    def _():
        outs[0][...] = expand
        outs[1][...] = contract

    @core_is(where_ref, 1)
    def _():
        outs[0][...] = contract
        outs[1][...] = expand


def attn_pack_kernel(
    relative, step, e, where_ref, triple_ref, grad_ref, norm_ref, unit_ref, pair_ref, x_ref,
    mixed_ref, out_ref
):
    x = x_ref[...]
    width = x.shape[1]
    vw = mixed_ref.shape[1]
    places = width // step
    local = grad_ref.shape[1] - 16
    grad = grad_ref[:, :local].reshape(x.shape)
    total = tn(x, triple_ref[...])
    last = total[:, width - vw :] + tn(grad, mixed_ref[...])
    weights = jnp.concatenate([total[:, : width - vw], last], axis=1).astype(BF16)
    small = jnp.concatenate(
        [norm_ref[:6], unit_ref[0:1], pair_ref[0:1], jnp.zeros((8, width), F32)], axis=0
    ).astype(BF16)
    for z in range(places):
        begin = z * step
        if relative:
            k = jnp.bitwise_xor(where_ref[PLACE], z) if places > 1 else 0
            out_ref[k, :step] = weights[begin : begin + step]
            out_ref[k, step:] = small
        else:
            half = step // 2
            for i in range(2):
                out_ref[i, z, :half] = weights[begin + i * half : begin + (i + 1) * half]
                out_ref[i, z, half:] = small


def pair_sum_kernel(mine_ref, other_ref, own_ref, *sent_refs):
    own_ref[...] = mine_ref[0].astype(F32) + other_ref[0].astype(F32)
    for k, sent in enumerate(sent_refs):
        sent[...] = (
            mine_ref[k + 1].astype(F32) + other_ref[k + 1].astype(F32)
        ).astype(BF16)


def attn_out_kernel(
    step, e, c, where_ref, *refs
):
    early, (mine_ref, other_ref), outs = (refs[:-8], refs[-8:-6], refs[-6:])
    projections_ref, output_ref, gain_ref, bias_ref, unit_ref, pair_ref = outs
    width = mine_ref.shape[1]

    def fill(total):
        weights = total[:step]
        small = total[step : step + 8]
        projections_ref[0, 0] = weights[:, :e]
        projections_ref[0, 1] = weights[:, 2 * e : 3 * e]
        projections_ref[0, 2] = pltpu.roll(weights, width - e, 1)[:, :e]
        output_ref[0] = pltpu.roll(weights, e, 1)[:, :e].T
        mine = pltpu.roll(small, lax.rem(width - where_ref[PLACE] * step, width), 1)
        gain_ref[0] = mine[0:2, :step]
        bias_ref[0] = mine[2:6, :step]

        def column(row, head):
            shift = lax.rem(2 * width - head * HD - where_ref[PLACE] * c, width)
            return pltpu.roll(small, shift, 1)[row : row + 1, :c]

        for head in range(unit_ref.shape[0]):
            unit_ref[head] = column(6, head)
        for head in range(pair_ref.shape[1]):
            pair_ref[0, head, 0:1] = column(7, head)
            pair_ref[0, head, 1:2] = column(7, head + e // HD)

    @core_is(where_ref, 0)
    def _():
        total = early[0][...]
        for term in early[1:]:
            total = total + term[...].astype(F32)
        fill(total)

    @core_is(where_ref, 1)
    def _():
        mine = mine_ref[...].astype(F32)
        other = other_ref[...].astype(F32)
        fill(jnp.concatenate([other[: step // 2], mine], axis=0))


def feed_out_kernel(where_ref, first_ref, second_ref, other_ref, expand_ref, contract_ref):
    @core_is(where_ref, 0)
    def _():
        expand_ref[0] = first_ref[...].astype(F32)
        contract_ref[0] = other_ref[...].astype(F32)

    @core_is(where_ref, 1)
    def _():
        expand_ref[0] = other_ref[...].astype(F32)
        contract_ref[0] = second_ref[...].astype(F32)


def swap(x):
    return lax.ppermute(x, "section", [(0, 1), (1, 0)])


def gather_rows(x):
    return lax.all_gather(x, "tensor", axis=0, tiled=True)


def scatter_rows(x):
    size = lax.axis_size("tensor")
    parts = x.reshape(size, x.shape[0] // size, x.shape[1])
    return lax.all_to_all(parts, "tensor", 0, 0)


def deal(x, micro, sub):
    section = lax.axis_index("section")
    across = lax.axis_size("dp")
    odd = lax.axis_index("dp") % 2
    got = []
    for p in range(2):
        route = []
        for c in range(2):
            for d in range(across):
                r, dd = (d // micro, d % micro)
                m = 2 * c + (p ^ (dd & 1))
                route.append((c * across + d, (dd >> 1) * across + m * sub + r))
        chosen = 2 * section + (p ^ odd)
        payload = lax.dynamic_index_in_dim(x, chosen, 0, keepdims=False)
        got.append(lax.ppermute(payload, PLACES, route))
    return got


def undeal(parts, micro, sub):
    across = lax.axis_size("dp")
    got = []
    for p in range(2):
        for u in range(2):
            route = []
            for s in range(2):
                for source in range(across):
                    m, r = (source // sub, source % sub)
                    j = p ^ (m & 1)
                    layer = u ^ (m >> 1)
                    route.append((s * across + source, layer * across + r * micro + 2 * s + j))
            got.append(lax.ppermute(parts[2 * p + u], PLACES, route))
    return got


def across_layer(x, layer, k):
    across = lax.axis_size("dp")
    route = [(layer * across + d, layer * across + (d ^ k)) for d in range(across)]
    return lax.ppermute(x, PLACES, route)


def together(*values):
    return lax.optimization_barrier(values)


def after(x, token):
    return lax.optimization_barrier((x, token))[0]


def body(
    tokens,
    cotangent,
    lengths,
    random_blocks,
    projections,
    query_value_bias,
    output_weight,
    expand_weight,
    expand_bias,
    contract_weight,
    norm_gains,
    row_biases,
):
    section = lax.axis_index("section")
    place = lax.axis_index("dp")
    seat = lax.axis_index("tensor")
    across = lax.axis_size("dp")
    ways = lax.axis_size("tensor")
    micro = tokens.shape[0]
    sub = across // micro
    plane = place // sub
    share = place % sub
    local = tokens.shape[2]
    width = tokens.shape[3]
    e = projections.shape[3]
    heads = e // HD
    units = expand_weight.shape[2]
    step = projections.shape[2]
    c = query_value_bias.shape[3]
    mine = 2 * local
    rows = mine * ways
    keys = rows * 2 * sub
    blocks = keys // BLOCK
    kw = -(-(e + blocks + 1) // 128) * 128
    vw = 256
    whole_tiles = step % 32 == 0
    start = (share * micro + 2 * section) * ways * local
    length = lax.dynamic_index_in_dim(lengths[:, 0], plane, 0, keepdims=False)
    where = jnp.stack([section, place, plane, seat, start, length, plane % 2, 0]).astype(jnp.int32)
    random_other = swap(random_blocks)

    attn_keep, attn_send, feed_keep, feed_send = call(
        prepare_kernel,
        [sds((step // 2 + 16, 4 * e), BF16)] * 2 + [sds((step, units), BF16)] * 2,
        where, Far(projections), Far(output_weight), Far(expand_weight),
        Far(contract_weight.transpose(0, 2, 1)), Far(query_value_bias.transpose(0, 2, 1, 3)),
        Far(expand_bias), Far(norm_gains), Far(row_biases),
        scratch=[pltpu.VMEM((step, 4 * e), BF16), pltpu.VMEM((16, 4 * e), F32)],
    )
    x = jnp.concatenate(deal(tokens[:, 0], micro, sub), axis=0)
    feed_send, x = together(feed_send, x)
    attn_traded = swap(attn_send)
    feed_traded = swap(feed_send)
    attn_all = []
    feed_all = []
    for l in range(2):
        own = section == l
        whole = lax.all_gather(jnp.where(own, attn_keep, attn_traded), PLACES, axis=0, tiled=True)
        attn_all.append(whole.reshape(2, across, step // 2 + 16, 4 * e))
        whole = lax.all_gather(jnp.where(own, feed_keep, feed_traded), PLACES, axis=0, tiled=True)
        feed_all.append(whole.reshape(2, width, units))

    upstream = jnp.concatenate(deal(cotangent[:, 0], micro, sub), axis=0)
    if not whole_tiles:
        attn_flat = [
            whole[:, :, : step // 2].transpose(1, 0, 2, 3).reshape(width, 4 * e)
            for whole in attn_all
        ]
    def small_rows(l):
        if not whole_tiles:
            return attn_all[l][0, :, step // 2 :]
        cuts = [((0, z, pl.ds(step // 2, 16)), (z,)) for z in range(across)]
        return Far(attn_all[l], (across, 16, 4 * e), cuts)

    def attn_weight(l, first, size, into=None):
        lanes = pl.ds(first, size)
        if not whole_tiles:
            return Far(attn_flat[l], (width, size), [((slice(None), lanes), ())], into=into)
        half = step // 2
        cuts = [
            ((i, z, pl.ds(0, half), lanes), (pl.ds(z * step + i * half, half),))
            for z in range(across)
            for i in range(2)
        ]
        return Far(attn_all[l], (width, size), cuts, into=into)

    def feed_weight(l, i, into=None):
        return Far(feed_all[l], (width, units), [((i,), ())], into=into)

    def all_parts(own):
        pair = [own, swap(own)]
        if sub == 1:
            return pair
        groups = [[m * sub + r for r in range(sub)] for m in range(micro)]
        return [
            lax.all_gather(
                jnp.concatenate(pair, axis=0), "dp", axis=0, tiled=True, axis_index_groups=groups
            )
        ]

    def own_parts(parts):
        if sub == 1:
            return parts
        groups = [[m * sub + r for r in range(sub)] for m in range(micro)]
        total = lax.psum_scatter(
            parts[0], "dp", scatter_dimension=0, tiled=True, axis_index_groups=groups
        )
        return [total[:rows], total[rows:]]

    chunk = min(rows, 256)
    near_rows = sds((mine, width), BF16)
    near_f32 = sds((mine, width), F32)
    turn_outs = [near_f32, near_rows, sds((8, width), F32), sds((width, units), BF16)]
    far_unit = [Far(sds((mine, width), F32)), Far(sds((mine, 128), F32))]

    saved = []
    vectors = []
    for l in range(2):
        x_all = gather_rows(x)
        q, kv, vec, x_kept, q_kept, kv_kept = call(
            partial(qkv_kernel, ways, local, blocks, c, e),
            [sds((rows, kw), BF16), sds((rows, kw + vw), BF16), sds((8, width), F32),
             Far(sds((rows, width), BF16), plain=True), Far(sds((rows, kw), BF16), plain=True),
             Far(sds((rows, kw + vw), BF16), plain=True)],
            where, x_all, small_rows(l), attn_weight(l, 0, 4 * e),
            flops=6 * rows * width * 256,
        )
        vectors.append(vec)
        parts = all_parts(kv)
        attended, mixed, totals, *others = call(
            partial(attention_kernel, heads, l, ways, local, blocks, chunk, len(parts)),
            [Far(sds((rows, width), BF16)), Far(sds((rows, vw), BF16)), Far(sds((8, rows), F32))]
            + [Far(sds(part.shape, BF16), plain=True) for part in parts[1:]],
            where, random_blocks, random_other, q, attn_weight(l, 4 * e - vw, vw), *parts,
            flops=4 * rows * keys * kw, limit=24,
        )
        parts_kept = [kv_kept, others[0]] if sub == 1 else parts
        terms = scatter_rows(attended)
        if l == 1:
            terms, upstream = together(terms, upstream)
        middle, middle_low, unit1, inverse1 = call(
            first_norm_kernel, [sds((mine, width), F32), near_rows] + far_unit, x, terms, vec
        )
        middle_all = gather_rows(middle_low)
        fed, active, slope, middle_kept = call(
            feed_kernel,
            [Far(sds((rows, width), BF16), parts=2), Far(sds((rows, units), BF16), parts=2),
             Far(sds((rows, units), BF16), parts=2), Far(sds((rows, width), BF16), plain=True)],
            middle_all, vec, feed_weight(l, 0), feed_weight(l, 1),
            flops=4 * rows * width * units,
        )
        terms = scatter_rows(fed)
        if l == 0:
            x, low_kept, unit2, inverse2 = call(
                partial(second_norm_kernel, ways),
                [near_rows, Far(near_rows, plain=True)] + far_unit,
                where, middle, terms, vec,
            )
            first_rows = lax.all_gather(low_kept, PLACES, axis=0, tiled=True)
        else:
            terms, first_rows = together(terms, first_rows)
            second, feed_low, second_sums, contract_ahead, last_kept = call(
                partial(turn_kernel, ways), turn_outs + [Far(near_rows)],
                where, middle, terms, vec, upstream, feed_weight(1, 1, into=3),
            )
        saved.append(
            (x_kept, q_kept, parts_kept, mixed, totals, unit1, inverse1, middle_kept, active,
             slope)
        )
        if l == 0:
            norm_kept = (unit2, inverse2)
    last_rows = lax.all_gather(last_kept, PLACES, axis=0, tiled=True)
    feed_parts = [None, None]
    for l in (1, 0):
        vec = vectors[l]
        (x_kept, q_kept, parts_kept, mixed, totals, unit1, inverse1, middle_kept, active,
         slope) = saved[l]
        feed_grad = gather_rows(feed_low)
        hidden, fed_back, unit_sums = call(
            feed_back_kernel,
            [Far(sds((rows, units), BF16), parts=2), Far(sds((rows, width), BF16), parts=2),
             sds((8, units), F32)],
            feed_grad, contract_ahead, Far(slope), feed_weight(l, 0),
            flops=4 * rows * width * units,
        )
        terms = scatter_rows(fed_back)
        pack_outs = [Far(sds((width, units), BF16))] * 2
        if l == 1:
            pack_outs = [Far(sds((2 * width, units), BF16))]
        feed_pack = call(
            feed_pack_kernel, pack_outs,
            where, Far(hidden), feed_grad, Far(middle_kept), Far(active),
            flops=4 * rows * width * units,
        )
        feed_halves = []
        if l == 1:
            terms, feed_pack = together(terms, feed_pack[0])
            feed_parts[l] = lax.psum_scatter(feed_pack, PLACES, scatter_dimension=0, tiled=True)
        else:
            terms, feed_sent = together(terms, feed_pack[1])
            feed_halves = [Far(feed_pack[0]), Far(swap(feed_sent))]
        if l == 0:
            terms, feed_parts[1] = together(terms, feed_parts[1])
        first_grad, first_low, attn_ahead = call(
            first_back_kernel,
            [Far(near_f32), sds((mine + 16, width), BF16), sds((width, 4 * e), BF16)],
            second, terms, vec, second_sums, Far(unit1), Far(inverse1),
            attn_weight(l, 0, 4 * e, into=2),
        )
        attended_grad = gather_rows(first_low).reshape(ways, mine + 16, width)
        if l == 1:
            attended_grad, last_rows = together(attended_grad, last_rows)
        dq, norm_sums, *dkv = call(
            partial(attention_back_kernel, heads, l, ways, local, blocks, chunk, len(parts_kept)),
            [sds((rows, 256), BF16), sds((16, width), F32)]
            + [sds((part.shape[0], 256 + vw), BF16) for part in parts_kept]
            + [Far(sds((width, units), BF16))] * (len(feed_halves) // 2),
            where, random_blocks, random_other, attended_grad, attn_ahead, Far(mixed),
            Far(q_kept), Far(totals), *[Far(part) for part in parts_kept], *feed_halves,
            flops=10 * rows * keys * kw, limit=44,
        )
        if l == 0:
            feed_half = dkv.pop()
            feed_parts[l] = lax.psum_scatter(feed_half, "dp", scatter_dimension=0, tiled=True)
        dkv_own, dkv_other = own_parts(dkv)
        dkv_traded = swap(dkv_other)
        triple, projected, pair_sums = call(
            partial(projection_back_kernel, e),
            [sds((rows, 4 * e), BF16), Far(sds((rows, width), BF16)), sds((8, 4 * e), F32)],
            dq, dkv_own, dkv_traded, attn_ahead,
            flops=6 * rows * width * 256,
        )
        terms = scatter_rows(projected)
        cut = step if whole_tiles else width
        pieces = width // cut
        pack_shape = (pieces, cut + 16, 4 * e) if l == 0 else (2, pieces, cut // 2 + 16, 4 * e)
        (pack,) = call(
            partial(attn_pack_kernel, l == 0, cut, e),
            [sds(pack_shape, BF16)],
            where, triple, attended_grad, norm_sums, unit_sums, pair_sums, Far(x_kept),
            Far(mixed),
            flops=8 * rows * width * 256,
        )
        if not whole_tiles:
            pack = split_pack(pack, l == 0, across)
        if l == 1:
            terms, pack = together(terms, pack)
            attn_part = lax.psum_scatter(
                pack.reshape((-1,) + pack.shape[2:]), PLACES, scatter_dimension=0
            )
            second, feed_low, second_sums, contract_ahead, later = call(
                partial(between_kernel, ways),
                turn_outs + [Far(near_rows)],
                where, terms, vectors[0], Far(first_grad), Far(norm_kept[0]), Far(norm_kept[1]),
                feed_weight(0, 1, into=3),
            )
        else:
            traded = lax.ppermute(pack, "section", [(1, 0)])
            if whole_tiles:
                sums = call(
                    pair_sum_kernel,
                    [sds(pack.shape[1:], F32)] + [sds(pack.shape[1:], BF16)] * (across - 1),
                    pack, traded,
                )
                terms, attn_part, *sums = together(terms, attn_part, *sums)
                early = [sums[0]] + [across_layer(sums[k], 0, k) for k in range(1, across)]
            else:
                total = (pack.astype(F32) + traded.astype(F32)).astype(BF16)
                early = [
                    lax.psum_scatter(total, "dp", scatter_dimension=0).astype(F32)
                ]
            places = call(
                last_input_kernel, [sds((local, width), BF16)] * 4,
                where, terms, Far(first_grad), Far(later),
            )
            back_rows = undeal(places, micro, sub)
            feed_parts = list(together(*feed_parts, places[0], early[-1])[:2])

    feed_other = swap(jnp.where(section == 0, feed_parts[1], feed_parts[0]))
    expand_out, contract_out = call(
        feed_out_kernel, [sds((1, step, units), F32)] * 2,
        where, feed_parts[0], feed_parts[1], feed_other,
    )
    attn_other = lax.ppermute(attn_part, "section", [(0, 1)])
    projections_out, output_out, gains_out, biases_out, units_out, pairs_out = call(
        partial(attn_out_kernel, step, e, c),
        [sds((1, 3, step, e), F32), sds((1, e, step), F32), sds((1, 2, step), F32),
         sds((1, 4, step), F32), sds((units // HD, 1, c), F32), sds((1, heads, 2, c), F32)],
        where, *early, attn_part, attn_other,
    )
    (activations,) = call(
        partial(activation_out_kernel, micro, sub),
        [sds((1, micro, 1, local, width), BF16)],
        where, Raw(first_rows), Raw(last_rows),
        scratch=[pltpu.SemaphoreType.DMA((micro,))],
    )
    back_rows[0], expand_out, contract_out, projections_out, activations = together(
        back_rows[0], expand_out, contract_out, projections_out, activations
    )
    (input_grads,) = call(
        place_out_kernel, [sds((1, micro, 1, local, width), F32)], where, *back_rows
    )
    return (
        activations,
        input_grads,
        projections_out,
        pairs_out.transpose(0, 2, 1, 3),
        output_out,
        expand_out,
        units_out.transpose(1, 0, 2),
        contract_out.transpose(0, 2, 1),
        gains_out,
        biases_out,
    )


def split_pack(pack, relative, across):
    if relative:
        weights, small = (pack[0, :-16], pack[0, -16:])
        weights = weights.reshape(across, -1, weights.shape[1])
        small = jnp.broadcast_to(small, (across,) + small.shape)
        return jnp.concatenate([weights, small], axis=1)
    weights = pack[:, 0, :-16].reshape(-1, pack.shape[3])
    weights = weights.reshape(across, 2, -1, pack.shape[3]).transpose(1, 0, 2, 3)
    small = jnp.broadcast_to(pack[0, 0, -16:], (2, across, 16, pack.shape[3]))
    return jnp.concatenate([weights, small], axis=2)


def solution(mesh):
    in_specs = (
        P(None, None, ("dp", "tensor"), None),
        P(None, None, ("dp", "tensor"), None),
        P(),
        P("section", "tensor", None, None),
        P("section", None, "dp", "tensor"),
        P("section", None, "tensor", "dp"),
        P("section", "tensor", "dp"),
        P("section", "dp", "tensor"),
        P("section", "tensor", "dp"),
        P("section", "tensor", "dp"),
        P("section", None, "dp"),
        P("section", None, "dp"),
    )
    out_specs = (
        P("section", None, None, ("dp", "tensor"), None),
        P("section", None, None, ("dp", "tensor"), None),
        P("section", None, "dp", "tensor"),
        P("section", None, "tensor", "dp"),
        P("section", "tensor", "dp"),
        P("section", "dp", "tensor"),
        P("section", "tensor", "dp"),
        P("section", "tensor", "dp"),
        P("section", None, "dp"),
        P("section", None, "dp"),
    )
    return jax.shard_map(body, mesh=mesh, in_specs=in_specs, out_specs=out_specs, check_vma=False)
```

```python
import math
from functools import partial

import jax
import jax.numpy as jnp
from jax import lax
from jax.experimental import pallas as pl
from jax.experimental.pallas import tpu as pltpu
from jax.sharding import PartitionSpec as P

HD = 64
BLOCK = 64
GLOBAL = 2
EPSILON = 1e-12
MASKED = -1e30
GELU_A = 0.7978845608028654
GELU_B = 0.044715
F32 = jnp.float32
BF16 = jnp.bfloat16
MIB = 1 << 20
PLACES = ("section", "dp")


def nt(a, b):
    return lax.dot_general(a, b, (((1,), (1,)), ((), ())), preferred_element_type=F32)


def tn(a, b):
    return lax.dot_general(a, b, (((0,), (0,)), ((), ())), preferred_element_type=F32)


def nn(a, b):
    return jnp.dot(a, b, preferred_element_type=F32)


def sds(shape, dtype):
    return jax.ShapeDtypeStruct(shape, dtype)


class Far:
    def __init__(self, array, shape=None, cuts=None, plain=False, into=None, parts=1):
        self.array = array
        self.shape = array.shape if shape is None else shape
        self.cuts = [((), ())] if cuts is None else cuts
        self.plain = plain
        self.into = into
        self.parts = parts


class Raw:
    def __init__(self, array):
        self.array = array


def at(ref, index):
    return ref.at[index] if index else ref


class Arriving:
    def __init__(self, source, buffer, sems, first, cuts):
        self.buffer = buffer
        self.shape = buffer.shape
        self.copies = [
            pltpu.make_async_copy(at(source, a), at(buffer, b), sems.at[first + i])
            for i, (a, b) in enumerate(cuts)
        ]
        for copy in self.copies:
            copy.start()
        self.there = False

    def settle(self):
        if not self.there:
            for copy in self.copies:
                copy.wait()
            self.there = True

    def __getitem__(self, index):
        self.settle()
        return self.buffer[index]


class Leaving:
    def __init__(self, target, buffer, sems, first):
        self.target = target
        self.buffer = buffer
        self.shape = target.shape
        self.sems = sems
        self.first = first
        self.copies = []

    def __setitem__(self, index, value):
        self.buffer[index] = value

    def send(self, source=None, rows=None):
        source = self.buffer if source is None else source
        target = self.target
        if rows is not None:
            source, target = (source.at[rows], target.at[rows])
        copy = pltpu.make_async_copy(source, target, self.sems.at[self.first + len(self.copies)])
        copy.start()
        self.copies.append(copy)

    def finish(self):
        if not self.copies:
            self.send()
        for copy in self.copies:
            copy.wait()


def flat(groups):
    return [item for group in groups for item in (group if isinstance(group, list) else [group])]


def grouped(items, groups):
    items = iter(items)
    return [
        [next(items) for _ in group] if isinstance(group, list) else next(items)
        for group in groups
    ]


def call(kernel, out_groups, *arg_groups, flops=0, limit=16, scratch=()):
    args = flat(arg_groups)
    outs = flat(out_groups)
    arrays = []
    in_specs = []
    out_specs = []
    out_shapes = []
    buffers = []
    size = 0
    semaphores = 0
    for arg in args:
        if isinstance(arg, Raw):
            arrays.append(pltpu.with_memory_space_constraint(arg.array, pltpu.HBM))
            in_specs.append(pl.BlockSpec(memory_space=pltpu.HBM))
        elif isinstance(arg, Far):
            arrays.append(pltpu.with_memory_space_constraint(arg.array, pltpu.HBM))
            in_specs.append(pl.BlockSpec(memory_space=pltpu.HBM))
            if arg.into is None:
                buffers.append(pltpu.VMEM(arg.shape, arg.array.dtype))
            semaphores += len(arg.cuts)
            size += math.prod(arg.shape) * arg.array.dtype.itemsize
        else:
            arrays.append(arg)
            scalar = arg.dtype == jnp.int32
            in_specs.append(pl.BlockSpec(memory_space=pltpu.SMEM if scalar else pltpu.VMEM))
            size += arg.size * arg.dtype.itemsize
    for out in outs:
        if isinstance(out, Raw):
            out_shapes.append(pltpu.HBM(out.array.shape, out.array.dtype))
            out_specs.append(pl.BlockSpec(memory_space=pltpu.HBM))
        elif isinstance(out, Far):
            out_shapes.append(pltpu.HBM(out.shape, out.array.dtype))
            out_specs.append(pl.BlockSpec(memory_space=pltpu.HBM))
            if not out.plain:
                buffers.append(pltpu.VMEM(out.shape, out.array.dtype))
            semaphores += out.parts
            size += math.prod(out.shape) * out.array.dtype.itemsize
        else:
            out_shapes.append(out)
            out_specs.append(pl.BlockSpec(memory_space=pltpu.VMEM))
            size += out.size * out.dtype.itemsize

    def whole(*refs):
        refs = list(refs)
        ins = refs[: len(args)]
        results = refs[len(args) : len(args) + len(outs)]
        rest = refs[len(args) + len(outs) :]
        sems = rest.pop() if semaphores else None
        given = []
        handed = []
        used = 0
        for arg, ref in zip(args, ins):
            if isinstance(arg, Far):
                buffer = rest.pop(0) if arg.into is None else results[arg.into]
                given.append(Arriving(ref, buffer, sems, used, arg.cuts))
                used += len(arg.cuts)
            else:
                given.append(ref)
        leaving = []
        for out, ref in zip(outs, results):
            if isinstance(out, Far):
                buffer = None if out.plain else rest.pop(0)
                leaving.append(Leaving(ref, buffer, sems, used))
                handed.append(leaving[-1])
                used += out.parts
            else:
                handed.append(ref)
        kernel(*grouped(given, arg_groups), *grouped(handed, out_groups), *rest)
        for item in given:
            if isinstance(item, Arriving):
                item.settle()
        for item in leaving:
            item.finish()

    scratch_shapes = buffers + list(scratch)
    if semaphores:
        scratch_shapes = scratch_shapes + [pltpu.SemaphoreType.DMA((semaphores,))]
    results = pl.pallas_call(
        whole,
        out_shape=tuple(out_shapes),
        in_specs=in_specs,
        out_specs=tuple(out_specs),
        scratch_shapes=scratch_shapes,
        compiler_params=pltpu.CompilerParams(vmem_limit_bytes=limit * MIB),
        cost_estimate=pl.CostEstimate(flops=flops, bytes_accessed=size, transcendentals=0),
    )(*arrays)
    return grouped(results, out_groups)


SECTION, PLACE, PLANE, SEAT, START, LENGTH, FLIP = range(7)


def positions(where_ref, count, ways, local, first):
    row = lax.broadcasted_iota(jnp.int32, (count, 1), 0) + first
    group = jnp.bitwise_xor(row // local % 2, where_ref[FLIP])
    return (
        where_ref[START] + group * (ways * local) + row // (2 * local) * local + row % local
    )


def row_halves(where_ref, rows):
    size = rows // 2
    own = where_ref[SEAT] // 2
    return [
        pl.ds(pl.multiple_of(jnp.bitwise_xor(own, i) * size, size), size) for i in range(2)
    ]


def send_parts(where_ref, outs, whole, half):
    count = len(outs) // 2
    mine = whole.shape[0] // len(outs)
    for k in range(half * count, (half + 1) * count):
        begin = pl.multiple_of(jnp.bitwise_xor(where_ref[SEAT], k) * mine, mine)
        if isinstance(outs[k], Leaving):
            outs[k].send(whole.at[pl.ds(begin, mine)])
        else:
            outs[k][...] = whole[pl.ds(begin, mine)]


def core_is(where_ref, core):
    return pl.when(where_ref[SECTION] == core)


def prepare_kernel(
    where_ref, projections_ref, output_ref, expand_ref, contract_ref, pair_ref, unit_ref,
    gain_ref, bias_ref, attn_keep, attn_send, keep_out, send_out, whole, small
):
    step, e = projections_ref.shape[2:]
    heads, _, c = pair_ref.shape[1:]
    half = step // 2
    whole[:, :e] = projections_ref[0, 0]
    whole[:, e : 2 * e] = projections_ref[0, 2]
    whole[:, 2 * e : 3 * e] = projections_ref[0, 1]
    whole[:, 3 * e :] = output_ref[0].T
    small[...] = jnp.zeros_like(small)
    small[0:2, :step] = gain_ref[0].astype(F32)
    small[2:6, :step] = bias_ref[0].astype(F32)
    small[: unit_ref.shape[1], 256 : 256 + c] = unit_ref[0].astype(F32)
    for i in range(heads):
        small[i : i + 1, 384 : 384 + c] = pair_ref[0, i, 0:1].astype(F32)
        small[i : i + 1, 512 : 512 + c] = pair_ref[0, i, 1:2].astype(F32)
    attn_keep[half:] = small[...].astype(BF16)
    attn_send[half:] = small[...].astype(BF16)
    expand = expand_ref[0]
    contract = contract_ref[0]

    @core_is(where_ref, 0)
    def _():
        attn_keep[:half] = whole[:half]
        attn_send[:half] = whole[half:]
        keep_out[...] = expand
        send_out[...] = contract

    @core_is(where_ref, 1)
    def _():
        attn_keep[:half] = whole[half:]
        attn_send[:half] = whole[:half]
        keep_out[...] = contract
        send_out[...] = expand


def unpack(c, e, raw_ref, vec_ref):
    places = raw_ref.shape[0]
    width = vec_ref.shape[1]
    w = width // places

    def of_heads(rows, lanes, z):
        source = lax.broadcasted_iota(jnp.int32, (128, lanes), 0)
        target = lax.broadcasted_iota(jnp.int32, (128, lanes), 1)
        repeat = ((target % c == source) & (source < c)).astype(F32).astype(BF16)
        spread_rows = nn(rows, repeat)
        head = lax.broadcasted_iota(jnp.int32, spread_rows.shape, 0)
        lane = lax.broadcasted_iota(jnp.int32, spread_rows.shape, 1)
        keep = (lane // HD == head) & (lane % HD // c == z)
        return jnp.sum(jnp.where(keep, spread_rows, 0.0), axis=0, keepdims=True)

    norms = jnp.zeros((16, width), F32)
    units = jnp.zeros((1, width), F32)
    queries = jnp.zeros((1, 256), F32)
    values = jnp.zeros((1, 256), F32)
    for z in range(places):
        rows = raw_ref[z]
        source = lax.broadcasted_iota(jnp.int32, (256, width), 0)
        target = lax.broadcasted_iota(jnp.int32, (256, width), 1)
        move = ((target == source + z * w) & (source < w)).astype(F32).astype(BF16)
        norms = norms + nn(rows[:, :256], move)
        units = units + of_heads(rows[:, 256:384], width, z)
        queries = queries + of_heads(rows[:, 384:512], 256, z)
        values = values + of_heads(rows[:, 512:640], 256, z)
    vec_ref[...] = norms[:8]
    vec_ref[6:7] = units
    lane = lax.broadcasted_iota(jnp.int32, (1, 256), 1)
    queries = jnp.where(lane < e, queries, 0.0)
    values = jnp.where(lane < e, values, 0.0)
    return (queries, pltpu.roll(values, 256 - e, 1))


def qkv_kernel(
    ways, local, blocks, c, e, where_ref, x_ref, raw_ref, w_ref, q_ref, kv_ref, vec_ref, *kept
):
    kw = q_ref.shape[1]
    vw = kv_ref.shape[1] - kw
    x = x_ref[...]
    kept[0].send(x_ref)
    query_bias, value_bias = unpack(c, e, raw_ref, vec_ref)
    lead = 2 * e // 128 * 128
    q = (nn(x, w_ref[:, :256]) + query_bias).astype(BF16).astype(F32) * HD ** (-0.5)
    lane = lax.broadcasted_iota(jnp.int32, (1, 256), 1)
    q = jnp.where(lane < e, q, 0.0).astype(BF16)
    q_ref[:, :256] = q
    if kw > 256:
        q_ref[:, 256:] = jnp.zeros((q.shape[0], kw - 256), BF16)
    kept[1].send(q_ref)
    position = positions(where_ref, x.shape[0], ways, local, 0)
    block = position // BLOCK
    lane = lax.broadcasted_iota(jnp.int32, (1, kw), 1)
    hidden = (position >= where_ref[LENGTH]) & (lane == e + blocks)
    tail = jnp.where(lane == e + block, 1.0, jnp.where(hidden, MASKED, 0.0))
    k = nn(x, w_ref[:, lead : lead + 256])
    if kw > 256:
        k = jnp.concatenate([k, jnp.zeros((k.shape[0], kw - 256), F32)], axis=1)
    kv_ref[:, :kw] = jnp.where(lane < e, k, tail).astype(BF16)
    kv_ref[:, kw:] = (nn(x, w_ref[:, 128 : 128 + vw]) + value_bias).astype(BF16)
    kept[2].send(kv_ref)


def head_mask(first, lanes):
    lane = lax.broadcasted_iota(jnp.int32, (1, lanes), 1)
    return ((lane >= first) & (lane < first + HD)).astype(F32)


def seen_rows(where_ref, random_refs, layer, h, rows, ways, local, kw, e, blocks):
    lane = lax.broadcasted_iota(jnp.int32, (1, kw), 1)
    key = lane - e
    parts = []
    for g in range(rows // local):
        group = jnp.bitwise_xor(g % 2, where_ref[FLIP])
        position = where_ref[START] + group * (ways * local) + g // 2 * local
        block = position // BLOCK
        seen = (key < GLOBAL) | (jnp.abs(key - block) <= 1) | (block < GLOBAL)
        for i in range(random_refs[0].shape[3]):
            picked = [ref[0, h, block, i] for ref in random_refs]
            seen = seen | (key == jnp.where(where_ref[SECTION] == layer, *picked))
        hidden = (key >= 0) & (key < blocks) & jnp.logical_not(seen)
        line = jnp.where(key == blocks, 1.0, jnp.where(hidden, MASKED, 0.0))
        parts.append(jnp.broadcast_to(line, (local, kw)))
    return jnp.concatenate(parts, axis=0)


def attention_kernel(
    heads, layer, ways, local, blocks, chunk, where_ref, random_refs, q_ref, w_ref, parts,
    outs, mixed_out, total_out, kept, whole
):
    rows, kw = q_ref.shape
    e = heads * HD
    vw = parts[0].shape[1] - kw
    shift = vw - e
    for out, part in zip(kept, parts[1:]):
        out.send(part)
    k = jnp.concatenate([part[:, :kw] for part in parts], axis=0)
    vt = jnp.concatenate([part[:, kw:] for part in parts], axis=0).T
    q = q_ref[...].astype(F32)
    lines = [jnp.zeros((shift, rows), F32)]
    totals = []
    for h in range(heads):
        seen = seen_rows(where_ref, random_refs, layer, h, rows, ways, local, kw, e, blocks)
        qa = (q * head_mask(h * HD, kw) + seen).astype(BF16)
        vh = vt[shift + h * HD : shift + (h + 1) * HD]
        cells = []
        sums = []
        for c in range(0, rows, chunk):
            scores = nt(k, qa[c : c + chunk])
            top = jnp.max(scores, axis=0, keepdims=True)
            p = jnp.exp(scores - top)
            total = jnp.sum(p, axis=0, keepdims=True)
            cells.append(nn(vh, p.astype(BF16)) / total)
            sums.append(top + jnp.log(total))
        lines.append(jnp.concatenate(cells, axis=1))
        totals.append(jnp.concatenate(sums, axis=1))
    total_out[...] = jnp.concatenate(totals + [jnp.zeros((8 - heads, rows), F32)], axis=0)
    total_out.send()
    mixed = jnp.concatenate(lines, axis=0).T.astype(BF16)
    mixed_out[...] = mixed
    mixed_out.send()
    for half in range(2):
        size = rows // 2
        part = slice(half * size, (half + 1) * size)
        whole[part] = nt(mixed[part], w_ref[...]).astype(BF16)
    for half in range(2):
        send_parts(where_ref, outs, whole, half)


def attention_back_kernel(
    heads, layer, ways, local, blocks, chunk, where_ref, random_refs, grad_ref, w_ref, mixed_ref,
    q_ref, total_ref, parts, adds, dq_ref, small_ref, outs, half_outs
):
    rows, kw = q_ref.shape
    e = heads * HD
    vw = mixed_ref.shape[1]
    shift = vw - e
    width = grad_ref.shape[2]
    grad = grad_ref[:, : 2 * local].reshape(rows, width)
    small = grad_ref[0, 2 * local :].astype(F32)
    for i in range(1, ways):
        small = small + grad_ref[i, 2 * local :].astype(F32)
    small_ref[...] = small
    mixed_grad = nn(grad, w_ref[:, w_ref.shape[1] - vw :]).astype(BF16).astype(F32)
    product = mixed_grad * mixed_ref[...].astype(F32)
    masks = jnp.concatenate([head_mask(shift + h * HD, vw) for h in range(8)], axis=0)
    inner = lax.dot_general(
        masks, product, (((1,), (1,)), ((), ())),
        preferred_element_type=F32, precision=lax.Precision.HIGHEST,
    )
    q = q_ref[...].astype(F32)
    k = jnp.concatenate([part[:, :kw] for part in parts], axis=0)
    v = jnp.concatenate([part[:, kw:] for part in parts], axis=0)
    kt = k[:, :256].T
    totals = total_ref[...]
    for half_out in half_outs:
        half_out[...] = (adds[0][...].astype(F32) + adds[1][...].astype(F32)).astype(BF16)
        half_out.send()
    dk = None
    dv = None
    lines = []
    for h in range(heads):
        seen = seen_rows(where_ref, random_refs, layer, h, rows, ways, local, kw, e, blocks)
        qm = q * head_mask(h * HD, kw)
        qa = (qm + seen).astype(BF16)
        qm = qm[:, :256].astype(BF16)
        gm = (mixed_grad * head_mask(shift + h * HD, vw)).astype(BF16)
        kh = kt[h * HD : (h + 1) * HD]
        cells = []
        for c in range(0, rows, chunk):
            scores = nt(k, qa[c : c + chunk])
            p = jnp.exp(scores - totals[h : h + 1, c : c + chunk])
            dp = nt(v, gm[c : c + chunk])
            ds = (p * (dp - inner[h : h + 1, c : c + chunk])).astype(BF16)
            dv_term = nn(p.astype(BF16), gm[c : c + chunk])
            dk_term = nn(ds, qm[c : c + chunk])
            dv = dv_term if dv is None else dv + dv_term
            dk = dk_term if dk is None else dk + dk_term
            cells.append(nn(kh, ds))
        lines.append(jnp.concatenate(cells, axis=1))
    lines.append(jnp.zeros((256 - e, rows), F32))
    dq = jnp.concatenate(lines, axis=0).T * HD ** (-0.5)
    dq_ref[...] = dq.astype(BF16)
    start = 0
    for out in outs:
        size = out.shape[0]
        out[:, :256] = dk[start : start + size].astype(BF16)
        out[:, 256:] = dv[start : start + size].astype(BF16)
        start += size


def projection_back_kernel(
    e, where_ref, dq_ref, own_ref, other_ref, w_ref, triple_ref, sums_ref, outs, whole
):
    vw = own_ref.shape[1] - 256
    width = w_ref.shape[1]
    lead = 2 * e // 128 * 128
    rows = dq_ref.shape[0]
    dq = dq_ref[...]
    dkv = (own_ref[...].astype(F32) + other_ref[...].astype(F32)).astype(BF16).astype(F32)
    dv = dkv[:, 256:]
    head = dq.astype(F32)
    nothing = jnp.zeros((rows, 128), F32)
    triple = jnp.concatenate(
        [head[:, :128], head[:, 128:] + dv[:, :128], dv[:, 128:], dkv[:, :256], nothing], axis=1
    ).astype(BF16)
    triple_ref[...] = triple
    sums_ref[...] = jnp.zeros_like(sums_ref)
    sums_ref[0:1] = jnp.sum(triple.astype(F32), axis=0, keepdims=True)
    for half, part in enumerate(row_halves(where_ref, rows)):
        whole[part] = nt(triple_ref[part], w_ref[...]).astype(BF16)
        send_parts(where_ref, outs, whole, half)


def norm(values):
    average = jnp.mean(values, axis=-1, keepdims=True)
    centered = values - average
    spread_now = jnp.mean(centered * centered, axis=-1, keepdims=True)
    inverse = lax.rsqrt(spread_now + EPSILON)
    return (centered * inverse, inverse)


def total_of(terms):
    total = terms[0][...].astype(F32)
    for term in terms[1:]:
        total = total + term[...].astype(F32)
    return total


def first_norm_kernel(x_ref, terms_ref, vec_ref, middle_ref, low_ref, unit_out, inverse_out):
    values = x_ref[...].astype(F32) + total_of(terms_ref) + vec_ref[2:3]
    unit, inverse = norm(values)
    unit_out[...] = unit
    unit_out.send()
    inverse_out[...] = jnp.broadcast_to(inverse, inverse_out.shape)
    inverse_out.send()
    middle = unit * vec_ref[0:1] + vec_ref[4:5]
    middle_ref[...] = middle
    low_ref[...] = middle.astype(BF16)


def valid_rows(where_ref, ways, local):
    position = positions(where_ref, 2 * local, ways, local, where_ref[SEAT] * 2 * local)
    return (position < where_ref[LENGTH]).astype(F32)


def place_parts(where_ref, early, later, outs):
    half = early.shape[0] // 2
    late_plane = where_ref[PLANE] // 2
    for u in range(2):
        for p in range(2):
            @pl.when(late_plane == u)
            def _(u=u, p=p):
                outs[2 * p + u][...] = early[p * half : (p + 1) * half]

            @pl.when(late_plane != u)
            def _(u=u, p=p):
                outs[2 * p + u][...] = later[p * half : (p + 1) * half]


def norm_back(grad, unit, inverse, gain):
    scaled = grad * gain
    return inverse * (
        scaled
        - jnp.mean(scaled, axis=-1, keepdims=True)
        - unit * jnp.mean(scaled * unit, axis=-1, keepdims=True)
    )


def second_norm(ways, where_ref, middle_ref, terms_ref, vec_ref):
    unit, inverse = norm(middle_ref[...] + total_of(terms_ref) + vec_ref[3:4])
    result = unit * vec_ref[1:2] + vec_ref[5:6]
    valid = valid_rows(where_ref, ways, unit.shape[0] // 2)
    return ((result * valid).astype(BF16), unit, inverse, valid)


def second_back(grad, unit, inverse, vec_ref, second_ref, low_ref, sums_ref):
    second = norm_back(grad, unit, inverse, vec_ref[1:2])
    low_ref[...] = second.astype(BF16)
    second_ref[...] = second
    second_ref.send()
    sums_ref[...] = jnp.zeros_like(sums_ref)
    sums_ref[0:1] = jnp.sum(grad * unit, axis=0, keepdims=True)
    sums_ref[1:2] = jnp.sum(grad, axis=0, keepdims=True)
    sums_ref[2:3] = jnp.sum(second, axis=0, keepdims=True)


def second_norm_kernel(
    ways, where_ref, middle_ref, terms_ref, vec_ref, low_ref, kept, unit_out, inverse_out
):
    low, unit, inverse, _ = second_norm(ways, where_ref, middle_ref, terms_ref, vec_ref)
    low_ref[...] = low
    kept.send(low_ref)
    unit_out[...] = unit
    unit_out.send()
    inverse_out[...] = jnp.broadcast_to(inverse, inverse_out.shape)
    inverse_out.send()


def turn_kernel(
    ways, where_ref, middle_ref, terms_ref, vec_ref, up_ref, _, second_ref, low_ref, sums_ref,
    ahead, kept
):
    low, unit, inverse, valid = second_norm(ways, where_ref, middle_ref, terms_ref, vec_ref)
    kept[...] = low
    kept.send()
    second_back(
        up_ref[...].astype(F32) * valid, unit, inverse, vec_ref, second_ref, low_ref, sums_ref
    )


def between_kernel(
    ways, where_ref, terms_ref, vec_ref, first_ref, unit_ref, inverse_ref, _, second_ref, low_ref,
    sums_ref, ahead, kept
):
    low = (first_ref[...] + total_of(terms_ref)).astype(BF16)
    kept[...] = low
    kept.send()
    grad = low.astype(F32) * valid_rows(where_ref, ways, low.shape[0] // 2)
    second_back(
        grad, unit_ref[...], inverse_ref[:, 0:1], vec_ref, second_ref, low_ref, sums_ref
    )


def first_back_kernel(
    second_ref, terms_ref, vec_ref, before_ref, unit_ref, inverse_ref, _, first_ref, low_ref, ahead
):
    grad = second_ref[...] + total_of(terms_ref)
    unit = unit_ref[...]
    first = norm_back(grad, unit, inverse_ref[:, 0:1], vec_ref[0:1])
    first_ref[...] = first
    rows = first.shape[0]
    low_ref[:rows] = first.astype(BF16)
    before = before_ref[...]
    low_ref[rows:] = jnp.concatenate(
        [jnp.sum(grad * unit, axis=0, keepdims=True), before[0:1],
         jnp.sum(first, axis=0, keepdims=True), before[2:3],
         jnp.sum(grad, axis=0, keepdims=True), before[1:2],
         jnp.zeros((10, first.shape[1]), F32)], axis=0
    ).astype(BF16)


def last_input_kernel(where_ref, first_ref, later_ref, terms, *outs):
    low = (first_ref[...] + total_of(terms)).astype(BF16)
    place_parts(where_ref, low, later_ref[...], outs)


def place_out_kernel(where_ref, *refs):
    parts, out_ref = (refs[:-1], refs[-1])
    odd = where_ref[PLACE] % 2
    for p in range(2):
        for u in range(2):
            m = 2 * jnp.bitwise_xor(where_ref[SECTION], u) + jnp.bitwise_xor(odd, p)
            out_ref[0, m, 0] = parts[2 * p + u][...].astype(F32)


def activation_out_kernel(micro, sub, where_ref, first_ref, last_ref, out_ref, sems):
    local = out_ref.shape[3]
    place = where_ref[PLACE]
    side = place % micro // 2

    def copies(ref):
        result = []
        for m in range(micro):
            source = side * (micro * sub) + m * sub + place // micro
            row = (2 * source + jnp.bitwise_xor(place % 2, m & 1)) * local
            rows = pl.ds(pl.multiple_of(row, local), local)
            result.append(pltpu.make_async_copy(ref.at[rows], out_ref.at[0, m, 0], sems.at[m]))
        return result

    for core, ref in enumerate((first_ref, last_ref)):
        @core_is(where_ref, core)
        def _(ref=ref):
            for copy in copies(ref):
                copy.start()
            for copy in copies(ref):
                copy.wait()


def feed_kernel(
    where_ref, x_ref, vec_ref, expand_ref, contract_ref, outs, active_out, slope_out, kept, whole
):
    kept.send(x_ref)
    parts = row_halves(where_ref, x_ref.shape[0])
    values = [nn(x_ref[part], expand_ref[...]) + vec_ref[6:7] for part in parts]
    for half, (part, v) in enumerate(zip(parts, values)):
        th = jnp.tanh(v * (GELU_A + GELU_A * GELU_B * (v * v)))
        upper = 0.5 + 0.5 * th
        active = (v * upper).astype(BF16)
        active_out[part] = active
        active_out.send(rows=part)
        slope = upper + v * (1.0 - th * th) * (0.5 * GELU_A + 1.5 * GELU_A * GELU_B * (v * v))
        slope_out[part] = slope.astype(BF16)
        slope_out.send(rows=part)
        whole[part] = nt(active, contract_ref[...]).astype(BF16)
        send_parts(where_ref, outs, whole, half)


def feed_back_kernel(
    where_ref, grad_ref, contract_ref, slope_ref, expand_ref, hidden_ref, outs, sums_ref, whole
):
    parts = row_halves(where_ref, grad_ref.shape[0])
    values = [nn(grad_ref[part], contract_ref[...]) for part in parts]
    total = jnp.zeros((1, hidden_ref.shape[1]), F32)
    for half, (part, value) in enumerate(zip(parts, values)):
        hidden = (value * slope_ref[part].astype(F32)).astype(BF16)
        hidden_ref[part] = hidden
        hidden_ref.send(rows=part)
        total = total + jnp.sum(hidden.astype(F32), axis=0, keepdims=True)
        whole[part] = nt(hidden, expand_ref[...]).astype(BF16)
        send_parts(where_ref, outs, whole, half)
    sums_ref[...] = jnp.zeros_like(sums_ref)
    sums_ref[0:1] = total


def feed_pack_kernel(where_ref, hidden_ref, grad_ref, middle_ref, active_ref, *outs):
    width = middle_ref.shape[1]
    expand = tn(middle_ref[...], hidden_ref[...]).astype(BF16)
    contract = tn(grad_ref[...], active_ref[...]).astype(BF16)
    if len(outs) == 1:
        outs[0][:width] = expand
        outs[0][width:] = contract
        return

    @core_is(where_ref, 0)
    def _():
        outs[0][...] = expand
        outs[1][...] = contract

    @core_is(where_ref, 1)
    def _():
        outs[0][...] = contract
        outs[1][...] = expand


def attn_pack_kernel(
    relative, step, e, where_ref, triple_ref, grad_ref, norm_ref, unit_ref, pair_ref, x_ref,
    mixed_ref, out_ref
):
    x = x_ref[...]
    width = x.shape[1]
    vw = mixed_ref.shape[1]
    places = width // step
    local = grad_ref.shape[1] - 16
    grad = grad_ref[:, :local].reshape(x.shape)
    total = tn(x, triple_ref[...])
    last = total[:, width - vw :] + tn(grad, mixed_ref[...])
    weights = jnp.concatenate([total[:, : width - vw], last], axis=1).astype(BF16)
    small = jnp.concatenate(
        [norm_ref[:6], unit_ref[0:1], pair_ref[0:1], jnp.zeros((8, width), F32)], axis=0
    ).astype(BF16)
    for z in range(places):
        begin = z * step
        if relative:
            k = jnp.bitwise_xor(where_ref[PLACE], z) if places > 1 else 0
            out_ref[k, :step] = weights[begin : begin + step]
            out_ref[k, step:] = small
        else:
            half = step // 2
            for i in range(2):
                out_ref[i, z, :half] = weights[begin + i * half : begin + (i + 1) * half]
                out_ref[i, z, half:] = small


def pair_sum_kernel(mine_ref, other_ref, own_ref, *sent_refs):
    own_ref[...] = mine_ref[0].astype(F32) + other_ref[0].astype(F32)
    for k, sent in enumerate(sent_refs):
        sent[...] = (
            mine_ref[k + 1].astype(F32) + other_ref[k + 1].astype(F32)
        ).astype(BF16)


def attn_out_kernel(
    step, e, c, where_ref, *refs
):
    early, (mine_ref, other_ref), outs = (refs[:-8], refs[-8:-6], refs[-6:])
    projections_ref, output_ref, gain_ref, bias_ref, unit_ref, pair_ref = outs
    width = mine_ref.shape[1]

    def fill(total):
        weights = total[:step]
        small = total[step : step + 8]
        projections_ref[0, 0] = weights[:, :e]
        projections_ref[0, 1] = weights[:, 2 * e : 3 * e]
        projections_ref[0, 2] = pltpu.roll(weights, width - e, 1)[:, :e]
        output_ref[0] = pltpu.roll(weights, e, 1)[:, :e].T
        mine = pltpu.roll(small, lax.rem(width - where_ref[PLACE] * step, width), 1)
        gain_ref[0] = mine[0:2, :step]
        bias_ref[0] = mine[2:6, :step]

        def column(row, head):
            shift = lax.rem(2 * width - head * HD - where_ref[PLACE] * c, width)
            return pltpu.roll(small, shift, 1)[row : row + 1, :c]

        for head in range(unit_ref.shape[0]):
            unit_ref[head] = column(6, head)
        for head in range(pair_ref.shape[1]):
            pair_ref[0, head, 0:1] = column(7, head)
            pair_ref[0, head, 1:2] = column(7, head + e // HD)

    @core_is(where_ref, 0)
    def _():
        total = early[0][...]
        for term in early[1:]:
            total = total + term[...].astype(F32)
        fill(total)

    @core_is(where_ref, 1)
    def _():
        mine = mine_ref[...].astype(F32)
        other = other_ref[...].astype(F32)
        fill(jnp.concatenate([other[: step // 2], mine], axis=0))


def feed_out_kernel(where_ref, first_ref, second_ref, other_ref, expand_ref, contract_ref):
    @core_is(where_ref, 0)
    def _():
        expand_ref[0] = first_ref[...].astype(F32)
        contract_ref[0] = other_ref[...].astype(F32)

    @core_is(where_ref, 1)
    def _():
        expand_ref[0] = other_ref[...].astype(F32)
        contract_ref[0] = second_ref[...].astype(F32)


def swap(x):
    return lax.ppermute(x, "section", [(0, 1), (1, 0)])


def gather_rows(x):
    return lax.all_gather(x, "tensor", axis=0, tiled=True)


def scatter_rows(parts):
    seats = range(lax.axis_size("tensor"))
    return parts[:1] + [
        lax.ppermute(parts[k], "tensor", [(i, i ^ k) for i in seats]) for k in seats if k
    ]


def deal(x, micro, sub):
    section = lax.axis_index("section")
    across = lax.axis_size("dp")
    odd = lax.axis_index("dp") % 2
    got = []
    for p in range(2):
        route = []
        for c in range(2):
            for d in range(across):
                r, dd = (d // micro, d % micro)
                m = 2 * c + (p ^ (dd & 1))
                route.append((c * across + d, (dd >> 1) * across + m * sub + r))
        chosen = 2 * section + (p ^ odd)
        payload = lax.dynamic_index_in_dim(x, chosen, 0, keepdims=False)
        got.append(lax.ppermute(payload, PLACES, route))
    return got


def undeal(parts, micro, sub):
    across = lax.axis_size("dp")
    got = []
    for p in range(2):
        for u in range(2):
            route = []
            for s in range(2):
                for source in range(across):
                    m, r = (source // sub, source % sub)
                    j = p ^ (m & 1)
                    layer = u ^ (m >> 1)
                    route.append((s * across + source, layer * across + r * micro + 2 * s + j))
            got.append(lax.ppermute(parts[2 * p + u], PLACES, route))
    return got


def across_layer(x, layer, k):
    across = lax.axis_size("dp")
    route = [(layer * across + d, layer * across + (d ^ k)) for d in range(across)]
    return lax.ppermute(x, PLACES, route)


def together(*values):
    return lax.optimization_barrier(values)


def after(x, token):
    return lax.optimization_barrier((x, token))[0]


def body(
    tokens,
    cotangent,
    lengths,
    random_blocks,
    projections,
    query_value_bias,
    output_weight,
    expand_weight,
    expand_bias,
    contract_weight,
    norm_gains,
    row_biases,
):
    section = lax.axis_index("section")
    place = lax.axis_index("dp")
    seat = lax.axis_index("tensor")
    across = lax.axis_size("dp")
    ways = lax.axis_size("tensor")
    micro = tokens.shape[0]
    sub = across // micro
    plane = place // sub
    share = place % sub
    local = tokens.shape[2]
    width = tokens.shape[3]
    e = projections.shape[3]
    heads = e // HD
    units = expand_weight.shape[2]
    step = projections.shape[2]
    c = query_value_bias.shape[3]
    mine = 2 * local
    rows = mine * ways
    keys = rows * 2 * sub
    blocks = keys // BLOCK
    kw = -(-(e + blocks + 1) // 128) * 128
    vw = 256
    whole_tiles = step % 32 == 0
    start = (share * micro + 2 * section) * ways * local
    length = lax.dynamic_index_in_dim(lengths[:, 0], plane, 0, keepdims=False)
    where = jnp.stack([section, place, plane, seat, start, length, plane % 2, 0]).astype(jnp.int32)
    random_other = swap(random_blocks)

    attn_keep, attn_send, feed_keep, feed_send = call(
        prepare_kernel,
        [sds((step // 2 + 16, 4 * e), BF16)] * 2 + [sds((step, units), BF16)] * 2,
        where, Far(projections), Far(output_weight), Far(expand_weight),
        Far(contract_weight.transpose(0, 2, 1)), Far(query_value_bias.transpose(0, 2, 1, 3)),
        Far(expand_bias), Far(norm_gains), Far(row_biases),
        scratch=[pltpu.VMEM((step, 4 * e), BF16), pltpu.VMEM((16, 4 * e), F32)],
    )
    x = jnp.concatenate(deal(tokens[:, 0], micro, sub), axis=0)
    feed_send, x = together(feed_send, x)
    attn_traded = swap(attn_send)
    feed_traded = swap(feed_send)
    attn_all = []
    feed_all = []
    for l in range(2):
        own = section == l
        whole = lax.all_gather(jnp.where(own, attn_keep, attn_traded), PLACES, axis=0, tiled=True)
        attn_all.append(whole.reshape(2, across, step // 2 + 16, 4 * e))
        whole = lax.all_gather(jnp.where(own, feed_keep, feed_traded), PLACES, axis=0, tiled=True)
        feed_all.append(whole.reshape(2, width, units))

    upstream = jnp.concatenate(deal(cotangent[:, 0], micro, sub), axis=0)
    if not whole_tiles:
        attn_flat = [
            whole[:, :, : step // 2].transpose(1, 0, 2, 3).reshape(width, 4 * e)
            for whole in attn_all
        ]
    def small_rows(l):
        if not whole_tiles:
            return attn_all[l][0, :, step // 2 :]
        cuts = [((0, z, pl.ds(step // 2, 16)), (z,)) for z in range(across)]
        return Far(attn_all[l], (across, 16, 4 * e), cuts)

    def attn_weight(l, first, size, into=None):
        lanes = pl.ds(first, size)
        if not whole_tiles:
            return Far(attn_flat[l], (width, size), [((slice(None), lanes), ())], into=into)
        half = step // 2
        cuts = [
            ((i, z, pl.ds(0, half), lanes), (pl.ds(z * step + i * half, half),))
            for z in range(across)
            for i in range(2)
        ]
        return Far(attn_all[l], (width, size), cuts, into=into)

    def feed_weight(l, i, into=None):
        return Far(feed_all[l], (width, units), [((i,), ())], into=into)

    def all_parts(own):
        pair = [own, swap(own)]
        if sub == 1:
            return pair
        groups = [[m * sub + r for r in range(sub)] for m in range(micro)]
        return [
            lax.all_gather(
                jnp.concatenate(pair, axis=0), "dp", axis=0, tiled=True, axis_index_groups=groups
            )
        ]

    def own_parts(parts):
        if sub == 1:
            return parts
        groups = [[m * sub + r for r in range(sub)] for m in range(micro)]
        total = lax.psum_scatter(
            parts[0], "dp", scatter_dimension=0, tiled=True, axis_index_groups=groups
        )
        return [total[:rows], total[rows:]]

    chunk = min(rows, 512)
    near_rows = sds((mine, width), BF16)
    exchanged = [near_rows] + [Far(near_rows, plain=True)] * (ways - 1)
    exchanged_back = [Far(near_rows, plain=True)] * ways
    whole = pltpu.VMEM((rows, width), BF16)
    near_f32 = sds((mine, width), F32)
    turn_outs = [Far(near_f32), near_rows, sds((8, width), F32), sds((width, units), BF16)]
    far_unit = [Far(sds((mine, width), F32)), Far(sds((mine, 128), F32))]

    saved = []
    vectors = []
    for l in range(2):
        x_all = gather_rows(x)
        q, kv, vec, x_kept, q_kept, kv_kept = call(
            partial(qkv_kernel, ways, local, blocks, c, e),
            [sds((rows, kw), BF16), sds((rows, kw + vw), BF16), sds((8, width), F32),
             Far(sds((rows, width), BF16), plain=True), Far(sds((rows, kw), BF16), plain=True),
             Far(sds((rows, kw + vw), BF16), plain=True)],
            where, x_all, small_rows(l), attn_weight(l, 0, 4 * e),
            flops=6 * rows * width * 256,
        )
        vectors.append(vec)
        parts = all_parts(kv)
        attended, mixed, totals, others = call(
            partial(attention_kernel, heads, l, ways, local, blocks, chunk),
            [exchanged, Far(sds((rows, vw), BF16)), Far(sds((8, rows), F32)),
             [Far(sds(part.shape, BF16), plain=True) for part in parts[1:]]],
            where, [random_blocks, random_other], q, attn_weight(l, 4 * e - vw, vw), parts,
            flops=4 * rows * keys * kw, limit=24, scratch=[whole],
        )
        parts_kept = [kv_kept, others[0]] if sub == 1 else parts
        terms = scatter_rows(attended)
        if l == 1:
            terms[0], upstream = together(terms[0], upstream)
        middle, middle_low, unit1, inverse1 = call(
            first_norm_kernel, [sds((mine, width), F32), near_rows] + far_unit, x, terms, vec
        )
        middle_all = gather_rows(middle_low)
        fed, active, slope, middle_kept = call(
            feed_kernel,
            [exchanged, Far(sds((rows, units), BF16), parts=2),
             Far(sds((rows, units), BF16), parts=2), Far(sds((rows, width), BF16), plain=True)],
            where, middle_all, vec, feed_weight(l, 0), feed_weight(l, 1),
            flops=4 * rows * width * units, scratch=[whole],
        )
        terms = scatter_rows(fed)
        if l == 0:
            x, low_kept, unit2, inverse2 = call(
                partial(second_norm_kernel, ways),
                [near_rows, Far(near_rows, plain=True)] + far_unit,
                where, middle, terms, vec,
            )
            first_rows = lax.all_gather(low_kept, PLACES, axis=0, tiled=True)
        else:
            second, feed_low, second_sums, contract_ahead, last_kept = call(
                partial(turn_kernel, ways), turn_outs + [Far(near_rows)],
                where, middle, terms, vec, upstream, feed_weight(1, 1, into=3),
            )
        saved.append(
            (x_kept, q_kept, parts_kept, mixed, totals, unit1, inverse1, middle_kept, active,
             slope)
        )
        if l == 0:
            norm_kept = (unit2, inverse2)
    last_rows = lax.all_gather(last_kept, PLACES, axis=0, tiled=True)
    feed_parts = [None, None]
    for l in (1, 0):
        vec = vectors[l]
        (x_kept, q_kept, parts_kept, mixed, totals, unit1, inverse1, middle_kept, active,
         slope) = saved[l]
        feed_grad = gather_rows(feed_low)
        if l == 1:
            feed_grad, first_rows = together(feed_grad, first_rows)
        hidden, fed_back, unit_sums = call(
            feed_back_kernel,
            [Far(sds((rows, units), BF16), parts=2), exchanged_back, sds((8, units), F32)],
            where, feed_grad, contract_ahead, Far(slope), feed_weight(l, 0),
            flops=4 * rows * width * units, scratch=[whole],
        )
        terms = scatter_rows(fed_back)
        pack_outs = [Far(sds((width, units), BF16))] * 2
        if l == 1:
            pack_outs = [Far(sds((2 * width, units), BF16))]
        feed_pack = call(
            feed_pack_kernel, pack_outs,
            where, Far(hidden), feed_grad, Far(middle_kept), Far(active),
            flops=4 * rows * width * units,
        )
        feed_halves = []
        if l == 1:
            *terms, feed_pack = together(*terms, feed_pack[0])
            feed_parts[l] = lax.psum_scatter(feed_pack, PLACES, scatter_dimension=0, tiled=True)
        else:
            *terms, feed_sent = together(*terms, feed_pack[1])
            feed_halves = [Far(feed_pack[0]), Far(swap(feed_sent))]
        if l == 0:
            terms[0], feed_parts[1] = together(terms[0], feed_parts[1])
        terms[0] = Far(terms[0])
        first_grad, first_low, attn_ahead = call(
            first_back_kernel,
            [Far(near_f32), sds((mine + 16, width), BF16), sds((width, 4 * e), BF16)],
            Far(second), terms, vec, second_sums, Far(unit1), Far(inverse1),
            attn_weight(l, 0, 4 * e, into=2),
        )
        attended_grad = gather_rows(first_low).reshape(ways, mine + 16, width)
        if l == 1:
            attended_grad, last_rows = together(attended_grad, last_rows)
        dq, norm_sums, dkv, feed_half = call(
            partial(attention_back_kernel, heads, l, ways, local, blocks, chunk),
            [sds((rows, 256), BF16), sds((16, width), F32),
             [sds((part.shape[0], 256 + vw), BF16) for part in parts_kept],
             [Far(sds((width, units), BF16))] * (len(feed_halves) // 2)],
            where, [random_blocks, random_other], attended_grad, attn_ahead, Far(mixed),
            Far(q_kept), Far(totals), [Far(part) for part in parts_kept], feed_halves,
            flops=10 * rows * keys * kw, limit=44,
        )
        if l == 0:
            feed_parts[l] = lax.psum_scatter(
                feed_half[0], "dp", scatter_dimension=0, tiled=True
            )
        dkv_own, dkv_other = own_parts(dkv)
        dkv_traded = swap(dkv_other)
        triple, pair_sums, projected = call(
            partial(projection_back_kernel, e),
            [sds((rows, 4 * e), BF16), sds((8, 4 * e), F32), exchanged_back],
            where, dq, dkv_own, dkv_traded, attn_ahead,
            flops=6 * rows * width * 256, scratch=[whole],
        )
        terms = scatter_rows(projected)
        cut = step if whole_tiles else width
        pieces = width // cut
        pack_shape = (pieces, cut + 16, 4 * e) if l == 0 else (2, pieces, cut // 2 + 16, 4 * e)
        (pack,) = call(
            partial(attn_pack_kernel, l == 0, cut, e),
            [sds(pack_shape, BF16)],
            where, triple, attended_grad, norm_sums, unit_sums, pair_sums, Far(x_kept),
            Far(mixed),
            flops=8 * rows * width * 256,
        )
        if not whole_tiles:
            pack = split_pack(pack, l == 0, across)
        if l == 1:
            *terms, pack = together(*terms, pack)
            attn_part = lax.psum_scatter(
                pack.reshape((-1,) + pack.shape[2:]), PLACES, scatter_dimension=0
            )
            terms[0] = Far(terms[0])
            second, feed_low, second_sums, contract_ahead, later = call(
                partial(between_kernel, ways),
                turn_outs + [Far(near_rows)],
                where, terms, vectors[0], Far(first_grad), Far(norm_kept[0]), Far(norm_kept[1]),
                feed_weight(0, 1, into=3),
            )
        else:
            traded = lax.ppermute(pack, "section", [(1, 0)])
            if whole_tiles:
                sums = call(
                    pair_sum_kernel,
                    [sds(pack.shape[1:], F32)] + [Far(sds(pack.shape[1:], BF16))] * (across - 1),
                    pack, traded,
                )
                terms[0], attn_part, *sums = together(terms[0], attn_part, *sums)
                early = [sums[0]] + [across_layer(sums[k], 0, k) for k in range(1, across)]
            else:
                total = (pack.astype(F32) + traded.astype(F32)).astype(BF16)
                early = [
                    lax.psum_scatter(total, "dp", scatter_dimension=0).astype(F32)
                ]
            terms[0] = Far(terms[0])
            places = call(
                last_input_kernel, [sds((local, width), BF16)] * 4,
                where, Far(first_grad), Far(later), terms,
            )
            back_rows = undeal(places, micro, sub)
            feed_parts = list(together(*feed_parts, places[0], early[-1])[:2])

    feed_other = swap(jnp.where(section == 0, feed_parts[1], feed_parts[0]))
    expand_out, contract_out = call(
        feed_out_kernel, [sds((1, step, units), F32)] * 2,
        where, feed_parts[0], feed_parts[1], feed_other,
    )
    attn_other = lax.ppermute(attn_part, "section", [(0, 1)])
    projections_out, output_out, gains_out, biases_out, units_out, pairs_out = call(
        partial(attn_out_kernel, step, e, c),
        [sds((1, 3, step, e), F32), sds((1, e, step), F32), sds((1, 2, step), F32),
         sds((1, 4, step), F32), sds((units // HD, 1, c), F32), sds((1, heads, 2, c), F32)],
        where, *early, attn_part, attn_other,
    )
    (activations,) = call(
        partial(activation_out_kernel, micro, sub),
        [sds((1, micro, 1, local, width), BF16)],
        where, Raw(first_rows), Raw(last_rows),
        scratch=[pltpu.SemaphoreType.DMA((micro,))],
    )
    back_rows[0], expand_out, contract_out, projections_out, activations = together(
        back_rows[0], expand_out, contract_out, projections_out, activations
    )
    (input_grads,) = call(
        place_out_kernel, [sds((1, micro, 1, local, width), F32)], where, *back_rows
    )
    return (
        activations,
        input_grads,
        projections_out,
        pairs_out.transpose(0, 2, 1, 3),
        output_out,
        expand_out,
        units_out.transpose(1, 0, 2),
        contract_out.transpose(0, 2, 1),
        gains_out,
        biases_out,
    )


def split_pack(pack, relative, across):
    if relative:
        weights, small = (pack[0, :-16], pack[0, -16:])
        weights = weights.reshape(across, -1, weights.shape[1])
        small = jnp.broadcast_to(small, (across,) + small.shape)
        return jnp.concatenate([weights, small], axis=1)
    weights = pack[:, 0, :-16].reshape(-1, pack.shape[3])
    weights = weights.reshape(across, 2, -1, pack.shape[3]).transpose(1, 0, 2, 3)
    small = jnp.broadcast_to(pack[0, 0, -16:], (2, across, 16, pack.shape[3]))
    return jnp.concatenate([weights, small], axis=2)


def solution(mesh):
    in_specs = (
        P(None, None, ("dp", "tensor"), None),
        P(None, None, ("dp", "tensor"), None),
        P(),
        P("section", "tensor", None, None),
        P("section", None, "dp", "tensor"),
        P("section", None, "tensor", "dp"),
        P("section", "tensor", "dp"),
        P("section", "dp", "tensor"),
        P("section", "tensor", "dp"),
        P("section", "tensor", "dp"),
        P("section", None, "dp"),
        P("section", None, "dp"),
    )
    out_specs = (
        P("section", None, None, ("dp", "tensor"), None),
        P("section", None, None, ("dp", "tensor"), None),
        P("section", None, "dp", "tensor"),
        P("section", None, "tensor", "dp"),
        P("section", "tensor", "dp"),
        P("section", "dp", "tensor"),
        P("section", "tensor", "dp"),
        P("section", "tensor", "dp"),
        P("section", None, "dp"),
        P("section", None, "dp"),
    )
    return jax.shard_map(body, mesh=mesh, in_specs=in_specs, out_specs=out_specs, check_vma=False)
```

```python
import math
from functools import partial

import jax
import jax.numpy as jnp
from jax import lax
from jax.experimental import pallas as pl
from jax.experimental.pallas import tpu as pltpu
from jax.sharding import PartitionSpec as P

HD = 64
BLOCK = 64
GLOBAL = 2
EPSILON = 1e-12
MASKED = -1e30
GELU_A = 0.7978845608028654
GELU_B = 0.044715
F32 = jnp.float32
BF16 = jnp.bfloat16
MIB = 1 << 20
PLACES = ("section", "dp")


def nt(a, b):
    return lax.dot_general(a, b, (((1,), (1,)), ((), ())), preferred_element_type=F32)


def tn(a, b):
    return lax.dot_general(a, b, (((0,), (0,)), ((), ())), preferred_element_type=F32)


def nn(a, b):
    return jnp.dot(a, b, preferred_element_type=F32)


def sds(shape, dtype):
    return jax.ShapeDtypeStruct(shape, dtype)


class Far:
    def __init__(self, array, shape=None, cuts=None, plain=False, into=None, parts=1):
        self.array = array
        self.shape = array.shape if shape is None else shape
        self.cuts = [((), ())] if cuts is None else cuts
        self.plain = plain
        self.into = into
        self.parts = parts


class Raw:
    def __init__(self, array):
        self.array = array


def at(ref, index):
    return ref.at[index] if index else ref


class Arriving:
    def __init__(self, source, buffer, sems, first, cuts):
        self.buffer = buffer
        self.shape = buffer.shape
        self.copies = [
            pltpu.make_async_copy(at(source, a), at(buffer, b), sems.at[first + i])
            for i, (a, b) in enumerate(cuts)
        ]
        for copy in self.copies:
            copy.start()
        self.there = False

    def settle(self):
        if not self.there:
            for copy in self.copies:
                copy.wait()
            self.there = True

    def __getitem__(self, index):
        self.settle()
        return self.buffer[index]


class Leaving:
    def __init__(self, target, buffer, sems, first):
        self.target = target
        self.buffer = buffer
        self.shape = target.shape
        self.sems = sems
        self.first = first
        self.copies = []

    def __setitem__(self, index, value):
        self.buffer[index] = value

    def send(self, source=None, rows=None):
        target = self.target if rows is None else self.target.at[rows]
        if source is None:
            source = self.buffer if rows is None else self.buffer.at[rows]
        copy = pltpu.make_async_copy(source, target, self.sems.at[self.first + len(self.copies)])
        copy.start()
        self.copies.append(copy)

    def finish(self):
        if not self.copies:
            self.send()
        for copy in self.copies:
            copy.wait()


def flat(groups):
    return [item for group in groups for item in (group if isinstance(group, list) else [group])]


def grouped(items, groups):
    items = iter(items)
    return [
        [next(items) for _ in group] if isinstance(group, list) else next(items)
        for group in groups
    ]


def call(kernel, out_groups, *arg_groups, flops=0, limit=16, scratch=()):
    args = flat(arg_groups)
    outs = flat(out_groups)
    arrays = []
    in_specs = []
    out_specs = []
    out_shapes = []
    buffers = []
    size = 0
    semaphores = 0
    for arg in args:
        if isinstance(arg, Raw):
            arrays.append(pltpu.with_memory_space_constraint(arg.array, pltpu.HBM))
            in_specs.append(pl.BlockSpec(memory_space=pltpu.HBM))
        elif isinstance(arg, Far):
            arrays.append(pltpu.with_memory_space_constraint(arg.array, pltpu.HBM))
            in_specs.append(pl.BlockSpec(memory_space=pltpu.HBM))
            if arg.into is None:
                buffers.append(pltpu.VMEM(arg.shape, arg.array.dtype))
            semaphores += len(arg.cuts)
            size += math.prod(arg.shape) * arg.array.dtype.itemsize
        else:
            arrays.append(arg)
            scalar = arg.dtype == jnp.int32
            in_specs.append(pl.BlockSpec(memory_space=pltpu.SMEM if scalar else pltpu.VMEM))
            size += arg.size * arg.dtype.itemsize
    for out in outs:
        if isinstance(out, Raw):
            out_shapes.append(pltpu.HBM(out.array.shape, out.array.dtype))
            out_specs.append(pl.BlockSpec(memory_space=pltpu.HBM))
        elif isinstance(out, Far):
            out_shapes.append(pltpu.HBM(out.shape, out.array.dtype))
            out_specs.append(pl.BlockSpec(memory_space=pltpu.HBM))
            if not out.plain:
                buffers.append(pltpu.VMEM(out.shape, out.array.dtype))
            semaphores += out.parts
            size += math.prod(out.shape) * out.array.dtype.itemsize
        else:
            out_shapes.append(out)
            out_specs.append(pl.BlockSpec(memory_space=pltpu.VMEM))
            size += out.size * out.dtype.itemsize

    def whole(*refs):
        refs = list(refs)
        ins = refs[: len(args)]
        results = refs[len(args) : len(args) + len(outs)]
        rest = refs[len(args) + len(outs) :]
        sems = rest.pop() if semaphores else None
        given = []
        handed = []
        used = 0
        for arg, ref in zip(args, ins):
            if isinstance(arg, Far):
                buffer = rest.pop(0) if arg.into is None else results[arg.into]
                given.append(Arriving(ref, buffer, sems, used, arg.cuts))
                used += len(arg.cuts)
            else:
                given.append(ref)
        leaving = []
        for out, ref in zip(outs, results):
            if isinstance(out, Far):
                buffer = None if out.plain else rest.pop(0)
                leaving.append(Leaving(ref, buffer, sems, used))
                handed.append(leaving[-1])
                used += out.parts
            else:
                handed.append(ref)
        kernel(*grouped(given, arg_groups), *grouped(handed, out_groups), *rest)
        for item in given:
            if isinstance(item, Arriving):
                item.settle()
        for item in leaving:
            item.finish()

    scratch_shapes = buffers + list(scratch)
    if semaphores:
        scratch_shapes = scratch_shapes + [pltpu.SemaphoreType.DMA((semaphores,))]
    results = pl.pallas_call(
        whole,
        out_shape=tuple(out_shapes),
        in_specs=in_specs,
        out_specs=tuple(out_specs),
        scratch_shapes=scratch_shapes,
        compiler_params=pltpu.CompilerParams(vmem_limit_bytes=limit * MIB),
        cost_estimate=pl.CostEstimate(flops=flops, bytes_accessed=size, transcendentals=0),
    )(*arrays)
    return grouped(results, out_groups)


SECTION, PLACE, PLANE, SEAT, START, LENGTH, FLIP = range(7)


def positions(where_ref, count, ways, local):
    row = lax.broadcasted_iota(jnp.int32, (count, 1), 0)
    group = jnp.bitwise_xor(row // local % 2, where_ref[FLIP])
    seat = jnp.bitwise_xor(row // (2 * local), where_ref[SEAT])
    return where_ref[START] + group * (ways * local) + seat * local + row % local


def row_halves(rows):
    return [slice(begin, begin + rows // 2) for begin in (0, rows // 2)]


def send_parts(outs, whole, half):
    count = len(outs) // 2
    mine = whole.shape[0] // len(outs)
    for k in range(half * count, (half + 1) * count):
        if isinstance(outs[k], Leaving):
            outs[k].send(whole.at[pl.ds(k * mine, mine)])
        else:
            outs[k][...] = whole[k * mine : (k + 1) * mine]


def joined(refs):
    return jnp.concatenate([ref[...] for ref in refs], axis=0)


def keep(out, refs):
    size = refs[0].shape[0]
    for k, ref in enumerate(refs):
        out.send(ref, pl.ds(k * size, size))


def core_is(where_ref, core):
    return pl.when(where_ref[SECTION] == core)


def prepare_kernel(
    where_ref, projections_ref, output_ref, expand_ref, contract_ref, pair_ref, unit_ref,
    gain_ref, bias_ref, attn_keep, attn_send, keep_out, send_out, whole, small
):
    step, e = projections_ref.shape[2:]
    heads, _, c = pair_ref.shape[1:]
    half = step // 2
    whole[:, :e] = projections_ref[0, 0]
    whole[:, e : 2 * e] = projections_ref[0, 2]
    whole[:, 2 * e : 3 * e] = projections_ref[0, 1]
    whole[:, 3 * e :] = output_ref[0].T
    small[...] = jnp.zeros_like(small)
    small[0:2, :step] = gain_ref[0].astype(F32)
    small[2:6, :step] = bias_ref[0].astype(F32)
    small[: unit_ref.shape[1], 256 : 256 + c] = unit_ref[0].astype(F32)
    for i in range(heads):
        small[i : i + 1, 384 : 384 + c] = pair_ref[0, i, 0:1].astype(F32)
        small[i : i + 1, 512 : 512 + c] = pair_ref[0, i, 1:2].astype(F32)
    attn_keep[half:] = small[...].astype(BF16)
    attn_send[half:] = small[...].astype(BF16)
    expand = expand_ref[0]
    contract = contract_ref[0]

    @core_is(where_ref, 0)
    def _():
        attn_keep[:half] = whole[:half]
        attn_send[:half] = whole[half:]
        keep_out[...] = expand
        send_out[...] = contract

    @core_is(where_ref, 1)
    def _():
        attn_keep[:half] = whole[half:]
        attn_send[:half] = whole[:half]
        keep_out[...] = contract
        send_out[...] = expand


def unpack(c, e, raw_ref, vec_ref):
    places = raw_ref.shape[0]
    width = vec_ref.shape[1]
    w = width // places

    def of_heads(rows, lanes, z):
        source = lax.broadcasted_iota(jnp.int32, (128, lanes), 0)
        target = lax.broadcasted_iota(jnp.int32, (128, lanes), 1)
        repeat = ((target % c == source) & (source < c)).astype(F32).astype(BF16)
        spread_rows = nn(rows, repeat)
        head = lax.broadcasted_iota(jnp.int32, spread_rows.shape, 0)
        lane = lax.broadcasted_iota(jnp.int32, spread_rows.shape, 1)
        keep = (lane // HD == head) & (lane % HD // c == z)
        return jnp.sum(jnp.where(keep, spread_rows, 0.0), axis=0, keepdims=True)

    norms = jnp.zeros((16, width), F32)
    units = jnp.zeros((1, width), F32)
    queries = jnp.zeros((1, 256), F32)
    values = jnp.zeros((1, 256), F32)
    for z in range(places):
        rows = raw_ref[z]
        source = lax.broadcasted_iota(jnp.int32, (256, width), 0)
        target = lax.broadcasted_iota(jnp.int32, (256, width), 1)
        move = ((target == source + z * w) & (source < w)).astype(F32).astype(BF16)
        norms = norms + nn(rows[:, :256], move)
        units = units + of_heads(rows[:, 256:384], width, z)
        queries = queries + of_heads(rows[:, 384:512], 256, z)
        values = values + of_heads(rows[:, 512:640], 256, z)
    vec_ref[...] = norms[:8]
    vec_ref[6:7] = units
    lane = lax.broadcasted_iota(jnp.int32, (1, 256), 1)
    queries = jnp.where(lane < e, queries, 0.0)
    values = jnp.where(lane < e, values, 0.0)
    return (queries, pltpu.roll(values, 256 - e, 1))


def qkv_kernel(
    ways, local, blocks, c, e, where_ref, x_refs, raw_ref, w_ref, q_ref, kv_ref, vec_ref, *kept
):
    kw = q_ref.shape[1]
    vw = kv_ref.shape[1] - kw
    x = joined(x_refs)
    keep(kept[0], x_refs)
    query_bias, value_bias = unpack(c, e, raw_ref, vec_ref)
    lead = 2 * e // 128 * 128
    q = (nn(x, w_ref[:, :256]) + query_bias).astype(BF16).astype(F32) * HD ** (-0.5)
    lane = lax.broadcasted_iota(jnp.int32, (1, 256), 1)
    q = jnp.where(lane < e, q, 0.0).astype(BF16)
    q_ref[:, :256] = q
    if kw > 256:
        q_ref[:, 256:] = jnp.zeros((q.shape[0], kw - 256), BF16)
    kept[1].send(q_ref)
    position = positions(where_ref, x.shape[0], ways, local)
    block = position // BLOCK
    lane = lax.broadcasted_iota(jnp.int32, (1, kw), 1)
    hidden = (position >= where_ref[LENGTH]) & (lane == e + blocks)
    tail = jnp.where(lane == e + block, 1.0, jnp.where(hidden, MASKED, 0.0))
    k = nn(x, w_ref[:, lead : lead + 256])
    if kw > 256:
        k = jnp.concatenate([k, jnp.zeros((k.shape[0], kw - 256), F32)], axis=1)
    kv_ref[:, :kw] = jnp.where(lane < e, k, tail).astype(BF16)
    kv_ref[:, kw:] = (nn(x, w_ref[:, 128 : 128 + vw]) + value_bias).astype(BF16)
    kept[2].send(kv_ref)


def head_mask(first, lanes):
    lane = lax.broadcasted_iota(jnp.int32, (1, lanes), 1)
    return ((lane >= first) & (lane < first + HD)).astype(F32)


def seen_rows(where_ref, random_refs, layer, h, rows, ways, local, kw, e, blocks):
    lane = lax.broadcasted_iota(jnp.int32, (1, kw), 1)
    key = lane - e
    parts = []
    for g in range(rows // local):
        group = jnp.bitwise_xor(g % 2, where_ref[FLIP])
        seat = jnp.bitwise_xor(g // 2, where_ref[SEAT])
        position = where_ref[START] + group * (ways * local) + seat * local
        block = position // BLOCK
        seen = (key < GLOBAL) | (jnp.abs(key - block) <= 1) | (block < GLOBAL)
        for i in range(random_refs[0].shape[3]):
            picked = [ref[0, h, block, i] for ref in random_refs]
            seen = seen | (key == jnp.where(where_ref[SECTION] == layer, *picked))
        hidden = (key >= 0) & (key < blocks) & jnp.logical_not(seen)
        line = jnp.where(key == blocks, 1.0, jnp.where(hidden, MASKED, 0.0))
        parts.append(jnp.broadcast_to(line, (local, kw)))
    return jnp.concatenate(parts, axis=0)


def attention_kernel(
    heads, layer, ways, local, blocks, chunk, where_ref, random_refs, q_ref, w_ref, parts,
    outs, mixed_out, total_out, kept, whole
):
    rows, kw = q_ref.shape
    e = heads * HD
    vw = parts[0].shape[1] - kw
    shift = vw - e
    for out, part in zip(kept, parts[1:]):
        out.send(part)
    k = jnp.concatenate([part[:, :kw] for part in parts], axis=0)
    vt = jnp.concatenate([part[:, kw:] for part in parts], axis=0).T
    q = q_ref[...].astype(F32)
    lines = [jnp.zeros((shift, rows), F32)]
    totals = []
    for h in range(heads):
        seen = seen_rows(where_ref, random_refs, layer, h, rows, ways, local, kw, e, blocks)
        qa = (q * head_mask(h * HD, kw) + seen).astype(BF16)
        vh = vt[shift + h * HD : shift + (h + 1) * HD]
        cells = []
        sums = []
        for c in range(0, rows, chunk):
            scores = nt(k, qa[c : c + chunk])
            top = jnp.max(scores, axis=0, keepdims=True)
            p = jnp.exp(scores - top)
            total = jnp.sum(p, axis=0, keepdims=True)
            cells.append(nn(vh, p.astype(BF16)) / total)
            sums.append(top + jnp.log(total))
        lines.append(jnp.concatenate(cells, axis=1))
        totals.append(jnp.concatenate(sums, axis=1))
    total_out[...] = jnp.concatenate(totals + [jnp.zeros((8 - heads, rows), F32)], axis=0)
    total_out.send()
    mixed = jnp.concatenate(lines, axis=0).T.astype(BF16)
    mixed_out[...] = mixed
    mixed_out.send()
    for half, part in enumerate(row_halves(rows)):
        whole[part] = nt(mixed[part], w_ref[...]).astype(BF16)
        send_parts(outs, whole, half)


def attention_back_kernel(
    heads, layer, ways, local, blocks, chunk, where_ref, random_refs, grad_refs, w_ref, mixed_ref,
    q_ref, total_ref, parts, dq_ref, small_ref, outs
):
    rows, kw = q_ref.shape
    e = heads * HD
    vw = mixed_ref.shape[1]
    shift = vw - e
    grad = jnp.concatenate([ref[: 2 * local] for ref in grad_refs], axis=0)
    small_ref[...] = total_of([ref.at[2 * local :] for ref in grad_refs])
    mixed_grad = nn(grad, w_ref[:, w_ref.shape[1] - vw :]).astype(BF16).astype(F32)
    product = mixed_grad * mixed_ref[...].astype(F32)
    masks = jnp.concatenate([head_mask(shift + h * HD, vw) for h in range(8)], axis=0)
    inner = lax.dot_general(
        masks, product, (((1,), (1,)), ((), ())),
        preferred_element_type=F32, precision=lax.Precision.HIGHEST,
    )
    q = q_ref[...].astype(F32)
    k = jnp.concatenate([part[:, :kw] for part in parts], axis=0)
    v = jnp.concatenate([part[:, kw:] for part in parts], axis=0)
    kt = k[:, :256].T
    totals = total_ref[...]
    dk = None
    dv = None
    lines = []
    for h in range(heads):
        seen = seen_rows(where_ref, random_refs, layer, h, rows, ways, local, kw, e, blocks)
        qm = q * head_mask(h * HD, kw)
        qa = (qm + seen).astype(BF16)
        qm = qm[:, :256].astype(BF16)
        gm = (mixed_grad * head_mask(shift + h * HD, vw)).astype(BF16)
        kh = kt[h * HD : (h + 1) * HD]
        cells = []
        for c in range(0, rows, chunk):
            scores = nt(k, qa[c : c + chunk])
            p = jnp.exp(scores - totals[h : h + 1, c : c + chunk])
            dp = nt(v, gm[c : c + chunk])
            ds = (p * (dp - inner[h : h + 1, c : c + chunk])).astype(BF16)
            dv_term = nn(p.astype(BF16), gm[c : c + chunk])
            dk_term = nn(ds, qm[c : c + chunk])
            dv = dv_term if dv is None else dv + dv_term
            dk = dk_term if dk is None else dk + dk_term
            cells.append(nn(kh, ds))
        lines.append(jnp.concatenate(cells, axis=1))
    lines.append(jnp.zeros((256 - e, rows), F32))
    dq = jnp.concatenate(lines, axis=0).T * HD ** (-0.5)
    dq_ref[...] = dq.astype(BF16)
    start = 0
    for out in outs:
        size = out.shape[0]
        out[:, :256] = dk[start : start + size].astype(BF16)
        out[:, 256:] = dv[start : start + size].astype(BF16)
        start += size


def projection_back_kernel(
    e, dq_ref, own_ref, other_ref, w_ref, triple_ref, sums_ref, outs, whole
):
    vw = own_ref.shape[1] - 256
    width = w_ref.shape[1]
    lead = 2 * e // 128 * 128
    rows = dq_ref.shape[0]
    dq = dq_ref[...]
    dkv = (own_ref[...].astype(F32) + other_ref[...].astype(F32)).astype(BF16).astype(F32)
    dv = dkv[:, 256:]
    head = dq.astype(F32)
    nothing = jnp.zeros((rows, 128), F32)
    triple = jnp.concatenate(
        [head[:, :128], head[:, 128:] + dv[:, :128], dv[:, 128:], dkv[:, :256], nothing], axis=1
    ).astype(BF16)
    triple_ref[...] = triple
    sums_ref[...] = jnp.zeros_like(sums_ref)
    sums_ref[0:1] = jnp.sum(triple.astype(F32), axis=0, keepdims=True)
    for half, part in enumerate(row_halves(rows)):
        whole[part] = nt(triple[part], w_ref[...]).astype(BF16)
        send_parts(outs, whole, half)


def norm(values):
    average = jnp.mean(values, axis=-1, keepdims=True)
    centered = values - average
    spread_now = jnp.mean(centered * centered, axis=-1, keepdims=True)
    inverse = lax.rsqrt(spread_now + EPSILON)
    return (centered * inverse, inverse)


def total_of(terms):
    total = terms[0][...].astype(F32)
    for term in terms[1:]:
        total = total + term[...].astype(F32)
    return total


def first_norm_kernel(x_ref, terms_ref, vec_ref, middle_ref, low_ref, unit_out, inverse_out):
    values = x_ref[...].astype(F32) + total_of(terms_ref) + vec_ref[2:3]
    unit, inverse = norm(values)
    unit_out[...] = unit
    unit_out.send()
    inverse_out[...] = jnp.broadcast_to(inverse, inverse_out.shape)
    inverse_out.send()
    middle = unit * vec_ref[0:1] + vec_ref[4:5]
    middle_ref[...] = middle
    low_ref[...] = middle.astype(BF16)


def valid_rows(where_ref, ways, local):
    position = positions(where_ref, 2 * local, ways, local)
    return (position < where_ref[LENGTH]).astype(F32)


def place_parts(where_ref, early, later, outs):
    half = early.shape[0] // 2
    late_plane = where_ref[PLANE] // 2
    for u in range(2):
        for p in range(2):
            @pl.when(late_plane == u)
            def _(u=u, p=p):
                outs[2 * p + u][...] = early[p * half : (p + 1) * half]

            @pl.when(late_plane != u)
            def _(u=u, p=p):
                outs[2 * p + u][...] = later[p * half : (p + 1) * half]


def norm_back(grad, unit, inverse, gain):
    scaled = grad * gain
    return inverse * (
        scaled
        - jnp.mean(scaled, axis=-1, keepdims=True)
        - unit * jnp.mean(scaled * unit, axis=-1, keepdims=True)
    )


def second_norm(ways, where_ref, middle_ref, terms_ref, vec_ref):
    unit, inverse = norm(middle_ref[...] + total_of(terms_ref) + vec_ref[3:4])
    result = unit * vec_ref[1:2] + vec_ref[5:6]
    valid = valid_rows(where_ref, ways, unit.shape[0] // 2)
    return ((result * valid).astype(BF16), unit, inverse, valid)


def second_back(grad, unit, inverse, vec_ref, second_ref, low_ref, sums_ref):
    second = norm_back(grad, unit, inverse, vec_ref[1:2])
    low_ref[...] = second.astype(BF16)
    second_ref[...] = second
    second_ref.send()
    sums_ref[...] = jnp.zeros_like(sums_ref)
    sums_ref[0:1] = jnp.sum(grad * unit, axis=0, keepdims=True)
    sums_ref[1:2] = jnp.sum(grad, axis=0, keepdims=True)
    sums_ref[2:3] = jnp.sum(second, axis=0, keepdims=True)


def second_norm_kernel(
    ways, where_ref, middle_ref, terms_ref, vec_ref, low_ref, kept, unit_out, inverse_out
):
    low, unit, inverse, _ = second_norm(ways, where_ref, middle_ref, terms_ref, vec_ref)
    low_ref[...] = low
    kept.send(low_ref)
    unit_out[...] = unit
    unit_out.send()
    inverse_out[...] = jnp.broadcast_to(inverse, inverse_out.shape)
    inverse_out.send()


def turn_kernel(
    ways, where_ref, middle_ref, terms_ref, vec_ref, up_ref, _, second_ref, low_ref, sums_ref,
    ahead, kept
):
    low, unit, inverse, valid = second_norm(ways, where_ref, middle_ref, terms_ref, vec_ref)
    kept[...] = low
    kept.send()
    second_back(
        up_ref[...].astype(F32) * valid, unit, inverse, vec_ref, second_ref, low_ref, sums_ref
    )


def between_kernel(
    ways, where_ref, terms_ref, vec_ref, first_ref, unit_ref, inverse_ref, _, second_ref, low_ref,
    sums_ref, ahead, kept
):
    low = (first_ref[...] + total_of(terms_ref)).astype(BF16)
    kept[...] = low
    kept.send()
    grad = low.astype(F32) * valid_rows(where_ref, ways, low.shape[0] // 2)
    second_back(
        grad, unit_ref[...], inverse_ref[:, 0:1], vec_ref, second_ref, low_ref, sums_ref
    )


def first_back_kernel(
    second_ref, terms_ref, vec_ref, before_ref, unit_ref, inverse_ref, _, first_ref, low_ref, ahead
):
    grad = second_ref[...] + total_of(terms_ref)
    unit = unit_ref[...]
    first = norm_back(grad, unit, inverse_ref[:, 0:1], vec_ref[0:1])
    first_ref[...] = first
    rows = first.shape[0]
    low_ref[:rows] = first.astype(BF16)
    before = before_ref[...]
    low_ref[rows:] = jnp.concatenate(
        [jnp.sum(grad * unit, axis=0, keepdims=True), before[0:1],
         jnp.sum(first, axis=0, keepdims=True), before[2:3],
         jnp.sum(grad, axis=0, keepdims=True), before[1:2],
         jnp.zeros((10, first.shape[1]), F32)], axis=0
    ).astype(BF16)


def last_input_kernel(where_ref, first_ref, later_ref, terms, *outs):
    low = (first_ref[...] + total_of(terms)).astype(BF16)
    place_parts(where_ref, low, later_ref[...], outs)


def place_out_kernel(where_ref, *refs):
    parts, out_ref = (refs[:-1], refs[-1])
    odd = where_ref[PLACE] % 2
    for p in range(2):
        for u in range(2):
            m = 2 * jnp.bitwise_xor(where_ref[SECTION], u) + jnp.bitwise_xor(odd, p)
            out_ref[0, m, 0] = parts[2 * p + u][...].astype(F32)


def activation_out_kernel(micro, sub, where_ref, first_ref, last_ref, out_ref, sems):
    local = out_ref.shape[3]
    place = where_ref[PLACE]
    side = place % micro // 2

    def copies(ref):
        result = []
        for m in range(micro):
            source = side * (micro * sub) + m * sub + place // micro
            row = (2 * source + jnp.bitwise_xor(place % 2, m & 1)) * local
            rows = pl.ds(pl.multiple_of(row, local), local)
            result.append(pltpu.make_async_copy(ref.at[rows], out_ref.at[0, m, 0], sems.at[m]))
        return result

    for core, ref in enumerate((first_ref, last_ref)):
        @core_is(where_ref, core)
        def _(ref=ref):
            for copy in copies(ref):
                copy.start()
            for copy in copies(ref):
                copy.wait()


def feed_kernel(
    x_refs, vec_ref, expand_ref, contract_ref, outs, active_out, slope_out, kept, whole
):
    keep(kept, x_refs)
    parts = row_halves(whole.shape[0])
    values = [nn(joined(refs), expand_ref[...]) + vec_ref[6:7] for refs in (x_refs[:2], x_refs[2:])]
    for half, (part, v) in enumerate(zip(parts, values)):
        th = jnp.tanh(v * (GELU_A + GELU_A * GELU_B * (v * v)))
        upper = 0.5 + 0.5 * th
        active = (v * upper).astype(BF16)
        active_out[part] = active
        active_out.send(rows=part)
        slope = upper + v * (1.0 - th * th) * (0.5 * GELU_A + 1.5 * GELU_A * GELU_B * (v * v))
        slope_out[part] = slope.astype(BF16)
        slope_out.send(rows=part)
        whole[part] = nt(active, contract_ref[...]).astype(BF16)
        send_parts(outs, whole, half)


def feed_back_kernel(
    grad_refs, contract_ref, slope_ref, expand_ref, hidden_ref, outs, sums_ref, whole
):
    parts = row_halves(whole.shape[0])
    values = [nn(joined(refs), contract_ref[...]) for refs in (grad_refs[:2], grad_refs[2:])]
    total = jnp.zeros((1, hidden_ref.shape[1]), F32)
    for half, (part, value) in enumerate(zip(parts, values)):
        hidden = (value * slope_ref[part].astype(F32)).astype(BF16)
        hidden_ref[part] = hidden
        hidden_ref.send(rows=part)
        total = total + jnp.sum(hidden.astype(F32), axis=0, keepdims=True)
        whole[part] = nt(hidden, expand_ref[...]).astype(BF16)
        send_parts(outs, whole, half)
    sums_ref[...] = jnp.zeros_like(sums_ref)
    sums_ref[0:1] = total


def feed_pack_kernel(where_ref, hidden_ref, grad_refs, middle_ref, active_ref, *outs):
    expand = tn(middle_ref[...], hidden_ref[...]).astype(BF16)
    contract = tn(joined(grad_refs), active_ref[...]).astype(BF16)

    @core_is(where_ref, 0)
    def _():
        outs[0][...] = expand
        outs[1][...] = contract

    @core_is(where_ref, 1)
    def _():
        outs[0][...] = contract
        outs[1][...] = expand


def attn_pack_kernel(
    relative, step, e, where_ref, triple_ref, grad_refs, norm_ref, unit_ref, pair_ref, x_ref,
    mixed_ref, out_ref
):
    x = x_ref[...]
    width = x.shape[1]
    vw = mixed_ref.shape[1]
    places = width // step
    mine = grad_refs[0].shape[0] - 16
    grad = jnp.concatenate([ref[:mine] for ref in grad_refs], axis=0)
    total = tn(x, triple_ref[...])
    last = total[:, width - vw :] + tn(grad, mixed_ref[...])
    weights = jnp.concatenate([total[:, : width - vw], last], axis=1).astype(BF16)
    small = jnp.concatenate(
        [norm_ref[:6], unit_ref[0:1], pair_ref[0:1], jnp.zeros((8, width), F32)], axis=0
    ).astype(BF16)
    for z in range(places):
        begin = z * step
        if relative:
            k = jnp.bitwise_xor(where_ref[PLACE], z) if places > 1 else 0
            out_ref[k, :step] = weights[begin : begin + step]
            out_ref[k, step:] = small
        else:
            half = step // 2
            for i in range(2):
                out_ref[i, z, :half] = weights[begin + i * half : begin + (i + 1) * half]
                out_ref[i, z, half:] = small


def pair_sum_kernel(mine_ref, other_ref, own_ref, *sent_refs):
    own_ref[...] = mine_ref[0].astype(F32) + other_ref[0].astype(F32)
    for k, sent in enumerate(sent_refs):
        sent[...] = (
            mine_ref[k + 1].astype(F32) + other_ref[k + 1].astype(F32)
        ).astype(BF16)


def attn_out_kernel(
    step, e, c, where_ref, *refs
):
    early, (mine_ref, other_ref), outs = (refs[:-8], refs[-8:-6], refs[-6:])
    projections_ref, output_ref, gain_ref, bias_ref, unit_ref, pair_ref = outs
    width = mine_ref.shape[1]

    def fill(total):
        weights = total[:step]
        small = total[step : step + 8]
        projections_ref[0, 0] = weights[:, :e]
        projections_ref[0, 1] = weights[:, 2 * e : 3 * e]
        projections_ref[0, 2] = pltpu.roll(weights, width - e, 1)[:, :e]
        output_ref[0] = pltpu.roll(weights, e, 1)[:, :e].T
        mine = pltpu.roll(small, lax.rem(width - where_ref[PLACE] * step, width), 1)
        gain_ref[0] = mine[0:2, :step]
        bias_ref[0] = mine[2:6, :step]

        def column(row, head):
            shift = lax.rem(2 * width - head * HD - where_ref[PLACE] * c, width)
            return pltpu.roll(small, shift, 1)[row : row + 1, :c]

        for head in range(unit_ref.shape[0]):
            unit_ref[head] = column(6, head)
        for head in range(pair_ref.shape[1]):
            pair_ref[0, head, 0:1] = column(7, head)
            pair_ref[0, head, 1:2] = column(7, head + e // HD)

    @core_is(where_ref, 0)
    def _():
        total = early[0][...]
        for term in early[1:]:
            total = total + term[...].astype(F32)
        fill(total)

    @core_is(where_ref, 1)
    def _():
        mine = mine_ref[...].astype(F32)
        other = other_ref[...].astype(F32)
        fill(jnp.concatenate([other[: step // 2], mine], axis=0))


def feed_out_kernel(where_ref, first_ref, second_ref, other_ref, expand_ref, contract_ref):
    @core_is(where_ref, 0)
    def _():
        expand_ref[0] = first_ref[...].astype(F32)
        contract_ref[0] = other_ref[...].astype(F32)

    @core_is(where_ref, 1)
    def _():
        expand_ref[0] = other_ref[...].astype(F32)
        contract_ref[0] = second_ref[...].astype(F32)


def swap(x):
    return lax.ppermute(x, "section", [(0, 1), (1, 0)])


def gather_rows(x):
    seats = range(lax.axis_size("tensor"))
    return [x] + [lax.ppermute(x, "tensor", [(i, i ^ k) for i in seats]) for k in seats if k]


def scatter_rows(parts):
    seats = range(lax.axis_size("tensor"))
    return parts[:1] + [
        lax.ppermute(parts[k], "tensor", [(i, i ^ k) for i in seats]) for k in seats if k
    ]


def deal(x, micro, sub):
    section = lax.axis_index("section")
    across = lax.axis_size("dp")
    odd = lax.axis_index("dp") % 2
    got = []
    for p in range(2):
        route = []
        for c in range(2):
            for d in range(across):
                r, dd = (d // micro, d % micro)
                m = 2 * c + (p ^ (dd & 1))
                route.append((c * across + d, (dd >> 1) * across + m * sub + r))
        chosen = 2 * section + (p ^ odd)
        payload = lax.dynamic_index_in_dim(x, chosen, 0, keepdims=False)
        got.append(lax.ppermute(payload, PLACES, route))
    return got


def undeal(parts, micro, sub):
    across = lax.axis_size("dp")
    got = []
    for p in range(2):
        for u in range(2):
            route = []
            for s in range(2):
                for source in range(across):
                    m, r = (source // sub, source % sub)
                    j = p ^ (m & 1)
                    layer = u ^ (m >> 1)
                    route.append((s * across + source, layer * across + r * micro + 2 * s + j))
            got.append(lax.ppermute(parts[2 * p + u], PLACES, route))
    return got


def across_layer(x, layer, k):
    across = lax.axis_size("dp")
    route = [(layer * across + d, layer * across + (d ^ k)) for d in range(across)]
    return lax.ppermute(x, PLACES, route)


def together(*values):
    return lax.optimization_barrier(values)


def after(x, token):
    return lax.optimization_barrier((x, token))[0]


def body(
    tokens,
    cotangent,
    lengths,
    random_blocks,
    projections,
    query_value_bias,
    output_weight,
    expand_weight,
    expand_bias,
    contract_weight,
    norm_gains,
    row_biases,
):
    section = lax.axis_index("section")
    place = lax.axis_index("dp")
    seat = lax.axis_index("tensor")
    across = lax.axis_size("dp")
    ways = lax.axis_size("tensor")
    micro = tokens.shape[0]
    sub = across // micro
    plane = place // sub
    share = place % sub
    local = tokens.shape[2]
    width = tokens.shape[3]
    e = projections.shape[3]
    heads = e // HD
    units = expand_weight.shape[2]
    step = projections.shape[2]
    c = query_value_bias.shape[3]
    mine = 2 * local
    rows = mine * ways
    keys = rows * 2 * sub
    blocks = keys // BLOCK
    kw = -(-(e + blocks + 1) // 128) * 128
    vw = 256
    whole_tiles = step % 32 == 0
    start = (share * micro + 2 * section) * ways * local
    length = lax.dynamic_index_in_dim(lengths[:, 0], plane, 0, keepdims=False)
    where = jnp.stack([section, place, plane, seat, start, length, plane % 2, 0]).astype(jnp.int32)
    random_other = swap(random_blocks)

    attn_keep, attn_send, feed_keep, feed_send = call(
        prepare_kernel,
        [sds((step // 2 + 16, 4 * e), BF16)] * 2 + [sds((step, units), BF16)] * 2,
        where, Far(projections), Far(output_weight), Far(expand_weight),
        Far(contract_weight.transpose(0, 2, 1)), Far(query_value_bias.transpose(0, 2, 1, 3)),
        Far(expand_bias), Far(norm_gains), Far(row_biases),
        scratch=[pltpu.VMEM((step, 4 * e), BF16), pltpu.VMEM((16, 4 * e), F32)],
    )
    x = deal(tokens[:, 0], micro, sub)
    upstream = deal(after(cotangent[:, 0], x[1]), micro, sub)
    x = jnp.concatenate(x, axis=0)
    feed_send, x = together(feed_send, x)
    attn_traded = swap(attn_send)
    feed_traded = swap(feed_send)
    attn_all = []
    feed_all = []
    for l in range(2):
        own = section == l
        whole = lax.all_gather(jnp.where(own, attn_keep, attn_traded), PLACES, axis=0, tiled=True)
        attn_all.append(whole.reshape(2, across, step // 2 + 16, 4 * e))
        whole = lax.all_gather(jnp.where(own, feed_keep, feed_traded), PLACES, axis=0, tiled=True)
        feed_all.append(whole.reshape(2, width, units))

    if not whole_tiles:
        attn_flat = [
            whole[:, :, : step // 2].transpose(1, 0, 2, 3).reshape(width, 4 * e)
            for whole in attn_all
        ]
    def small_rows(l):
        if not whole_tiles:
            return attn_all[l][0, :, step // 2 :]
        cuts = [((0, z, pl.ds(step // 2, 16)), (z,)) for z in range(across)]
        return Far(attn_all[l], (across, 16, 4 * e), cuts)

    def attn_weight(l, first, size, into=None):
        lanes = pl.ds(first, size)
        if not whole_tiles:
            return Far(attn_flat[l], (width, size), [((slice(None), lanes), ())], into=into)
        half = step // 2
        cuts = [
            ((i, z, pl.ds(0, half), lanes), (pl.ds(z * step + i * half, half),))
            for z in range(across)
            for i in range(2)
        ]
        return Far(attn_all[l], (width, size), cuts, into=into)

    def feed_weight(l, i, into=None):
        return Far(feed_all[l], (width, units), [((i,), ())], into=into)

    def all_parts(own):
        pair = [own, swap(own)]
        if sub == 1:
            return pair
        groups = [[m * sub + r for r in range(sub)] for m in range(micro)]
        return [
            lax.all_gather(
                jnp.concatenate(pair, axis=0), "dp", axis=0, tiled=True, axis_index_groups=groups
            )
        ]

    def own_parts(parts):
        if sub == 1:
            return parts
        groups = [[m * sub + r for r in range(sub)] for m in range(micro)]
        total = lax.psum_scatter(
            parts[0], "dp", scatter_dimension=0, tiled=True, axis_index_groups=groups
        )
        return [total[:rows], total[rows:]]

    chunk = min(rows, 512)
    near_rows = sds((mine, width), BF16)
    exchanged = [near_rows] + [Far(near_rows, plain=True)] * (ways - 1)
    exchanged_back = [Far(near_rows, plain=True)] * ways
    whole = pltpu.VMEM((rows, width), BF16)
    near_f32 = sds((mine, width), F32)
    turn_outs = [Far(near_f32), near_rows, sds((8, width), F32), sds((width, units), BF16)]
    far_unit = [Far(sds((mine, width), F32)), Far(sds((mine, 128), F32))]

    saved = []
    vectors = []
    for l in range(2):
        x_all = gather_rows(x)
        if l == 0:
            x_all[0], *upstream = together(x_all[0], *upstream)
            upstream = jnp.concatenate(upstream, axis=0)
        q, kv, vec, x_kept, q_kept, kv_kept = call(
            partial(qkv_kernel, ways, local, blocks, c, e),
            [sds((rows, kw), BF16), sds((rows, kw + vw), BF16), sds((8, width), F32),
             Far(sds((rows, width), BF16), plain=True, parts=ways),
             Far(sds((rows, kw), BF16), plain=True),
             Far(sds((rows, kw + vw), BF16), plain=True)],
            where, x_all, small_rows(l), attn_weight(l, 0, 4 * e),
            flops=6 * rows * width * 256,
        )
        vectors.append(vec)
        parts = all_parts(kv)
        attended, mixed, totals, others = call(
            partial(attention_kernel, heads, l, ways, local, blocks, chunk),
            [exchanged, Far(sds((rows, vw), BF16)), Far(sds((8, rows), F32)),
             [Far(sds(part.shape, BF16), plain=True) for part in parts[1:]]],
            where, [random_blocks, random_other], q, attn_weight(l, 4 * e - vw, vw), parts,
            flops=4 * rows * keys * kw, limit=24, scratch=[whole],
        )
        parts_kept = [kv_kept, others[0]] if sub == 1 else parts
        terms = scatter_rows(attended)
        middle, middle_low, unit1, inverse1 = call(
            first_norm_kernel, [sds((mine, width), F32), near_rows] + far_unit, x, terms, vec
        )
        middle_all = gather_rows(middle_low)
        fed, active, slope, middle_kept = call(
            feed_kernel,
            [exchanged, Far(sds((rows, units), BF16), parts=2),
             Far(sds((rows, units), BF16), parts=2),
             Far(sds((rows, width), BF16), plain=True, parts=ways)],
            middle_all, vec, feed_weight(l, 0), feed_weight(l, 1),
            flops=4 * rows * width * units, scratch=[whole],
        )
        terms = scatter_rows(fed)
        if l == 0:
            x, low_kept, unit2, inverse2 = call(
                partial(second_norm_kernel, ways),
                [near_rows, Far(near_rows, plain=True)] + far_unit,
                where, middle, terms, vec,
            )
            first_rows = lax.all_gather(low_kept, PLACES, axis=0, tiled=True)
        else:
            second, feed_low, second_sums, contract_ahead, last_kept = call(
                partial(turn_kernel, ways), turn_outs + [Far(near_rows)],
                where, middle, terms, vec, upstream, feed_weight(1, 1, into=3),
            )
        saved.append(
            (x_kept, q_kept, parts_kept, mixed, totals, unit1, inverse1, middle_kept, active,
             slope)
        )
        if l == 0:
            norm_kept = (unit2, inverse2)
    last_rows = lax.all_gather(last_kept, PLACES, axis=0, tiled=True)
    feed_parts = [None, None]
    for l in (1, 0):
        vec = vectors[l]
        (x_kept, q_kept, parts_kept, mixed, totals, unit1, inverse1, middle_kept, active,
         slope) = saved[l]
        feed_grad = gather_rows(feed_low)
        if l == 1:
            feed_grad[0], first_rows = together(feed_grad[0], first_rows)
        hidden, fed_back, unit_sums = call(
            feed_back_kernel,
            [Far(sds((rows, units), BF16), parts=2), exchanged_back, sds((8, units), F32)],
            feed_grad, contract_ahead, Far(slope), feed_weight(l, 0),
            flops=4 * rows * width * units, scratch=[whole],
        )
        terms = scatter_rows(fed_back)
        feed_kept, feed_sent = call(
            feed_pack_kernel, [Far(sds((width, units), BF16))] * 2,
            where, Far(hidden), feed_grad, Far(middle_kept), Far(active),
            flops=4 * rows * width * units,
        )
        *terms, feed_sent = together(*terms, feed_sent)
        feed_half = (feed_kept.astype(F32) + swap(feed_sent).astype(F32)).astype(BF16)
        if l == 0:
            terms[0], feed_parts[1] = together(terms[0], feed_parts[1])
        terms[0] = Far(terms[0])
        first_grad, first_low, attn_ahead = call(
            first_back_kernel,
            [Far(near_f32), sds((mine + 16, width), BF16), sds((width, 4 * e), BF16)],
            Far(second), terms, vec, second_sums, Far(unit1), Far(inverse1),
            attn_weight(l, 0, 4 * e, into=2),
        )
        attended_grad = gather_rows(first_low)
        if l == 1:
            attended_grad[0], last_rows = together(attended_grad[0], last_rows)
        attended_grad[0], feed_half = together(attended_grad[0], feed_half)
        feed_parts[l] = lax.psum_scatter(feed_half, "dp", scatter_dimension=0, tiled=True)
        dq, norm_sums, dkv = call(
            partial(attention_back_kernel, heads, l, ways, local, blocks, chunk),
            [sds((rows, 256), BF16), sds((16, width), F32),
             [sds((part.shape[0], 256 + vw), BF16) for part in parts_kept]],
            where, [random_blocks, random_other], attended_grad, attn_ahead, Far(mixed),
            Far(q_kept), Far(totals), [Far(part) for part in parts_kept],
            flops=10 * rows * keys * kw, limit=44,
        )
        dkv_own, dkv_other = own_parts(dkv)
        dkv_traded = swap(dkv_other)
        triple, pair_sums, projected = call(
            partial(projection_back_kernel, e),
            [sds((rows, 4 * e), BF16), sds((8, 4 * e), F32), exchanged_back],
            dq, dkv_own, dkv_traded, attn_ahead,
            flops=6 * rows * width * 256, scratch=[whole],
        )
        terms = scatter_rows(projected)
        cut = step if whole_tiles else width
        pieces = width // cut
        pack_shape = (pieces, cut + 16, 4 * e) if l == 0 else (2, pieces, cut // 2 + 16, 4 * e)
        (pack,) = call(
            partial(attn_pack_kernel, l == 0, cut, e),
            [sds(pack_shape, BF16)],
            where, triple, attended_grad, norm_sums, unit_sums, pair_sums, Far(x_kept),
            Far(mixed),
            flops=8 * rows * width * 256,
        )
        if not whole_tiles:
            pack = split_pack(pack, l == 0, across)
        if l == 1:
            (activations,) = call(
                partial(activation_out_kernel, micro, sub),
                [sds((1, micro, 1, local, width), BF16)],
                where, Raw(first_rows), Raw(last_rows),
                scratch=[pltpu.SemaphoreType.DMA((micro,))],
            )
            *terms, pack, activations = together(*terms, pack, activations)
            attn_part = lax.psum_scatter(
                pack.reshape((-1,) + pack.shape[2:]), PLACES, scatter_dimension=0
            )
            terms[0] = Far(terms[0])
            second, feed_low, second_sums, contract_ahead, later = call(
                partial(between_kernel, ways),
                turn_outs + [Far(near_rows)],
                where, terms, vectors[0], Far(first_grad), Far(norm_kept[0]), Far(norm_kept[1]),
                feed_weight(0, 1, into=3),
            )
        else:
            traded = lax.ppermute(pack, "section", [(1, 0)])
            if whole_tiles:
                sums = call(
                    pair_sum_kernel,
                    [sds(pack.shape[1:], F32)] + [Far(sds(pack.shape[1:], BF16))] * (across - 1),
                    pack, traded,
                )
                terms[0], attn_part, *sums = together(terms[0], attn_part, *sums)
                early = [sums[0]] + [across_layer(sums[k], 0, k) for k in range(1, across)]
            else:
                total = (pack.astype(F32) + traded.astype(F32)).astype(BF16)
                early = [
                    lax.psum_scatter(total, "dp", scatter_dimension=0).astype(F32)
                ]
            terms[0] = Far(terms[0])
            places = call(
                last_input_kernel, [sds((local, width), BF16)] * 4,
                where, Far(first_grad), Far(later), terms,
            )
            back_rows = undeal(places, micro, sub)
            feed_parts = list(together(*feed_parts, places[0], early[-1])[:2])

    feed_other = swap(jnp.where(section == 0, feed_parts[1], feed_parts[0]))
    expand_out, contract_out = call(
        feed_out_kernel, [sds((1, step, units), F32)] * 2,
        where, feed_parts[0], feed_parts[1], feed_other,
    )
    attn_other = lax.ppermute(attn_part, "section", [(0, 1)])
    projections_out, output_out, gains_out, biases_out, units_out, pairs_out = call(
        partial(attn_out_kernel, step, e, c),
        [sds((1, 3, step, e), F32), sds((1, e, step), F32), sds((1, 2, step), F32),
         sds((1, 4, step), F32), sds((units // HD, 1, c), F32), sds((1, heads, 2, c), F32)],
        where, *early, attn_part, attn_other,
    )
    back_rows[0], expand_out, contract_out, projections_out = together(
        back_rows[0], expand_out, contract_out, projections_out
    )
    (input_grads,) = call(
        place_out_kernel, [sds((1, micro, 1, local, width), F32)], where, *back_rows
    )
    return (
        activations,
        input_grads,
        projections_out,
        pairs_out.transpose(0, 2, 1, 3),
        output_out,
        expand_out,
        units_out.transpose(1, 0, 2),
        contract_out.transpose(0, 2, 1),
        gains_out,
        biases_out,
    )


def split_pack(pack, relative, across):
    if relative:
        weights, small = (pack[0, :-16], pack[0, -16:])
        weights = weights.reshape(across, -1, weights.shape[1])
        small = jnp.broadcast_to(small, (across,) + small.shape)
        return jnp.concatenate([weights, small], axis=1)
    weights = pack[:, 0, :-16].reshape(-1, pack.shape[3])
    weights = weights.reshape(across, 2, -1, pack.shape[3]).transpose(1, 0, 2, 3)
    small = jnp.broadcast_to(pack[0, 0, -16:], (2, across, 16, pack.shape[3]))
    return jnp.concatenate([weights, small], axis=2)


def solution(mesh):
    in_specs = (
        P(None, None, ("dp", "tensor"), None),
        P(None, None, ("dp", "tensor"), None),
        P(),
        P("section", "tensor", None, None),
        P("section", None, "dp", "tensor"),
        P("section", None, "tensor", "dp"),
        P("section", "tensor", "dp"),
        P("section", "dp", "tensor"),
        P("section", "tensor", "dp"),
        P("section", "tensor", "dp"),
        P("section", None, "dp"),
        P("section", None, "dp"),
    )
    out_specs = (
        P("section", None, None, ("dp", "tensor"), None),
        P("section", None, None, ("dp", "tensor"), None),
        P("section", None, "dp", "tensor"),
        P("section", None, "tensor", "dp"),
        P("section", "tensor", "dp"),
        P("section", "dp", "tensor"),
        P("section", "tensor", "dp"),
        P("section", "tensor", "dp"),
        P("section", None, "dp"),
        P("section", None, "dp"),
    )
    return jax.shard_map(body, mesh=mesh, in_specs=in_specs, out_specs=out_specs, check_vma=False)
```

```python
import math
from functools import partial

import jax
import jax.numpy as jnp
from jax import lax
from jax.experimental import pallas as pl
from jax.experimental.pallas import tpu as pltpu
from jax.sharding import PartitionSpec as P

HD = 64
BLOCK = 64
GLOBAL = 2
EPSILON = 1e-12
MASKED = -1e30
GELU_A = 0.7978845608028654
GELU_B = 0.044715
F32 = jnp.float32
BF16 = jnp.bfloat16
MIB = 1 << 20
PLACES = ("section", "dp")


def nt(a, b):
    return lax.dot_general(a, b, (((1,), (1,)), ((), ())), preferred_element_type=F32)


def tn(a, b):
    return lax.dot_general(a, b, (((0,), (0,)), ((), ())), preferred_element_type=F32)


def nn(a, b):
    return jnp.dot(a, b, preferred_element_type=F32)


def sds(shape, dtype):
    return jax.ShapeDtypeStruct(shape, dtype)


class Far:
    def __init__(self, array, shape=None, cuts=None, plain=False, into=None, parts=1):
        self.array = array
        self.shape = array.shape if shape is None else shape
        self.cuts = [((), ())] if cuts is None else cuts
        self.plain = plain
        self.into = into
        self.parts = parts


class Raw:
    def __init__(self, array):
        self.array = array


def at(ref, index):
    return ref.at[index] if index else ref


class Arriving:
    def __init__(self, source, buffer, sems, first, cuts):
        self.buffer = buffer
        self.shape = buffer.shape
        self.copies = [
            pltpu.make_async_copy(at(source, a), at(buffer, b), sems.at[first + i])
            for i, (a, b) in enumerate(cuts)
        ]
        for copy in self.copies:
            copy.start()
        self.there = False

    def settle(self):
        if not self.there:
            for copy in self.copies:
                copy.wait()
            self.there = True

    def __getitem__(self, index):
        self.settle()
        return self.buffer[index]


class Leaving:
    def __init__(self, target, buffer, sems, first):
        self.target = target
        self.buffer = buffer
        self.shape = target.shape
        self.sems = sems
        self.first = first
        self.copies = []

    def __setitem__(self, index, value):
        self.buffer[index] = value

    def send(self, source=None, rows=None):
        target = self.target if rows is None else self.target.at[rows]
        if source is None:
            source = self.buffer if rows is None else self.buffer.at[rows]
        copy = pltpu.make_async_copy(source, target, self.sems.at[self.first + len(self.copies)])
        copy.start()
        self.copies.append(copy)

    def finish(self):
        if not self.copies:
            self.send()
        for copy in self.copies:
            copy.wait()


def flat(groups):
    return [item for group in groups for item in (group if isinstance(group, list) else [group])]


def grouped(items, groups):
    items = iter(items)
    return [
        [next(items) for _ in group] if isinstance(group, list) else next(items)
        for group in groups
    ]


def call(kernel, out_groups, *arg_groups, flops=0, limit=16, scratch=()):
    args = flat(arg_groups)
    outs = flat(out_groups)
    arrays = []
    in_specs = []
    out_specs = []
    out_shapes = []
    buffers = []
    size = 0
    semaphores = 0
    for arg in args:
        if isinstance(arg, Raw):
            arrays.append(pltpu.with_memory_space_constraint(arg.array, pltpu.HBM))
            in_specs.append(pl.BlockSpec(memory_space=pltpu.HBM))
        elif isinstance(arg, Far):
            arrays.append(pltpu.with_memory_space_constraint(arg.array, pltpu.HBM))
            in_specs.append(pl.BlockSpec(memory_space=pltpu.HBM))
            if arg.into is None:
                buffers.append(pltpu.VMEM(arg.shape, arg.array.dtype))
            semaphores += len(arg.cuts)
            size += math.prod(arg.shape) * arg.array.dtype.itemsize
        else:
            arrays.append(arg)
            scalar = arg.dtype == jnp.int32
            in_specs.append(pl.BlockSpec(memory_space=pltpu.SMEM if scalar else pltpu.VMEM))
            size += arg.size * arg.dtype.itemsize
    for out in outs:
        if isinstance(out, Raw):
            out_shapes.append(pltpu.HBM(out.array.shape, out.array.dtype))
            out_specs.append(pl.BlockSpec(memory_space=pltpu.HBM))
        elif isinstance(out, Far):
            out_shapes.append(pltpu.HBM(out.shape, out.array.dtype))
            out_specs.append(pl.BlockSpec(memory_space=pltpu.HBM))
            if not out.plain:
                buffers.append(pltpu.VMEM(out.shape, out.array.dtype))
            semaphores += out.parts
            size += math.prod(out.shape) * out.array.dtype.itemsize
        else:
            out_shapes.append(out)
            out_specs.append(pl.BlockSpec(memory_space=pltpu.VMEM))
            size += out.size * out.dtype.itemsize

    def whole(*refs):
        refs = list(refs)
        ins = refs[: len(args)]
        results = refs[len(args) : len(args) + len(outs)]
        rest = refs[len(args) + len(outs) :]
        sems = rest.pop() if semaphores else None
        given = []
        handed = []
        used = 0
        for arg, ref in zip(args, ins):
            if isinstance(arg, Far):
                buffer = rest.pop(0) if arg.into is None else results[arg.into]
                given.append(Arriving(ref, buffer, sems, used, arg.cuts))
                used += len(arg.cuts)
            else:
                given.append(ref)
        leaving = []
        for out, ref in zip(outs, results):
            if isinstance(out, Far):
                buffer = None if out.plain else rest.pop(0)
                leaving.append(Leaving(ref, buffer, sems, used))
                handed.append(leaving[-1])
                used += out.parts
            else:
                handed.append(ref)
        kernel(*grouped(given, arg_groups), *grouped(handed, out_groups), *rest)
        for item in given:
            if isinstance(item, Arriving):
                item.settle()
        for item in leaving:
            item.finish()

    scratch_shapes = buffers + list(scratch)
    if semaphores:
        scratch_shapes = scratch_shapes + [pltpu.SemaphoreType.DMA((semaphores,))]
    results = pl.pallas_call(
        whole,
        out_shape=tuple(out_shapes),
        in_specs=in_specs,
        out_specs=tuple(out_specs),
        scratch_shapes=scratch_shapes,
        compiler_params=pltpu.CompilerParams(vmem_limit_bytes=limit * MIB),
        cost_estimate=pl.CostEstimate(flops=flops, bytes_accessed=size, transcendentals=0),
    )(*arrays)
    return grouped(results, out_groups)


SECTION, PLACE, PLANE, SEAT, START, LENGTH, FLIP = range(7)


def positions(where_ref, count, ways, local):
    row = lax.broadcasted_iota(jnp.int32, (count, 1), 0)
    group = jnp.bitwise_xor(row // local % 2, where_ref[FLIP])
    seat = jnp.bitwise_xor(row // (2 * local), where_ref[SEAT])
    return where_ref[START] + group * (ways * local) + seat * local + row % local


def row_halves(rows):
    return [slice(begin, begin + rows // 2) for begin in (0, rows // 2)]


def send_parts(outs, whole, half):
    count = len(outs) // 2
    mine = whole.shape[0] // len(outs)
    for k in range(half * count, (half + 1) * count):
        if isinstance(outs[k], Leaving):
            outs[k].send(whole.at[pl.ds(k * mine, mine)])
        else:
            outs[k][...] = whole[k * mine : (k + 1) * mine]


def joined(refs):
    return jnp.concatenate([ref[...] for ref in refs], axis=0)


def keep(out, refs):
    size = refs[0].shape[0]
    for k, ref in enumerate(refs):
        out.send(ref, pl.ds(k * size, size))


def core_is(where_ref, core):
    return pl.when(where_ref[SECTION] == core)


def prepare_kernel(
    projections_ref, output_ref, expand_ref, contract_ref, pair_ref, unit_ref,
    gain_ref, bias_ref, attn_keep, attn_send, keep_out, send_out, whole, small
):
    step, e = projections_ref.shape[2:]
    heads, _, c = pair_ref.shape[1:]
    half = step // 2
    whole[:, :e] = projections_ref[0, 0]
    whole[:, e : 2 * e] = projections_ref[0, 2]
    whole[:, 2 * e : 3 * e] = projections_ref[0, 1]
    whole[:, 3 * e :] = output_ref[0].T
    small[...] = jnp.zeros_like(small)
    small[0:2, :step] = gain_ref[0].astype(F32)
    small[2:6, :step] = bias_ref[0].astype(F32)
    small[: unit_ref.shape[1], 256 : 256 + c] = unit_ref[0].astype(F32)
    for i in range(heads):
        small[i : i + 1, 384 : 384 + c] = pair_ref[0, i, 0:1].astype(F32)
        small[i : i + 1, 512 : 512 + c] = pair_ref[0, i, 1:2].astype(F32)
    attn_keep[half:] = small[...].astype(BF16)
    attn_send[half:] = small[...].astype(BF16)
    expand = expand_ref[0]
    contract = contract_ref[0]
    section = lax.axis_index("section")

    @pl.when(section == 0)
    def _():
        attn_keep[:half] = whole[:half]
        attn_send[:half] = whole[half:]
        keep_out[...] = expand
        send_out[...] = contract

    @pl.when(section == 1)
    def _():
        attn_keep[:half] = whole[half:]
        attn_send[:half] = whole[:half]
        keep_out[...] = contract
        send_out[...] = expand


def unpack(c, e, raw_ref, vec_ref):
    places = raw_ref.shape[0]
    width = vec_ref.shape[1]
    w = width // places

    def of_heads(rows, lanes, z):
        source = lax.broadcasted_iota(jnp.int32, (128, lanes), 0)
        target = lax.broadcasted_iota(jnp.int32, (128, lanes), 1)
        repeat = ((target % c == source) & (source < c)).astype(F32).astype(BF16)
        spread_rows = nn(rows, repeat)
        head = lax.broadcasted_iota(jnp.int32, spread_rows.shape, 0)
        lane = lax.broadcasted_iota(jnp.int32, spread_rows.shape, 1)
        keep = (lane // HD == head) & (lane % HD // c == z)
        return jnp.sum(jnp.where(keep, spread_rows, 0.0), axis=0, keepdims=True)

    norms = jnp.zeros((16, width), F32)
    units = jnp.zeros((1, width), F32)
    queries = jnp.zeros((1, 256), F32)
    values = jnp.zeros((1, 256), F32)
    for z in range(places):
        rows = raw_ref[z]
        source = lax.broadcasted_iota(jnp.int32, (256, width), 0)
        target = lax.broadcasted_iota(jnp.int32, (256, width), 1)
        move = ((target == source + z * w) & (source < w)).astype(F32).astype(BF16)
        norms = norms + nn(rows[:, :256], move)
        units = units + of_heads(rows[:, 256:384], width, z)
        queries = queries + of_heads(rows[:, 384:512], 256, z)
        values = values + of_heads(rows[:, 512:640], 256, z)
    vec_ref[...] = norms[:8]
    vec_ref[6:7] = units
    lane = lax.broadcasted_iota(jnp.int32, (1, 256), 1)
    queries = jnp.where(lane < e, queries, 0.0)
    values = jnp.where(lane < e, values, 0.0)
    return (queries, pltpu.roll(values, 256 - e, 1))


def qkv_kernel(
    ways, local, blocks, c, e, where_ref, x_refs, raw_ref, w_ref, q_ref, kv_ref, vec_ref, *kept
):
    kw = q_ref.shape[1]
    vw = kv_ref.shape[1] - kw
    x = joined(x_refs)
    keep(kept[0], x_refs)
    query_bias, value_bias = unpack(c, e, raw_ref, vec_ref)
    lead = 2 * e // 128 * 128
    q = (nn(x, w_ref[:, :256]) + query_bias).astype(BF16).astype(F32) * HD ** (-0.5)
    lane = lax.broadcasted_iota(jnp.int32, (1, 256), 1)
    q = jnp.where(lane < e, q, 0.0).astype(BF16)
    q_ref[:, :256] = q
    if kw > 256:
        q_ref[:, 256:] = jnp.zeros((q.shape[0], kw - 256), BF16)
    kept[1].send(q_ref)
    position = positions(where_ref, x.shape[0], ways, local)
    block = position // BLOCK
    lane = lax.broadcasted_iota(jnp.int32, (1, kw), 1)
    hidden = (position >= where_ref[LENGTH]) & (lane == e + blocks)
    tail = jnp.where(lane == e + block, 1.0, jnp.where(hidden, MASKED, 0.0))
    k = nn(x, w_ref[:, lead : lead + 256])
    if kw > 256:
        k = jnp.concatenate([k, jnp.zeros((k.shape[0], kw - 256), F32)], axis=1)
    kv_ref[:, :kw] = jnp.where(lane < e, k, tail).astype(BF16)
    kv_ref[:, kw:] = (nn(x, w_ref[:, 128 : 128 + vw]) + value_bias).astype(BF16)
    kept[2].send(kv_ref)


def head_mask(first, lanes):
    lane = lax.broadcasted_iota(jnp.int32, (1, lanes), 1)
    return ((lane >= first) & (lane < first + HD)).astype(F32)


def seen_rows(where_ref, random_refs, layer, h, rows, ways, local, kw, e, blocks):
    lane = lax.broadcasted_iota(jnp.int32, (1, kw), 1)
    key = lane - e
    parts = []
    for g in range(rows // local):
        group = jnp.bitwise_xor(g % 2, where_ref[FLIP])
        seat = jnp.bitwise_xor(g // 2, where_ref[SEAT])
        position = where_ref[START] + group * (ways * local) + seat * local
        block = position // BLOCK
        seen = (key < GLOBAL) | (jnp.abs(key - block) <= 1) | (block < GLOBAL)
        for i in range(random_refs[0].shape[3]):
            picked = [ref[0, h, block, i] for ref in random_refs]
            seen = seen | (key == jnp.where(where_ref[SECTION] == layer, *picked))
        hidden = (key >= 0) & (key < blocks) & jnp.logical_not(seen)
        line = jnp.where(key == blocks, 1.0, jnp.where(hidden, MASKED, 0.0))
        parts.append(jnp.broadcast_to(line, (local, kw)))
    return jnp.concatenate(parts, axis=0)


def attention_kernel(
    heads, layer, ways, local, blocks, chunk, where_ref, random_refs, q_ref, w_ref, parts,
    outs, mixed_out, total_out, kept, whole
):
    rows, kw = q_ref.shape
    e = heads * HD
    vw = parts[0].shape[1] - kw
    shift = vw - e
    for out, part in zip(kept, parts[1:]):
        out.send(part)
    k = jnp.concatenate([part[:, :kw] for part in parts], axis=0)
    vt = jnp.concatenate([part[:, kw:] for part in parts], axis=0).T
    q = q_ref[...].astype(F32)
    lines = [jnp.zeros((shift, rows), F32)]
    totals = []
    for h in range(heads):
        seen = seen_rows(where_ref, random_refs, layer, h, rows, ways, local, kw, e, blocks)
        qa = (q * head_mask(h * HD, kw) + seen).astype(BF16)
        vh = vt[shift + h * HD : shift + (h + 1) * HD]
        cells = []
        sums = []
        for c in range(0, rows, chunk):
            scores = nt(k, qa[c : c + chunk])
            top = jnp.max(scores, axis=0, keepdims=True)
            p = jnp.exp(scores - top)
            total = jnp.sum(p, axis=0, keepdims=True)
            cells.append(nn(vh, p.astype(BF16)) / total)
            sums.append(top + jnp.log(total))
        lines.append(jnp.concatenate(cells, axis=1))
        totals.append(jnp.concatenate(sums, axis=1))
    total_out[...] = jnp.concatenate(totals + [jnp.zeros((8 - heads, rows), F32)], axis=0)
    total_out.send()
    mixed = jnp.concatenate(lines, axis=0).T.astype(BF16)
    mixed_out[...] = mixed
    mixed_out.send()
    for half, part in enumerate(row_halves(rows)):
        whole[part] = nt(mixed[part], w_ref[...]).astype(BF16)
        send_parts(outs, whole, half)


def attention_back_kernel(
    heads, layer, ways, local, blocks, chunk, where_ref, random_refs, grad_refs, w_ref, mixed_ref,
    q_ref, total_ref, parts, dq_ref, small_ref, outs
):
    rows, kw = q_ref.shape
    e = heads * HD
    vw = mixed_ref.shape[1]
    shift = vw - e
    grad = jnp.concatenate([ref[: 2 * local] for ref in grad_refs], axis=0)
    small_ref[...] = total_of([ref.at[2 * local :] for ref in grad_refs])
    mixed_grad = nn(grad, w_ref[:, w_ref.shape[1] - vw :]).astype(BF16).astype(F32)
    product = mixed_grad * mixed_ref[...].astype(F32)
    masks = jnp.concatenate([head_mask(shift + h * HD, vw) for h in range(8)], axis=0)
    inner = lax.dot_general(
        masks, product, (((1,), (1,)), ((), ())),
        preferred_element_type=F32, precision=lax.Precision.HIGHEST,
    )
    q = q_ref[...].astype(F32)
    k = jnp.concatenate([part[:, :kw] for part in parts], axis=0)
    v = jnp.concatenate([part[:, kw:] for part in parts], axis=0)
    kt = k[:, :256].T
    totals = total_ref[...]
    dk = None
    dv = None
    lines = []
    for h in range(heads):
        seen = seen_rows(where_ref, random_refs, layer, h, rows, ways, local, kw, e, blocks)
        qm = q * head_mask(h * HD, kw)
        qa = (qm + seen).astype(BF16)
        qm = qm[:, :256].astype(BF16)
        gm = (mixed_grad * head_mask(shift + h * HD, vw)).astype(BF16)
        kh = kt[h * HD : (h + 1) * HD]
        cells = []
        for c in range(0, rows, chunk):
            scores = nt(k, qa[c : c + chunk])
            p = jnp.exp(scores - totals[h : h + 1, c : c + chunk])
            dp = nt(v, gm[c : c + chunk])
            ds = (p * (dp - inner[h : h + 1, c : c + chunk])).astype(BF16)
            dv_term = nn(p.astype(BF16), gm[c : c + chunk])
            dk_term = nn(ds, qm[c : c + chunk])
            dv = dv_term if dv is None else dv + dv_term
            dk = dk_term if dk is None else dk + dk_term
            cells.append(nn(kh, ds))
        lines.append(jnp.concatenate(cells, axis=1))
    lines.append(jnp.zeros((256 - e, rows), F32))
    dq = jnp.concatenate(lines, axis=0).T * HD ** (-0.5)
    dq_ref[...] = dq.astype(BF16)
    start = 0
    for out in outs:
        size = out.shape[0]
        out[:, :256] = dk[start : start + size].astype(BF16)
        out[:, 256:] = dv[start : start + size].astype(BF16)
        start += size


def projection_back_kernel(
    e, dq_ref, own_ref, other_ref, w_ref, triple_ref, sums_ref, outs, whole
):
    vw = own_ref.shape[1] - 256
    width = w_ref.shape[1]
    lead = 2 * e // 128 * 128
    rows = dq_ref.shape[0]
    dq = dq_ref[...]
    dkv = (own_ref[...].astype(F32) + other_ref[...].astype(F32)).astype(BF16).astype(F32)
    dv = dkv[:, 256:]
    head = dq.astype(F32)
    nothing = jnp.zeros((rows, 128), F32)
    triple = jnp.concatenate(
        [head[:, :128], head[:, 128:] + dv[:, :128], dv[:, 128:], dkv[:, :256], nothing], axis=1
    ).astype(BF16)
    triple_ref[...] = triple
    sums_ref[...] = jnp.zeros_like(sums_ref)
    sums_ref[0:1] = jnp.sum(triple.astype(F32), axis=0, keepdims=True)
    for half, part in enumerate(row_halves(rows)):
        whole[part] = nt(triple[part], w_ref[...]).astype(BF16)
        send_parts(outs, whole, half)


def norm(values):
    average = jnp.mean(values, axis=-1, keepdims=True)
    centered = values - average
    spread_now = jnp.mean(centered * centered, axis=-1, keepdims=True)
    inverse = lax.rsqrt(spread_now + EPSILON)
    return (centered * inverse, inverse)


def total_of(terms):
    total = terms[0][...].astype(F32)
    for term in terms[1:]:
        total = total + term[...].astype(F32)
    return total


def first_norm_kernel(x_ref, terms_ref, vec_ref, middle_ref, low_ref, unit_out, inverse_out):
    values = x_ref[...].astype(F32) + total_of(terms_ref) + vec_ref[2:3]
    unit, inverse = norm(values)
    unit_out[...] = unit
    unit_out.send()
    inverse_out[...] = jnp.broadcast_to(inverse, inverse_out.shape)
    inverse_out.send()
    middle = unit * vec_ref[0:1] + vec_ref[4:5]
    middle_ref[...] = middle
    low_ref[...] = middle.astype(BF16)


def valid_rows(where_ref, ways, local):
    position = positions(where_ref, 2 * local, ways, local)
    return (position < where_ref[LENGTH]).astype(F32)


def place_parts(where_ref, early, later, outs):
    half = early.shape[0] // 2
    late_plane = where_ref[PLANE] // 2
    for u in range(2):
        for p in range(2):
            @pl.when(late_plane == u)
            def _(u=u, p=p):
                outs[2 * p + u][...] = early[p * half : (p + 1) * half]

            @pl.when(late_plane != u)
            def _(u=u, p=p):
                outs[2 * p + u][...] = later[p * half : (p + 1) * half]


def norm_back(grad, unit, inverse, gain):
    scaled = grad * gain
    return inverse * (
        scaled
        - jnp.mean(scaled, axis=-1, keepdims=True)
        - unit * jnp.mean(scaled * unit, axis=-1, keepdims=True)
    )


def second_norm(ways, where_ref, middle_ref, terms_ref, vec_ref):
    unit, inverse = norm(middle_ref[...] + total_of(terms_ref) + vec_ref[3:4])
    result = unit * vec_ref[1:2] + vec_ref[5:6]
    valid = valid_rows(where_ref, ways, unit.shape[0] // 2)
    return ((result * valid).astype(BF16), unit, inverse, valid)


def second_back(grad, unit, inverse, vec_ref, second_ref, low_ref, sums_ref):
    second = norm_back(grad, unit, inverse, vec_ref[1:2])
    low_ref[...] = second.astype(BF16)
    second_ref[...] = second
    second_ref.send()
    sums_ref[...] = jnp.zeros_like(sums_ref)
    sums_ref[0:1] = jnp.sum(grad * unit, axis=0, keepdims=True)
    sums_ref[1:2] = jnp.sum(grad, axis=0, keepdims=True)
    sums_ref[2:3] = jnp.sum(second, axis=0, keepdims=True)


def second_norm_kernel(
    ways, where_ref, middle_ref, terms_ref, vec_ref, low_ref, kept, unit_out, inverse_out
):
    low, unit, inverse, _ = second_norm(ways, where_ref, middle_ref, terms_ref, vec_ref)
    low_ref[...] = low
    kept.send(low_ref)
    unit_out[...] = unit
    unit_out.send()
    inverse_out[...] = jnp.broadcast_to(inverse, inverse_out.shape)
    inverse_out.send()


def turn_kernel(
    ways, where_ref, middle_ref, terms_ref, vec_ref, up_ref, _, second_ref, low_ref, sums_ref,
    ahead, kept
):
    low, unit, inverse, valid = second_norm(ways, where_ref, middle_ref, terms_ref, vec_ref)
    kept[...] = low
    kept.send()
    second_back(
        up_ref[...].astype(F32) * valid, unit, inverse, vec_ref, second_ref, low_ref, sums_ref
    )


def between_kernel(
    ways, where_ref, terms_ref, vec_ref, first_ref, unit_ref, inverse_ref, _, second_ref, low_ref,
    sums_ref, ahead, kept
):
    low = (first_ref[...] + total_of(terms_ref)).astype(BF16)
    kept[...] = low
    kept.send()
    grad = low.astype(F32) * valid_rows(where_ref, ways, low.shape[0] // 2)
    second_back(
        grad, unit_ref[...], inverse_ref[:, 0:1], vec_ref, second_ref, low_ref, sums_ref
    )


def first_back_kernel(
    second_ref, terms_ref, vec_ref, before_ref, unit_ref, inverse_ref, _, first_ref, low_ref, ahead
):
    grad = second_ref[...] + total_of(terms_ref)
    unit = unit_ref[...]
    first = norm_back(grad, unit, inverse_ref[:, 0:1], vec_ref[0:1])
    first_ref[...] = first
    rows = first.shape[0]
    low_ref[:rows] = first.astype(BF16)
    before = before_ref[...]
    low_ref[rows:] = jnp.concatenate(
        [jnp.sum(grad * unit, axis=0, keepdims=True), before[0:1],
         jnp.sum(first, axis=0, keepdims=True), before[2:3],
         jnp.sum(grad, axis=0, keepdims=True), before[1:2],
         jnp.zeros((10, first.shape[1]), F32)], axis=0
    ).astype(BF16)


def last_input_kernel(where_ref, first_ref, later_ref, terms, *outs):
    low = (first_ref[...] + total_of(terms)).astype(BF16)
    place_parts(where_ref, low, later_ref[...], outs)


def place_out_kernel(where_ref, *refs):
    parts, out_ref = (refs[:-1], refs[-1])
    odd = where_ref[PLACE] % 2
    for p in range(2):
        for u in range(2):
            m = 2 * jnp.bitwise_xor(where_ref[SECTION], u) + jnp.bitwise_xor(odd, p)
            out_ref[0, m, 0] = parts[2 * p + u][...].astype(F32)


def activation_out_kernel(micro, sub, where_ref, first_ref, last_ref, out_ref, sems):
    local = out_ref.shape[3]
    place = where_ref[PLACE]
    side = place % micro // 2

    def copies(ref):
        result = []
        for m in range(micro):
            source = side * (micro * sub) + m * sub + place // micro
            row = (2 * source + jnp.bitwise_xor(place % 2, m & 1)) * local
            rows = pl.ds(pl.multiple_of(row, local), local)
            result.append(pltpu.make_async_copy(ref.at[rows], out_ref.at[0, m, 0], sems.at[m]))
        return result

    for core, ref in enumerate((first_ref, last_ref)):
        @core_is(where_ref, core)
        def _(ref=ref):
            for copy in copies(ref):
                copy.start()
            for copy in copies(ref):
                copy.wait()


def feed_kernel(
    x_refs, vec_ref, expand_ref, contract_ref, outs, active_out, slope_out, kept, whole
):
    keep(kept, x_refs)
    parts = row_halves(whole.shape[0])
    values = [nn(joined(refs), expand_ref[...]) + vec_ref[6:7] for refs in (x_refs[:2], x_refs[2:])]
    for half, (part, v) in enumerate(zip(parts, values)):
        th = jnp.tanh(v * (GELU_A + GELU_A * GELU_B * (v * v)))
        upper = 0.5 + 0.5 * th
        active = (v * upper).astype(BF16)
        active_out[part] = active
        active_out.send(rows=part)
        slope = upper + v * (1.0 - th * th) * (0.5 * GELU_A + 1.5 * GELU_A * GELU_B * (v * v))
        slope_out[part] = slope.astype(BF16)
        slope_out.send(rows=part)
        whole[part] = nt(active, contract_ref[...]).astype(BF16)
        send_parts(outs, whole, half)


def feed_back_kernel(
    grad_refs, contract_ref, slope_ref, expand_ref, hidden_ref, outs, sums_ref, whole
):
    parts = row_halves(whole.shape[0])
    values = [nn(joined(refs), contract_ref[...]) for refs in (grad_refs[:2], grad_refs[2:])]
    total = jnp.zeros((1, hidden_ref.shape[1]), F32)
    for half, (part, value) in enumerate(zip(parts, values)):
        hidden = (value * slope_ref[part].astype(F32)).astype(BF16)
        hidden_ref[part] = hidden
        hidden_ref.send(rows=part)
        total = total + jnp.sum(hidden.astype(F32), axis=0, keepdims=True)
        whole[part] = nt(hidden, expand_ref[...]).astype(BF16)
        send_parts(outs, whole, half)
    sums_ref[...] = jnp.zeros_like(sums_ref)
    sums_ref[0:1] = total


def feed_pack_kernel(where_ref, hidden_ref, grad_refs, middle_ref, active_ref, *outs):
    expand = tn(middle_ref[...], hidden_ref[...]).astype(BF16)
    contract = tn(joined(grad_refs), active_ref[...]).astype(BF16)

    @core_is(where_ref, 0)
    def _():
        outs[0][...] = expand
        outs[1][...] = contract

    @core_is(where_ref, 1)
    def _():
        outs[0][...] = contract
        outs[1][...] = expand


def attn_pack_kernel(
    step, e, where_ref, triple_ref, grad_refs, norm_ref, unit_ref, pair_ref, x_ref, mixed_ref, *outs
):
    x = x_ref[...]
    width = x.shape[1]
    vw = mixed_ref.shape[1]
    places = width // step
    mine = grad_refs[0].shape[0] - 16
    grad = jnp.concatenate([ref[:mine] for ref in grad_refs], axis=0)
    total = tn(x, triple_ref[...])
    last = total[:, width - vw :] + tn(grad, mixed_ref[...])
    weights = jnp.concatenate([total[:, : width - vw], last], axis=1).astype(BF16)
    small = jnp.concatenate(
        [norm_ref[:6], unit_ref[0:1], pair_ref[0:1], jnp.zeros((8, width), F32)], axis=0
    ).astype(BF16)
    if len(outs) == 1:
        half = step // 2
        for z in range(places):
            for i in range(2):
                begin = z * step + i * half
                outs[0][i, z, :half] = weights[begin : begin + half]
                outs[0][i, z, half:] = small
        return
    for z in range(places):
        k = jnp.bitwise_xor(where_ref[PLACE], z)
        kept = k // 2 == where_ref[SECTION]
        for out, is_mine in zip(outs, (kept, jnp.logical_not(kept))):
            @pl.when(is_mine)
            def _(out=out, k=k, z=z):
                out[k % 2, :step] = weights[z * step : (z + 1) * step]
                out[k % 2, step:] = small


def pair_sum_kernel(mine_ref, other_ref, own_ref, first_out, second_out):
    total = mine_ref[0].astype(F32) + other_ref[0].astype(F32)
    own_ref[...] = total
    first_out[...] = total.astype(BF16)
    first_out.send()
    second_out[...] = (mine_ref[1].astype(F32) + other_ref[1].astype(F32)).astype(BF16)


def attn_out_kernel(
    step, e, c, where_ref, *refs
):
    early, (mine_ref, other_ref), outs = (refs[:-8], refs[-8:-6], refs[-6:])
    projections_ref, output_ref, gain_ref, bias_ref, unit_ref, pair_ref = outs
    width = mine_ref.shape[1]

    def fill(total):
        weights = total[:step]
        small = total[step : step + 8]
        projections_ref[0, 0] = weights[:, :e]
        projections_ref[0, 1] = weights[:, 2 * e : 3 * e]
        projections_ref[0, 2] = pltpu.roll(weights, width - e, 1)[:, :e]
        output_ref[0] = pltpu.roll(weights, e, 1)[:, :e].T
        mine = pltpu.roll(small, lax.rem(width - where_ref[PLACE] * step, width), 1)
        gain_ref[0] = mine[0:2, :step]
        bias_ref[0] = mine[2:6, :step]

        def column(row, head):
            shift = lax.rem(2 * width - head * HD - where_ref[PLACE] * c, width)
            return pltpu.roll(small, shift, 1)[row : row + 1, :c]

        for head in range(unit_ref.shape[0]):
            unit_ref[head] = column(6, head)
        for head in range(pair_ref.shape[1]):
            pair_ref[0, head, 0:1] = column(7, head)
            pair_ref[0, head, 1:2] = column(7, head + e // HD)

    @core_is(where_ref, 0)
    def _():
        total = early[0][...]
        for term in early[1:]:
            total = total + term[...].astype(F32)
        fill(total)

    @core_is(where_ref, 1)
    def _():
        mine = mine_ref[...].astype(F32)
        other = other_ref[...].astype(F32)
        fill(jnp.concatenate([other[: step // 2], mine], axis=0))


def feed_out_kernel(where_ref, first_ref, second_ref, other_ref, expand_ref, contract_ref):
    @core_is(where_ref, 0)
    def _():
        expand_ref[0] = first_ref[...].astype(F32)
        contract_ref[0] = other_ref[...].astype(F32)

    @core_is(where_ref, 1)
    def _():
        expand_ref[0] = other_ref[...].astype(F32)
        contract_ref[0] = second_ref[...].astype(F32)


def swap(x):
    return lax.ppermute(x, "section", [(0, 1), (1, 0)])


def gather_rows(x):
    seats = range(lax.axis_size("tensor"))
    return [x] + [lax.ppermute(x, "tensor", [(i, i ^ k) for i in seats]) for k in seats if k]


def scatter_rows(parts):
    seats = range(lax.axis_size("tensor"))
    return parts[:1] + [
        lax.ppermute(parts[k], "tensor", [(i, i ^ k) for i in seats]) for k in seats if k
    ]


def deal(x, micro, sub):
    section = lax.axis_index("section")
    across = lax.axis_size("dp")
    odd = lax.axis_index("dp") % 2
    got = []
    for p in range(2):
        route = []
        for c in range(2):
            for d in range(across):
                r, dd = (d // micro, d % micro)
                m = 2 * c + (p ^ (dd & 1))
                route.append((c * across + d, (dd >> 1) * across + m * sub + r))
        chosen = 2 * section + (p ^ odd)
        payload = lax.dynamic_index_in_dim(x, chosen, 0, keepdims=False)
        got.append(lax.ppermute(payload, PLACES, route))
    return got


def undeal(parts, micro, sub):
    across = lax.axis_size("dp")
    got = []
    for p in range(2):
        for u in range(2):
            route = []
            for s in range(2):
                for source in range(across):
                    m, r = (source // sub, source % sub)
                    j = p ^ (m & 1)
                    layer = u ^ (m >> 1)
                    route.append((s * across + source, layer * across + r * micro + 2 * s + j))
            got.append(lax.ppermute(parts[2 * p + u], PLACES, route))
    return got


def across_places(x, section, k):
    across = lax.axis_size("dp")
    route = [(section * across + d, d ^ k) for d in range(across)]
    return lax.ppermute(x, PLACES, route)


def together(*values):
    return lax.optimization_barrier(values)


def after(x, token):
    return lax.optimization_barrier((x, token))[0]


def body(
    tokens,
    cotangent,
    lengths,
    random_blocks,
    projections,
    query_value_bias,
    output_weight,
    expand_weight,
    expand_bias,
    contract_weight,
    norm_gains,
    row_biases,
):
    section = lax.axis_index("section")
    place = lax.axis_index("dp")
    seat = lax.axis_index("tensor")
    across = lax.axis_size("dp")
    ways = lax.axis_size("tensor")
    micro = tokens.shape[0]
    sub = across // micro
    plane = place // sub
    share = place % sub
    local = tokens.shape[2]
    width = tokens.shape[3]
    e = projections.shape[3]
    heads = e // HD
    units = expand_weight.shape[2]
    step = projections.shape[2]
    c = query_value_bias.shape[3]
    mine = 2 * local
    rows = mine * ways
    keys = rows * 2 * sub
    blocks = keys // BLOCK
    kw = -(-(e + blocks + 1) // 128) * 128
    vw = 256
    whole_tiles = step % 32 == 0
    start = (share * micro + 2 * section) * ways * local
    length = lax.dynamic_index_in_dim(lengths[:, 0], plane, 0, keepdims=False)
    where = jnp.stack([section, place, plane, seat, start, length, plane % 2, 0]).astype(jnp.int32)
    random_other = swap(random_blocks)

    attn_keep, attn_send, feed_keep, feed_send = call(
        prepare_kernel,
        [sds((step // 2 + 16, 4 * e), BF16)] * 2 + [sds((step, units), BF16)] * 2,
        Far(projections), Far(output_weight), Far(expand_weight),
        Far(contract_weight.transpose(0, 2, 1)), Far(query_value_bias.transpose(0, 2, 1, 3)),
        Far(expand_bias), Far(norm_gains), Far(row_biases),
        scratch=[pltpu.VMEM((step, 4 * e), BF16), pltpu.VMEM((16, 4 * e), F32)],
    )
    x = deal(tokens[:, 0], micro, sub)
    upstream = deal(after(cotangent[:, 0], x[1]), micro, sub)
    x = jnp.concatenate(x, axis=0)
    feed_send, x = together(feed_send, x)
    attn_traded = swap(attn_send)
    feed_traded = swap(feed_send)
    attn_all = []
    feed_all = []
    for l in range(2):
        own = section == l
        whole = lax.all_gather(jnp.where(own, attn_keep, attn_traded), PLACES, axis=0, tiled=True)
        attn_all.append(whole.reshape(2, across, step // 2 + 16, 4 * e))
        whole = lax.all_gather(jnp.where(own, feed_keep, feed_traded), PLACES, axis=0, tiled=True)
        feed_all.append(whole.reshape(2, width, units))

    if not whole_tiles:
        attn_flat = [
            whole[:, :, : step // 2].transpose(1, 0, 2, 3).reshape(width, 4 * e)
            for whole in attn_all
        ]
    def small_rows(l):
        if not whole_tiles:
            return attn_all[l][0, :, step // 2 :]
        cuts = [((0, z, pl.ds(step // 2, 16)), (z,)) for z in range(across)]
        return Far(attn_all[l], (across, 16, 4 * e), cuts)

    def attn_weight(l, first, size, into=None):
        lanes = pl.ds(first, size)
        if not whole_tiles:
            return Far(attn_flat[l], (width, size), [((slice(None), lanes), ())], into=into)
        half = step // 2
        cuts = [
            ((i, z, pl.ds(0, half), lanes), (pl.ds(z * step + i * half, half),))
            for z in range(across)
            for i in range(2)
        ]
        return Far(attn_all[l], (width, size), cuts, into=into)

    def feed_weight(l, i, into=None):
        return Far(feed_all[l], (width, units), [((i,), ())], into=into)

    def all_parts(own):
        pair = [own, swap(own)]
        if sub == 1:
            return pair
        groups = [[m * sub + r for r in range(sub)] for m in range(micro)]
        return [
            lax.all_gather(
                jnp.concatenate(pair, axis=0), "dp", axis=0, tiled=True, axis_index_groups=groups
            )
        ]

    def own_parts(parts):
        if sub == 1:
            return parts
        groups = [[m * sub + r for r in range(sub)] for m in range(micro)]
        total = lax.psum_scatter(
            parts[0], "dp", scatter_dimension=0, tiled=True, axis_index_groups=groups
        )
        return [total[:rows], total[rows:]]

    chunk = min(rows, 512)
    near_rows = sds((mine, width), BF16)
    exchanged = [near_rows] + [Far(near_rows, plain=True)] * (ways - 1)
    exchanged_back = [Far(near_rows, plain=True)] * ways
    whole = pltpu.VMEM((rows, width), BF16)
    near_f32 = sds((mine, width), F32)
    turn_outs = [Far(near_f32), near_rows, sds((8, width), F32), sds((width, units), BF16)]
    far_unit = [Far(sds((mine, width), F32)), Far(sds((mine, 128), F32))]

    saved = []
    vectors = []
    for l in range(2):
        x_all = gather_rows(x)
        q, kv, vec, x_kept, q_kept, kv_kept = call(
            partial(qkv_kernel, ways, local, blocks, c, e),
            [sds((rows, kw), BF16), sds((rows, kw + vw), BF16), sds((8, width), F32),
             Far(sds((rows, width), BF16), plain=True, parts=ways),
             Far(sds((rows, kw), BF16), plain=True),
             Far(sds((rows, kw + vw), BF16), plain=True)],
            where, x_all, small_rows(l), attn_weight(l, 0, 4 * e),
            flops=6 * rows * width * 256,
        )
        vectors.append(vec)
        if l == 0:
            kv, *upstream = together(kv, *upstream)
            upstream = jnp.concatenate(upstream, axis=0)
        parts = all_parts(kv)
        attended, mixed, totals, others = call(
            partial(attention_kernel, heads, l, ways, local, blocks, chunk),
            [exchanged, Far(sds((rows, vw), BF16)), Far(sds((8, rows), F32)),
             [Far(sds(part.shape, BF16), plain=True) for part in parts[1:]]],
            where, [random_blocks, random_other], q, attn_weight(l, 4 * e - vw, vw), parts,
            flops=4 * rows * keys * kw, limit=24, scratch=[whole],
        )
        parts_kept = [kv_kept, others[0]] if sub == 1 else parts
        terms = scatter_rows(attended)
        middle, middle_low, unit1, inverse1 = call(
            first_norm_kernel, [sds((mine, width), F32), near_rows] + far_unit, x, terms, vec
        )
        middle_all = gather_rows(middle_low)
        fed, active, slope, middle_kept = call(
            feed_kernel,
            [exchanged, Far(sds((rows, units), BF16), parts=2),
             Far(sds((rows, units), BF16), parts=2),
             Far(sds((rows, width), BF16), plain=True, parts=ways)],
            middle_all, vec, feed_weight(l, 0), feed_weight(l, 1),
            flops=4 * rows * width * units, scratch=[whole],
        )
        terms = scatter_rows(fed)
        if l == 0:
            x, low_kept, unit2, inverse2 = call(
                partial(second_norm_kernel, ways),
                [near_rows, Far(near_rows, plain=True)] + far_unit,
                where, middle, terms, vec,
            )
            first_rows = lax.all_gather(low_kept, PLACES, axis=0, tiled=True)
        else:
            second, feed_low, second_sums, contract_ahead, last_kept = call(
                partial(turn_kernel, ways), turn_outs + [Far(near_rows)],
                where, middle, terms, vec, upstream, feed_weight(1, 1, into=3),
            )
        saved.append(
            (x_kept, q_kept, parts_kept, mixed, totals, unit1, inverse1, middle_kept, active,
             slope)
        )
        if l == 0:
            norm_kept = (unit2, inverse2)
    last_rows = lax.all_gather(last_kept, PLACES, axis=0, tiled=True)
    feed_parts = [None, None]
    for l in (1, 0):
        vec = vectors[l]
        (x_kept, q_kept, parts_kept, mixed, totals, unit1, inverse1, middle_kept, active,
         slope) = saved[l]
        feed_grad = gather_rows(feed_low)
        if l == 1:
            feed_grad[0], first_rows = together(feed_grad[0], first_rows)
        hidden, fed_back, unit_sums = call(
            feed_back_kernel,
            [Far(sds((rows, units), BF16), parts=2), exchanged_back, sds((8, units), F32)],
            feed_grad, contract_ahead, Far(slope), feed_weight(l, 0),
            flops=4 * rows * width * units, scratch=[whole],
        )
        terms = scatter_rows(fed_back)
        feed_kept, feed_sent = call(
            feed_pack_kernel, [Far(sds((width, units), BF16))] * 2,
            where, Far(hidden), feed_grad, Far(middle_kept), Far(active),
            flops=4 * rows * width * units,
        )
        *terms, feed_sent = together(*terms, feed_sent)
        feed_traded = swap(feed_sent)
        if l == 0:
            terms[0], feed_parts[1] = together(terms[0], feed_parts[1])
        terms[0] = Far(terms[0])
        first_grad, first_low, attn_ahead = call(
            first_back_kernel,
            [Far(near_f32), sds((mine + 16, width), BF16), sds((width, 4 * e), BF16)],
            Far(second), terms, vec, second_sums, Far(unit1), Far(inverse1),
            attn_weight(l, 0, 4 * e, into=2),
        )
        attended_grad = gather_rows(first_low)
        feed_traded = after(feed_traded, first_low)
        feed_half = (feed_kept.astype(F32) + feed_traded.astype(F32)).astype(BF16)
        if l == 1:
            attended_grad[0], last_rows = together(attended_grad[0], last_rows)
        attended_grad[0], feed_half = together(attended_grad[0], feed_half)
        feed_parts[l] = lax.psum_scatter(feed_half, "dp", scatter_dimension=0, tiled=True)
        dq, norm_sums, dkv = call(
            partial(attention_back_kernel, heads, l, ways, local, blocks, chunk),
            [sds((rows, 256), BF16), sds((16, width), F32),
             [sds((part.shape[0], 256 + vw), BF16) for part in parts_kept]],
            where, [random_blocks, random_other], attended_grad, attn_ahead, Far(mixed),
            Far(q_kept), Far(totals), [Far(part) for part in parts_kept],
            flops=10 * rows * keys * kw, limit=44,
        )
        dkv_own, dkv_other = own_parts(dkv)
        dkv_traded = swap(dkv_other)
        triple, pair_sums, projected = call(
            partial(projection_back_kernel, e),
            [sds((rows, 4 * e), BF16), sds((8, 4 * e), F32), exchanged_back],
            dq, dkv_own, dkv_traded, attn_ahead,
            flops=6 * rows * width * 256, scratch=[whole],
        )
        terms = scatter_rows(projected)
        cut = step if whole_tiles else width
        pieces = width // cut
        traded_pack = l == 0 and across == 4
        pack_outs = [sds((2, cut + 16, 4 * e), BF16)] * 2
        if not traded_pack:
            pack_outs = [sds((2, pieces, cut // 2 + 16, 4 * e), BF16)]
        pack, *sent_pack = call(
            partial(attn_pack_kernel, cut, e), pack_outs,
            where, triple, attended_grad, norm_sums, unit_sums, pair_sums, Far(x_kept),
            Far(mixed),
            flops=8 * rows * width * 256,
        )
        if not whole_tiles:
            pack = split_pack(pack, l == 0, across)
        if l == 1:
            (activations,) = call(
                partial(activation_out_kernel, micro, sub),
                [sds((1, micro, 1, local, width), BF16)],
                where, Raw(first_rows), Raw(last_rows),
                scratch=[pltpu.SemaphoreType.DMA((micro,))],
            )
            *terms, pack, activations = together(*terms, pack, activations)
            attn_part = lax.psum_scatter(
                pack.reshape((-1,) + pack.shape[2:]), PLACES, scatter_dimension=0
            )
            terms[0] = Far(terms[0])
            second, feed_low, second_sums, contract_ahead, later = call(
                partial(between_kernel, ways),
                turn_outs + [Far(near_rows)],
                where, terms, vectors[0], Far(first_grad), Far(norm_kept[0]), Far(norm_kept[1]),
                feed_weight(0, 1, into=3),
            )
        else:
            if traded_pack:
                own, first_sum, second_sum = call(
                    pair_sum_kernel,
                    [sds(pack.shape[1:], F32)] + [Far(sds(pack.shape[1:], BF16))] * 2,
                    pack, swap(sent_pack[0]),
                )
                terms[0], attn_part, own, first_sum, second_sum = together(
                    terms[0], attn_part, own, first_sum, second_sum
                )
                early = [
                    own,
                    across_places(second_sum, 0, 1),
                    across_places(first_sum, 1, 2),
                    across_places(second_sum, 1, 3),
                ]
            else:
                traded = lax.ppermute(pack, "section", [(1, 0)])
                total = (pack.astype(F32) + traded.astype(F32)).astype(BF16)
                early = [
                    lax.psum_scatter(total, "dp", scatter_dimension=0).astype(F32)
                ]
            terms[0] = Far(terms[0])
            places = call(
                last_input_kernel, [sds((local, width), BF16)] * 4,
                where, Far(first_grad), Far(later), terms,
            )
            back_rows = undeal(places, micro, sub)
            feed_parts = list(together(*feed_parts, places[0], early[-1])[:2])

    feed_other = swap(jnp.where(section == 0, feed_parts[1], feed_parts[0]))
    expand_out, contract_out = call(
        feed_out_kernel, [sds((1, step, units), F32)] * 2,
        where, feed_parts[0], feed_parts[1], feed_other,
    )
    attn_other = lax.ppermute(attn_part, "section", [(0, 1)])
    projections_out, output_out, gains_out, biases_out, units_out, pairs_out = call(
        partial(attn_out_kernel, step, e, c),
        [sds((1, 3, step, e), F32), sds((1, e, step), F32), sds((1, 2, step), F32),
         sds((1, 4, step), F32), sds((units // HD, 1, c), F32), sds((1, heads, 2, c), F32)],
        where, *early, attn_part, attn_other,
    )
    back_rows[0], expand_out, contract_out, projections_out = together(
        back_rows[0], expand_out, contract_out, projections_out
    )
    (input_grads,) = call(
        place_out_kernel, [sds((1, micro, 1, local, width), F32)], where, *back_rows
    )
    return (
        activations,
        input_grads,
        projections_out,
        pairs_out.transpose(0, 2, 1, 3),
        output_out,
        expand_out,
        units_out.transpose(1, 0, 2),
        contract_out.transpose(0, 2, 1),
        gains_out,
        biases_out,
    )


def split_pack(pack, relative, across):
    weights = pack[:, 0, :-16].reshape(-1, pack.shape[3])
    small = pack[0, 0, -16:]
    if relative:
        weights = weights.reshape(across, -1, weights.shape[1])
        small = jnp.broadcast_to(small, (across,) + small.shape)
        return jnp.concatenate([weights, small], axis=1)
    weights = weights.reshape(across, 2, -1, pack.shape[3]).transpose(1, 0, 2, 3)
    small = jnp.broadcast_to(small, (2, across, 16, pack.shape[3]))
    return jnp.concatenate([weights, small], axis=2)


def solution(mesh):
    in_specs = (
        P(None, None, ("dp", "tensor"), None),
        P(None, None, ("dp", "tensor"), None),
        P(),
        P("section", "tensor", None, None),
        P("section", None, "dp", "tensor"),
        P("section", None, "tensor", "dp"),
        P("section", "tensor", "dp"),
        P("section", "dp", "tensor"),
        P("section", "tensor", "dp"),
        P("section", "tensor", "dp"),
        P("section", None, "dp"),
        P("section", None, "dp"),
    )
    out_specs = (
        P("section", None, None, ("dp", "tensor"), None),
        P("section", None, None, ("dp", "tensor"), None),
        P("section", None, "dp", "tensor"),
        P("section", None, "tensor", "dp"),
        P("section", "tensor", "dp"),
        P("section", "dp", "tensor"),
        P("section", "tensor", "dp"),
        P("section", "tensor", "dp"),
        P("section", None, "dp"),
        P("section", None, "dp"),
    )
    return jax.shard_map(body, mesh=mesh, in_specs=in_specs, out_specs=out_specs, check_vma=False)
```

```python
import math
from functools import partial

import jax
import jax.numpy as jnp
from jax import lax
from jax.experimental import pallas as pl
from jax.experimental.pallas import tpu as pltpu
from jax.sharding import PartitionSpec as P

HD = 64
BLOCK = 64
GLOBAL = 2
EPSILON = 1e-12
MASKED = -1e30
GELU_A = 0.7978845608028654
GELU_B = 0.044715
F32 = jnp.float32
BF16 = jnp.bfloat16
MIB = 1 << 20
PLACES = ("section", "dp")


def nt(a, b):
    return lax.dot_general(a, b, (((1,), (1,)), ((), ())), preferred_element_type=F32)


def tn(a, b):
    return lax.dot_general(a, b, (((0,), (0,)), ((), ())), preferred_element_type=F32)


def nn(a, b):
    return jnp.dot(a, b, preferred_element_type=F32)


def sds(shape, dtype):
    return jax.ShapeDtypeStruct(shape, dtype)


class Far:
    def __init__(self, array, shape=None, cuts=None, plain=False, into=None, parts=1):
        self.array = array
        self.shape = array.shape if shape is None else shape
        self.cuts = [((), ())] if cuts is None else cuts
        self.plain = plain
        self.into = into
        self.parts = parts


class Raw:
    def __init__(self, array):
        self.array = array


def at(ref, index):
    return ref.at[index] if index else ref


class Arriving:
    def __init__(self, source, buffer, sems, first, cuts):
        self.buffer = buffer
        self.shape = buffer.shape
        self.copies = [
            pltpu.make_async_copy(at(source, a), at(buffer, b), sems.at[first + i])
            for i, (a, b) in enumerate(cuts)
        ]
        for copy in self.copies:
            copy.start()
        self.there = False

    def settle(self):
        if not self.there:
            for copy in self.copies:
                copy.wait()
            self.there = True

    def __getitem__(self, index):
        self.settle()
        return self.buffer[index]


class Leaving:
    def __init__(self, target, buffer, sems, first):
        self.target = target
        self.buffer = buffer
        self.shape = target.shape
        self.sems = sems
        self.first = first
        self.copies = []

    def __setitem__(self, index, value):
        self.buffer[index] = value

    def send(self, source=None, rows=None):
        target = self.target if rows is None else self.target.at[rows]
        if source is None:
            source = self.buffer if rows is None else self.buffer.at[rows]
        copy = pltpu.make_async_copy(source, target, self.sems.at[self.first + len(self.copies)])
        copy.start()
        self.copies.append(copy)

    def finish(self):
        if not self.copies:
            self.send()
        for copy in self.copies:
            copy.wait()


def flat(groups):
    return [item for group in groups for item in (group if isinstance(group, list) else [group])]


def grouped(items, groups):
    items = iter(items)
    return [
        [next(items) for _ in group] if isinstance(group, list) else next(items)
        for group in groups
    ]


def call(kernel, out_groups, *arg_groups, flops=0, limit=16, scratch=()):
    args = flat(arg_groups)
    outs = flat(out_groups)
    arrays = []
    in_specs = []
    out_specs = []
    out_shapes = []
    buffers = []
    size = 0
    semaphores = 0
    for arg in args:
        if isinstance(arg, Raw):
            arrays.append(pltpu.with_memory_space_constraint(arg.array, pltpu.HBM))
            in_specs.append(pl.BlockSpec(memory_space=pltpu.HBM))
        elif isinstance(arg, Far):
            arrays.append(pltpu.with_memory_space_constraint(arg.array, pltpu.HBM))
            in_specs.append(pl.BlockSpec(memory_space=pltpu.HBM))
            if arg.into is None:
                buffers.append(pltpu.VMEM(arg.shape, arg.array.dtype))
            semaphores += len(arg.cuts)
            size += math.prod(arg.shape) * arg.array.dtype.itemsize
        else:
            arrays.append(arg)
            scalar = arg.dtype == jnp.int32
            in_specs.append(pl.BlockSpec(memory_space=pltpu.SMEM if scalar else pltpu.VMEM))
            size += arg.size * arg.dtype.itemsize
    for out in outs:
        if isinstance(out, Raw):
            out_shapes.append(pltpu.HBM(out.array.shape, out.array.dtype))
            out_specs.append(pl.BlockSpec(memory_space=pltpu.HBM))
        elif isinstance(out, Far):
            out_shapes.append(pltpu.HBM(out.shape, out.array.dtype))
            out_specs.append(pl.BlockSpec(memory_space=pltpu.HBM))
            if not out.plain:
                buffers.append(pltpu.VMEM(out.shape, out.array.dtype))
            semaphores += out.parts
            size += math.prod(out.shape) * out.array.dtype.itemsize
        else:
            out_shapes.append(out)
            out_specs.append(pl.BlockSpec(memory_space=pltpu.VMEM))
            size += out.size * out.dtype.itemsize

    def whole(*refs):
        refs = list(refs)
        ins = refs[: len(args)]
        results = refs[len(args) : len(args) + len(outs)]
        rest = refs[len(args) + len(outs) :]
        sems = rest.pop() if semaphores else None
        given = []
        handed = []
        used = 0
        for arg, ref in zip(args, ins):
            if isinstance(arg, Far):
                buffer = rest.pop(0) if arg.into is None else results[arg.into]
                given.append(Arriving(ref, buffer, sems, used, arg.cuts))
                used += len(arg.cuts)
            else:
                given.append(ref)
        leaving = []
        for out, ref in zip(outs, results):
            if isinstance(out, Far):
                buffer = None if out.plain else rest.pop(0)
                leaving.append(Leaving(ref, buffer, sems, used))
                handed.append(leaving[-1])
                used += out.parts
            else:
                handed.append(ref)
        kernel(*grouped(given, arg_groups), *grouped(handed, out_groups), *rest)
        for item in given:
            if isinstance(item, Arriving):
                item.settle()
        for item in leaving:
            item.finish()

    scratch_shapes = buffers + list(scratch)
    if semaphores:
        scratch_shapes = scratch_shapes + [pltpu.SemaphoreType.DMA((semaphores,))]
    results = pl.pallas_call(
        whole,
        out_shape=tuple(out_shapes),
        in_specs=in_specs,
        out_specs=tuple(out_specs),
        scratch_shapes=scratch_shapes,
        compiler_params=pltpu.CompilerParams(vmem_limit_bytes=limit * MIB),
        cost_estimate=pl.CostEstimate(flops=flops, bytes_accessed=size, transcendentals=0),
    )(*arrays)
    return grouped(results, out_groups)


SECTION, PLACE, PLANE, SEAT, START, LENGTH, FLIP = range(7)


def positions(where_ref, count, ways, local):
    row = lax.broadcasted_iota(jnp.int32, (count, 1), 0)
    group = jnp.bitwise_xor(row // local % 2, where_ref[FLIP])
    seat = jnp.bitwise_xor(row // (2 * local), where_ref[SEAT])
    return where_ref[START] + group * (ways * local) + seat * local + row % local


def row_halves(rows):
    return [slice(begin, begin + rows // 2) for begin in (0, rows // 2)]


def send_parts(outs, whole, half):
    count = len(outs) // 2
    mine = whole.shape[0] // len(outs)
    for k in range(half * count, (half + 1) * count):
        if isinstance(outs[k], Leaving):
            outs[k].send(whole.at[pl.ds(k * mine, mine)])
        else:
            outs[k][...] = whole[k * mine : (k + 1) * mine]


def joined(refs):
    return jnp.concatenate([ref[...] for ref in refs], axis=0)


def keep(out, refs):
    size = refs[0].shape[0]
    for k, ref in enumerate(refs):
        out.send(ref, pl.ds(k * size, size))


def core_is(where_ref, core):
    return pl.when(where_ref[SECTION] == core)


def prepare_kernel(
    projections_ref, output_ref, expand_ref, contract_ref, pair_ref, unit_ref,
    gain_ref, bias_ref, attn_keep, attn_send, keep_out, send_out, whole, small
):
    step, e = projections_ref.shape[2:]
    heads, _, c = pair_ref.shape[1:]
    half = step // 2
    whole[:, :e] = projections_ref[0, 0]
    whole[:, e : 2 * e] = projections_ref[0, 2]
    whole[:, 2 * e : 3 * e] = projections_ref[0, 1]
    whole[:, 3 * e :] = output_ref[0].T
    small[...] = jnp.zeros_like(small)
    small[0:2, :step] = gain_ref[0].astype(F32)
    small[2:6, :step] = bias_ref[0].astype(F32)
    small[: unit_ref.shape[1], 256 : 256 + c] = unit_ref[0].astype(F32)
    for i in range(heads):
        small[i : i + 1, 384 : 384 + c] = pair_ref[0, i, 0:1].astype(F32)
        small[i : i + 1, 512 : 512 + c] = pair_ref[0, i, 1:2].astype(F32)
    attn_keep[half:] = small[...].astype(BF16)
    attn_send[half:] = small[...].astype(BF16)
    expand = expand_ref[0]
    contract = contract_ref[0]
    section = lax.axis_index("section")

    @pl.when(section == 0)
    def _():
        attn_keep[:half] = whole[:half]
        attn_send[:half] = whole[half:]
        keep_out[...] = expand
        send_out[...] = contract

    @pl.when(section == 1)
    def _():
        attn_keep[:half] = whole[half:]
        attn_send[:half] = whole[:half]
        keep_out[...] = contract
        send_out[...] = expand


def unpack(c, e, raw_ref, vec_ref):
    places = raw_ref.shape[0]
    width = vec_ref.shape[1]
    w = width // places

    def of_heads(rows, lanes, z):
        source = lax.broadcasted_iota(jnp.int32, (128, lanes), 0)
        target = lax.broadcasted_iota(jnp.int32, (128, lanes), 1)
        repeat = ((target % c == source) & (source < c)).astype(F32).astype(BF16)
        spread_rows = nn(rows, repeat)
        head = lax.broadcasted_iota(jnp.int32, spread_rows.shape, 0)
        lane = lax.broadcasted_iota(jnp.int32, spread_rows.shape, 1)
        keep = (lane // HD == head) & (lane % HD // c == z)
        return jnp.sum(jnp.where(keep, spread_rows, 0.0), axis=0, keepdims=True)

    norms = jnp.zeros((16, width), F32)
    units = jnp.zeros((1, width), F32)
    queries = jnp.zeros((1, 256), F32)
    values = jnp.zeros((1, 256), F32)
    for z in range(places):
        rows = raw_ref[z]
        source = lax.broadcasted_iota(jnp.int32, (256, width), 0)
        target = lax.broadcasted_iota(jnp.int32, (256, width), 1)
        move = ((target == source + z * w) & (source < w)).astype(F32).astype(BF16)
        norms = norms + nn(rows[:, :256], move)
        units = units + of_heads(rows[:, 256:384], width, z)
        queries = queries + of_heads(rows[:, 384:512], 256, z)
        values = values + of_heads(rows[:, 512:640], 256, z)
    vec_ref[...] = norms[:8]
    vec_ref[6:7] = units
    lane = lax.broadcasted_iota(jnp.int32, (1, 256), 1)
    queries = jnp.where(lane < e, queries, 0.0)
    values = jnp.where(lane < e, values, 0.0)
    return (queries, pltpu.roll(values, 256 - e, 1))


def qkv_kernel(
    ways, local, blocks, c, e, where_ref, x_refs, raw_ref, w_ref, q_ref, kv_ref, vec_ref, *kept
):
    kw = q_ref.shape[1]
    vw = kv_ref.shape[1] - kw
    x = joined(x_refs)
    keep(kept[0], x_refs)
    query_bias, value_bias = unpack(c, e, raw_ref, vec_ref)
    lead = 2 * e // 128 * 128
    q = (nn(x, w_ref[:, :256]) + query_bias).astype(BF16).astype(F32) * HD ** (-0.5)
    lane = lax.broadcasted_iota(jnp.int32, (1, 256), 1)
    q = jnp.where(lane < e, q, 0.0).astype(BF16)
    q_ref[:, :256] = q
    if kw > 256:
        q_ref[:, 256:] = jnp.zeros((q.shape[0], kw - 256), BF16)
    kept[1].send(q_ref)
    position = positions(where_ref, x.shape[0], ways, local)
    block = position // BLOCK
    lane = lax.broadcasted_iota(jnp.int32, (1, kw), 1)
    hidden = (position >= where_ref[LENGTH]) & (lane == e + blocks)
    tail = jnp.where(lane == e + block, 1.0, jnp.where(hidden, MASKED, 0.0))
    k = nn(x, w_ref[:, lead : lead + 256])
    if kw > 256:
        k = jnp.concatenate([k, jnp.zeros((k.shape[0], kw - 256), F32)], axis=1)
    kv_ref[:, :kw] = jnp.where(lane < e, k, tail).astype(BF16)
    kv_ref[:, kw:] = (nn(x, w_ref[:, 128 : 128 + vw]) + value_bias).astype(BF16)
    kept[2].send(kv_ref)


def head_mask(first, lanes):
    lane = lax.broadcasted_iota(jnp.int32, (1, lanes), 1)
    return ((lane >= first) & (lane < first + HD)).astype(F32)


def seen_rows(where_ref, random_refs, layer, h, rows, ways, local, kw, e, blocks):
    lane = lax.broadcasted_iota(jnp.int32, (1, kw), 1)
    key = lane - e
    parts = []
    for g in range(rows // local):
        group = jnp.bitwise_xor(g % 2, where_ref[FLIP])
        seat = jnp.bitwise_xor(g // 2, where_ref[SEAT])
        position = where_ref[START] + group * (ways * local) + seat * local
        block = position // BLOCK
        seen = (key < GLOBAL) | (jnp.abs(key - block) <= 1) | (block < GLOBAL)
        for i in range(random_refs[0].shape[3]):
            picked = [ref[0, h, block, i] for ref in random_refs]
            seen = seen | (key == jnp.where(where_ref[SECTION] == layer, *picked))
        hidden = (key >= 0) & (key < blocks) & jnp.logical_not(seen)
        line = jnp.where(key == blocks, 1.0, jnp.where(hidden, MASKED, 0.0))
        parts.append(jnp.broadcast_to(line, (local, kw)))
    return jnp.concatenate(parts, axis=0)


def attention_kernel(
    heads, layer, ways, local, blocks, chunk, where_ref, random_refs, q_ref, w_ref, parts,
    outs, mixed_out, total_out, kept, whole
):
    rows, kw = q_ref.shape
    e = heads * HD
    vw = parts[0].shape[1] - kw
    shift = vw - e
    for out, part in zip(kept, parts[1:]):
        out.send(part)
    k = jnp.concatenate([part[:, :kw] for part in parts], axis=0)
    vt = jnp.concatenate([part[:, kw:] for part in parts], axis=0).T
    q = q_ref[...].astype(F32)
    lines = [jnp.zeros((shift, rows), F32)]
    totals = []
    for h in range(heads):
        seen = seen_rows(where_ref, random_refs, layer, h, rows, ways, local, kw, e, blocks)
        qa = (q * head_mask(h * HD, kw) + seen).astype(BF16)
        vh = vt[shift + h * HD : shift + (h + 1) * HD]
        cells = []
        sums = []
        for c in range(0, rows, chunk):
            scores = nt(k, qa[c : c + chunk])
            top = jnp.max(scores, axis=0, keepdims=True)
            p = jnp.exp(scores - top)
            total = jnp.sum(p, axis=0, keepdims=True)
            cells.append(nn(vh, p.astype(BF16)) / total)
            sums.append(top + jnp.log(total))
        lines.append(jnp.concatenate(cells, axis=1))
        totals.append(jnp.concatenate(sums, axis=1))
    total_out[...] = jnp.concatenate(totals + [jnp.zeros((8 - heads, rows), F32)], axis=0)
    total_out.send()
    mixed = jnp.concatenate(lines, axis=0).T.astype(BF16)
    mixed_out[...] = mixed
    mixed_out.send()
    for half, part in enumerate(row_halves(rows)):
        whole[part] = nt(mixed[part], w_ref[...]).astype(BF16)
        send_parts(outs, whole, half)


def attention_back_kernel(
    heads, layer, ways, local, blocks, chunk, where_ref, random_refs, grad_refs, w_ref, mixed_ref,
    q_ref, total_ref, parts, adds, dq_ref, small_ref, outs, half_outs
):
    rows, kw = q_ref.shape
    e = heads * HD
    vw = mixed_ref.shape[1]
    shift = vw - e
    grad = jnp.concatenate([ref[: 2 * local] for ref in grad_refs], axis=0)
    small_ref[...] = total_of([ref.at[2 * local :] for ref in grad_refs])
    mixed_grad = nn(grad, w_ref[:, w_ref.shape[1] - vw :]).astype(BF16).astype(F32)
    product = mixed_grad * mixed_ref[...].astype(F32)
    masks = jnp.concatenate([head_mask(shift + h * HD, vw) for h in range(8)], axis=0)
    inner = lax.dot_general(
        masks, product, (((1,), (1,)), ((), ())),
        preferred_element_type=F32, precision=lax.Precision.HIGHEST,
    )
    q = q_ref[...].astype(F32)
    k = jnp.concatenate([part[:, :kw] for part in parts], axis=0)
    v = jnp.concatenate([part[:, kw:] for part in parts], axis=0)
    kt = k[:, :256].T
    totals = total_ref[...]
    for half_out in half_outs:
        half_out[...] = (adds[0][...].astype(F32) + adds[1][...].astype(F32)).astype(BF16)
        half_out.send()
    dk = None
    dv = None
    lines = []
    for h in range(heads):
        seen = seen_rows(where_ref, random_refs, layer, h, rows, ways, local, kw, e, blocks)
        qm = q * head_mask(h * HD, kw)
        qa = (qm + seen).astype(BF16)
        qm = qm[:, :256].astype(BF16)
        gm = (mixed_grad * head_mask(shift + h * HD, vw)).astype(BF16)
        kh = kt[h * HD : (h + 1) * HD]
        cells = []
        for c in range(0, rows, chunk):
            scores = nt(k, qa[c : c + chunk])
            p = jnp.exp(scores - totals[h : h + 1, c : c + chunk])
            dp = nt(v, gm[c : c + chunk])
            ds = (p * (dp - inner[h : h + 1, c : c + chunk])).astype(BF16)
            dv_term = nn(p.astype(BF16), gm[c : c + chunk])
            dk_term = nn(ds, qm[c : c + chunk])
            dv = dv_term if dv is None else dv + dv_term
            dk = dk_term if dk is None else dk + dk_term
            cells.append(nn(kh, ds))
        lines.append(jnp.concatenate(cells, axis=1))
    lines.append(jnp.zeros((256 - e, rows), F32))
    dq = jnp.concatenate(lines, axis=0).T * HD ** (-0.5)
    dq_ref[...] = dq.astype(BF16)
    start = 0
    for out in outs:
        size = out.shape[0]
        out[:, :256] = dk[start : start + size].astype(BF16)
        out[:, 256:] = dv[start : start + size].astype(BF16)
        start += size


def projection_back_kernel(
    e, dq_ref, own_ref, other_ref, w_ref, triple_ref, sums_ref, outs, whole
):
    vw = own_ref.shape[1] - 256
    width = w_ref.shape[1]
    lead = 2 * e // 128 * 128
    rows = dq_ref.shape[0]
    dq = dq_ref[...]
    dkv = (own_ref[...].astype(F32) + other_ref[...].astype(F32)).astype(BF16).astype(F32)
    dv = dkv[:, 256:]
    head = dq.astype(F32)
    nothing = jnp.zeros((rows, 128), F32)
    triple = jnp.concatenate(
        [head[:, :128], head[:, 128:] + dv[:, :128], dv[:, 128:], dkv[:, :256], nothing], axis=1
    ).astype(BF16)
    triple_ref[...] = triple
    sums_ref[...] = jnp.zeros_like(sums_ref)
    sums_ref[0:1] = jnp.sum(triple.astype(F32), axis=0, keepdims=True)
    for half, part in enumerate(row_halves(rows)):
        whole[part] = nt(triple[part], w_ref[...]).astype(BF16)
        send_parts(outs, whole, half)


def norm(values):
    average = jnp.mean(values, axis=-1, keepdims=True)
    centered = values - average
    spread_now = jnp.mean(centered * centered, axis=-1, keepdims=True)
    inverse = lax.rsqrt(spread_now + EPSILON)
    return (centered * inverse, inverse)


def total_of(terms):
    total = terms[0][...].astype(F32)
    for term in terms[1:]:
        total = total + term[...].astype(F32)
    return total


def first_norm_kernel(x_ref, terms_ref, vec_ref, middle_ref, low_ref, unit_out, inverse_out):
    values = x_ref[...].astype(F32) + total_of(terms_ref) + vec_ref[2:3]
    unit, inverse = norm(values)
    unit_out[...] = unit
    unit_out.send()
    inverse_out[...] = jnp.broadcast_to(inverse, inverse_out.shape)
    inverse_out.send()
    middle = unit * vec_ref[0:1] + vec_ref[4:5]
    middle_ref[...] = middle
    low_ref[...] = middle.astype(BF16)


def valid_rows(where_ref, ways, local):
    position = positions(where_ref, 2 * local, ways, local)
    return (position < where_ref[LENGTH]).astype(F32)


def place_parts(where_ref, early, later, outs):
    half = early.shape[0] // 2
    late_plane = where_ref[PLANE] // 2
    for u in range(2):
        for p in range(2):
            @pl.when(late_plane == u)
            def _(u=u, p=p):
                outs[2 * p + u][...] = early[p * half : (p + 1) * half]

            @pl.when(late_plane != u)
            def _(u=u, p=p):
                outs[2 * p + u][...] = later[p * half : (p + 1) * half]


def norm_back(grad, unit, inverse, gain):
    scaled = grad * gain
    return inverse * (
        scaled
        - jnp.mean(scaled, axis=-1, keepdims=True)
        - unit * jnp.mean(scaled * unit, axis=-1, keepdims=True)
    )


def second_norm(ways, where_ref, middle_ref, terms_ref, vec_ref):
    unit, inverse = norm(middle_ref[...] + total_of(terms_ref) + vec_ref[3:4])
    result = unit * vec_ref[1:2] + vec_ref[5:6]
    valid = valid_rows(where_ref, ways, unit.shape[0] // 2)
    return ((result * valid).astype(BF16), unit, inverse, valid)


def second_back(grad, unit, inverse, vec_ref, second_ref, low_ref, sums_ref):
    second = norm_back(grad, unit, inverse, vec_ref[1:2])
    low_ref[...] = second.astype(BF16)
    second_ref[...] = second
    second_ref.send()
    sums_ref[...] = jnp.zeros_like(sums_ref)
    sums_ref[0:1] = jnp.sum(grad * unit, axis=0, keepdims=True)
    sums_ref[1:2] = jnp.sum(grad, axis=0, keepdims=True)
    sums_ref[2:3] = jnp.sum(second, axis=0, keepdims=True)


def second_norm_kernel(
    ways, where_ref, middle_ref, terms_ref, vec_ref, low_ref, kept, unit_out, inverse_out
):
    low, unit, inverse, _ = second_norm(ways, where_ref, middle_ref, terms_ref, vec_ref)
    low_ref[...] = low
    kept.send(low_ref)
    unit_out[...] = unit
    unit_out.send()
    inverse_out[...] = jnp.broadcast_to(inverse, inverse_out.shape)
    inverse_out.send()


def turn_kernel(
    ways, where_ref, middle_ref, terms_ref, vec_ref, up_ref, _, second_ref, low_ref, sums_ref,
    ahead, kept
):
    low, unit, inverse, valid = second_norm(ways, where_ref, middle_ref, terms_ref, vec_ref)
    kept[...] = low
    kept.send()
    second_back(
        up_ref[...].astype(F32) * valid, unit, inverse, vec_ref, second_ref, low_ref, sums_ref
    )


def between_kernel(
    ways, where_ref, terms_ref, vec_ref, first_ref, unit_ref, inverse_ref, _, second_ref, low_ref,
    sums_ref, ahead, kept
):
    low = (first_ref[...] + total_of(terms_ref)).astype(BF16)
    kept[...] = low
    kept.send()
    grad = low.astype(F32) * valid_rows(where_ref, ways, low.shape[0] // 2)
    second_back(
        grad, unit_ref[...], inverse_ref[:, 0:1], vec_ref, second_ref, low_ref, sums_ref
    )


def first_back_kernel(
    second_ref, terms_ref, vec_ref, before_ref, unit_ref, inverse_ref, _, first_ref, low_ref, ahead
):
    grad = second_ref[...] + total_of(terms_ref)
    unit = unit_ref[...]
    first = norm_back(grad, unit, inverse_ref[:, 0:1], vec_ref[0:1])
    first_ref[...] = first
    rows = first.shape[0]
    low_ref[:rows] = first.astype(BF16)
    before = before_ref[...]
    low_ref[rows:] = jnp.concatenate(
        [jnp.sum(grad * unit, axis=0, keepdims=True), before[0:1],
         jnp.sum(first, axis=0, keepdims=True), before[2:3],
         jnp.sum(grad, axis=0, keepdims=True), before[1:2],
         jnp.zeros((10, first.shape[1]), F32)], axis=0
    ).astype(BF16)


def last_input_kernel(where_ref, first_ref, later_ref, terms, *outs):
    low = (first_ref[...] + total_of(terms)).astype(BF16)
    place_parts(where_ref, low, later_ref[...], outs)


def place_out_kernel(where_ref, *refs):
    parts, out_ref = (refs[:-1], refs[-1])
    odd = where_ref[PLACE] % 2
    for p in range(2):
        for u in range(2):
            m = 2 * jnp.bitwise_xor(where_ref[SECTION], u) + jnp.bitwise_xor(odd, p)
            out_ref[0, m, 0] = parts[2 * p + u][...].astype(F32)


def activation_out_kernel(micro, sub, where_ref, first_ref, last_ref, out_ref, sems):
    local = out_ref.shape[3]
    place = where_ref[PLACE]
    side = place % micro // 2

    def copies(ref):
        result = []
        for m in range(micro):
            source = side * (micro * sub) + m * sub + place // micro
            row = (2 * source + jnp.bitwise_xor(place % 2, m & 1)) * local
            rows = pl.ds(pl.multiple_of(row, local), local)
            result.append(pltpu.make_async_copy(ref.at[rows], out_ref.at[0, m, 0], sems.at[m]))
        return result

    for core, ref in enumerate((first_ref, last_ref)):
        @core_is(where_ref, core)
        def _(ref=ref):
            for copy in copies(ref):
                copy.start()
            for copy in copies(ref):
                copy.wait()


def feed_kernel(
    x_refs, vec_ref, expand_ref, contract_ref, outs, active_out, slope_out, kept, whole
):
    keep(kept, x_refs)
    parts = row_halves(whole.shape[0])
    values = [nn(joined(refs), expand_ref[...]) + vec_ref[6:7] for refs in (x_refs[:2], x_refs[2:])]
    for half, (part, v) in enumerate(zip(parts, values)):
        th = jnp.tanh(v * (GELU_A + GELU_A * GELU_B * (v * v)))
        upper = 0.5 + 0.5 * th
        active = (v * upper).astype(BF16)
        active_out[part] = active
        active_out.send(rows=part)
        slope = upper + v * (1.0 - th * th) * (0.5 * GELU_A + 1.5 * GELU_A * GELU_B * (v * v))
        slope_out[part] = slope.astype(BF16)
        slope_out.send(rows=part)
        whole[part] = nt(active, contract_ref[...]).astype(BF16)
        send_parts(outs, whole, half)


def feed_back_kernel(
    grad_refs, contract_ref, slope_ref, expand_ref, hidden_ref, outs, sums_ref, whole
):
    parts = row_halves(whole.shape[0])
    values = [nn(joined(refs), contract_ref[...]) for refs in (grad_refs[:2], grad_refs[2:])]
    total = jnp.zeros((1, hidden_ref.shape[1]), F32)
    for half, (part, value) in enumerate(zip(parts, values)):
        hidden = (value * slope_ref[part].astype(F32)).astype(BF16)
        hidden_ref[part] = hidden
        hidden_ref.send(rows=part)
        total = total + jnp.sum(hidden.astype(F32), axis=0, keepdims=True)
        whole[part] = nt(hidden, expand_ref[...]).astype(BF16)
        send_parts(outs, whole, half)
    sums_ref[...] = jnp.zeros_like(sums_ref)
    sums_ref[0:1] = total


def feed_pack_kernel(where_ref, hidden_ref, grad_refs, middle_ref, active_ref, *outs):
    expand = tn(middle_ref[...], hidden_ref[...]).astype(BF16)
    contract = tn(joined(grad_refs), active_ref[...]).astype(BF16)

    @core_is(where_ref, 0)
    def _():
        outs[0][...] = expand
        outs[1][...] = contract

    @core_is(where_ref, 1)
    def _():
        outs[0][...] = contract
        outs[1][...] = expand


def attn_pack_kernel(
    step, e, where_ref, triple_ref, grad_refs, norm_ref, unit_ref, pair_ref, x_ref, mixed_ref, *outs
):
    x = x_ref[...]
    width = x.shape[1]
    vw = mixed_ref.shape[1]
    places = width // step
    mine = grad_refs[0].shape[0] - 16
    grad = jnp.concatenate([ref[:mine] for ref in grad_refs], axis=0)
    total = tn(x, triple_ref[...])
    last = total[:, width - vw :] + tn(grad, mixed_ref[...])
    weights = jnp.concatenate([total[:, : width - vw], last], axis=1).astype(BF16)
    small = jnp.concatenate(
        [norm_ref[:6], unit_ref[0:1], pair_ref[0:1], jnp.zeros((8, width), F32)], axis=0
    ).astype(BF16)
    if len(outs) == 1:
        half = step // 2
        for z in range(places):
            for i in range(2):
                begin = z * step + i * half
                outs[0][i, z, :half] = weights[begin : begin + half]
                outs[0][i, z, half:] = small
        return
    for z in range(places):
        k = jnp.bitwise_xor(where_ref[PLACE], z)
        kept = k // 2 == where_ref[SECTION]
        for out, is_mine in zip(outs, (kept, jnp.logical_not(kept))):
            @pl.when(is_mine)
            def _(out=out, k=k, z=z):
                out[k % 2, :step] = weights[z * step : (z + 1) * step]
                out[k % 2, step:] = small


def pair_sum_kernel(mine_ref, other_ref, own_ref, first_out, second_out):
    total = mine_ref[0].astype(F32) + other_ref[0].astype(F32)
    own_ref[...] = total
    first_out[...] = total.astype(BF16)
    first_out.send()
    second_out[...] = (mine_ref[1].astype(F32) + other_ref[1].astype(F32)).astype(BF16)


def attn_out_kernel(
    step, e, c, where_ref, *refs
):
    early, (mine_ref, other_ref), outs = (refs[:-8], refs[-8:-6], refs[-6:])
    projections_ref, output_ref, gain_ref, bias_ref, unit_ref, pair_ref = outs
    width = mine_ref.shape[1]

    def fill(total):
        weights = total[:step]
        small = total[step : step + 8]
        projections_ref[0, 0] = weights[:, :e]
        projections_ref[0, 1] = weights[:, 2 * e : 3 * e]
        projections_ref[0, 2] = pltpu.roll(weights, width - e, 1)[:, :e]
        output_ref[0] = pltpu.roll(weights, e, 1)[:, :e].T
        mine = pltpu.roll(small, lax.rem(width - where_ref[PLACE] * step, width), 1)
        gain_ref[0] = mine[0:2, :step]
        bias_ref[0] = mine[2:6, :step]

        def column(row, head):
            shift = lax.rem(2 * width - head * HD - where_ref[PLACE] * c, width)
            return pltpu.roll(small, shift, 1)[row : row + 1, :c]

        for head in range(unit_ref.shape[0]):
            unit_ref[head] = column(6, head)
        for head in range(pair_ref.shape[1]):
            pair_ref[0, head, 0:1] = column(7, head)
            pair_ref[0, head, 1:2] = column(7, head + e // HD)

    @core_is(where_ref, 0)
    def _():
        total = early[0][...]
        for term in early[1:]:
            total = total + term[...].astype(F32)
        fill(total)

    @core_is(where_ref, 1)
    def _():
        mine = mine_ref[...].astype(F32)
        other = other_ref[...].astype(F32)
        fill(jnp.concatenate([other[: step // 2], mine], axis=0))


def feed_out_kernel(where_ref, first_ref, second_ref, other_ref, expand_ref, contract_ref):
    @core_is(where_ref, 0)
    def _():
        expand_ref[0] = first_ref[...].astype(F32)
        contract_ref[0] = other_ref[...].astype(F32)

    @core_is(where_ref, 1)
    def _():
        expand_ref[0] = other_ref[...].astype(F32)
        contract_ref[0] = second_ref[...].astype(F32)


def swap(x):
    return lax.ppermute(x, "section", [(0, 1), (1, 0)])


def gather_rows(x):
    seats = range(lax.axis_size("tensor"))
    return [x] + [lax.ppermute(x, "tensor", [(i, i ^ k) for i in seats]) for k in seats if k]


def scatter_rows(parts):
    seats = range(lax.axis_size("tensor"))
    return parts[:1] + [
        lax.ppermute(parts[k], "tensor", [(i, i ^ k) for i in seats]) for k in seats if k
    ]


def deal(x, micro, sub):
    section = lax.axis_index("section")
    across = lax.axis_size("dp")
    odd = lax.axis_index("dp") % 2
    got = []
    for p in range(2):
        route = []
        for c in range(2):
            for d in range(across):
                r, dd = (d // micro, d % micro)
                m = 2 * c + (p ^ (dd & 1))
                route.append((c * across + d, (dd >> 1) * across + m * sub + r))
        chosen = 2 * section + (p ^ odd)
        payload = lax.dynamic_index_in_dim(x, chosen, 0, keepdims=False)
        got.append(lax.ppermute(payload, PLACES, route))
    return got


def undeal(parts, micro, sub):
    across = lax.axis_size("dp")
    got = []
    for p in range(2):
        for u in range(2):
            route = []
            for s in range(2):
                for source in range(across):
                    m, r = (source // sub, source % sub)
                    j = p ^ (m & 1)
                    layer = u ^ (m >> 1)
                    route.append((s * across + source, layer * across + r * micro + 2 * s + j))
            got.append(lax.ppermute(parts[2 * p + u], PLACES, route))
    return got


def across_places(x, section, k):
    across = lax.axis_size("dp")
    route = [(section * across + d, d ^ k) for d in range(across)]
    return lax.ppermute(x, PLACES, route)


def together(*values):
    return lax.optimization_barrier(values)


def after(x, token):
    return lax.optimization_barrier((x, token))[0]


def body(
    tokens,
    cotangent,
    lengths,
    random_blocks,
    projections,
    query_value_bias,
    output_weight,
    expand_weight,
    expand_bias,
    contract_weight,
    norm_gains,
    row_biases,
):
    section = lax.axis_index("section")
    place = lax.axis_index("dp")
    seat = lax.axis_index("tensor")
    across = lax.axis_size("dp")
    ways = lax.axis_size("tensor")
    micro = tokens.shape[0]
    sub = across // micro
    plane = place // sub
    share = place % sub
    local = tokens.shape[2]
    width = tokens.shape[3]
    e = projections.shape[3]
    heads = e // HD
    units = expand_weight.shape[2]
    step = projections.shape[2]
    c = query_value_bias.shape[3]
    mine = 2 * local
    rows = mine * ways
    keys = rows * 2 * sub
    blocks = keys // BLOCK
    kw = -(-(e + blocks + 1) // 128) * 128
    vw = 256
    whole_tiles = step % 32 == 0
    start = (share * micro + 2 * section) * ways * local
    length = lax.dynamic_index_in_dim(lengths[:, 0], plane, 0, keepdims=False)
    where = jnp.stack([section, place, plane, seat, start, length, plane % 2, 0]).astype(jnp.int32)
    random_other = swap(random_blocks)

    attn_keep, attn_send, feed_keep, feed_send = call(
        prepare_kernel,
        [sds((step // 2 + 16, 4 * e), BF16)] * 2 + [sds((step, units), BF16)] * 2,
        Far(projections), Far(output_weight), Far(expand_weight),
        Far(contract_weight.transpose(0, 2, 1)), Far(query_value_bias.transpose(0, 2, 1, 3)),
        Far(expand_bias), Far(norm_gains), Far(row_biases),
        scratch=[pltpu.VMEM((step, 4 * e), BF16), pltpu.VMEM((16, 4 * e), F32)],
    )
    x = deal(tokens[:, 0], micro, sub)
    upstream = deal(after(cotangent[:, 0], x[1]), micro, sub)
    x = jnp.concatenate(x, axis=0)
    feed_send, x = together(feed_send, x)
    attn_traded = swap(attn_send)
    feed_traded = swap(feed_send)
    attn_all = []
    feed_all = []
    for l in range(2):
        own = section == l
        whole = lax.all_gather(jnp.where(own, attn_keep, attn_traded), PLACES, axis=0, tiled=True)
        attn_all.append(whole.reshape(2, across, step // 2 + 16, 4 * e))
        whole = lax.all_gather(jnp.where(own, feed_keep, feed_traded), PLACES, axis=0, tiled=True)
        feed_all.append(whole.reshape(2, width, units))

    if not whole_tiles:
        attn_flat = [
            whole[:, :, : step // 2].transpose(1, 0, 2, 3).reshape(width, 4 * e)
            for whole in attn_all
        ]
    def small_rows(l):
        if not whole_tiles:
            return attn_all[l][0, :, step // 2 :]
        cuts = [((0, z, pl.ds(step // 2, 16)), (z,)) for z in range(across)]
        return Far(attn_all[l], (across, 16, 4 * e), cuts)

    def attn_weight(l, first, size, into=None):
        lanes = pl.ds(first, size)
        if not whole_tiles:
            return Far(attn_flat[l], (width, size), [((slice(None), lanes), ())], into=into)
        half = step // 2
        cuts = [
            ((i, z, pl.ds(0, half), lanes), (pl.ds(z * step + i * half, half),))
            for z in range(across)
            for i in range(2)
        ]
        return Far(attn_all[l], (width, size), cuts, into=into)

    def feed_weight(l, i, into=None):
        return Far(feed_all[l], (width, units), [((i,), ())], into=into)

    def all_parts(own):
        pair = [own, swap(own)]
        if sub == 1:
            return pair
        groups = [[m * sub + r for r in range(sub)] for m in range(micro)]
        return [
            lax.all_gather(
                jnp.concatenate(pair, axis=0), "dp", axis=0, tiled=True, axis_index_groups=groups
            )
        ]

    def own_parts(parts):
        if sub == 1:
            return parts
        groups = [[m * sub + r for r in range(sub)] for m in range(micro)]
        total = lax.psum_scatter(
            parts[0], "dp", scatter_dimension=0, tiled=True, axis_index_groups=groups
        )
        return [total[:rows], total[rows:]]

    chunk = min(rows, 512)
    near_rows = sds((mine, width), BF16)
    exchanged = [near_rows] + [Far(near_rows, plain=True)] * (ways - 1)
    exchanged_back = [Far(near_rows, plain=True)] * ways
    whole = pltpu.VMEM((rows, width), BF16)
    near_f32 = sds((mine, width), F32)
    turn_outs = [Far(near_f32), near_rows, sds((8, width), F32), sds((width, units), BF16)]
    far_unit = [Far(sds((mine, width), F32)), Far(sds((mine, 128), F32))]

    saved = []
    vectors = []
    for l in range(2):
        x_all = gather_rows(x)
        q, kv, vec, x_kept, q_kept, kv_kept = call(
            partial(qkv_kernel, ways, local, blocks, c, e),
            [sds((rows, kw), BF16), sds((rows, kw + vw), BF16), sds((8, width), F32),
             Far(sds((rows, width), BF16), plain=True, parts=ways),
             Far(sds((rows, kw), BF16), plain=True),
             Far(sds((rows, kw + vw), BF16), plain=True)],
            where, x_all, small_rows(l), attn_weight(l, 0, 4 * e),
            flops=6 * rows * width * 256,
        )
        vectors.append(vec)
        if l == 0:
            kv, *upstream = together(kv, *upstream)
            upstream = jnp.concatenate(upstream, axis=0)
        parts = all_parts(kv)
        attended, mixed, totals, others = call(
            partial(attention_kernel, heads, l, ways, local, blocks, chunk),
            [exchanged, Far(sds((rows, vw), BF16)), Far(sds((8, rows), F32)),
             [Far(sds(part.shape, BF16), plain=True) for part in parts[1:]]],
            where, [random_blocks, random_other], q, attn_weight(l, 4 * e - vw, vw), parts,
            flops=4 * rows * keys * kw, limit=24, scratch=[whole],
        )
        parts_kept = [kv_kept, others[0]] if sub == 1 else parts
        terms = scatter_rows(attended)
        middle, middle_low, unit1, inverse1 = call(
            first_norm_kernel, [sds((mine, width), F32), near_rows] + far_unit, x, terms, vec
        )
        middle_all = gather_rows(middle_low)
        fed, active, slope, middle_kept = call(
            feed_kernel,
            [exchanged, Far(sds((rows, units), BF16), parts=2),
             Far(sds((rows, units), BF16), parts=2),
             Far(sds((rows, width), BF16), plain=True, parts=ways)],
            middle_all, vec, feed_weight(l, 0), feed_weight(l, 1),
            flops=4 * rows * width * units, scratch=[whole],
        )
        terms = scatter_rows(fed)
        if l == 0:
            x, low_kept, unit2, inverse2 = call(
                partial(second_norm_kernel, ways),
                [near_rows, Far(near_rows, plain=True)] + far_unit,
                where, middle, terms, vec,
            )
            first_rows = lax.all_gather(low_kept, PLACES, axis=0, tiled=True)
        else:
            second, feed_low, second_sums, contract_ahead, last_kept = call(
                partial(turn_kernel, ways), turn_outs + [Far(near_rows)],
                where, middle, terms, vec, upstream, feed_weight(1, 1, into=3),
            )
        saved.append(
            (x_kept, q_kept, parts_kept, mixed, totals, unit1, inverse1, middle_kept, active,
             slope)
        )
        if l == 0:
            norm_kept = (unit2, inverse2)
    last_rows = lax.all_gather(last_kept, PLACES, axis=0, tiled=True)
    feed_parts = [None, None]
    for l in (1, 0):
        vec = vectors[l]
        (x_kept, q_kept, parts_kept, mixed, totals, unit1, inverse1, middle_kept, active,
         slope) = saved[l]
        feed_grad = gather_rows(feed_low)
        if l == 1:
            feed_grad[0], first_rows = together(feed_grad[0], first_rows)
        hidden, fed_back, unit_sums = call(
            feed_back_kernel,
            [Far(sds((rows, units), BF16), parts=2), exchanged_back, sds((8, units), F32)],
            feed_grad, contract_ahead, Far(slope), feed_weight(l, 0),
            flops=4 * rows * width * units, scratch=[whole],
        )
        terms = scatter_rows(fed_back)
        feed_kept, feed_sent = call(
            feed_pack_kernel, [Far(sds((width, units), BF16))] * 2,
            where, Far(hidden), feed_grad, Far(middle_kept), Far(active),
            flops=4 * rows * width * units,
        )
        *terms, feed_sent = together(*terms, feed_sent)
        feed_traded = swap(feed_sent)
        if l == 0:
            terms[0], feed_parts[1] = together(terms[0], feed_parts[1])
        terms[0] = Far(terms[0])
        first_grad, first_low, attn_ahead = call(
            first_back_kernel,
            [Far(near_f32), sds((mine + 16, width), BF16), sds((width, 4 * e), BF16)],
            Far(second), terms, vec, second_sums, Far(unit1), Far(inverse1),
            attn_weight(l, 0, 4 * e, into=2),
        )
        attended_grad = gather_rows(first_low)
        if l == 1:
            attended_grad[0], last_rows = together(attended_grad[0], last_rows)
        adds = [Far(feed_kept), Far(feed_traded)]
        if l == 1:
            feed_traded = after(feed_traded, first_low)
            feed_half = (feed_kept.astype(F32) + feed_traded.astype(F32)).astype(BF16)
            attended_grad[0], feed_half = together(attended_grad[0], feed_half)
            feed_parts[l] = lax.psum_scatter(feed_half, "dp", scatter_dimension=0, tiled=True)
            adds = []
        dq, norm_sums, dkv, feed_half = call(
            partial(attention_back_kernel, heads, l, ways, local, blocks, chunk),
            [sds((rows, 256), BF16), sds((16, width), F32),
             [sds((part.shape[0], 256 + vw), BF16) for part in parts_kept],
             [Far(sds((width, units), BF16))] * (len(adds) // 2)],
            where, [random_blocks, random_other], attended_grad, attn_ahead, Far(mixed),
            Far(q_kept), Far(totals), [Far(part) for part in parts_kept], adds,
            flops=10 * rows * keys * kw, limit=44,
        )
        if l == 0:
            feed_parts[l] = lax.psum_scatter(
                feed_half[0], "dp", scatter_dimension=0, tiled=True
            )
        dkv_own, dkv_other = own_parts(dkv)
        dkv_traded = swap(dkv_other)
        triple, pair_sums, projected = call(
            partial(projection_back_kernel, e),
            [sds((rows, 4 * e), BF16), sds((8, 4 * e), F32), exchanged_back],
            dq, dkv_own, dkv_traded, attn_ahead,
            flops=6 * rows * width * 256, scratch=[whole],
        )
        terms = scatter_rows(projected)
        cut = step if whole_tiles else width
        pieces = width // cut
        traded_pack = l == 0 and across == 4
        pack_outs = [sds((2, cut + 16, 4 * e), BF16)] * 2
        if not traded_pack:
            pack_outs = [sds((2, pieces, cut // 2 + 16, 4 * e), BF16)]
        pack, *sent_pack = call(
            partial(attn_pack_kernel, cut, e), pack_outs,
            where, triple, attended_grad, norm_sums, unit_sums, pair_sums, Far(x_kept),
            Far(mixed),
            flops=8 * rows * width * 256,
        )
        if not whole_tiles:
            pack = split_pack(pack, l == 0, across)
        if l == 1:
            (activations,) = call(
                partial(activation_out_kernel, micro, sub),
                [sds((1, micro, 1, local, width), BF16)],
                where, Raw(first_rows), Raw(last_rows),
                scratch=[pltpu.SemaphoreType.DMA((micro,))],
            )
            *terms, pack, activations = together(*terms, pack, activations)
            attn_part = lax.psum_scatter(
                pack.reshape((-1,) + pack.shape[2:]), PLACES, scatter_dimension=0
            )
            terms[0] = Far(terms[0])
            second, feed_low, second_sums, contract_ahead, later = call(
                partial(between_kernel, ways),
                turn_outs + [Far(near_rows)],
                where, terms, vectors[0], Far(first_grad), Far(norm_kept[0]), Far(norm_kept[1]),
                feed_weight(0, 1, into=3),
            )
        else:
            if traded_pack:
                own, first_sum, second_sum = call(
                    pair_sum_kernel,
                    [sds(pack.shape[1:], F32)] + [Far(sds(pack.shape[1:], BF16))] * 2,
                    pack, swap(sent_pack[0]),
                )
                terms[0], attn_part, own, first_sum, second_sum = together(
                    terms[0], attn_part, own, first_sum, second_sum
                )
                early = [
                    own,
                    across_places(second_sum, 0, 1),
                    across_places(first_sum, 1, 2),
                    across_places(second_sum, 1, 3),
                ]
            else:
                traded = lax.ppermute(pack, "section", [(1, 0)])
                total = (pack.astype(F32) + traded.astype(F32)).astype(BF16)
                early = [
                    lax.psum_scatter(total, "dp", scatter_dimension=0).astype(F32)
                ]
            terms[0] = Far(terms[0])
            places = call(
                last_input_kernel, [sds((local, width), BF16)] * 4,
                where, Far(first_grad), Far(later), terms,
            )
            back_rows = undeal(places, micro, sub)
            feed_parts = list(together(*feed_parts, places[0], early[-1])[:2])

    feed_other = swap(jnp.where(section == 0, feed_parts[1], feed_parts[0]))
    expand_out, contract_out = call(
        feed_out_kernel, [sds((1, step, units), F32)] * 2,
        where, feed_parts[0], feed_parts[1], feed_other,
    )
    attn_other = lax.ppermute(attn_part, "section", [(0, 1)])
    projections_out, output_out, gains_out, biases_out, units_out, pairs_out = call(
        partial(attn_out_kernel, step, e, c),
        [sds((1, 3, step, e), F32), sds((1, e, step), F32), sds((1, 2, step), F32),
         sds((1, 4, step), F32), sds((units // HD, 1, c), F32), sds((1, heads, 2, c), F32)],
        where, *early, attn_part, attn_other,
    )
    back_rows[0], expand_out, contract_out, projections_out = together(
        back_rows[0], expand_out, contract_out, projections_out
    )
    (input_grads,) = call(
        place_out_kernel, [sds((1, micro, 1, local, width), F32)], where, *back_rows
    )
    return (
        activations,
        input_grads,
        projections_out,
        pairs_out.transpose(0, 2, 1, 3),
        output_out,
        expand_out,
        units_out.transpose(1, 0, 2),
        contract_out.transpose(0, 2, 1),
        gains_out,
        biases_out,
    )


def split_pack(pack, relative, across):
    weights = pack[:, 0, :-16].reshape(-1, pack.shape[3])
    small = pack[0, 0, -16:]
    if relative:
        weights = weights.reshape(across, -1, weights.shape[1])
        small = jnp.broadcast_to(small, (across,) + small.shape)
        return jnp.concatenate([weights, small], axis=1)
    weights = weights.reshape(across, 2, -1, pack.shape[3]).transpose(1, 0, 2, 3)
    small = jnp.broadcast_to(small, (2, across, 16, pack.shape[3]))
    return jnp.concatenate([weights, small], axis=2)


def solution(mesh):
    in_specs = (
        P(None, None, ("dp", "tensor"), None),
        P(None, None, ("dp", "tensor"), None),
        P(),
        P("section", "tensor", None, None),
        P("section", None, "dp", "tensor"),
        P("section", None, "tensor", "dp"),
        P("section", "tensor", "dp"),
        P("section", "dp", "tensor"),
        P("section", "tensor", "dp"),
        P("section", "tensor", "dp"),
        P("section", None, "dp"),
        P("section", None, "dp"),
    )
    out_specs = (
        P("section", None, None, ("dp", "tensor"), None),
        P("section", None, None, ("dp", "tensor"), None),
        P("section", None, "dp", "tensor"),
        P("section", None, "tensor", "dp"),
        P("section", "tensor", "dp"),
        P("section", "dp", "tensor"),
        P("section", "tensor", "dp"),
        P("section", "tensor", "dp"),
        P("section", None, "dp"),
        P("section", None, "dp"),
    )
    return jax.shard_map(body, mesh=mesh, in_specs=in_specs, out_specs=out_specs, check_vma=False)
```

```python
import math
from functools import partial

import jax
import jax.numpy as jnp
from jax import lax
from jax.experimental import pallas as pl
from jax.experimental.pallas import tpu as pltpu
from jax.sharding import PartitionSpec as P

HD = 64
BLOCK = 64
GLOBAL = 2
EPSILON = 1e-12
MASKED = -1e30
GELU_A = 0.7978845608028654
GELU_B = 0.044715
F32 = jnp.float32
BF16 = jnp.bfloat16
MIB = 1 << 20
PLACES = ("section", "dp")


def nt(a, b):
    return lax.dot_general(a, b, (((1,), (1,)), ((), ())), preferred_element_type=F32)


def tn(a, b):
    return lax.dot_general(a, b, (((0,), (0,)), ((), ())), preferred_element_type=F32)


def nn(a, b):
    return jnp.dot(a, b, preferred_element_type=F32)


def sds(shape, dtype):
    return jax.ShapeDtypeStruct(shape, dtype)


class Far:
    def __init__(self, array, shape=None, cuts=None, plain=False, into=None, parts=1):
        self.array = array
        self.shape = array.shape if shape is None else shape
        self.cuts = [((), ())] if cuts is None else cuts
        self.plain = plain
        self.into = into
        self.parts = parts


class Raw:
    def __init__(self, array):
        self.array = array


def at(ref, index):
    return ref.at[index] if index else ref


class Arriving:
    def __init__(self, source, buffer, sems, first, cuts):
        self.buffer = buffer
        self.shape = buffer.shape
        self.copies = [
            pltpu.make_async_copy(at(source, a), at(buffer, b), sems.at[first + i])
            for i, (a, b) in enumerate(cuts)
        ]
        for copy in self.copies:
            copy.start()
        self.there = False

    def settle(self):
        if not self.there:
            for copy in self.copies:
                copy.wait()
            self.there = True

    def __getitem__(self, index):
        self.settle()
        return self.buffer[index]


class Leaving:
    def __init__(self, target, buffer, sems, first):
        self.target = target
        self.buffer = buffer
        self.shape = target.shape
        self.sems = sems
        self.first = first
        self.copies = []

    def __setitem__(self, index, value):
        self.buffer[index] = value

    def send(self, source=None, rows=None):
        target = self.target if rows is None else self.target.at[rows]
        if source is None:
            source = self.buffer if rows is None else self.buffer.at[rows]
        copy = pltpu.make_async_copy(source, target, self.sems.at[self.first + len(self.copies)])
        copy.start()
        self.copies.append(copy)

    def finish(self):
        if not self.copies:
            self.send()
        for copy in self.copies:
            copy.wait()


def flat(groups):
    return [item for group in groups for item in (group if isinstance(group, list) else [group])]


def grouped(items, groups):
    items = iter(items)
    return [
        [next(items) for _ in group] if isinstance(group, list) else next(items)
        for group in groups
    ]


def call(kernel, out_groups, *arg_groups, flops=0, limit=16, scratch=()):
    args = flat(arg_groups)
    outs = flat(out_groups)
    arrays = []
    in_specs = []
    out_specs = []
    out_shapes = []
    buffers = []
    size = 0
    semaphores = 0
    for arg in args:
        if isinstance(arg, Raw):
            arrays.append(pltpu.with_memory_space_constraint(arg.array, pltpu.HBM))
            in_specs.append(pl.BlockSpec(memory_space=pltpu.HBM))
        elif isinstance(arg, Far):
            arrays.append(pltpu.with_memory_space_constraint(arg.array, pltpu.HBM))
            in_specs.append(pl.BlockSpec(memory_space=pltpu.HBM))
            if arg.into is None:
                buffers.append(pltpu.VMEM(arg.shape, arg.array.dtype))
            semaphores += len(arg.cuts)
            size += math.prod(arg.shape) * arg.array.dtype.itemsize
        else:
            arrays.append(arg)
            scalar = arg.dtype == jnp.int32
            in_specs.append(pl.BlockSpec(memory_space=pltpu.SMEM if scalar else pltpu.VMEM))
            size += arg.size * arg.dtype.itemsize
    for out in outs:
        if isinstance(out, Raw):
            out_shapes.append(pltpu.HBM(out.array.shape, out.array.dtype))
            out_specs.append(pl.BlockSpec(memory_space=pltpu.HBM))
        elif isinstance(out, Far):
            out_shapes.append(pltpu.HBM(out.shape, out.array.dtype))
            out_specs.append(pl.BlockSpec(memory_space=pltpu.HBM))
            if not out.plain:
                buffers.append(pltpu.VMEM(out.shape, out.array.dtype))
            semaphores += out.parts
            size += math.prod(out.shape) * out.array.dtype.itemsize
        else:
            out_shapes.append(out)
            out_specs.append(pl.BlockSpec(memory_space=pltpu.VMEM))
            size += out.size * out.dtype.itemsize

    def whole(*refs):
        refs = list(refs)
        ins = refs[: len(args)]
        results = refs[len(args) : len(args) + len(outs)]
        rest = refs[len(args) + len(outs) :]
        sems = rest.pop() if semaphores else None
        given = []
        handed = []
        used = 0
        for arg, ref in zip(args, ins):
            if isinstance(arg, Far):
                buffer = rest.pop(0) if arg.into is None else results[arg.into]
                given.append(Arriving(ref, buffer, sems, used, arg.cuts))
                used += len(arg.cuts)
            else:
                given.append(ref)
        leaving = []
        for out, ref in zip(outs, results):
            if isinstance(out, Far):
                buffer = None if out.plain else rest.pop(0)
                leaving.append(Leaving(ref, buffer, sems, used))
                handed.append(leaving[-1])
                used += out.parts
            else:
                handed.append(ref)
        kernel(*grouped(given, arg_groups), *grouped(handed, out_groups), *rest)
        for item in given:
            if isinstance(item, Arriving):
                item.settle()
        for item in leaving:
            item.finish()

    scratch_shapes = buffers + list(scratch)
    if semaphores:
        scratch_shapes = scratch_shapes + [pltpu.SemaphoreType.DMA((semaphores,))]
    results = pl.pallas_call(
        whole,
        out_shape=tuple(out_shapes),
        in_specs=in_specs,
        out_specs=tuple(out_specs),
        scratch_shapes=scratch_shapes,
        compiler_params=pltpu.CompilerParams(vmem_limit_bytes=limit * MIB),
        cost_estimate=pl.CostEstimate(flops=flops, bytes_accessed=size, transcendentals=0),
    )(*arrays)
    return grouped(results, out_groups)


SECTION, PLACE, PLANE, SEAT, START, LENGTH, FLIP = range(7)


def positions(where_ref, count, ways, local):
    row = lax.broadcasted_iota(jnp.int32, (count, 1), 0)
    group = jnp.bitwise_xor(row // local % 2, where_ref[FLIP])
    seat = jnp.bitwise_xor(row // (2 * local), where_ref[SEAT])
    return where_ref[START] + group * (ways * local) + seat * local + row % local


def row_halves(rows):
    return [slice(begin, begin + rows // 2) for begin in (0, rows // 2)]


def send_parts(outs, whole, half):
    count = len(outs) // 2
    mine = whole.shape[0] // len(outs)
    for k in range(half * count, (half + 1) * count):
        if isinstance(outs[k], Leaving):
            outs[k].send(whole.at[pl.ds(k * mine, mine)])
        else:
            outs[k][...] = whole[k * mine : (k + 1) * mine]


def joined(refs):
    return jnp.concatenate([ref[...] for ref in refs], axis=0)


def keep(out, refs):
    size = refs[0].shape[0]
    for k, ref in enumerate(refs):
        out.send(ref, pl.ds(k * size, size))


def core_is(where_ref, core):
    return pl.when(where_ref[SECTION] == core)


def prepare_kernel(
    projections_ref, output_ref, expand_ref, contract_ref, pair_ref, unit_ref,
    gain_ref, bias_ref, attn_keep, attn_send, keep_out, send_out, whole, small
):
    step, e = projections_ref.shape[2:]
    heads, _, c = pair_ref.shape[1:]
    half = step // 2
    whole[:, :e] = projections_ref[0, 0]
    whole[:, e : 2 * e] = projections_ref[0, 2]
    whole[:, 2 * e : 3 * e] = projections_ref[0, 1]
    whole[:, 3 * e :] = output_ref[0].T
    small[...] = jnp.zeros_like(small)
    small[0:2, :step] = gain_ref[0].astype(F32)
    small[2:6, :step] = bias_ref[0].astype(F32)
    small[: unit_ref.shape[1], 256 : 256 + c] = unit_ref[0].astype(F32)
    for i in range(heads):
        small[i : i + 1, 384 : 384 + c] = pair_ref[0, i, 0:1].astype(F32)
        small[i : i + 1, 512 : 512 + c] = pair_ref[0, i, 1:2].astype(F32)
    attn_keep[half:] = small[...].astype(BF16)
    attn_send[half:] = small[...].astype(BF16)
    expand = expand_ref[0]
    contract = contract_ref[0]
    section = lax.axis_index("section")

    @pl.when(section == 0)
    def _():
        attn_keep[:half] = whole[:half]
        attn_send[:half] = whole[half:]
        keep_out[...] = expand
        send_out[...] = contract

    @pl.when(section == 1)
    def _():
        attn_keep[:half] = whole[half:]
        attn_send[:half] = whole[:half]
        keep_out[...] = contract
        send_out[...] = expand


def unpack(c, e, raw_ref, vec_ref):
    places = raw_ref.shape[0]
    width = vec_ref.shape[1]
    w = width // places

    def of_heads(rows, lanes, z):
        source = lax.broadcasted_iota(jnp.int32, (128, lanes), 0)
        target = lax.broadcasted_iota(jnp.int32, (128, lanes), 1)
        repeat = ((target % c == source) & (source < c)).astype(F32).astype(BF16)
        spread_rows = nn(rows, repeat)
        head = lax.broadcasted_iota(jnp.int32, spread_rows.shape, 0)
        lane = lax.broadcasted_iota(jnp.int32, spread_rows.shape, 1)
        keep = (lane // HD == head) & (lane % HD // c == z)
        return jnp.sum(jnp.where(keep, spread_rows, 0.0), axis=0, keepdims=True)

    norms = jnp.zeros((16, width), F32)
    units = jnp.zeros((1, width), F32)
    queries = jnp.zeros((1, 256), F32)
    values = jnp.zeros((1, 256), F32)
    for z in range(places):
        rows = raw_ref[z]
        source = lax.broadcasted_iota(jnp.int32, (256, width), 0)
        target = lax.broadcasted_iota(jnp.int32, (256, width), 1)
        move = ((target == source + z * w) & (source < w)).astype(F32).astype(BF16)
        norms = norms + nn(rows[:, :256], move)
        units = units + of_heads(rows[:, 256:384], width, z)
        queries = queries + of_heads(rows[:, 384:512], 256, z)
        values = values + of_heads(rows[:, 512:640], 256, z)
    vec_ref[...] = norms[:8]
    vec_ref[6:7] = units
    lane = lax.broadcasted_iota(jnp.int32, (1, 256), 1)
    queries = jnp.where(lane < e, queries, 0.0)
    values = jnp.where(lane < e, values, 0.0)
    return (queries, pltpu.roll(values, 256 - e, 1))


def qkv_kernel(
    ways, local, blocks, c, e, where_ref, x_refs, raw_ref, w_ref, q_ref, kv_ref, vec_ref, *kept
):
    kw = q_ref.shape[1]
    vw = kv_ref.shape[1] - kw
    x = joined(x_refs)
    keep(kept[0], x_refs)
    query_bias, value_bias = unpack(c, e, raw_ref, vec_ref)
    lead = 2 * e // 128 * 128
    q = (nn(x, w_ref[:, :256]) + query_bias).astype(BF16).astype(F32) * HD ** (-0.5)
    lane = lax.broadcasted_iota(jnp.int32, (1, 256), 1)
    q = jnp.where(lane < e, q, 0.0).astype(BF16)
    q_ref[:, :256] = q
    if kw > 256:
        q_ref[:, 256:] = jnp.zeros((q.shape[0], kw - 256), BF16)
    kept[1].send(q_ref)
    position = positions(where_ref, x.shape[0], ways, local)
    block = position // BLOCK
    lane = lax.broadcasted_iota(jnp.int32, (1, kw), 1)
    hidden = (position >= where_ref[LENGTH]) & (lane == e + blocks)
    tail = jnp.where(lane == e + block, 1.0, jnp.where(hidden, MASKED, 0.0))
    k = nn(x, w_ref[:, lead : lead + 256])
    if kw > 256:
        k = jnp.concatenate([k, jnp.zeros((k.shape[0], kw - 256), F32)], axis=1)
    kv_ref[:, :kw] = jnp.where(lane < e, k, tail).astype(BF16)
    kv_ref[:, kw:] = (nn(x, w_ref[:, 128 : 128 + vw]) + value_bias).astype(BF16)
    kept[2].send(kv_ref)


def head_mask(first, lanes):
    lane = lax.broadcasted_iota(jnp.int32, (1, lanes), 1)
    return ((lane >= first) & (lane < first + HD)).astype(F32)


def seen_rows(where_ref, random_refs, layer, h, rows, ways, local, kw, e, blocks):
    lane = lax.broadcasted_iota(jnp.int32, (1, kw), 1)
    key = lane - e
    parts = []
    for g in range(rows // local):
        group = jnp.bitwise_xor(g % 2, where_ref[FLIP])
        seat = jnp.bitwise_xor(g // 2, where_ref[SEAT])
        position = where_ref[START] + group * (ways * local) + seat * local
        block = position // BLOCK
        seen = (key < GLOBAL) | (jnp.abs(key - block) <= 1) | (block < GLOBAL)
        for i in range(random_refs[0].shape[3]):
            picked = [ref[0, h, block, i] for ref in random_refs]
            seen = seen | (key == jnp.where(where_ref[SECTION] == layer, *picked))
        hidden = (key >= 0) & (key < blocks) & jnp.logical_not(seen)
        line = jnp.where(key == blocks, 1.0, jnp.where(hidden, MASKED, 0.0))
        parts.append(jnp.broadcast_to(line, (local, kw)))
    return jnp.concatenate(parts, axis=0)


def attention_kernel(
    heads, layer, ways, local, blocks, chunk, where_ref, random_refs, q_ref, w_ref, parts,
    outs, mixed_out, total_out, kept, whole
):
    rows, kw = q_ref.shape
    e = heads * HD
    vw = parts[0].shape[1] - kw
    shift = vw - e
    for out, part in zip(kept, parts[1:]):
        out.send(part)
    k = jnp.concatenate([part[:, :kw] for part in parts], axis=0)
    vt = jnp.concatenate([part[:, kw:] for part in parts], axis=0).T
    q = q_ref[...].astype(F32)
    lines = [jnp.zeros((shift, rows), F32)]
    totals = []
    for h in range(heads):
        seen = seen_rows(where_ref, random_refs, layer, h, rows, ways, local, kw, e, blocks)
        qa = (q * head_mask(h * HD, kw) + seen).astype(BF16)
        vh = vt[shift + h * HD : shift + (h + 1) * HD]
        cells = []
        sums = []
        for c in range(0, rows, chunk):
            scores = nt(k, qa[c : c + chunk])
            top = jnp.max(scores, axis=0, keepdims=True)
            p = jnp.exp(scores - top)
            total = jnp.sum(p, axis=0, keepdims=True)
            cells.append(nn(vh, p.astype(BF16)) / total)
            sums.append(top + jnp.log(total))
        lines.append(jnp.concatenate(cells, axis=1))
        totals.append(jnp.concatenate(sums, axis=1))
    total_out[...] = jnp.concatenate(totals + [jnp.zeros((8 - heads, rows), F32)], axis=0)
    total_out.send()
    mixed = jnp.concatenate(lines, axis=0).T.astype(BF16)
    mixed_out[...] = mixed
    mixed_out.send()
    for half, part in enumerate(row_halves(rows)):
        whole[part] = nt(mixed[part], w_ref[...]).astype(BF16)
        send_parts(outs, whole, half)


def attention_back_kernel(
    heads, layer, ways, local, blocks, chunk, where_ref, random_refs, grad_refs, w_ref, mixed_ref,
    q_ref, total_ref, parts, dq_ref, small_ref, outs
):
    rows, kw = q_ref.shape
    e = heads * HD
    vw = mixed_ref.shape[1]
    shift = vw - e
    grad = jnp.concatenate([ref[: 2 * local] for ref in grad_refs], axis=0)
    small_ref[...] = total_of([ref.at[2 * local :] for ref in grad_refs])
    mixed_grad = nn(grad, w_ref[:, w_ref.shape[1] - vw :]).astype(BF16).astype(F32)
    product = mixed_grad * mixed_ref[...].astype(F32)
    masks = jnp.concatenate([head_mask(shift + h * HD, vw) for h in range(8)], axis=0)
    inner = lax.dot_general(
        masks, product, (((1,), (1,)), ((), ())),
        preferred_element_type=F32, precision=lax.Precision.HIGHEST,
    )
    q = q_ref[...].astype(F32)
    k = jnp.concatenate([part[:, :kw] for part in parts], axis=0)
    v = jnp.concatenate([part[:, kw:] for part in parts], axis=0)
    kt = k[:, :256].T
    totals = total_ref[...]
    dk = None
    dv = None
    lines = []
    for h in range(heads):
        seen = seen_rows(where_ref, random_refs, layer, h, rows, ways, local, kw, e, blocks)
        qm = q * head_mask(h * HD, kw)
        qa = (qm + seen).astype(BF16)
        qm = qm[:, :256].astype(BF16)
        gm = (mixed_grad * head_mask(shift + h * HD, vw)).astype(BF16)
        kh = kt[h * HD : (h + 1) * HD]
        cells = []
        for c in range(0, rows, chunk):
            scores = nt(k, qa[c : c + chunk])
            p = jnp.exp(scores - totals[h : h + 1, c : c + chunk])
            dp = nt(v, gm[c : c + chunk])
            ds = (p * (dp - inner[h : h + 1, c : c + chunk])).astype(BF16)
            dv_term = nn(p.astype(BF16), gm[c : c + chunk])
            dk_term = nn(ds, qm[c : c + chunk])
            dv = dv_term if dv is None else dv + dv_term
            dk = dk_term if dk is None else dk + dk_term
            cells.append(nn(kh, ds))
        lines.append(jnp.concatenate(cells, axis=1))
    lines.append(jnp.zeros((256 - e, rows), F32))
    dq = jnp.concatenate(lines, axis=0).T * HD ** (-0.5)
    dq_ref[...] = dq.astype(BF16)
    start = 0
    for out in outs:
        size = out.shape[0]
        out[:, :256] = dk[start : start + size].astype(BF16)
        out[:, 256:] = dv[start : start + size].astype(BF16)
        start += size


def projection_back_kernel(
    e, dq_ref, own_ref, other_ref, w_ref, triple_ref, sums_ref, outs, whole
):
    vw = own_ref.shape[1] - 256
    width = w_ref.shape[1]
    lead = 2 * e // 128 * 128
    rows = dq_ref.shape[0]
    dq = dq_ref[...]
    dkv = (own_ref[...].astype(F32) + other_ref[...].astype(F32)).astype(BF16).astype(F32)
    dv = dkv[:, 256:]
    head = dq.astype(F32)
    nothing = jnp.zeros((rows, 128), F32)
    triple = jnp.concatenate(
        [head[:, :128], head[:, 128:] + dv[:, :128], dv[:, 128:], dkv[:, :256], nothing], axis=1
    ).astype(BF16)
    triple_ref[...] = triple
    sums_ref[...] = jnp.zeros_like(sums_ref)
    sums_ref[0:1] = jnp.sum(triple.astype(F32), axis=0, keepdims=True)
    for half, part in enumerate(row_halves(rows)):
        whole[part] = nt(triple[part], w_ref[...]).astype(BF16)
        send_parts(outs, whole, half)


def norm(values):
    average = jnp.mean(values, axis=-1, keepdims=True)
    centered = values - average
    spread_now = jnp.mean(centered * centered, axis=-1, keepdims=True)
    inverse = lax.rsqrt(spread_now + EPSILON)
    return (centered * inverse, inverse)


def total_of(terms):
    total = terms[0][...].astype(F32)
    for term in terms[1:]:
        total = total + term[...].astype(F32)
    return total


def first_norm_kernel(x_ref, terms_ref, vec_ref, middle_ref, low_ref, unit_out, inverse_out):
    values = x_ref[...].astype(F32) + total_of(terms_ref) + vec_ref[2:3]
    unit, inverse = norm(values)
    unit_out[...] = unit
    unit_out.send()
    inverse_out[...] = jnp.broadcast_to(inverse, inverse_out.shape)
    inverse_out.send()
    middle = unit * vec_ref[0:1] + vec_ref[4:5]
    middle_ref[...] = middle
    low_ref[...] = middle.astype(BF16)


def valid_rows(where_ref, ways, local):
    position = positions(where_ref, 2 * local, ways, local)
    return (position < where_ref[LENGTH]).astype(F32)


def place_parts(where_ref, early, later, outs):
    half = early.shape[0] // 2
    late_plane = where_ref[PLANE] // 2
    for u in range(2):
        for p in range(2):
            @pl.when(late_plane == u)
            def _(u=u, p=p):
                outs[2 * p + u][...] = early[p * half : (p + 1) * half]

            @pl.when(late_plane != u)
            def _(u=u, p=p):
                outs[2 * p + u][...] = later[p * half : (p + 1) * half]


def norm_back(grad, unit, inverse, gain):
    scaled = grad * gain
    return inverse * (
        scaled
        - jnp.mean(scaled, axis=-1, keepdims=True)
        - unit * jnp.mean(scaled * unit, axis=-1, keepdims=True)
    )


def second_norm(ways, where_ref, middle_ref, terms_ref, vec_ref):
    unit, inverse = norm(middle_ref[...] + total_of(terms_ref) + vec_ref[3:4])
    result = unit * vec_ref[1:2] + vec_ref[5:6]
    valid = valid_rows(where_ref, ways, unit.shape[0] // 2)
    return ((result * valid).astype(BF16), unit, inverse, valid)


def second_back(grad, unit, inverse, vec_ref, second_ref, low_ref, sums_ref):
    second = norm_back(grad, unit, inverse, vec_ref[1:2])
    low_ref[...] = second.astype(BF16)
    second_ref[...] = second
    second_ref.send()
    sums_ref[...] = jnp.zeros_like(sums_ref)
    sums_ref[0:1] = jnp.sum(grad * unit, axis=0, keepdims=True)
    sums_ref[1:2] = jnp.sum(grad, axis=0, keepdims=True)
    sums_ref[2:3] = jnp.sum(second, axis=0, keepdims=True)


def second_norm_kernel(
    ways, where_ref, middle_ref, terms_ref, vec_ref, low_ref, kept, unit_out, inverse_out
):
    low, unit, inverse, _ = second_norm(ways, where_ref, middle_ref, terms_ref, vec_ref)
    low_ref[...] = low
    kept.send(low_ref)
    unit_out[...] = unit
    unit_out.send()
    inverse_out[...] = jnp.broadcast_to(inverse, inverse_out.shape)
    inverse_out.send()


def turn_kernel(
    ways, where_ref, middle_ref, terms_ref, vec_ref, up_ref, _, second_ref, low_ref, sums_ref,
    ahead, kept
):
    low, unit, inverse, valid = second_norm(ways, where_ref, middle_ref, terms_ref, vec_ref)
    kept[...] = low
    kept.send()
    second_back(
        up_ref[...].astype(F32) * valid, unit, inverse, vec_ref, second_ref, low_ref, sums_ref
    )


def between_kernel(
    ways, where_ref, terms_ref, vec_ref, first_ref, unit_ref, inverse_ref, _, second_ref, low_ref,
    sums_ref, ahead, kept
):
    low = (first_ref[...] + total_of(terms_ref)).astype(BF16)
    kept[...] = low
    kept.send()
    grad = low.astype(F32) * valid_rows(where_ref, ways, low.shape[0] // 2)
    second_back(
        grad, unit_ref[...], inverse_ref[:, 0:1], vec_ref, second_ref, low_ref, sums_ref
    )


def first_back_kernel(
    second_ref, terms_ref, vec_ref, before_ref, unit_ref, inverse_ref, _, first_ref, low_ref, ahead
):
    grad = second_ref[...] + total_of(terms_ref)
    unit = unit_ref[...]
    first = norm_back(grad, unit, inverse_ref[:, 0:1], vec_ref[0:1])
    first_ref[...] = first
    rows = first.shape[0]
    low_ref[:rows] = first.astype(BF16)
    before = before_ref[...]
    low_ref[rows:] = jnp.concatenate(
        [jnp.sum(grad * unit, axis=0, keepdims=True), before[0:1],
         jnp.sum(first, axis=0, keepdims=True), before[2:3],
         jnp.sum(grad, axis=0, keepdims=True), before[1:2],
         jnp.zeros((10, first.shape[1]), F32)], axis=0
    ).astype(BF16)


def last_input_kernel(where_ref, first_ref, later_ref, terms, *outs):
    low = (first_ref[...] + total_of(terms)).astype(BF16)
    place_parts(where_ref, low, later_ref[...], outs)


def place_out_kernel(where_ref, *refs):
    parts, out_ref = (refs[:-1], refs[-1])
    odd = where_ref[PLACE] % 2
    for p in range(2):
        for u in range(2):
            m = 2 * jnp.bitwise_xor(where_ref[SECTION], u) + jnp.bitwise_xor(odd, p)
            out_ref[0, m, 0] = parts[2 * p + u][...].astype(F32)


def activation_out_kernel(micro, sub, where_ref, first_ref, last_ref, out_ref, sems):
    local = out_ref.shape[3]
    place = where_ref[PLACE]
    side = place % micro // 2

    def copies(ref):
        result = []
        for m in range(micro):
            source = side * (micro * sub) + m * sub + place // micro
            row = (2 * source + jnp.bitwise_xor(place % 2, m & 1)) * local
            rows = pl.ds(pl.multiple_of(row, local), local)
            result.append(pltpu.make_async_copy(ref.at[rows], out_ref.at[0, m, 0], sems.at[m]))
        return result

    for core, ref in enumerate((first_ref, last_ref)):
        @core_is(where_ref, core)
        def _(ref=ref):
            for copy in copies(ref):
                copy.start()
            for copy in copies(ref):
                copy.wait()


def feed_kernel(
    x_refs, vec_ref, expand_ref, contract_ref, outs, active_out, slope_out, kept, whole
):
    keep(kept, x_refs)
    parts = row_halves(whole.shape[0])
    values = [nn(joined(refs), expand_ref[...]) + vec_ref[6:7] for refs in (x_refs[:2], x_refs[2:])]
    for half, (part, v) in enumerate(zip(parts, values)):
        th = jnp.tanh(v * (GELU_A + GELU_A * GELU_B * (v * v)))
        upper = 0.5 + 0.5 * th
        active = (v * upper).astype(BF16)
        active_out[part] = active
        active_out.send(rows=part)
        slope = upper + v * (1.0 - th * th) * (0.5 * GELU_A + 1.5 * GELU_A * GELU_B * (v * v))
        slope_out[part] = slope.astype(BF16)
        slope_out.send(rows=part)
        whole[part] = nt(active, contract_ref[...]).astype(BF16)
        send_parts(outs, whole, half)


def feed_back_kernel(
    grad_refs, contract_ref, slope_ref, expand_ref, hidden_ref, outs, sums_ref, whole
):
    parts = row_halves(whole.shape[0])
    values = [nn(joined(refs), contract_ref[...]) for refs in (grad_refs[:2], grad_refs[2:])]
    total = jnp.zeros((1, hidden_ref.shape[1]), F32)
    for half, (part, value) in enumerate(zip(parts, values)):
        hidden = (value * slope_ref[part].astype(F32)).astype(BF16)
        hidden_ref[part] = hidden
        hidden_ref.send(rows=part)
        total = total + jnp.sum(hidden.astype(F32), axis=0, keepdims=True)
        whole[part] = nt(hidden, expand_ref[...]).astype(BF16)
        send_parts(outs, whole, half)
    sums_ref[...] = jnp.zeros_like(sums_ref)
    sums_ref[0:1] = total


def feed_pack_kernel(where_ref, hidden_ref, grad_refs, middle_ref, active_ref, *outs):
    expand = tn(middle_ref[...], hidden_ref[...]).astype(BF16)
    contract = tn(joined(grad_refs), active_ref[...]).astype(BF16)

    @core_is(where_ref, 0)
    def _():
        outs[0][...] = expand
        outs[1][...] = contract

    @core_is(where_ref, 1)
    def _():
        outs[0][...] = contract
        outs[1][...] = expand


def attn_pack_kernel(
    step, e, where_ref, triple_ref, grad_refs, norm_ref, unit_ref, pair_ref, x_ref, mixed_ref, *outs
):
    x = x_ref[...]
    width = x.shape[1]
    vw = mixed_ref.shape[1]
    places = width // step
    mine = grad_refs[0].shape[0] - 16
    grad = jnp.concatenate([ref[:mine] for ref in grad_refs], axis=0)
    total = tn(x, triple_ref[...])
    last = total[:, width - vw :] + tn(grad, mixed_ref[...])
    weights = jnp.concatenate([total[:, : width - vw], last], axis=1).astype(BF16)
    small = jnp.concatenate(
        [norm_ref[:6], unit_ref[0:1], pair_ref[0:1], jnp.zeros((8, width), F32)], axis=0
    ).astype(BF16)
    if len(outs) == 1:
        half = step // 2
        for z in range(places):
            for i in range(2):
                begin = z * step + i * half
                outs[0][i, z, :half] = weights[begin : begin + half]
                outs[0][i, z, half:] = small
        return
    for z in range(places):
        k = jnp.bitwise_xor(where_ref[PLACE], z)
        kept = k // 2 == where_ref[SECTION]
        for out, is_mine in zip(outs, (kept, jnp.logical_not(kept))):
            @pl.when(is_mine)
            def _(out=out, k=k, z=z):
                out[k % 2, :step] = weights[z * step : (z + 1) * step]
                out[k % 2, step:] = small


def pair_sum_kernel(mine_ref, other_ref, own_ref, first_out, second_out):
    total = mine_ref[0].astype(F32) + other_ref[0].astype(F32)
    own_ref[...] = total
    first_out[...] = total.astype(BF16)
    first_out.send()
    second_out[...] = (mine_ref[1].astype(F32) + other_ref[1].astype(F32)).astype(BF16)


def attn_out_kernel(
    step, e, c, where_ref, *refs
):
    early, (mine_ref, other_ref), outs = (refs[:-8], refs[-8:-6], refs[-6:])
    projections_ref, output_ref, gain_ref, bias_ref, unit_ref, pair_ref = outs
    width = mine_ref.shape[1]

    def fill(total):
        weights = total[:step]
        small = total[step : step + 8]
        projections_ref[0, 0] = weights[:, :e]
        projections_ref[0, 1] = weights[:, 2 * e : 3 * e]
        projections_ref[0, 2] = pltpu.roll(weights, width - e, 1)[:, :e]
        output_ref[0] = pltpu.roll(weights, e, 1)[:, :e].T
        mine = pltpu.roll(small, lax.rem(width - where_ref[PLACE] * step, width), 1)
        gain_ref[0] = mine[0:2, :step]
        bias_ref[0] = mine[2:6, :step]

        def column(row, head):
            shift = lax.rem(2 * width - head * HD - where_ref[PLACE] * c, width)
            return pltpu.roll(small, shift, 1)[row : row + 1, :c]

        for head in range(unit_ref.shape[0]):
            unit_ref[head] = column(6, head)
        for head in range(pair_ref.shape[1]):
            pair_ref[0, head, 0:1] = column(7, head)
            pair_ref[0, head, 1:2] = column(7, head + e // HD)

    @core_is(where_ref, 0)
    def _():
        total = early[0][...]
        for term in early[1:]:
            total = total + term[...].astype(F32)
        fill(total)

    @core_is(where_ref, 1)
    def _():
        mine = mine_ref[...].astype(F32)
        other = other_ref[...].astype(F32)
        fill(jnp.concatenate([other[: step // 2], mine], axis=0))


def feed_out_kernel(where_ref, first_ref, second_ref, other_ref, expand_ref, contract_ref):
    @core_is(where_ref, 0)
    def _():
        expand_ref[0] = first_ref[...].astype(F32)
        contract_ref[0] = other_ref[...].astype(F32)

    @core_is(where_ref, 1)
    def _():
        expand_ref[0] = other_ref[...].astype(F32)
        contract_ref[0] = second_ref[...].astype(F32)


def swap(x):
    return lax.ppermute(x, "section", [(0, 1), (1, 0)])


def gather_rows(x):
    seats = range(lax.axis_size("tensor"))
    return [x] + [lax.ppermute(x, "tensor", [(i, i ^ k) for i in seats]) for k in seats if k]


def scatter_rows(parts):
    seats = range(lax.axis_size("tensor"))
    return parts[:1] + [
        lax.ppermute(parts[k], "tensor", [(i, i ^ k) for i in seats]) for k in seats if k
    ]


def deal(x, micro, sub):
    section = lax.axis_index("section")
    across = lax.axis_size("dp")
    odd = lax.axis_index("dp") % 2
    got = []
    for p in range(2):
        route = []
        for c in range(2):
            for d in range(across):
                r, dd = (d // micro, d % micro)
                m = 2 * c + (p ^ (dd & 1))
                route.append((c * across + d, (dd >> 1) * across + m * sub + r))
        chosen = 2 * section + (p ^ odd)
        payload = lax.dynamic_index_in_dim(x, chosen, 0, keepdims=False)
        got.append(lax.ppermute(payload, PLACES, route))
    return got


def undeal(parts, micro, sub):
    across = lax.axis_size("dp")
    got = []
    for p in range(2):
        for u in range(2):
            route = []
            for s in range(2):
                for source in range(across):
                    m, r = (source // sub, source % sub)
                    j = p ^ (m & 1)
                    layer = u ^ (m >> 1)
                    route.append((s * across + source, layer * across + r * micro + 2 * s + j))
            got.append(lax.ppermute(parts[2 * p + u], PLACES, route))
    return got


def across_places(x, section, k):
    across = lax.axis_size("dp")
    route = [(section * across + d, d ^ k) for d in range(across)]
    return lax.ppermute(x, PLACES, route)


def together(*values):
    return lax.optimization_barrier(values)


def after(x, token):
    return lax.optimization_barrier((x, token))[0]


def body(
    tokens,
    cotangent,
    lengths,
    random_blocks,
    projections,
    query_value_bias,
    output_weight,
    expand_weight,
    expand_bias,
    contract_weight,
    norm_gains,
    row_biases,
):
    section = lax.axis_index("section")
    place = lax.axis_index("dp")
    seat = lax.axis_index("tensor")
    across = lax.axis_size("dp")
    ways = lax.axis_size("tensor")
    micro = tokens.shape[0]
    sub = across // micro
    plane = place // sub
    share = place % sub
    local = tokens.shape[2]
    width = tokens.shape[3]
    e = projections.shape[3]
    heads = e // HD
    units = expand_weight.shape[2]
    step = projections.shape[2]
    c = query_value_bias.shape[3]
    mine = 2 * local
    rows = mine * ways
    keys = rows * 2 * sub
    blocks = keys // BLOCK
    kw = -(-(e + blocks + 1) // 128) * 128
    vw = 256
    whole_tiles = step % 32 == 0
    start = (share * micro + 2 * section) * ways * local
    length = lax.dynamic_index_in_dim(lengths[:, 0], plane, 0, keepdims=False)
    where = jnp.stack([section, place, plane, seat, start, length, plane % 2, 0]).astype(jnp.int32)
    random_other = swap(random_blocks)

    attn_keep, attn_send, feed_keep, feed_send = call(
        prepare_kernel,
        [sds((step // 2 + 16, 4 * e), BF16)] * 2 + [sds((step, units), BF16)] * 2,
        Far(projections), Far(output_weight), Far(expand_weight),
        Far(contract_weight.transpose(0, 2, 1)), Far(query_value_bias.transpose(0, 2, 1, 3)),
        Far(expand_bias), Far(norm_gains), Far(row_biases),
        scratch=[pltpu.VMEM((step, 4 * e), BF16), pltpu.VMEM((16, 4 * e), F32)],
    )
    x = deal(tokens[:, 0], micro, sub)
    upstream = deal(after(cotangent[:, 0], x[1]), micro, sub)
    x = jnp.concatenate(x, axis=0)
    x_first = gather_rows(x)
    feed_send = after(feed_send, x_first[1])
    attn_traded = swap(attn_send)
    feed_traded = swap(feed_send)
    attn_all = []
    feed_all = []
    for l in range(2):
        own = section == l
        whole = lax.all_gather(jnp.where(own, attn_keep, attn_traded), PLACES, axis=0, tiled=True)
        attn_all.append(whole.reshape(2, across, step // 2 + 16, 4 * e))
        whole = lax.all_gather(jnp.where(own, feed_keep, feed_traded), PLACES, axis=0, tiled=True)
        feed_all.append(whole.reshape(2, width, units))

    if not whole_tiles:
        attn_flat = [
            whole[:, :, : step // 2].transpose(1, 0, 2, 3).reshape(width, 4 * e)
            for whole in attn_all
        ]
    def small_rows(l):
        if not whole_tiles:
            return attn_all[l][0, :, step // 2 :]
        cuts = [((0, z, pl.ds(step // 2, 16)), (z,)) for z in range(across)]
        return Far(attn_all[l], (across, 16, 4 * e), cuts)

    def attn_weight(l, first, size, into=None):
        lanes = pl.ds(first, size)
        if not whole_tiles:
            return Far(attn_flat[l], (width, size), [((slice(None), lanes), ())], into=into)
        half = step // 2
        cuts = [
            ((i, z, pl.ds(0, half), lanes), (pl.ds(z * step + i * half, half),))
            for z in range(across)
            for i in range(2)
        ]
        return Far(attn_all[l], (width, size), cuts, into=into)

    def feed_weight(l, i, into=None):
        return Far(feed_all[l], (width, units), [((i,), ())], into=into)

    def all_parts(own):
        pair = [own, swap(own)]
        if sub == 1:
            return pair
        groups = [[m * sub + r for r in range(sub)] for m in range(micro)]
        return [
            lax.all_gather(
                jnp.concatenate(pair, axis=0), "dp", axis=0, tiled=True, axis_index_groups=groups
            )
        ]

    def own_parts(parts):
        if sub == 1:
            return parts
        groups = [[m * sub + r for r in range(sub)] for m in range(micro)]
        total = lax.psum_scatter(
            parts[0], "dp", scatter_dimension=0, tiled=True, axis_index_groups=groups
        )
        return [total[:rows], total[rows:]]

    chunk = min(rows, 512)
    near_rows = sds((mine, width), BF16)
    exchanged = [near_rows] + [Far(near_rows, plain=True)] * (ways - 1)
    exchanged_back = [Far(near_rows, plain=True)] * ways
    whole = pltpu.VMEM((rows, width), BF16)
    near_f32 = sds((mine, width), F32)
    turn_outs = [Far(near_f32), near_rows, sds((8, width), F32), sds((width, units), BF16)]
    far_unit = [Far(sds((mine, width), F32)), Far(sds((mine, 128), F32))]

    saved = []
    vectors = []
    for l in range(2):
        x_all = x_first if l == 0 else gather_rows(x)
        q, kv, vec, x_kept, q_kept, kv_kept = call(
            partial(qkv_kernel, ways, local, blocks, c, e),
            [sds((rows, kw), BF16), sds((rows, kw + vw), BF16), sds((8, width), F32),
             Far(sds((rows, width), BF16), plain=True, parts=ways),
             Far(sds((rows, kw), BF16), plain=True),
             Far(sds((rows, kw + vw), BF16), plain=True)],
            where, x_all, small_rows(l), attn_weight(l, 0, 4 * e),
            flops=6 * rows * width * 256,
        )
        vectors.append(vec)
        if l == 0:
            kv, *upstream = together(kv, *upstream)
            upstream = jnp.concatenate(upstream, axis=0)
        parts = all_parts(kv)
        attended, mixed, totals, others = call(
            partial(attention_kernel, heads, l, ways, local, blocks, chunk),
            [exchanged, Far(sds((rows, vw), BF16)), Far(sds((8, rows), F32)),
             [Far(sds(part.shape, BF16), plain=True) for part in parts[1:]]],
            where, [random_blocks, random_other], q, attn_weight(l, 4 * e - vw, vw), parts,
            flops=4 * rows * keys * kw, limit=24, scratch=[whole],
        )
        parts_kept = [kv_kept, others[0]] if sub == 1 else parts
        terms = scatter_rows(attended)
        middle, middle_low, unit1, inverse1 = call(
            first_norm_kernel, [sds((mine, width), F32), near_rows] + far_unit, x, terms, vec
        )
        middle_all = gather_rows(middle_low)
        fed, active, slope, middle_kept = call(
            feed_kernel,
            [exchanged, Far(sds((rows, units), BF16), parts=2),
             Far(sds((rows, units), BF16), parts=2),
             Far(sds((rows, width), BF16), plain=True, parts=ways)],
            middle_all, vec, feed_weight(l, 0), feed_weight(l, 1),
            flops=4 * rows * width * units, scratch=[whole],
        )
        terms = scatter_rows(fed)
        if l == 0:
            x, low_kept, unit2, inverse2 = call(
                partial(second_norm_kernel, ways),
                [near_rows, Far(near_rows, plain=True)] + far_unit,
                where, middle, terms, vec,
            )
            first_rows = lax.all_gather(low_kept, PLACES, axis=0, tiled=True)
        else:
            second, feed_low, second_sums, contract_ahead, last_kept = call(
                partial(turn_kernel, ways), turn_outs + [Far(near_rows)],
                where, middle, terms, vec, upstream, feed_weight(1, 1, into=3),
            )
        saved.append(
            (x_kept, q_kept, parts_kept, mixed, totals, unit1, inverse1, middle_kept, active,
             slope)
        )
        if l == 0:
            norm_kept = (unit2, inverse2)
    last_rows = lax.all_gather(last_kept, PLACES, axis=0, tiled=True)
    feed_parts = [None, None]
    for l in (1, 0):
        vec = vectors[l]
        (x_kept, q_kept, parts_kept, mixed, totals, unit1, inverse1, middle_kept, active,
         slope) = saved[l]
        feed_grad = gather_rows(feed_low)
        if l == 1:
            feed_grad[0], first_rows = together(feed_grad[0], first_rows)
        hidden, fed_back, unit_sums = call(
            feed_back_kernel,
            [Far(sds((rows, units), BF16), parts=2), exchanged_back, sds((8, units), F32)],
            feed_grad, contract_ahead, Far(slope), feed_weight(l, 0),
            flops=4 * rows * width * units, scratch=[whole],
        )
        terms = scatter_rows(fed_back)
        feed_kept, feed_sent = call(
            feed_pack_kernel, [Far(sds((width, units), BF16))] * 2,
            where, Far(hidden), feed_grad, Far(middle_kept), Far(active),
            flops=4 * rows * width * units,
        )
        *terms, feed_sent = together(*terms, feed_sent)
        feed_traded = swap(feed_sent)
        if l == 0:
            terms[0], feed_parts[1] = together(terms[0], feed_parts[1])
        terms[0] = Far(terms[0])
        first_grad, first_low, attn_ahead = call(
            first_back_kernel,
            [Far(near_f32), sds((mine + 16, width), BF16), sds((width, 4 * e), BF16)],
            Far(second), terms, vec, second_sums, Far(unit1), Far(inverse1),
            attn_weight(l, 0, 4 * e, into=2),
        )
        attended_grad = gather_rows(first_low)
        feed_traded = after(feed_traded, first_low)
        feed_half = (feed_kept.astype(F32) + feed_traded.astype(F32)).astype(BF16)
        if l == 1:
            attended_grad[0], last_rows = together(attended_grad[0], last_rows)
        attended_grad[0], feed_half = together(attended_grad[0], feed_half)
        feed_parts[l] = lax.psum_scatter(feed_half, "dp", scatter_dimension=0, tiled=True)
        dq, norm_sums, dkv = call(
            partial(attention_back_kernel, heads, l, ways, local, blocks, chunk),
            [sds((rows, 256), BF16), sds((16, width), F32),
             [sds((part.shape[0], 256 + vw), BF16) for part in parts_kept]],
            where, [random_blocks, random_other], attended_grad, attn_ahead, Far(mixed),
            Far(q_kept), Far(totals), [Far(part) for part in parts_kept],
            flops=10 * rows * keys * kw, limit=44,
        )
        dkv_own, dkv_other = own_parts(dkv)
        dkv_traded = swap(dkv_other)
        triple, pair_sums, projected = call(
            partial(projection_back_kernel, e),
            [sds((rows, 4 * e), BF16), sds((8, 4 * e), F32), exchanged_back],
            dq, dkv_own, dkv_traded, attn_ahead,
            flops=6 * rows * width * 256, scratch=[whole],
        )
        terms = scatter_rows(projected)
        cut = step if whole_tiles else width
        pieces = width // cut
        traded_pack = l == 0 and across == 4
        pack_outs = [sds((2, cut + 16, 4 * e), BF16)] * 2
        if not traded_pack:
            pack_outs = [sds((2, pieces, cut // 2 + 16, 4 * e), BF16)]
        pack, *sent_pack = call(
            partial(attn_pack_kernel, cut, e), pack_outs,
            where, triple, attended_grad, norm_sums, unit_sums, pair_sums, Far(x_kept),
            Far(mixed),
            flops=8 * rows * width * 256,
        )
        if not whole_tiles:
            pack = split_pack(pack, l == 0, across)
        if l == 1:
            (activations,) = call(
                partial(activation_out_kernel, micro, sub),
                [sds((1, micro, 1, local, width), BF16)],
                where, Raw(first_rows), Raw(last_rows),
                scratch=[pltpu.SemaphoreType.DMA((micro,))],
            )
            *terms, pack, activations = together(*terms, pack, activations)
            attn_part = lax.psum_scatter(
                pack.reshape((-1,) + pack.shape[2:]), PLACES, scatter_dimension=0
            )
            terms[0] = Far(terms[0])
            second, feed_low, second_sums, contract_ahead, later = call(
                partial(between_kernel, ways),
                turn_outs + [Far(near_rows)],
                where, terms, vectors[0], Far(first_grad), Far(norm_kept[0]), Far(norm_kept[1]),
                feed_weight(0, 1, into=3),
            )
        else:
            if traded_pack:
                own, first_sum, second_sum = call(
                    pair_sum_kernel,
                    [sds(pack.shape[1:], F32)] + [Far(sds(pack.shape[1:], BF16))] * 2,
                    pack, swap(sent_pack[0]),
                )
                terms[0], attn_part, own, first_sum, second_sum = together(
                    terms[0], attn_part, own, first_sum, second_sum
                )
                early = [
                    own,
                    across_places(second_sum, 0, 1),
                    across_places(first_sum, 1, 2),
                    across_places(second_sum, 1, 3),
                ]
            else:
                traded = lax.ppermute(pack, "section", [(1, 0)])
                total = (pack.astype(F32) + traded.astype(F32)).astype(BF16)
                early = [
                    lax.psum_scatter(total, "dp", scatter_dimension=0).astype(F32)
                ]
            terms[0] = Far(terms[0])
            places = call(
                last_input_kernel, [sds((local, width), BF16)] * 4,
                where, Far(first_grad), Far(later), terms,
            )
            back_rows = undeal(places, micro, sub)
            feed_parts = list(together(*feed_parts, places[0], early[-1])[:2])

    feed_other = swap(jnp.where(section == 0, feed_parts[1], feed_parts[0]))
    expand_out, contract_out = call(
        feed_out_kernel, [sds((1, step, units), F32)] * 2,
        where, feed_parts[0], feed_parts[1], feed_other,
    )
    attn_other = lax.ppermute(attn_part, "section", [(0, 1)])
    projections_out, output_out, gains_out, biases_out, units_out, pairs_out = call(
        partial(attn_out_kernel, step, e, c),
        [sds((1, 3, step, e), F32), sds((1, e, step), F32), sds((1, 2, step), F32),
         sds((1, 4, step), F32), sds((units // HD, 1, c), F32), sds((1, heads, 2, c), F32)],
        where, *early, attn_part, attn_other,
    )
    back_rows[0], expand_out, contract_out, projections_out = together(
        back_rows[0], expand_out, contract_out, projections_out
    )
    (input_grads,) = call(
        place_out_kernel, [sds((1, micro, 1, local, width), F32)], where, *back_rows
    )
    return (
        activations,
        input_grads,
        projections_out,
        pairs_out.transpose(0, 2, 1, 3),
        output_out,
        expand_out,
        units_out.transpose(1, 0, 2),
        contract_out.transpose(0, 2, 1),
        gains_out,
        biases_out,
    )


def split_pack(pack, relative, across):
    weights = pack[:, 0, :-16].reshape(-1, pack.shape[3])
    small = pack[0, 0, -16:]
    if relative:
        weights = weights.reshape(across, -1, weights.shape[1])
        small = jnp.broadcast_to(small, (across,) + small.shape)
        return jnp.concatenate([weights, small], axis=1)
    weights = weights.reshape(across, 2, -1, pack.shape[3]).transpose(1, 0, 2, 3)
    small = jnp.broadcast_to(small, (2, across, 16, pack.shape[3]))
    return jnp.concatenate([weights, small], axis=2)


def solution(mesh):
    in_specs = (
        P(None, None, ("dp", "tensor"), None),
        P(None, None, ("dp", "tensor"), None),
        P(),
        P("section", "tensor", None, None),
        P("section", None, "dp", "tensor"),
        P("section", None, "tensor", "dp"),
        P("section", "tensor", "dp"),
        P("section", "dp", "tensor"),
        P("section", "tensor", "dp"),
        P("section", "tensor", "dp"),
        P("section", None, "dp"),
        P("section", None, "dp"),
    )
    out_specs = (
        P("section", None, None, ("dp", "tensor"), None),
        P("section", None, None, ("dp", "tensor"), None),
        P("section", None, "dp", "tensor"),
        P("section", None, "tensor", "dp"),
        P("section", "tensor", "dp"),
        P("section", "dp", "tensor"),
        P("section", "tensor", "dp"),
        P("section", "tensor", "dp"),
        P("section", None, "dp"),
        P("section", None, "dp"),
    )
    return jax.shard_map(body, mesh=mesh, in_specs=in_specs, out_specs=out_specs, check_vma=False)
```
